32 devices in a mesh: fsdp: 8 (over z, core), ctx: 4 (over y, x).
Axes of the slice: x: 2, y: 2, z: 4, core: 2. Of those that a mesh axis runs over, the one named last changes fastest.
Arguments:
- tokens: bfloat16 [8, 4096, 1088], P('fsdp', 'ctx'), may hold values from -6 to 6
- cotangent: bfloat16 [8, 4096, 1088], P('fsdp', 'ctx'), may hold values from -6 to 6
- lengths: int32 [8], P('fsdp'), may hold values from 1024 to 4096, as said below
- block_order: int32 [8, 8], P('fsdp'), may hold values from 0 to 7, each once within a row
- ln1_gain: float32 [2, 1088], P(None, 'fsdp'), may hold values from 0.25 to 1.75
- ln1_bias: float32 [2, 1088], P(None, 'fsdp'), may hold values from -1 to 1
- qkv_weight: float32 [2, 1088, 3264], P(None, 'fsdp'), may hold values from -0.1875 to 0.1875
- q_bias: float32 [2, 1088], P(None, 'fsdp'), may hold values from -1.5 to 1.5
- v_bias: float32 [2, 1088], P(None, 'fsdp'), may hold values from -1.5 to 1.5
- out_weight: float32 [2, 1088, 1088], P(None, 'fsdp'), may hold values from -1.5 to 1.5
- out_bias: float32 [2, 1088], P(None, 'fsdp'), may hold values from -1 to 1
- ln2_gain: float32 [2, 1088], P(None, 'fsdp'), may hold values from 0.25 to 1.75
- ln2_bias: float32 [2, 1088], P(None, 'fsdp'), may hold values from -1 to 1
- up_weight: float32 [2, 1088, 4352], P(None, 'fsdp'), may hold values from -0.1875 to 0.1875
- up_bias: float32 [2, 4352], P(None, 'fsdp'), may hold values from -1.5 to 1.5
- down_weight: float32 [2, 4352, 1088], P(None, 'fsdp'), may hold values from -0.09375 to 0.09375
- down_bias: float32 [2, 1088], P(None, 'fsdp'), may hold values from -1 to 1
Outputs:
- activations: bfloat16 [8, 4096, 1088], P('fsdp', 'ctx')
- tokens_grad: float32 [8, 4096, 1088], P('fsdp', 'ctx')
- ln1_gain_grad: float32 [2, 1088], P(None, 'fsdp')
- ln1_bias_grad: float32 [2, 1088], P(None, 'fsdp')
- qkv_weight_grad: float32 [2, 1088, 3264], P(None, 'fsdp')
- q_bias_grad: float32 [2, 1088], P(None, 'fsdp')
- v_bias_grad: float32 [2, 1088], P(None, 'fsdp')
- out_weight_grad: float32 [2, 1088, 1088], P(None, 'fsdp')
- out_bias_grad: float32 [2, 1088], P(None, 'fsdp')
- ln2_gain_grad: float32 [2, 1088], P(None, 'fsdp')
- ln2_bias_grad: float32 [2, 1088], P(None, 'fsdp')
- up_weight_grad: float32 [2, 1088, 4352], P(None, 'fsdp')
- up_bias_grad: float32 [2, 4352], P(None, 'fsdp')
- down_weight_grad: float32 [2, 4352, 1088], P(None, 'fsdp')
- down_bias_grad: float32 [2, 1088], P(None, 'fsdp')
The draws below stay inside these ranges and needn't reach their ends.
Inputs may be any that keep to these rules, and one draw needn't show every extreme that they name: Some slot holds exactly 4096 valid tokens and some exactly 1024; valid tokens are the first lengths of the sequence positions. `block_order`: each row names every block of its slot once.
All inputs are finite; a program needn't handle non-finite values.
Results may differ from the reference program's by a relative error of at most 0.019.
Values may be sent and summed in bfloat16 or wider, within the bound.
A program may use at most 512 MiB of HBM per device.

```python
import jax
import jax.numpy as jnp
from jax import lax

D = 1088
HEADS = 17
HEAD_DIM = 64
FF = 4352
LAYERS = 2
SLOT_LEN = 4096
MIN_LEN = 1024
SLOTS = 8
BLOCK = 512
N_CTX = 4


def draw_lengths(key, part):
    first_key = jax.random.fold_in(key, 11)
    second_key = jax.random.fold_in(key, 12)
    third_key = jax.random.fold_in(key, 13)
    values = jax.random.randint(first_key, (SLOTS,), MIN_LEN, SLOT_LEN + 1)
    longest = jax.random.randint(second_key, (), 0, SLOTS)
    shortest = (longest + 1 + jax.random.randint(third_key, (), 0, SLOTS - 1)) % SLOTS
    indices = jnp.arange(SLOTS)
    values = jnp.where(indices == longest, SLOT_LEN, values)
    values = jnp.where(indices == shortest, MIN_LEN, values)
    return values.astype(jnp.int32)


def shard_levels(key, extent, shards, least, largest):
    def one(position, parts):
        draws = jax.random.uniform(jax.random.fold_in(jax.random.fold_in(key, 6), position), (parts,), jnp.float32, least / len(shards), largest / len(shards))
        return jnp.repeat(jnp.exp(draws), extent[position] // parts).reshape((-1,) + (1,) * (len(extent) - position - 1))

    level = one(*shards[0])
    for cut in shards[1:]:
        level = level * one(*cut)
    return level


def scatter_about(stream_key, extent, width, limit, split=(), kind=jnp.bfloat16):
    loudness = shard_levels(stream_key, extent, split, -0.22, 0.18) if split else 1.0
    values = jax.random.normal(stream_key, extent, jnp.float32) * width * loudness
    return jnp.minimum(jnp.maximum(values, -limit), limit).astype(kind)


def setup_inputs(seed: int = 0) -> dict:
    seeds = jax.random.split(jax.random.key(seed), 18)
    return {
        "tokens": scatter_about(seeds[0], (SLOTS, SLOT_LEN, D), 1.0, 6.0, ((0, 8), (1, 4))),
        "cotangent": scatter_about(seeds[1], (SLOTS, SLOT_LEN, D), 1.0, 6.0, ((0, 8), (1, 4))),
        "lengths": draw_lengths(jax.random.fold_in(seeds[17], 71), 0),
        "block_order": jax.vmap(lambda own: jax.random.permutation(own, 2 * N_CTX))(jax.random.split(seeds[3], SLOTS)).reshape((SLOTS, 2 * N_CTX)).astype(jnp.int32),
        "ln1_gain": jnp.clip(1.0 + 0.15 * jax.random.normal(seeds[4], (LAYERS, D), jnp.float32), 0.25, 1.75),
        "ln1_bias": scatter_about(seeds[5], (LAYERS, D), 0.2, 1.0, ((1, 8),), jnp.float32),
        "qkv_weight": scatter_about(seeds[6], (LAYERS, D, 3 * D), D ** -0.5, 0.1875, ((1, 8),), jnp.float32),
        "q_bias": scatter_about(seeds[7], (LAYERS, D), 0.3, 1.5, ((1, 8),), jnp.float32),
        "v_bias": scatter_about(seeds[8], (LAYERS, D), 0.3, 1.5, ((1, 8),), jnp.float32),
        "out_weight": scatter_about(seeds[9], (LAYERS, D, D), (D // 64) ** -0.5, 1.5, ((1, 8),), jnp.float32),
        "out_bias": scatter_about(seeds[10], (LAYERS, D), 0.2, 1.0, ((1, 8),), jnp.float32),
        "ln2_gain": jnp.clip(1.0 + 0.15 * jax.random.normal(seeds[11], (LAYERS, D), jnp.float32), 0.25, 1.75),
        "ln2_bias": scatter_about(seeds[12], (LAYERS, D), 0.2, 1.0, ((1, 8),), jnp.float32),
        "up_weight": scatter_about(seeds[13], (LAYERS, D, FF), D ** -0.5, 0.1875, ((1, 8),), jnp.float32),
        "up_bias": scatter_about(seeds[14], (LAYERS, FF), 0.3, 1.5, ((1, 8),), jnp.float32),
        "down_weight": scatter_about(seeds[15], (LAYERS, FF, D), FF ** -0.5, 0.09375, ((1, 8),), jnp.float32),
        "down_bias": scatter_about(seeds[16], (LAYERS, D), 0.2, 1.0, ((1, 8),), jnp.float32),
    }


@jax.custom_vjp
def low(v):
    return lax.optimization_barrier(v.astype(jnp.bfloat16)).astype(jnp.float32)

@jax.custom_vjp
def low_back(v):
    return v

def low_keep(v):
    return (low(v), None)

def low_pass(kept, grad):
    return (grad,)

def back_keep(v):
    return (v, None)

def back_low(kept, grad):
    return (low(grad),)
low.defvjp(low_keep, low_pass)
low_back.defvjp(back_keep, back_low)
HIGHEST = lax.Precision.HIGHEST
MASKED = -1000000000.0
EPSILON = 1e-05

def layer_norm(values, norm_gain, norm_bias):
    average = lax.optimization_barrier(jnp.mean(values, axis=-1, keepdims=True))
    centred = values - average
    variance = lax.optimization_barrier(jnp.mean(centred * centred, axis=-1, keepdims=True))
    return centred * lax.rsqrt(variance + EPSILON) * norm_gain + norm_bias

def matmul(left, right):
    return jnp.dot(left, right, precision=HIGHEST, preferred_element_type=jnp.float32)

def attention(queries, key_rows, value_rows, positions, length):
    total_rows = queries.shape[0]
    height = 512 if total_rows % 512 == 0 else total_rows
    factor = HEAD_DIM ** (-0.5)
    query_blocks = queries.reshape(total_rows // height, height, HEADS, HEAD_DIM)
    place_blocks = positions.reshape(total_rows // height, height)

    def one_block(couple):
        query_part, place_part = couple
        scores = jnp.einsum('qhe,khe->hqk', query_part, key_rows, precision=HIGHEST) * factor
        scores = low_back(scores)
        allowed = (positions[None, :] <= place_part[:, None]) & (positions[None, :] < length)
        scores = jnp.where(allowed[None], scores, MASKED)
        soft_out = low(jax.nn.softmax(scores, axis=-1))
        return jnp.einsum('hqk,khe->qhe', soft_out, value_rows, precision=HIGHEST)
    outputs = lax.map(jax.checkpoint(one_block), (query_blocks, place_blocks))
    return outputs.reshape(total_rows, HEADS * HEAD_DIM)

def run_layer(stream, params, positions, length):
    gain_one, bias_one, qkv_w, q_b, v_b, out_w, out_b, gain_two, bias_two, up_w, up_b, down_w, down_b = params
    normed = low(layer_norm(stream, gain_one, bias_one))
    qkv_bias = jnp.concatenate([q_b, jnp.zeros_like(q_b), v_b])
    projected = low(low_back(matmul(normed, qkv_w) + qkv_bias))
    queries = projected[:, :D].reshape(-1, HEADS, HEAD_DIM)
    key_rows = projected[:, D:2 * D].reshape(-1, HEADS, HEAD_DIM)
    value_rows = projected[:, 2 * D:].reshape(-1, HEADS, HEAD_DIM)
    mixed = low(low_back(attention(queries, key_rows, value_rows, positions, length)))
    branch = low_back(matmul(mixed, out_w) + out_b)
    middle = stream + branch
    normed_two = low(layer_norm(middle, gain_two, bias_two))
    hidden_pre = low_back(matmul(normed_two, up_w) + up_b)
    hidden = low(jax.nn.gelu(hidden_pre, approximate=False))
    branch_two = low_back(matmul(hidden, down_w) + down_b)
    return middle + branch_two

def reference(tokens, cotangent, lengths, block_order, ln1_gain, ln1_bias, qkv_weight, q_bias, v_bias, out_weight, out_bias, ln2_gain, ln2_bias, up_weight, up_bias, down_weight, down_bias):
    positions = (block_order[:, :, None] * BLOCK + jnp.arange(BLOCK, dtype=jnp.int32)[None, None, :]).reshape(SLOTS, SLOT_LEN).astype(jnp.int32)
    live = (positions < lengths[:, None]).astype(jnp.float32)
    masters = (ln1_gain, ln1_bias, qkv_weight, q_bias, v_bias, out_weight, out_bias, ln2_gain, ln2_bias, up_weight, up_bias, down_weight, down_bias)

    def forward(inputs, weights):
        rounded = tuple((low(weight) for weight in weights))

        def slot_fn(stream, slot_places, length, slot_live):
            for layer in range(LAYERS):
                params = tuple((weight[layer] for weight in rounded))
                stream = run_layer(stream, params, slot_places, length)
            return stream * slot_live[:, None]
        checked = jax.checkpoint(slot_fn)

        def visit(carry_in, item):
            return (carry_in, checked(item[0], item[1], item[2], item[3]))
        carry_out, outputs = lax.scan(visit, None, (inputs, positions, lengths, live))
        return outputs
    result, pull = jax.vjp(forward, tokens.astype(jnp.float32), masters)
    input_grad, grads = pull(cotangent.astype(jnp.float32))
    return (result.astype(jnp.bfloat16), input_grad, grads[0], grads[1], grads[2], grads[3], grads[4], grads[5], grads[6], grads[7], grads[8], grads[9], grads[10], grads[11], grads[12])
```

```python
import functools
import jax, jax.numpy as jnp
from jax import lax
from jax.experimental import pallas as pl
from jax.experimental.pallas import tpu as pltpu
from jax.sharding import Mesh, PartitionSpec as P
f32=jnp.float32; bf16=jnp.bfloat16
NEG=-1e30
def dot_nt(a,b): return lax.dot_general(a,b,(((1,),(1,)),((),())),preferred_element_type=f32)
def dot_nn(a,b): return lax.dot_general(a,b,(((1,),(0,)),((),())),preferred_element_type=f32)

LOG2E=1.4426950408889634
def split(q,h,low):
    qs=q.astype(f32)*(0.125*LOG2E)
    hi=qs.astype(bf16).astype(f32); lo=qs-hi
    rl=pltpu.roll(lo,64,1)
    c=jnp.where(low,hi,rl) if h==0 else jnp.where(low,rl,hi)
    return c.astype(bf16)
def dup(k,h,low):
    kf=k.astype(f32); rl=pltpu.roll(kf,64,1)
    c=jnp.where(low,kf,rl) if h==0 else jnp.where(low,rl,kf)
    return c.astype(bf16)
def fwd_kernel(inv_ref, nb_ref, x_ref, o_ref, lse_ref, vt, kd, sb, acc, *, B, NB):
    s=pl.program_id(0)
    nb=nb_ref[s]
    lane=lax.broadcasted_iota(jnp.int32,(1,128),1)
    low=lane<64
    def tv(j,_):
        r=pl.multiple_of(inv_ref[s,j]*B,B)
        w=pl.multiple_of(j*B,B)
        t=x_ref[0,pl.ds(r,B),256:384].T
        one=(lax.broadcasted_iota(jnp.int32,(16,B),0)==0).astype(bf16)
        for h in range(2):
            vt[80*h:80*h+64,pl.ds(w,B)]=t[64*h:64*h+64,:]
            vt[80*h+64:80*h+80,pl.ds(w,B)]=one
            kd[h,pl.ds(w,B),:]=dup(x_ref[0,pl.ds(r,B),128:256],h,low)
        return 0
    lax.fori_loop(0,nb,tv,0)
    rr=lax.broadcasted_iota(jnp.int32,(B,B),0)
    cc=lax.broadcasted_iota(jnp.int32,(B,B),1)
    def qblock(i,_):
        r=pl.multiple_of(inv_ref[s,i]*B,B)
        q=x_ref[0,pl.ds(r,B),0:128]
        qh=[split(q,h,low) for h in range(2)]
        acc[...]=jnp.zeros_like(acc)
        def scores(j,slot):
            for h in range(2):
                sb[slot,h]=dot_nt(kd[h,pl.ds(pl.multiple_of(j*B,B),B),:],qh[h])
        def step(j,carry,diag):
            out=[]
            for h in range(2):
                m=carry[h]
                st=sb[j%2,h]
                if diag: st=jnp.where(rr<=cc,st,NEG)
                mn=jnp.maximum(m,jnp.max(st,axis=0,keepdims=True))
                p=jnp.exp2(st-mn)
                al=jnp.exp2(m-mn)
                v=vt[80*h:80*h+80,pl.ds(pl.multiple_of(j*B,B),B)]
                acc[h]=acc[h]*al+dot_nn(v,p.astype(bf16))
                out.append(mn)
            return tuple(out)
        scores(0,0)
        def both(j,c):
            scores(j+1,(j+1)%2)
            return step(j,c,False)
        n=jnp.full((1,B),NEG,f32)
        c=lax.fori_loop(0,i,both,(n,n))
        c=step(i,c,True)
        os=[]
        for h in range(2):
            l=acc[h,64:65,:]
            os.append(acc[h,0:64,:]*(1.0/l))
            lse_ref[0,pl.ds(h,1),pl.ds(r,B)]=c[h]+jnp.log2(l)
        o_ref[0,pl.ds(r,B),:]=jnp.concatenate(os,0).T.astype(bf16)
        return 0
    lax.fori_loop(0,nb,qblock,0)
    def pad(i,_):
        r=pl.multiple_of(inv_ref[s,i]*B,B)
        o_ref[0,pl.ds(r,B),:]=jnp.zeros((B,128),bf16)
        lse_ref[0,:,pl.ds(r,B)]=jnp.zeros((8,B),f32)
        return 0
    lax.fori_loop(nb,NB,pad,0)

def flash_fwd(x,inv,nb,B):
    S,N,_=x.shape
    NB=N//B
    return pl.pallas_call(functools.partial(fwd_kernel,B=B,NB=NB),
      out_shape=(jax.ShapeDtypeStruct((S,N,128),bf16),jax.ShapeDtypeStruct((S,8,N),f32)),
      grid_spec=pltpu.PrefetchScalarGridSpec(num_scalar_prefetch=2,grid=(S,),
        in_specs=[pl.BlockSpec((1,N,384),lambda s,*_:(s,0,0))],
        out_specs=[pl.BlockSpec((1,N,128),lambda s,*_:(s,0,0)),pl.BlockSpec((1,8,N),lambda s,*_:(s,0,0))],
        scratch_shapes=[pltpu.VMEM((160,N),bf16),pltpu.VMEM((2,N,128),bf16),pltpu.VMEM((2,2,B,B),f32),pltpu.VMEM((2,80,B),f32)]),
      compiler_params=pltpu.CompilerParams(vmem_limit_bytes=48<<20),
      cost_estimate=pl.CostEstimate(flops=S*4*N*N*128,bytes_accessed=S*N*1024,transcendentals=S*N*N),
      )(inv,nb,x)

def bwd_kernel(inv_ref, nb_ref, x_ref, o_ref, do_ref, lse_ref, dx_ref, kt, qd, dq, dk, dv, dl, *, B, NB):
    s=pl.program_id(0)
    nb=nb_ref[s]
    lane=lax.broadcasted_iota(jnp.int32,(1,128),1)
    low=lane<64
    hm=(lax.broadcasted_iota(jnp.int32,(8,128),1)//64==lax.broadcasted_iota(jnp.int32,(8,128),0)).astype(bf16)
    def prep(j,_):
        r=pl.multiple_of(inv_ref[s,j]*B,B)
        w=pl.multiple_of(j*B,B)
        kt[:,pl.ds(w,B)]=x_ref[0,pl.ds(r,B),128:256].T
        for h in range(2): qd[h,pl.ds(w,B),:]=split(x_ref[0,pl.ds(r,B),0:128],h,low)
        prod=o_ref[0,pl.ds(r,B),:].astype(f32)*do_ref[0,pl.ds(r,B),:].astype(f32)
        hi=prod.astype(bf16); lo=(prod-hi.astype(f32)).astype(bf16)
        dl[:,pl.ds(w,B)]=dot_nt(hm,hi)+dot_nt(hm,lo)
        dq[:,pl.ds(w,B)]=jnp.zeros((128,B),f32)
        return 0
    lax.fori_loop(0,nb,prep,0)
    rr=lax.broadcasted_iota(jnp.int32,(B,B),0)
    cc=lax.broadcasted_iota(jnp.int32,(B,B),1)
    def kblock(j,_):
        r=pl.multiple_of(inv_ref[s,j]*B,B)
        k=x_ref[0,pl.ds(r,B),128:256]
        v=x_ref[0,pl.ds(r,B),256:384]
        kdh=[dup(k,h,low) for h in range(2)]
        dk[...]=jnp.zeros_like(dk); dv[...]=jnp.zeros_like(dv)
        def step(i,diag):
            ri=pl.multiple_of(inv_ref[s,i]*B,B)
            wi=pl.multiple_of(i*B,B)
            q=x_ref[0,pl.ds(ri,B),0:128]*jnp.asarray(0.125,bf16)
            do=do_ref[0,pl.ds(ri,B),:]
            zero=jnp.zeros_like(q)
            dvs=[];dks=[]
            for h in range(2):
                qh=jnp.where(low,q,zero) if h==0 else jnp.where(low,zero,q)
                doh=jnp.where(low,do,zero) if h==0 else jnp.where(low,zero,do)
                st=dot_nt(kdh[h],qd[h,pl.ds(wi,B),:])
                p=jnp.exp2(st-lse_ref[0,pl.ds(h,1),pl.ds(ri,B)])
                if diag: p=jnp.where(rr<=cc,p,0.0)
                dvs.append(dot_nn(p.astype(bf16),doh))
                dp=dot_nt(v,doh)
                ds=(p*(dp-dl[pl.ds(h,1),pl.ds(wi,B)])).astype(bf16)
                dks.append(dot_nn(ds,qh))
                kh=kt[64*h:64*h+64,pl.ds(pl.multiple_of(j*B,B),B)]
                dq[64*h:64*h+64,pl.ds(wi,B)]+=dot_nn(kh,ds)
            dv[...]+=dvs[0]+dvs[1]
            dk[...]+=dks[0]+dks[1]
        step(j,True)
        def body(i,_):
            step(i,False); return 0
        lax.fori_loop(j+1,nb,body,0)
        dx_ref[0,pl.ds(r,B),128:256]=dk[...].astype(bf16)
        dx_ref[0,pl.ds(r,B),256:384]=dv[...].astype(bf16)
        return 0
    lax.fori_loop(0,nb,kblock,0)
    def fin(i,_):
        r=pl.multiple_of(inv_ref[s,i]*B,B)
        dx_ref[0,pl.ds(r,B),0:128]=(dq[:,pl.ds(pl.multiple_of(i*B,B),B)].T*0.125).astype(bf16)
        return 0
    lax.fori_loop(0,nb,fin,0)
    def pad(i,_):
        r=pl.multiple_of(inv_ref[s,i]*B,B)
        dx_ref[0,pl.ds(r,B),:]=jnp.zeros((B,384),bf16)
        return 0
    lax.fori_loop(nb,NB,pad,0)

def flash_bwd(x,o,do,lse,inv,nb,B):
    S,N,_=x.shape
    NB=N//B
    return pl.pallas_call(functools.partial(bwd_kernel,B=B,NB=NB),
      out_shape=jax.ShapeDtypeStruct((S,N,384),bf16),
      grid_spec=pltpu.PrefetchScalarGridSpec(num_scalar_prefetch=2,grid=(S,),
        in_specs=[pl.BlockSpec((1,N,384),lambda s,*_:(s,0,0)),pl.BlockSpec((1,N,128),lambda s,*_:(s,0,0)),
                  pl.BlockSpec((1,N,128),lambda s,*_:(s,0,0)),pl.BlockSpec((1,8,N),lambda s,*_:(s,0,0))],
        out_specs=pl.BlockSpec((1,N,384),lambda s,*_:(s,0,0)),
        scratch_shapes=[pltpu.VMEM((128,N),bf16),pltpu.VMEM((2,N,128),bf16),pltpu.VMEM((128,N),f32),pltpu.VMEM((B,128),f32),pltpu.VMEM((B,128),f32),pltpu.VMEM((8,N),f32)]),
      compiler_params=pltpu.CompilerParams(vmem_limit_bytes=48<<20),
      cost_estimate=pl.CostEstimate(flops=S*10*N*N*128,bytes_accessed=S*N*2400,transcendentals=S*N*N),
      )(inv,nb,x,o,do,lse)


def one_fwd_kernel(own_ref, q_ref, x_ref, o_ref, lse_ref, vt, sb, acc, *, B, NB):
    nb = own_ref[NB + 2]
    def tv(j,_):
        r=pl.multiple_of(own_ref[j]*B,B)
        t=x_ref[pl.ds(r,B),:].T
        w=pl.multiple_of(j*B,B)
        vt[0:64,pl.ds(w,B)]=t[64:128,:]
        vt[64:80,pl.ds(w,B)]=(lax.broadcasted_iota(jnp.int32,(16,B),0)==0).astype(bf16)
        return 0
    lax.fori_loop(0,nb,tv,0)
    rr=lax.broadcasted_iota(jnp.int32,(B,B),0)
    cc=lax.broadcasted_iota(jnp.int32,(B,B),1)
    for t in range(2):
        i=own_ref[NB+t]
        @pl.when(i>=nb)
        def _():
            o_ref[t*B:(t+1)*B,:]=jnp.zeros((B,64),bf16)
            lse_ref[:,t*B:(t+1)*B]=jnp.zeros((8,B),f32)
        @pl.when(i<nb)
        def _():
            qs=q_ref[t*B:(t+1)*B,:].astype(f32)*(0.125*LOG2E)
            q=qs.astype(bf16)
            ql=(qs-q.astype(f32)).astype(bf16)
            acc[...]=jnp.zeros_like(acc)
            def step(j,m,diag):
                k=x_ref[pl.ds(pl.multiple_of(own_ref[j]*B,B),B),0:64]
                st=dot_nt(k,q)+dot_nt(k,ql)
                if diag: st=jnp.where(rr<=cc,st,NEG)
                mn=jnp.maximum(m,jnp.max(st,axis=0,keepdims=True))
                p=jnp.exp2(st-mn)
                al=jnp.exp2(m-mn)
                v=vt[:,pl.ds(pl.multiple_of(j*B,B),B)]
                acc[...]=acc[...]*al+dot_nn(v,p.astype(bf16))
                return mn
            m=lax.fori_loop(0,i,lambda j,m: step(j,m,False),jnp.full((1,B),NEG,f32))
            m=step(i,m,True)
            l=acc[64:65,:]
            o_ref[t*B:(t+1)*B,:]=(acc[0:64,:]*(1.0/l)).T.astype(bf16)
            lse_ref[:,t*B:(t+1)*B]=jnp.broadcast_to(m+jnp.log2(l),(8,B))


def one_fwd(q,x,own,B):
    N=x.shape[0]; R=q.shape[0]; NB=N//B
    full=lambda *_:(0,0)
    return pl.pallas_call(functools.partial(one_fwd_kernel,B=B,NB=NB),
      out_shape=(jax.ShapeDtypeStruct((R,64),bf16),jax.ShapeDtypeStruct((8,R),f32)),
      grid_spec=pltpu.PrefetchScalarGridSpec(num_scalar_prefetch=1,grid=(1,),
        in_specs=[pl.BlockSpec((R,64),full),pl.BlockSpec((N,128),full)],
        out_specs=[pl.BlockSpec((R,64),full),pl.BlockSpec((8,R),full)],
        scratch_shapes=[pltpu.VMEM((80,N),bf16),pltpu.VMEM((B,B),f32),pltpu.VMEM((80,B),f32)]),
      compiler_params=pltpu.CompilerParams(vmem_limit_bytes=48<<20),
      cost_estimate=pl.CostEstimate(flops=4*R*N*128,bytes_accessed=N*256+R*512,transcendentals=R*N),
      )(own,q,x)


def one_bwd_kernel(own_ref, q_ref, x_ref, o_ref, do_ref, lse_ref, dq_ref, dx_ref, dkv, dq, *, B, NB):
    nb = own_ref[NB + 2]
    rr=lax.broadcasted_iota(jnp.int32,(B,B),0)
    cc=lax.broadcasted_iota(jnp.int32,(B,B),1)
    ones=jnp.ones((8,64),bf16)
    dkv[...]=jnp.zeros_like(dkv)
    for t in range(2):
        i=own_ref[NB+t]
        sl=slice(t*B,(t+1)*B)
        @pl.when(i>=nb)
        def _():
            dq_ref[sl,:]=jnp.zeros((B,64),bf16)
        @pl.when(i<nb)
        def _():
            qr=q_ref[sl,:]
            qs=qr.astype(f32)*(0.125*LOG2E)
            q=qs.astype(bf16)
            ql=(qs-q.astype(f32)).astype(bf16)
            qd=qr*jnp.asarray(0.125,bf16)
            do=do_ref[sl,:]
            prod=o_ref[sl,:].astype(f32)*do.astype(f32)
            hi=prod.astype(bf16); lo=(prod-hi.astype(f32)).astype(bf16)
            dl=(dot_nt(ones,hi)+dot_nt(ones,lo))[0:1,:]
            lse=lse_ref[0:1,sl]
            dq[...]=jnp.zeros_like(dq)
            def step(j,diag):
                r=pl.multiple_of(own_ref[j]*B,B)
                k=x_ref[pl.ds(r,B),0:64]
                v=x_ref[pl.ds(r,B),64:128]
                st=dot_nt(k,q)+dot_nt(k,ql)
                p=jnp.exp2(st-lse)
                if diag: p=jnp.where(rr<=cc,p,0.0)
                dp=dot_nt(v,do)
                ds=(p*(dp-dl)).astype(bf16)
                dkv[pl.ds(r,B),64:128]+=dot_nn(p.astype(bf16),do)
                dkv[pl.ds(r,B),0:64]+=dot_nn(ds,qd)
                dq[...]+=dot_nn(k.T,ds)
            def body(j,_):
                step(j,False); return 0
            lax.fori_loop(0,i,body,0)
            step(i,True)
            dq_ref[sl,:]=(dq[...].T*0.125).astype(bf16)
    dx_ref[...]=dkv[...].astype(bf16)


def one_bwd(q,x,o,do,lse,own,B):
    N=x.shape[0]; R=q.shape[0]; NB=N//B
    full=lambda *_:(0,0)
    return pl.pallas_call(functools.partial(one_bwd_kernel,B=B,NB=NB),
      out_shape=(jax.ShapeDtypeStruct((R,64),bf16),jax.ShapeDtypeStruct((N,128),bf16)),
      grid_spec=pltpu.PrefetchScalarGridSpec(num_scalar_prefetch=1,grid=(1,),
        in_specs=[pl.BlockSpec((R,64),full),pl.BlockSpec((N,128),full),pl.BlockSpec((R,64),full),pl.BlockSpec((R,64),full),pl.BlockSpec((8,R),full)],
        out_specs=[pl.BlockSpec((R,64),full),pl.BlockSpec((N,128),full)],
        scratch_shapes=[pltpu.VMEM((N,128),f32),pltpu.VMEM((64,B),f32)]),
      compiler_params=pltpu.CompilerParams(vmem_limit_bytes=48<<20),
      cost_estimate=pl.CostEstimate(flops=10*R*N*128,bytes_accessed=N*512+R*1024,transcendentals=R*N),
      )(own,q,x,o,do,lse)


HEADS = 17
EPSILON = 1e-05
FS = ("zz", "core")


def norm_parts(v):
    mean = jnp.mean(v, axis=-1, keepdims=True)
    c = v - mean
    r = lax.rsqrt(jnp.mean(c * c, axis=-1, keepdims=True) + EPSILON)
    return c * r, r


def norm_back(dn, v, gain):
    xhat, r = norm_parts(v)
    y = dn * gain
    a = jnp.mean(y, axis=-1, keepdims=True)
    b = jnp.mean(y * xhat, axis=-1, keepdims=True)
    return r * (y - a - xhat * b), jnp.sum(dn * xhat, axis=0), jnp.sum(dn, axis=0)


def gelu_parts(u):
    z = jnp.abs(u) * 0.7071067811865476
    t = 1.0 / (1.0 + 0.3275911 * z)
    e = jnp.exp(-z * z)
    poly = t * (0.254829592 + t * (-0.284496736 + t * (1.421413741 + t * (-1.453152027 + t * 1.061405429))))
    half = 0.5 * poly * e
    cdf = jnp.where(u >= 0, 1.0 - half, half)
    return u * cdf, cdf + u * e * 0.3989422804014327


def local(
    tokens, cotangent, lengths, block_order,
    ln1_gain, ln1_bias, qkv_weight, q_bias, v_bias, out_weight, out_bias,
    ln2_gain, ln2_bias, up_weight, up_bias, down_weight, down_bias,
    *, G, S,
):
    slots, rows, width = tokens.shape
    C = lax.axis_size("ctx")
    me = lax.axis_index("ctx")
    group = ("core", "ctx") if S == 2 else ("ctx",)
    N = rows * C
    B = rows // 2
    NB = 2 * C
    L = ln1_gain.shape[0]
    shard = ln1_gain.shape[1]
    HW = G * 128
    x_tokens = tokens[0]

    steps = jnp.arange(NB, dtype=jnp.int32)
    order = block_order[0]
    inverse = jnp.sum(jnp.where(order[None, :] == steps[:, None], steps[None, :], 0), axis=1).astype(jnp.int32)
    count = (lengths + (B - 1)) // B
    meta = jnp.concatenate([inverse, count])
    both = lax.all_gather(meta, "core") if S == 2 else meta[None]
    inv, nb = both[:, :NB], both[:, NB]
    own = jnp.concatenate([inverse, lax.dynamic_slice_in_dim(order, 2 * me, 2, 0), count])
    own_pos = (lax.dynamic_slice_in_dim(order, 2 * me, 2, 0)[:, None] * B + jnp.arange(B, dtype=jnp.int32)).reshape(rows, 1)
    live = (own_pos < lengths[0]).astype(f32)

    vectors = [ln1_gain, ln1_bias, q_bias, v_bias, out_bias, ln2_gain, ln2_bias, down_bias, up_bias]
    vec = jnp.concatenate(vectors, axis=1).astype(bf16)
    vec = lax.all_gather(vec, FS).astype(f32)

    def vector(index, layer):
        if index < 8:
            return vec[:, layer, index * shard:(index + 1) * shard].reshape(-1)
        return vec[:, layer, 8 * shard:].reshape(-1)

    def pack(w):
        n = w.shape[0]
        w = w.reshape(n, 3, HEADS, 64)
        main = w[:, :, :16].reshape(n, 3, G, 128)
        main = jnp.transpose(main, (0, 2, 1, 3)).reshape(n, G * 384)
        tail = jnp.stack([w[:, 1, 16], w[:, 2, 16], w[:, 0, 16]], axis=1).reshape(n, 192)
        return jnp.concatenate([main, tail], axis=1)

    def unpack(w):
        n = w.shape[0]
        main = jnp.transpose(w[:, :G * 384].reshape(n, G, 3, 128), (0, 2, 1, 3)).reshape(n, 3, 1024)
        tail = w[:, G * 384:].reshape(n, 3, 64)
        tail = jnp.stack([tail[:, 2], tail[:, 0], tail[:, 1]], axis=1)
        return jnp.concatenate([main, tail], axis=2).reshape(n, 3 * width)

    def fetch(w):
        return lax.all_gather(w.astype(bf16), FS, axis=0, tiled=True)

    weights = []
    for layer in range(L):
        weights.append((
            fetch(pack(qkv_weight[layer].astype(bf16))),
            fetch(out_weight[layer]),
            fetch(up_weight[layer]),
            fetch(down_weight[layer]),
        ))

    def exchange(x):
        return lax.all_to_all(x, group, 0, 0)

    stream = x_tokens.astype(f32)
    records = []
    for layer in range(L):
        qkv_w, out_w, up_w, down_w = weights[layer]
        xhat, _ = norm_parts(stream)
        n1 = (xhat * vector(0, layer) + vector(1, layer)).astype(bf16)
        q_b, v_b = vector(2, layer), vector(3, layer)
        bias = pack(jnp.concatenate([q_b, jnp.zeros_like(q_b), v_b])[None])[0]
        wide = jnp.einsum("rd,dgc->grc", n1, qkv_w[:, :G * 384].reshape(width, G, 384), preferred_element_type=f32)
        wide = (wide + bias[:G * 384].reshape(G, 1, 384)).astype(bf16)
        tail = (jnp.dot(n1, qkv_w[:, G * 384:], preferred_element_type=f32) + bias[G * 384:]).astype(bf16)
        kv16 = lax.all_gather(tail[:, :128], "ctx", axis=0, tiled=True)
        q16 = tail[:, 128:]
        heads = exchange(wide).reshape(S, N, 384)
        o, lse = flash_fwd(heads, inv, nb, B)
        o16, lse16 = one_fwd(q16, kv16, own, B)
        o_back = exchange(o.reshape(G, rows, 128))
        mixed = jnp.concatenate([jnp.transpose(o_back, (1, 0, 2)).reshape(rows, HW), o16], axis=1)
        m = stream + jnp.dot(mixed, out_w, preferred_element_type=f32) + vector(4, layer)
        xhat2, _ = norm_parts(m)
        n2 = (xhat2 * vector(5, layer) + vector(6, layer)).astype(bf16)
        u = jnp.dot(n2, up_w, preferred_element_type=f32) + vector(8, layer)
        a, slope = gelu_parts(u)
        a = a.astype(bf16)
        slope = slope.astype(bf16)
        records.append((stream, n1, heads, kv16, q16, o, lse, o16, lse16, mixed, m, n2, a, slope))
        stream = m + jnp.dot(a, down_w, preferred_element_type=f32) + vector(7, layer)
    activations = (stream * live).astype(bf16)[None]

    def reduce_fsdp(g):
        return lax.psum_scatter(g.astype(bf16), FS, scatter_dimension=0, tiled=True)

    def reduce_ctx(g):
        t = lax.psum_scatter(g, "ctx", scatter_dimension=0, tiled=True)
        return lax.all_gather(t, "ctx", axis=0, tiled=True).astype(f32)

    grad = cotangent[0].astype(f32) * live
    matrices = [None] * L
    small = [None] * L
    for layer in reversed(range(L)):
        stream_in, n1, heads, kv16, q16, o, lse, o16, lse16, mixed, m, n2, a, slope = records[layer]
        qkv_w, out_w, up_w, down_w = weights[layer]
        gb = grad.astype(bf16)
        d_down_b = jnp.sum(gb.astype(f32), axis=0)
        d_down = reduce_fsdp(jnp.einsum("rf,rd->fd", a, gb, preferred_element_type=f32))
        du = (jnp.einsum("rd,fd->rf", gb, down_w, preferred_element_type=f32) * slope.astype(f32)).astype(bf16)
        d_up_b = jnp.sum(du.astype(f32), axis=0)
        d_up = reduce_fsdp(jnp.einsum("rd,rf->df", n2, du, preferred_element_type=f32))
        dn2 = jnp.einsum("rf,df->rd", du, up_w, preferred_element_type=f32)
        back, d_gain2, d_bias2 = norm_back(dn2, m, vector(5, layer))
        gm = grad + back
        gmb = gm.astype(bf16)
        d_out_b = jnp.sum(gmb.astype(f32), axis=0)
        d_out = reduce_fsdp(jnp.einsum("rd,re->de", mixed, gmb, preferred_element_type=f32))
        d_o = jnp.einsum("re,gce->grc", gmb, out_w[:HW].reshape(G, 128, width), preferred_element_type=f32).astype(bf16)
        d_o16 = jnp.einsum("re,ce->rc", gmb, out_w[HW:], preferred_element_type=f32).astype(bf16)
        d_oh = exchange(d_o).reshape(S, N, 128)
        d_heads = flash_bwd(heads, o, d_oh, lse, inv, nb, B)
        dq16, dkv16 = one_bwd(q16, kv16, o16, d_o16, lse16, own, B)
        dkv16 = lax.psum_scatter(dkv16, "ctx", scatter_dimension=0, tiled=True)
        d_wide = exchange(d_heads.reshape(G, rows, 384))
        d_tail = jnp.concatenate([dkv16.astype(bf16), dq16], axis=1)
        d_row = jnp.concatenate([jnp.transpose(d_wide, (1, 0, 2)).reshape(rows, G * 384), d_tail], axis=1)
        d_qkv = reduce_fsdp(jnp.einsum("rd,rc->dc", n1, d_row, preferred_element_type=f32))
        sums = unpack(jnp.sum(d_row.astype(f32), axis=0)[None])[0]
        dn1 = jnp.einsum("rc,dc->rd", d_row, qkv_w, preferred_element_type=f32)
        back, d_gain1, d_bias1 = norm_back(dn1, stream_in, vector(0, layer))
        grad = gm + back
        parts = [jnp.transpose(d_qkv.reshape(shard, 3, width), (1, 0, 2)).reshape(3 * shard, width), d_out,
                 jnp.transpose(d_up.reshape(shard, 4, width), (1, 0, 2)).reshape(4 * shard, width), d_down]
        matrices[layer] = reduce_ctx(jnp.concatenate(parts, axis=0))
        small[layer] = jnp.concatenate([
            t.reshape(-1, n) for t, n in (
                (d_gain1, shard), (d_bias1, shard), (sums[:width], shard), (sums[2 * width:], shard), (d_out_b, shard),
                (d_gain2, shard), (d_bias2, shard), (d_down_b, shard), (d_up_b, 4 * shard))], axis=1)

    vec_grads = jnp.stack(small, axis=1)
    vec_grads = lax.psum_scatter(vec_grads, FS, scatter_dimension=0, tiled=True)
    vec_grads = lax.psum(vec_grads, "ctx")[0]
    vg = [vec_grads[:, i * shard:(i + 1) * shard] for i in range(8)] + [vec_grads[:, 8 * shard:]]

    def take(layer, start, cols):
        t = matrices[layer][start * shard:(start + cols) * shard]
        return jnp.transpose(t.reshape(cols, shard, width), (1, 0, 2)).reshape(shard, cols * width)

    g_qkv = jnp.stack([unpack(take(layer, 0, 3)) for layer in range(L)])
    g_out = jnp.stack([take(layer, 3, 1) for layer in range(L)])
    g_up = jnp.stack([take(layer, 4, 4) for layer in range(L)])
    g_down = jnp.stack([matrices[layer][8 * shard:] for layer in range(L)])
    return (activations, grad[None], vg[0], vg[1], g_qkv, vg[2], vg[3], g_out, vg[4], vg[5], vg[6], g_up, vg[8], g_down, vg[7])


def solution(mesh):
    F, C = mesh.devices.shape
    inner = Mesh(mesh.devices.reshape(F // 2, 2, C), ("zz", "core", "ctx"))
    S = 2 if 16 // (2 * C) >= 2 else 1
    G = S * C
    rows = P(FS, "ctx", None)
    vec, mat = P(None, FS), P(None, FS, None)
    return jax.shard_map(
        functools.partial(local, G=G, S=S),
        mesh=inner,
        in_specs=(rows, rows, P(FS), P(FS, None), vec, vec, mat, vec, vec, mat, vec, vec, vec, mat, vec, mat, vec),
        out_specs=(rows, rows, vec, vec, mat, vec, vec, mat, vec, vec, vec, mat, vec, mat, vec),
        check_vma=False,
    )
```

```python
import functools
import jax, jax.numpy as jnp
from jax import lax
from jax.experimental import pallas as pl
from jax.experimental.pallas import tpu as pltpu
from jax.sharding import Mesh, PartitionSpec as P
f32=jnp.float32; bf16=jnp.bfloat16
NEG=-1e30
def dot_nt(a,b): return lax.dot_general(a,b,(((1,),(1,)),((),())),preferred_element_type=f32)
def dot_nn(a,b): return lax.dot_general(a,b,(((1,),(0,)),((),())),preferred_element_type=f32)

LOG2E=1.4426950408889634
def split(q,h,low):
    qs=q.astype(f32)*(0.125*LOG2E)
    hi=qs.astype(bf16).astype(f32); lo=qs-hi
    rl=pltpu.roll(lo,64,1)
    c=jnp.where(low,hi,rl) if h==0 else jnp.where(low,rl,hi)
    return c.astype(bf16)
def dup(k,h,low):
    kf=k.astype(f32); rl=pltpu.roll(kf,64,1)
    c=jnp.where(low,kf,rl) if h==0 else jnp.where(low,rl,kf)
    return c.astype(bf16)
def fwd_kernel(inv_ref, nb_ref, x_ref, o_ref, lse_ref, vt, kd, sb, acc, *, B, NB):
    s=pl.program_id(0)
    nb=nb_ref[s]
    lane=lax.broadcasted_iota(jnp.int32,(1,128),1)
    low=lane<64
    def tv(j,_):
        r=pl.multiple_of(inv_ref[s,j]*B,B)
        w=pl.multiple_of(j*B,B)
        t=x_ref[0,pl.ds(r,B),256:384].T
        one=(lax.broadcasted_iota(jnp.int32,(16,B),0)==0).astype(bf16)
        for h in range(2):
            vt[80*h:80*h+64,pl.ds(w,B)]=t[64*h:64*h+64,:]
            vt[80*h+64:80*h+80,pl.ds(w,B)]=one
            kd[h,pl.ds(w,B),:]=dup(x_ref[0,pl.ds(r,B),128:256],h,low)
        return 0
    lax.fori_loop(0,nb,tv,0)
    rr=lax.broadcasted_iota(jnp.int32,(B,B),0)
    cc=lax.broadcasted_iota(jnp.int32,(B,B),1)
    def qblock(i,_):
        r=pl.multiple_of(inv_ref[s,i]*B,B)
        q=x_ref[0,pl.ds(r,B),0:128]
        qh=[split(q,h,low) for h in range(2)]
        acc[...]=jnp.zeros_like(acc)
        def scores(j,slot):
            for h in range(2):
                sb[slot,h]=dot_nt(kd[h,pl.ds(pl.multiple_of(j*B,B),B),:],qh[h])
        def step(j,carry,diag):
            out=[]
            for h in range(2):
                m=carry[h]
                st=sb[j%2,h]
                if diag: st=jnp.where(rr<=cc,st,NEG)
                mn=jnp.maximum(m,jnp.max(st,axis=0,keepdims=True))
                p=jnp.exp2(st-mn)
                al=jnp.exp2(m-mn)
                v=vt[80*h:80*h+80,pl.ds(pl.multiple_of(j*B,B),B)]
                acc[h]=acc[h]*al+dot_nn(v,p.astype(bf16))
                out.append(mn)
            return tuple(out)
        scores(0,0)
        def both(j,c):
            scores(j+1,(j+1)%2)
            return step(j,c,False)
        n=jnp.full((1,B),NEG,f32)
        c=lax.fori_loop(0,i,both,(n,n))
        c=step(i,c,True)
        os=[]
        for h in range(2):
            l=acc[h,64:65,:]
            os.append(acc[h,0:64,:]*(1.0/l))
            lse_ref[0,pl.ds(h,1),pl.ds(r,B)]=c[h]+jnp.log2(l)
        o_ref[0,pl.ds(r,B),:]=jnp.concatenate(os,0).T.astype(bf16)
        return 0
    lax.fori_loop(0,nb,qblock,0)
    def pad(i,_):
        r=pl.multiple_of(inv_ref[s,i]*B,B)
        o_ref[0,pl.ds(r,B),:]=jnp.zeros((B,128),bf16)
        lse_ref[0,:,pl.ds(r,B)]=jnp.zeros((8,B),f32)
        return 0
    lax.fori_loop(nb,NB,pad,0)

def flash_fwd(x,inv,nb,B):
    S,N,_=x.shape
    NB=N//B
    return pl.pallas_call(functools.partial(fwd_kernel,B=B,NB=NB),
      out_shape=(jax.ShapeDtypeStruct((S,N,128),bf16),jax.ShapeDtypeStruct((S,8,N),f32)),
      grid_spec=pltpu.PrefetchScalarGridSpec(num_scalar_prefetch=2,grid=(S,),
        in_specs=[pl.BlockSpec((1,N,384),lambda s,*_:(s,0,0))],
        out_specs=[pl.BlockSpec((1,N,128),lambda s,*_:(s,0,0)),pl.BlockSpec((1,8,N),lambda s,*_:(s,0,0))],
        scratch_shapes=[pltpu.VMEM((160,N),bf16),pltpu.VMEM((2,N,128),bf16),pltpu.VMEM((2,2,B,B),f32),pltpu.VMEM((2,80,B),f32)]),
      compiler_params=pltpu.CompilerParams(vmem_limit_bytes=48<<20),
      cost_estimate=pl.CostEstimate(flops=S*4*N*N*128,bytes_accessed=S*N*1024,transcendentals=S*N*N),
      )(inv,nb,x)

def bwd_kernel(inv_ref, nb_ref, x_ref, o_ref, do_ref, lse_ref, dx_ref, kt, qd, dq, dk, dv, dl, *, B, NB):
    s=pl.program_id(0)
    nb=nb_ref[s]
    lane=lax.broadcasted_iota(jnp.int32,(1,128),1)
    low=lane<64
    hm=(lax.broadcasted_iota(jnp.int32,(8,128),1)//64==lax.broadcasted_iota(jnp.int32,(8,128),0)).astype(bf16)
    def prep(j,_):
        r=pl.multiple_of(inv_ref[s,j]*B,B)
        w=pl.multiple_of(j*B,B)
        kt[:,pl.ds(w,B)]=x_ref[0,pl.ds(r,B),128:256].T
        for h in range(2): qd[h,pl.ds(w,B),:]=split(x_ref[0,pl.ds(r,B),0:128],h,low)
        prod=o_ref[0,pl.ds(r,B),:].astype(f32)*do_ref[0,pl.ds(r,B),:].astype(f32)
        hi=prod.astype(bf16); lo=(prod-hi.astype(f32)).astype(bf16)
        dl[:,pl.ds(w,B)]=dot_nt(hm,hi)+dot_nt(hm,lo)
        dq[:,pl.ds(w,B)]=jnp.zeros((128,B),f32)
        return 0
    lax.fori_loop(0,nb,prep,0)
    rr=lax.broadcasted_iota(jnp.int32,(B,B),0)
    cc=lax.broadcasted_iota(jnp.int32,(B,B),1)
    def kblock(j,_):
        r=pl.multiple_of(inv_ref[s,j]*B,B)
        k=x_ref[0,pl.ds(r,B),128:256]
        v=x_ref[0,pl.ds(r,B),256:384]
        kdh=[dup(k,h,low) for h in range(2)]
        dk[...]=jnp.zeros_like(dk); dv[...]=jnp.zeros_like(dv)
        def step(i,diag):
            ri=pl.multiple_of(inv_ref[s,i]*B,B)
            wi=pl.multiple_of(i*B,B)
            q=x_ref[0,pl.ds(ri,B),0:128]*jnp.asarray(0.125,bf16)
            do=do_ref[0,pl.ds(ri,B),:]
            zero=jnp.zeros_like(q)
            dvs=[];dks=[]
            for h in range(2):
                qh=jnp.where(low,q,zero) if h==0 else jnp.where(low,zero,q)
                doh=jnp.where(low,do,zero) if h==0 else jnp.where(low,zero,do)
                st=dot_nt(kdh[h],qd[h,pl.ds(wi,B),:])
                p=jnp.exp2(st-lse_ref[0,pl.ds(h,1),pl.ds(ri,B)])
                if diag: p=jnp.where(rr<=cc,p,0.0)
                dvs.append(dot_nn(p.astype(bf16),doh))
                dp=dot_nt(v,doh)
                ds=(p*(dp-dl[pl.ds(h,1),pl.ds(wi,B)])).astype(bf16)
                dks.append(dot_nn(ds,qh))
                kh=kt[64*h:64*h+64,pl.ds(pl.multiple_of(j*B,B),B)]
                dq[64*h:64*h+64,pl.ds(wi,B)]+=dot_nn(kh,ds)
            dv[...]+=dvs[0]+dvs[1]
            dk[...]+=dks[0]+dks[1]
        step(j,True)
        def body(i,_):
            step(i,False); return 0
        lax.fori_loop(j+1,nb,body,0)
        dx_ref[0,pl.ds(r,B),128:256]=dk[...].astype(bf16)
        dx_ref[0,pl.ds(r,B),256:384]=dv[...].astype(bf16)
        return 0
    lax.fori_loop(0,nb,kblock,0)
    def fin(i,_):
        r=pl.multiple_of(inv_ref[s,i]*B,B)
        dx_ref[0,pl.ds(r,B),0:128]=(dq[:,pl.ds(pl.multiple_of(i*B,B),B)].T*0.125).astype(bf16)
        return 0
    lax.fori_loop(0,nb,fin,0)
    def pad(i,_):
        r=pl.multiple_of(inv_ref[s,i]*B,B)
        dx_ref[0,pl.ds(r,B),:]=jnp.zeros((B,384),bf16)
        return 0
    lax.fori_loop(nb,NB,pad,0)

def flash_bwd(x,o,do,lse,inv,nb,B):
    S,N,_=x.shape
    NB=N//B
    return pl.pallas_call(functools.partial(bwd_kernel,B=B,NB=NB),
      out_shape=jax.ShapeDtypeStruct((S,N,384),bf16),
      grid_spec=pltpu.PrefetchScalarGridSpec(num_scalar_prefetch=2,grid=(S,),
        in_specs=[pl.BlockSpec((1,N,384),lambda s,*_:(s,0,0)),pl.BlockSpec((1,N,128),lambda s,*_:(s,0,0)),
                  pl.BlockSpec((1,N,128),lambda s,*_:(s,0,0)),pl.BlockSpec((1,8,N),lambda s,*_:(s,0,0))],
        out_specs=pl.BlockSpec((1,N,384),lambda s,*_:(s,0,0)),
        scratch_shapes=[pltpu.VMEM((128,N),bf16),pltpu.VMEM((2,N,128),bf16),pltpu.VMEM((128,N),f32),pltpu.VMEM((B,128),f32),pltpu.VMEM((B,128),f32),pltpu.VMEM((8,N),f32)]),
      compiler_params=pltpu.CompilerParams(vmem_limit_bytes=48<<20),
      cost_estimate=pl.CostEstimate(flops=S*10*N*N*128,bytes_accessed=S*N*2400,transcendentals=S*N*N),
      )(inv,nb,x,o,do,lse)


def one_fwd_kernel(own_ref, q_ref, x_ref, o_ref, lse_ref, vt, sb, acc, *, B, NB):
    nb = own_ref[NB + 2]
    def tv(j,_):
        r=pl.multiple_of(own_ref[j]*B,B)
        t=x_ref[pl.ds(r,B),:].T
        w=pl.multiple_of(j*B,B)
        vt[0:64,pl.ds(w,B)]=t[64:128,:]
        vt[64:80,pl.ds(w,B)]=(lax.broadcasted_iota(jnp.int32,(16,B),0)==0).astype(bf16)
        return 0
    lax.fori_loop(0,nb,tv,0)
    rr=lax.broadcasted_iota(jnp.int32,(B,B),0)
    cc=lax.broadcasted_iota(jnp.int32,(B,B),1)
    for t in range(2):
        i=own_ref[NB+t]
        @pl.when(i>=nb)
        def _():
            o_ref[t*B:(t+1)*B,:]=jnp.zeros((B,64),bf16)
            lse_ref[:,t*B:(t+1)*B]=jnp.zeros((8,B),f32)
        @pl.when(i<nb)
        def _():
            qs=q_ref[t*B:(t+1)*B,:].astype(f32)*(0.125*LOG2E)
            q=qs.astype(bf16)
            ql=(qs-q.astype(f32)).astype(bf16)
            acc[...]=jnp.zeros_like(acc)
            def step(j,m,diag):
                k=x_ref[pl.ds(pl.multiple_of(own_ref[j]*B,B),B),0:64]
                st=dot_nt(k,q)+dot_nt(k,ql)
                if diag: st=jnp.where(rr<=cc,st,NEG)
                mn=jnp.maximum(m,jnp.max(st,axis=0,keepdims=True))
                p=jnp.exp2(st-mn)
                al=jnp.exp2(m-mn)
                v=vt[:,pl.ds(pl.multiple_of(j*B,B),B)]
                acc[...]=acc[...]*al+dot_nn(v,p.astype(bf16))
                return mn
            m=lax.fori_loop(0,i,lambda j,m: step(j,m,False),jnp.full((1,B),NEG,f32))
            m=step(i,m,True)
            l=acc[64:65,:]
            o_ref[t*B:(t+1)*B,:]=(acc[0:64,:]*(1.0/l)).T.astype(bf16)
            lse_ref[:,t*B:(t+1)*B]=jnp.broadcast_to(m+jnp.log2(l),(8,B))


def one_fwd(q,x,own,B):
    N=x.shape[0]; R=q.shape[0]; NB=N//B
    full=lambda *_:(0,0)
    last=lambda *_:(0,3)
    return pl.pallas_call(functools.partial(one_fwd_kernel,B=B,NB=NB),
      out_shape=(jax.ShapeDtypeStruct((R,64),bf16),jax.ShapeDtypeStruct((8,R),f32)),
      grid_spec=pltpu.PrefetchScalarGridSpec(num_scalar_prefetch=1,grid=(1,),
        in_specs=[pl.BlockSpec((R,64),full),pl.BlockSpec((N,128),last)],
        out_specs=[pl.BlockSpec((R,64),full),pl.BlockSpec((8,R),full)],
        scratch_shapes=[pltpu.VMEM((80,N),bf16),pltpu.VMEM((B,B),f32),pltpu.VMEM((80,B),f32)]),
      compiler_params=pltpu.CompilerParams(vmem_limit_bytes=48<<20),
      cost_estimate=pl.CostEstimate(flops=4*R*N*128,bytes_accessed=N*256+R*512,transcendentals=R*N),
      )(own,q,x)


def one_bwd_kernel(own_ref, q_ref, x_ref, o_ref, do_ref, lse_ref, dq_ref, dx_ref, dkv, dq, *, B, NB):
    nb = own_ref[NB + 2]
    rr=lax.broadcasted_iota(jnp.int32,(B,B),0)
    cc=lax.broadcasted_iota(jnp.int32,(B,B),1)
    ones=jnp.ones((8,64),bf16)
    dkv[...]=jnp.zeros_like(dkv)
    for t in range(2):
        i=own_ref[NB+t]
        sl=slice(t*B,(t+1)*B)
        @pl.when(i>=nb)
        def _():
            dq_ref[sl,:]=jnp.zeros((B,64),bf16)
        @pl.when(i<nb)
        def _():
            qr=q_ref[sl,:]
            qs=qr.astype(f32)*(0.125*LOG2E)
            q=qs.astype(bf16)
            ql=(qs-q.astype(f32)).astype(bf16)
            qd=qr*jnp.asarray(0.125,bf16)
            do=do_ref[sl,:]
            prod=o_ref[sl,:].astype(f32)*do.astype(f32)
            hi=prod.astype(bf16); lo=(prod-hi.astype(f32)).astype(bf16)
            dl=(dot_nt(ones,hi)+dot_nt(ones,lo))[0:1,:]
            lse=lse_ref[0:1,sl]
            dq[...]=jnp.zeros_like(dq)
            def step(j,diag):
                r=pl.multiple_of(own_ref[j]*B,B)
                k=x_ref[pl.ds(r,B),0:64]
                v=x_ref[pl.ds(r,B),64:128]
                st=dot_nt(k,q)+dot_nt(k,ql)
                p=jnp.exp2(st-lse)
                if diag: p=jnp.where(rr<=cc,p,0.0)
                dp=dot_nt(v,do)
                ds=(p*(dp-dl)).astype(bf16)
                dkv[pl.ds(r,B),64:128]+=dot_nn(p.astype(bf16),do)
                dkv[pl.ds(r,B),0:64]+=dot_nn(ds,qd)
                dq[...]+=dot_nn(k.T,ds)
            def body(j,_):
                step(j,False); return 0
            lax.fori_loop(0,i,body,0)
            step(i,True)
            dq_ref[sl,:]=(dq[...].T*0.125).astype(bf16)
    dx_ref[...]=dkv[...].astype(bf16)


def one_bwd(q,x,o,do,lse,own,B):
    N=x.shape[0]; R=q.shape[0]; NB=N//B
    full=lambda *_:(0,0)
    last=lambda *_:(0,3)
    return pl.pallas_call(functools.partial(one_bwd_kernel,B=B,NB=NB),
      out_shape=(jax.ShapeDtypeStruct((R,64),bf16),jax.ShapeDtypeStruct((N,128),bf16)),
      grid_spec=pltpu.PrefetchScalarGridSpec(num_scalar_prefetch=1,grid=(1,),
        in_specs=[pl.BlockSpec((R,64),full),pl.BlockSpec((N,128),last),pl.BlockSpec((R,64),full),pl.BlockSpec((R,64),full),pl.BlockSpec((8,R),full)],
        out_specs=[pl.BlockSpec((R,64),full),pl.BlockSpec((N,128),full)],
        scratch_shapes=[pltpu.VMEM((N,128),f32),pltpu.VMEM((64,B),f32)]),
      compiler_params=pltpu.CompilerParams(vmem_limit_bytes=48<<20),
      cost_estimate=pl.CostEstimate(flops=10*R*N*128,bytes_accessed=N*512+R*1024,transcendentals=R*N),
      )(own,q,x,o,do,lse)


HEADS = 17
EPSILON = 1e-05
FS = ("zz", "core")


def norm_parts(v):
    mean = jnp.mean(v, axis=-1, keepdims=True)
    c = v - mean
    r = lax.rsqrt(jnp.mean(c * c, axis=-1, keepdims=True) + EPSILON)
    return c * r, r


def norm_back(dn, v, gain):
    xhat, r = norm_parts(v)
    y = dn * gain
    a = jnp.mean(y, axis=-1, keepdims=True)
    b = jnp.mean(y * xhat, axis=-1, keepdims=True)
    return r * (y - a - xhat * b), jnp.sum(dn * xhat, axis=0), jnp.sum(dn, axis=0)


def gelu_parts(u):
    z = jnp.abs(u) * 0.7071067811865476
    t = 1.0 / (1.0 + 0.3275911 * z)
    e = jnp.exp(-z * z)
    poly = t * (0.254829592 + t * (-0.284496736 + t * (1.421413741 + t * (-1.453152027 + t * 1.061405429))))
    half = 0.5 * poly * e
    cdf = jnp.where(u >= 0, 1.0 - half, half)
    return u * cdf, cdf + u * e * 0.3989422804014327


def local(
    tokens, cotangent, lengths, block_order,
    ln1_gain, ln1_bias, qkv_weight, q_bias, v_bias, out_weight, out_bias,
    ln2_gain, ln2_bias, up_weight, up_bias, down_weight, down_bias,
    *, G, S,
):
    slots, rows, width = tokens.shape
    C = lax.axis_size("ctx")
    me = lax.axis_index("ctx")
    N = rows * C
    B = rows // 2
    NB = 2 * C
    L = ln1_gain.shape[0]
    shard = ln1_gain.shape[1]
    HW = G * 128
    x_tokens = tokens[0]

    steps = jnp.arange(NB, dtype=jnp.int32)
    order = block_order[0]
    inverse = jnp.sum(jnp.where(order[None, :] == steps[:, None], steps[None, :], 0), axis=1).astype(jnp.int32)
    count = (lengths + (B - 1)) // B
    meta = jnp.concatenate([inverse, count])
    def swap(x):
        return lax.ppermute(x, "core", [(0, 1), (1, 0)])

    metas = [meta, swap(meta)][:S]
    phase_inv = [t[None, :NB] for t in metas]
    phase_nb = [t[NB:] for t in metas]
    core = lax.axis_index("core")
    own = jnp.concatenate([inverse, lax.dynamic_slice_in_dim(order, 2 * me, 2, 0), count])
    own_pos = (lax.dynamic_slice_in_dim(order, 2 * me, 2, 0)[:, None] * B + jnp.arange(B, dtype=jnp.int32)).reshape(rows, 1)
    live = (own_pos < lengths[0]).astype(f32)

    vectors = [ln1_gain, ln1_bias, q_bias, v_bias, out_bias, ln2_gain, ln2_bias, down_bias, up_bias]
    vec = jnp.concatenate(vectors, axis=1).astype(bf16)
    vec = lax.all_gather(vec, FS).astype(f32)

    def vector(index, layer):
        if index < 8:
            return vec[:, layer, index * shard:(index + 1) * shard].reshape(-1)
        return vec[:, layer, 8 * shard:].reshape(-1)

    def pack(w):
        n = w.shape[0]
        w = w.reshape(n, 3, HEADS, 64)
        main = w[:, :, :16].reshape(n, 3, G, 128)
        main = jnp.transpose(main, (0, 2, 1, 3)).reshape(n, G * 384)
        tail = jnp.stack([w[:, 1, 16], w[:, 2, 16], w[:, 0, 16]], axis=1).reshape(n, 192)
        return jnp.concatenate([main, tail], axis=1)

    def unpack(w):
        n = w.shape[0]
        main = jnp.transpose(w[:, :G * 384].reshape(n, G, 3, 128), (0, 2, 1, 3)).reshape(n, 3, 1024)
        tail = w[:, G * 384:].reshape(n, 3, 64)
        tail = jnp.stack([tail[:, 2], tail[:, 0], tail[:, 1]], axis=1)
        return jnp.concatenate([main, tail], axis=2).reshape(n, 3 * width)

    def fetch(w):
        return lax.all_gather(w.astype(bf16), FS, axis=0, tiled=True)

    weights = []
    for layer in range(L):
        weights.append((
            fetch(pack(qkv_weight[layer].astype(bf16))),
            fetch(out_weight[layer]),
            fetch(up_weight[layer]),
            fetch(down_weight[layer]),
        ))

    def ordered(x, axis):
        if S == 1:
            return x
        a, b = jnp.split(x, 2, axis=axis)
        return jnp.where(core == 0, jnp.concatenate([a, b], axis), jnp.concatenate([b, a], axis))

    def exchange(x):
        return lax.all_to_all(x, "ctx", 0, 0)

    def after(x, *others):
        return lax.optimization_barrier((x,) + others)

    stream = x_tokens.astype(f32)
    records = []
    for layer in range(L):
        qkv_w, out_w, up_w, down_w = weights[layer]
        xhat, _ = norm_parts(stream)
        n1 = (xhat * vector(0, layer) + vector(1, layer)).astype(bf16)
        q_b, v_b = vector(2, layer), vector(3, layer)
        bias = pack(jnp.concatenate([q_b, jnp.zeros_like(q_b), v_b])[None])[0]
        wide = []
        for s in range(S):
            half = C * 384
            first = half * (core if s == 0 else 1 - core) if S == 2 else 0
            w = lax.dynamic_slice_in_dim(qkv_w, first, half, 1).reshape(width, C, 384)
            b = lax.dynamic_slice_in_dim(bias, first, half, 0).reshape(C, 1, 384)
            wide.append((jnp.einsum("rd,dgc->grc", n1, w, preferred_element_type=f32) + b).astype(bf16))
        if S == 2:
            wide[1] = swap(wide[1])
        tail = (jnp.dot(n1, qkv_w[:, G * 384:], preferred_element_type=f32) + bias[G * 384:]).astype(bf16)
        kv16 = jnp.broadcast_to(tail[None, :, :128], (C, rows, 128))
        q16 = tail[:, 128:]
        heads, o, lse, o_back = [], [], [], []
        for s in range(S):
            t = wide[s]
            if s == S - 1:
                t = jnp.concatenate([t, kv16], axis=2)
            if s:
                t, heads[0] = after(t, heads[0])
            heads.append(exchange(t).reshape(1, N, -1))
        for s in range(S):
            o_s, lse_s = flash_fwd(heads[s], phase_inv[s], phase_nb[s], B)
            o.append(o_s)
            lse.append(lse_s)
            t = o_s.reshape(C, rows, 128)
            if s:
                t, o_back[0] = after(t, o_back[0])
            o_back.append(exchange(swap(t) if s else t))
        o16, lse16 = one_fwd(q16, heads[-1][0], own, B)
        o_all = ordered(jnp.concatenate(o_back, axis=0), 0)
        mixed = jnp.concatenate([jnp.transpose(o_all, (1, 0, 2)).reshape(rows, HW), o16], axis=1)
        m = stream + jnp.dot(mixed, out_w, preferred_element_type=f32) + vector(4, layer)
        xhat2, _ = norm_parts(m)
        n2 = (xhat2 * vector(5, layer) + vector(6, layer)).astype(bf16)
        u = jnp.dot(n2, up_w, preferred_element_type=f32) + vector(8, layer)
        a, slope = gelu_parts(u)
        a = a.astype(bf16)
        slope = slope.astype(bf16)
        records.append((stream, n1, heads, q16, o, lse, o16, lse16, mixed, m, n2, a, slope))
        stream = m + jnp.dot(a, down_w, preferred_element_type=f32) + vector(7, layer)
    activations = (stream * live).astype(bf16)[None]

    def reduce_fsdp(g):
        return lax.psum_scatter(g.astype(bf16), FS, scatter_dimension=0, tiled=True)

    def reduce_ctx(g):
        return lax.psum(g, "ctx").astype(f32)

    grad = cotangent[0].astype(f32) * live
    matrices = [None] * L
    fours = [None] * L
    small = [None] * L

    def finish(layer):
        d_four, d_up, d_down = fours[layer]
        parts = [jnp.transpose(t.reshape(shard, 4, width), (1, 0, 2)).reshape(4 * shard, width) for t in (d_four, d_up)]
        matrices[layer] = reduce_ctx(jnp.concatenate(parts + [d_down], axis=0))

    for layer in reversed(range(L)):
        stream_in, n1, heads, q16, o, lse, o16, lse16, mixed, m, n2, a, slope = records[layer]
        qkv_w, out_w, up_w, down_w = weights[layer]
        gb = grad.astype(bf16)
        d_down_b = jnp.sum(gb.astype(f32), axis=0)
        d_down = jnp.einsum("rf,rd->fd", a, gb, preferred_element_type=f32).astype(bf16)
        gb, d_down = after(gb, d_down)
        d_down = reduce_fsdp(d_down)
        du = (jnp.einsum("rd,fd->rf", gb, down_w, preferred_element_type=f32) * slope.astype(f32)).astype(bf16)
        d_up_b = jnp.sum(du.astype(f32), axis=0)
        d_up = jnp.einsum("rd,rf->df", n2, du, preferred_element_type=f32).astype(bf16)
        du, d_up = after(du, d_up)
        d_up = reduce_fsdp(d_up)
        dn2 = jnp.einsum("rf,df->rd", du, up_w, preferred_element_type=f32)
        back, d_gain2, d_bias2 = norm_back(dn2, m, vector(5, layer))
        gm = grad + back
        gmb = gm.astype(bf16)
        d_out_b = jnp.sum(gmb.astype(f32), axis=0)
        d_out = jnp.einsum("rd,re->de", mixed, gmb, preferred_element_type=f32).astype(bf16)
        d_o = []
        for s in range(S):
            first = C * 128 * (core if s == 0 else 1 - core) if S == 2 else 0
            w = lax.dynamic_slice_in_dim(out_w, first, C * 128, 0).reshape(C, 128, width)
            d_o.append(jnp.einsum("re,gce->grc", gmb, w, preferred_element_type=f32).astype(bf16))
        d_o16 = jnp.einsum("re,ce->rc", gmb, out_w[HW:], preferred_element_type=f32).astype(bf16)
        dq16, dkv16 = one_bwd(q16, heads[-1][0], o16, d_o16, lse16, own, B)
        d_oh, d_wide = [], []
        for s in range(S):
            t = d_o[s]
            if s:
                t = swap(t)
            if s == S - 1:
                t = jnp.concatenate([t, dkv16.reshape(C, rows, 128)], axis=2)
            if s == S - 1 and layer < L - 1:
                t, fours[layer + 1] = after(t, fours[layer + 1])
                finish(layer + 1)
            if s:
                t, d_oh[0] = after(t, d_oh[0])
            d_oh.append(exchange(t).reshape(1, N, -1))
        dkv16 = jnp.sum(d_oh[-1].reshape(C, rows, 256)[:, :, 128:].astype(f32), axis=0)
        for s in range(S):
            t = flash_bwd(heads[s], o[s], d_oh[s], lse[s], phase_inv[s], phase_nb[s], B)
            t = t.reshape(C, rows, 384)
            if s:
                t, d_wide[0], d_down = after(t, d_wide[0], d_down)
            d_wide.append(exchange(swap(t) if s else t))
        d_wide = ordered(jnp.concatenate(d_wide, axis=0), 0)
        d_tail = jnp.concatenate([dkv16.astype(bf16), dq16], axis=1)
        d_row = jnp.concatenate([jnp.transpose(d_wide, (1, 0, 2)).reshape(rows, G * 384), d_tail], axis=1)
        d_qkv = jnp.einsum("rd,rc->dc", n1, d_row, preferred_element_type=f32).astype(bf16)
        d_four = jnp.concatenate([d_qkv, d_out], axis=1)
        if layer:
            d_row, d_four = after(d_row, d_four)
            d_row, d_up = after(d_row, d_up)
        else:
            d_four, matrices[layer + 1] = after(d_four, matrices[layer + 1])
        d_four = reduce_fsdp(d_four)
        sums = unpack(jnp.sum(d_row.astype(f32), axis=0)[None])[0]
        dn1 = jnp.einsum("rc,dc->rd", d_row, qkv_w, preferred_element_type=f32)
        back, d_gain1, d_bias1 = norm_back(dn1, stream_in, vector(0, layer))
        grad = gm + back
        fours[layer] = (d_four, d_up, d_down)
        if layer == 0:
            finish(0)
        small[layer] = jnp.concatenate([
            t.reshape(-1, n) for t, n in (
                (d_gain1, shard), (d_bias1, shard), (sums[:width], shard), (sums[2 * width:], shard), (d_out_b, shard),
                (d_gain2, shard), (d_bias2, shard), (d_down_b, shard), (d_up_b, 4 * shard))], axis=1)

    vec_grads = jnp.stack(small, axis=1)
    vec_grads = lax.psum_scatter(vec_grads, FS, scatter_dimension=0, tiled=True)
    vec_grads = lax.psum(vec_grads, "ctx")[0]
    vg = [vec_grads[:, i * shard:(i + 1) * shard] for i in range(8)] + [vec_grads[:, 8 * shard:]]

    def take(layer, start, cols):
        t = matrices[layer][start * shard:(start + cols) * shard]
        return jnp.transpose(t.reshape(cols, shard, width), (1, 0, 2)).reshape(shard, cols * width)

    g_qkv = jnp.stack([unpack(take(layer, 0, 3)) for layer in range(L)])
    g_out = jnp.stack([take(layer, 3, 1) for layer in range(L)])
    g_up = jnp.stack([take(layer, 4, 4) for layer in range(L)])
    g_down = jnp.stack([matrices[layer][8 * shard:] for layer in range(L)])
    return (activations, grad[None], vg[0], vg[1], g_qkv, vg[2], vg[3], g_out, vg[4], vg[5], vg[6], g_up, vg[8], g_down, vg[7])


def solution(mesh):
    F, C = mesh.devices.shape
    inner = Mesh(mesh.devices.reshape(F // 2, 2, C), ("zz", "core", "ctx"))
    S = 2 if 16 // (2 * C) >= 2 else 1
    G = S * C
    rows = P(FS, "ctx", None)
    vec, mat = P(None, FS), P(None, FS, None)
    return jax.shard_map(
        functools.partial(local, G=G, S=S),
        mesh=inner,
        in_specs=(rows, rows, P(FS), P(FS, None), vec, vec, mat, vec, vec, mat, vec, vec, vec, mat, vec, mat, vec),
        out_specs=(rows, rows, vec, vec, mat, vec, vec, mat, vec, vec, vec, mat, vec, mat, vec),
        check_vma=False,
    )
```

```python
import functools
import jax, jax.numpy as jnp
from jax import lax
from jax.experimental import pallas as pl
from jax.experimental.pallas import tpu as pltpu
from jax.experimental.layout import Layout, with_layout_constraint
from jax.sharding import Mesh, PartitionSpec as P
f32=jnp.float32; bf16=jnp.bfloat16
NEG=-1e30
def dot_nt(a,b): return lax.dot_general(a,b,(((1,),(1,)),((),())),preferred_element_type=f32)
def dot_nn(a,b): return lax.dot_general(a,b,(((1,),(0,)),((),())),preferred_element_type=f32)

LOG2E=1.4426950408889634
def split(q,h,low):
    qs=q.astype(f32)*(0.125*LOG2E)
    hi=qs.astype(bf16).astype(f32); lo=qs-hi
    rl=pltpu.roll(lo,64,1)
    c=jnp.where(low,hi,rl) if h==0 else jnp.where(low,rl,hi)
    return c.astype(bf16)
def dup(k,h,low):
    kf=k.astype(f32); rl=pltpu.roll(kf,64,1)
    c=jnp.where(low,kf,rl) if h==0 else jnp.where(low,rl,kf)
    return c.astype(bf16)
def fwd_kernel(inv_ref, nb_ref, x_ref, o_ref, lse_ref, vt, kd, sb, acc, *, B, NB):
    s=pl.program_id(0)
    nb=nb_ref[s]
    lane=lax.broadcasted_iota(jnp.int32,(1,128),1)
    low=lane<64
    def tv(j,_):
        r=pl.multiple_of(inv_ref[s,j]*B,B)
        w=pl.multiple_of(j*B,B)
        t=x_ref[0,pl.ds(r,B),256:384].T
        one=(lax.broadcasted_iota(jnp.int32,(16,B),0)==0).astype(bf16)
        for h in range(2):
            vt[80*h:80*h+64,pl.ds(w,B)]=t[64*h:64*h+64,:]
            vt[80*h+64:80*h+80,pl.ds(w,B)]=one
            kd[h,pl.ds(w,B),:]=dup(x_ref[0,pl.ds(r,B),128:256],h,low)
        return 0
    lax.fori_loop(0,nb,tv,0)
    rr=lax.broadcasted_iota(jnp.int32,(B,B),0)
    cc=lax.broadcasted_iota(jnp.int32,(B,B),1)
    def qblock(i,_):
        r=pl.multiple_of(inv_ref[s,i]*B,B)
        q=x_ref[0,pl.ds(r,B),0:128]
        qh=[split(q,h,low) for h in range(2)]
        acc[...]=jnp.zeros_like(acc)
        def scores(j,slot):
            for h in range(2):
                sb[slot,h]=dot_nt(kd[h,pl.ds(pl.multiple_of(j*B,B),B),:],qh[h])
        def step(j,carry,diag):
            out=[]
            for h in range(2):
                m=carry[h]
                st=sb[j%2,h]
                if diag: st=jnp.where(rr<=cc,st,NEG)
                mn=jnp.maximum(m,jnp.max(st,axis=0,keepdims=True))
                p=jnp.exp2(st-mn)
                al=jnp.exp2(m-mn)
                v=vt[80*h:80*h+80,pl.ds(pl.multiple_of(j*B,B),B)]
                acc[h]=acc[h]*al+dot_nn(v,p.astype(bf16))
                out.append(mn)
            return tuple(out)
        scores(0,0)
        def both(j,c):
            scores(j+1,(j+1)%2)
            return step(j,c,False)
        n=jnp.full((1,B),NEG,f32)
        c=lax.fori_loop(0,i,both,(n,n))
        c=step(i,c,True)
        os=[]
        for h in range(2):
            l=acc[h,64:65,:]
            os.append(acc[h,0:64,:]*(1.0/l))
            lse_ref[0,pl.ds(h,1),pl.ds(r,B)]=c[h]+jnp.log2(l)
        o_ref[0,pl.ds(r,B),:]=jnp.concatenate(os,0).T.astype(bf16)
        return 0
    lax.fori_loop(0,nb,qblock,0)
    def pad(i,_):
        r=pl.multiple_of(inv_ref[s,i]*B,B)
        o_ref[0,pl.ds(r,B),:]=jnp.zeros((B,128),bf16)
        lse_ref[0,:,pl.ds(r,B)]=jnp.zeros((8,B),f32)
        return 0
    lax.fori_loop(nb,NB,pad,0)

def flash_fwd(x,inv,nb,B):
    S,N,_=x.shape
    NB=N//B
    return pl.pallas_call(functools.partial(fwd_kernel,B=B,NB=NB),
      out_shape=(jax.ShapeDtypeStruct((S,N,128),bf16),jax.ShapeDtypeStruct((S,8,N),f32)),
      grid_spec=pltpu.PrefetchScalarGridSpec(num_scalar_prefetch=2,grid=(S,),
        in_specs=[pl.BlockSpec((1,N,384),lambda s,*_:(s,0,0))],
        out_specs=[pl.BlockSpec((1,N,128),lambda s,*_:(s,0,0)),pl.BlockSpec((1,8,N),lambda s,*_:(s,0,0))],
        scratch_shapes=[pltpu.VMEM((160,N),bf16),pltpu.VMEM((2,N,128),bf16),pltpu.VMEM((2,2,B,B),f32),pltpu.VMEM((2,80,B),f32)]),
      compiler_params=pltpu.CompilerParams(vmem_limit_bytes=48<<20),
      cost_estimate=pl.CostEstimate(flops=S*4*N*N*128,bytes_accessed=S*N*1024,transcendentals=S*N*N),
      )(inv,nb,x)

def bwd_kernel(inv_ref, nb_ref, x_ref, o_ref, do_ref, lse_ref, dx_ref, kt, qd, dq, dk, dv, dl, *, B, NB):
    s=pl.program_id(0)
    nb=nb_ref[s]
    lane=lax.broadcasted_iota(jnp.int32,(1,128),1)
    low=lane<64
    hm=(lax.broadcasted_iota(jnp.int32,(8,128),1)//64==lax.broadcasted_iota(jnp.int32,(8,128),0)).astype(bf16)
    def prep(j,_):
        r=pl.multiple_of(inv_ref[s,j]*B,B)
        w=pl.multiple_of(j*B,B)
        kt[:,pl.ds(w,B)]=x_ref[0,pl.ds(r,B),128:256].T
        for h in range(2): qd[h,pl.ds(w,B),:]=split(x_ref[0,pl.ds(r,B),0:128],h,low)
        prod=o_ref[0,pl.ds(r,B),:].astype(f32)*do_ref[0,pl.ds(r,B),:].astype(f32)
        hi=prod.astype(bf16); lo=(prod-hi.astype(f32)).astype(bf16)
        dl[:,pl.ds(w,B)]=dot_nt(hm,hi)+dot_nt(hm,lo)
        dq[:,pl.ds(w,B)]=jnp.zeros((128,B),f32)
        return 0
    lax.fori_loop(0,nb,prep,0)
    rr=lax.broadcasted_iota(jnp.int32,(B,B),0)
    cc=lax.broadcasted_iota(jnp.int32,(B,B),1)
    def kblock(j,_):
        r=pl.multiple_of(inv_ref[s,j]*B,B)
        k=x_ref[0,pl.ds(r,B),128:256]
        v=x_ref[0,pl.ds(r,B),256:384]
        kdh=[dup(k,h,low) for h in range(2)]
        dk[...]=jnp.zeros_like(dk); dv[...]=jnp.zeros_like(dv)
        def step(i,diag):
            ri=pl.multiple_of(inv_ref[s,i]*B,B)
            wi=pl.multiple_of(i*B,B)
            q=x_ref[0,pl.ds(ri,B),0:128]*jnp.asarray(0.125,bf16)
            do=do_ref[0,pl.ds(ri,B),:]
            zero=jnp.zeros_like(q)
            dvs=[];dks=[]
            for h in range(2):
                qh=jnp.where(low,q,zero) if h==0 else jnp.where(low,zero,q)
                doh=jnp.where(low,do,zero) if h==0 else jnp.where(low,zero,do)
                st=dot_nt(kdh[h],qd[h,pl.ds(wi,B),:])
                p=jnp.exp2(st-lse_ref[0,pl.ds(h,1),pl.ds(ri,B)])
                if diag: p=jnp.where(rr<=cc,p,0.0)
                dvs.append(dot_nn(p.astype(bf16),doh))
                dp=dot_nt(v,doh)
                ds=(p*(dp-dl[pl.ds(h,1),pl.ds(wi,B)])).astype(bf16)
                dks.append(dot_nn(ds,qh))
                kh=kt[64*h:64*h+64,pl.ds(pl.multiple_of(j*B,B),B)]
                dq[64*h:64*h+64,pl.ds(wi,B)]+=dot_nn(kh,ds)
            dv[...]+=dvs[0]+dvs[1]
            dk[...]+=dks[0]+dks[1]
        step(j,True)
        def body(i,_):
            step(i,False); return 0
        lax.fori_loop(j+1,nb,body,0)
        dx_ref[0,pl.ds(r,B),128:256]=dk[...].astype(bf16)
        dx_ref[0,pl.ds(r,B),256:384]=dv[...].astype(bf16)
        return 0
    lax.fori_loop(0,nb,kblock,0)
    def fin(i,_):
        r=pl.multiple_of(inv_ref[s,i]*B,B)
        dx_ref[0,pl.ds(r,B),0:128]=(dq[:,pl.ds(pl.multiple_of(i*B,B),B)].T*0.125).astype(bf16)
        return 0
    lax.fori_loop(0,nb,fin,0)
    def pad(i,_):
        r=pl.multiple_of(inv_ref[s,i]*B,B)
        dx_ref[0,pl.ds(r,B),:]=jnp.zeros((B,384),bf16)
        return 0
    lax.fori_loop(nb,NB,pad,0)

def flash_bwd(x,o,do,lse,inv,nb,B):
    S,N,_=x.shape
    NB=N//B
    return pl.pallas_call(functools.partial(bwd_kernel,B=B,NB=NB),
      out_shape=jax.ShapeDtypeStruct((S,N,384),bf16),
      grid_spec=pltpu.PrefetchScalarGridSpec(num_scalar_prefetch=2,grid=(S,),
        in_specs=[pl.BlockSpec((1,N,384),lambda s,*_:(s,0,0)),pl.BlockSpec((1,N,128),lambda s,*_:(s,0,0)),
                  pl.BlockSpec((1,N,128),lambda s,*_:(s,0,0)),pl.BlockSpec((1,8,N),lambda s,*_:(s,0,0))],
        out_specs=pl.BlockSpec((1,N,384),lambda s,*_:(s,0,0)),
        scratch_shapes=[pltpu.VMEM((128,N),bf16),pltpu.VMEM((2,N,128),bf16),pltpu.VMEM((128,N),f32),pltpu.VMEM((B,128),f32),pltpu.VMEM((B,128),f32),pltpu.VMEM((8,N),f32)]),
      compiler_params=pltpu.CompilerParams(vmem_limit_bytes=48<<20),
      cost_estimate=pl.CostEstimate(flops=S*10*N*N*128,bytes_accessed=S*N*2400,transcendentals=S*N*N),
      )(inv,nb,x,o,do,lse)


def one_fwd_kernel(own_ref, q_ref, x_ref, o_ref, lse_ref, vt, sb, acc, *, B, NB):
    nb = own_ref[NB + 2]
    def tv(j,_):
        r=pl.multiple_of(own_ref[j]*B,B)
        t=x_ref[pl.ds(r,B),:].T
        w=pl.multiple_of(j*B,B)
        vt[0:64,pl.ds(w,B)]=t[64:128,:]
        vt[64:80,pl.ds(w,B)]=(lax.broadcasted_iota(jnp.int32,(16,B),0)==0).astype(bf16)
        return 0
    lax.fori_loop(0,nb,tv,0)
    rr=lax.broadcasted_iota(jnp.int32,(B,B),0)
    cc=lax.broadcasted_iota(jnp.int32,(B,B),1)
    for t in range(2):
        i=own_ref[NB+t]
        @pl.when(i>=nb)
        def _():
            o_ref[t*B:(t+1)*B,:]=jnp.zeros((B,64),bf16)
            lse_ref[:,t*B:(t+1)*B]=jnp.zeros((8,B),f32)
        @pl.when(i<nb)
        def _():
            qs=q_ref[t*B:(t+1)*B,:].astype(f32)*(0.125*LOG2E)
            q=qs.astype(bf16)
            ql=(qs-q.astype(f32)).astype(bf16)
            acc[...]=jnp.zeros_like(acc)
            def step(j,m,diag):
                k=x_ref[pl.ds(pl.multiple_of(own_ref[j]*B,B),B),0:64]
                st=dot_nt(k,q)+dot_nt(k,ql)
                if diag: st=jnp.where(rr<=cc,st,NEG)
                mn=jnp.maximum(m,jnp.max(st,axis=0,keepdims=True))
                p=jnp.exp2(st-mn)
                al=jnp.exp2(m-mn)
                v=vt[:,pl.ds(pl.multiple_of(j*B,B),B)]
                acc[...]=acc[...]*al+dot_nn(v,p.astype(bf16))
                return mn
            m=lax.fori_loop(0,i,lambda j,m: step(j,m,False),jnp.full((1,B),NEG,f32))
            m=step(i,m,True)
            l=acc[64:65,:]
            o_ref[t*B:(t+1)*B,:]=(acc[0:64,:]*(1.0/l)).T.astype(bf16)
            lse_ref[:,t*B:(t+1)*B]=jnp.broadcast_to(m+jnp.log2(l),(8,B))


def one_fwd(q,x,own,B):
    N=x.shape[0]; R=q.shape[0]; NB=N//B
    full=lambda *_:(0,0)
    last=lambda *_:(0,3)
    return pl.pallas_call(functools.partial(one_fwd_kernel,B=B,NB=NB),
      out_shape=(jax.ShapeDtypeStruct((R,64),bf16),jax.ShapeDtypeStruct((8,R),f32)),
      grid_spec=pltpu.PrefetchScalarGridSpec(num_scalar_prefetch=1,grid=(1,),
        in_specs=[pl.BlockSpec((R,64),full),pl.BlockSpec((N,128),last)],
        out_specs=[pl.BlockSpec((R,64),full),pl.BlockSpec((8,R),full)],
        scratch_shapes=[pltpu.VMEM((80,N),bf16),pltpu.VMEM((B,B),f32),pltpu.VMEM((80,B),f32)]),
      compiler_params=pltpu.CompilerParams(vmem_limit_bytes=48<<20),
      cost_estimate=pl.CostEstimate(flops=4*R*N*128,bytes_accessed=N*256+R*512,transcendentals=R*N),
      )(own,q,x)


def one_bwd_kernel(own_ref, q_ref, x_ref, o_ref, do_ref, lse_ref, dq_ref, dx_ref, dkv, dq, *, B, NB):
    nb = own_ref[NB + 2]
    rr=lax.broadcasted_iota(jnp.int32,(B,B),0)
    cc=lax.broadcasted_iota(jnp.int32,(B,B),1)
    ones=jnp.ones((8,64),bf16)
    dkv[...]=jnp.zeros_like(dkv)
    for t in range(2):
        i=own_ref[NB+t]
        sl=slice(t*B,(t+1)*B)
        @pl.when(i>=nb)
        def _():
            dq_ref[sl,:]=jnp.zeros((B,64),bf16)
        @pl.when(i<nb)
        def _():
            qr=q_ref[sl,:]
            qs=qr.astype(f32)*(0.125*LOG2E)
            q=qs.astype(bf16)
            ql=(qs-q.astype(f32)).astype(bf16)
            qd=qr*jnp.asarray(0.125,bf16)
            do=do_ref[sl,:]
            prod=o_ref[sl,:].astype(f32)*do.astype(f32)
            hi=prod.astype(bf16); lo=(prod-hi.astype(f32)).astype(bf16)
            dl=(dot_nt(ones,hi)+dot_nt(ones,lo))[0:1,:]
            lse=lse_ref[0:1,sl]
            dq[...]=jnp.zeros_like(dq)
            def step(j,diag):
                r=pl.multiple_of(own_ref[j]*B,B)
                k=x_ref[pl.ds(r,B),0:64]
                v=x_ref[pl.ds(r,B),64:128]
                st=dot_nt(k,q)+dot_nt(k,ql)
                p=jnp.exp2(st-lse)
                if diag: p=jnp.where(rr<=cc,p,0.0)
                dp=dot_nt(v,do)
                ds=(p*(dp-dl)).astype(bf16)
                dkv[pl.ds(r,B),64:128]+=dot_nn(p.astype(bf16),do)
                dkv[pl.ds(r,B),0:64]+=dot_nn(ds,qd)
                dq[...]+=dot_nn(k.T,ds)
            def body(j,_):
                step(j,False); return 0
            lax.fori_loop(0,i,body,0)
            step(i,True)
            dq_ref[sl,:]=(dq[...].T*0.125).astype(bf16)
    dx_ref[...]=dkv[...].astype(bf16)


def one_bwd(q,x,o,do,lse,own,B):
    N=x.shape[0]; R=q.shape[0]; NB=N//B
    full=lambda *_:(0,0)
    last=lambda *_:(0,3)
    return pl.pallas_call(functools.partial(one_bwd_kernel,B=B,NB=NB),
      out_shape=(jax.ShapeDtypeStruct((R,64),bf16),jax.ShapeDtypeStruct((N,128),bf16)),
      grid_spec=pltpu.PrefetchScalarGridSpec(num_scalar_prefetch=1,grid=(1,),
        in_specs=[pl.BlockSpec((R,64),full),pl.BlockSpec((N,128),last),pl.BlockSpec((R,64),full),pl.BlockSpec((R,64),full),pl.BlockSpec((8,R),full)],
        out_specs=[pl.BlockSpec((R,64),full),pl.BlockSpec((N,128),full)],
        scratch_shapes=[pltpu.VMEM((N,128),f32),pltpu.VMEM((64,B),f32)]),
      compiler_params=pltpu.CompilerParams(vmem_limit_bytes=48<<20),
      cost_estimate=pl.CostEstimate(flops=10*R*N*128,bytes_accessed=N*512+R*1024,transcendentals=R*N),
      )(own,q,x,o,do,lse)


HEADS = 17
EPSILON = 1e-05
FS = ("zz", "core")


def norm_parts(v):
    mean = jnp.mean(v, axis=-1, keepdims=True)
    c = v - mean
    r = lax.rsqrt(jnp.mean(c * c, axis=-1, keepdims=True) + EPSILON)
    return c * r, r


def norm_back(dn, v, gain):
    xhat, r = norm_parts(v)
    y = dn * gain
    a = jnp.mean(y, axis=-1, keepdims=True)
    b = jnp.mean(y * xhat, axis=-1, keepdims=True)
    return r * (y - a - xhat * b), jnp.sum(dn * xhat, axis=0), jnp.sum(dn, axis=0)


def col_sum(x):
    return jnp.dot(jnp.ones((16, x.shape[0]), bf16), x, preferred_element_type=f32)[0]


def gelu_parts(u):
    z = jnp.abs(u) * 0.7071067811865476
    t = 1.0 / (1.0 + 0.3275911 * z)
    e = jnp.exp(-z * z)
    poly = t * (0.254829592 + t * (-0.284496736 + t * (1.421413741 + t * (-1.453152027 + t * 1.061405429))))
    half = 0.5 * poly * e
    cdf = jnp.where(u >= 0, 1.0 - half, half)
    return u * cdf, cdf + u * e * 0.3989422804014327


def local(
    tokens, cotangent, lengths, block_order,
    ln1_gain, ln1_bias, qkv_weight, q_bias, v_bias, out_weight, out_bias,
    ln2_gain, ln2_bias, up_weight, up_bias, down_weight, down_bias,
    *, G, S,
):
    slots, rows, width = tokens.shape
    C = lax.axis_size("ctx")
    me = lax.axis_index("ctx")
    N = rows * C
    B = rows // 2
    NB = 2 * C
    L = ln1_gain.shape[0]
    shard = ln1_gain.shape[1]
    HW = G * 128
    x_tokens = tokens[0]

    steps = jnp.arange(NB, dtype=jnp.int32)
    order = block_order[0]
    inverse = jnp.sum(jnp.where(order[None, :] == steps[:, None], steps[None, :], 0), axis=1).astype(jnp.int32)
    count = (lengths + (B - 1)) // B
    meta = jnp.concatenate([inverse, count])
    def swap(x):
        return lax.ppermute(x, "core", [(0, 1), (1, 0)])

    metas = [meta, swap(meta)][:S]
    phase_inv = [t[None, :NB] for t in metas]
    phase_nb = [t[NB:] for t in metas]
    own = jnp.concatenate([inverse, lax.dynamic_slice_in_dim(order, 2 * me, 2, 0), count])
    own_pos = (lax.dynamic_slice_in_dim(order, 2 * me, 2, 0)[:, None] * B + jnp.arange(B, dtype=jnp.int32)).reshape(rows, 1)
    live = (own_pos < lengths[0]).astype(f32)

    vectors = [ln1_gain, ln1_bias, q_bias, v_bias, out_bias, ln2_gain, ln2_bias, down_bias, up_bias]
    vec = jnp.concatenate(vectors, axis=1).astype(bf16)
    vec = lax.all_gather(vec, FS).astype(f32)

    def vector(index, layer):
        if index < 8:
            return vec[:, layer, index * shard:(index + 1) * shard].reshape(-1)
        return vec[:, layer, 8 * shard:].reshape(-1)

    def pack(w):
        parts = []
        for g in range(G):
            parts += [w[:, kind * width + g * 128:kind * width + g * 128 + 128] for kind in range(3)]
        last = width - 64
        parts += [w[:, kind * width + last:kind * width + width] for kind in (1, 2, 0)]
        return jnp.concatenate(parts, axis=1)

    def unpack(w):
        tail = G * 384
        parts = []
        for kind, last in enumerate((128, 0, 64)):
            parts += [w[:, g * 384 + kind * 128:g * 384 + kind * 128 + 128] for g in range(G)]
            parts.append(w[:, tail + last:tail + last + 64])
        return jnp.concatenate(parts, axis=1)

    def fetch(w):
        return lax.all_gather(w.astype(bf16), FS, axis=0, tiled=True)

    weights = []
    for layer in range(L):
        weights.append((
            fetch(pack(qkv_weight[layer].astype(bf16))),
            fetch(out_weight[layer]),
            fetch(up_weight[layer]),
            fetch(down_weight[layer]),
        ))

    def plain(x):
        return with_layout_constraint(x, Layout(major_to_minor=tuple(range(x.ndim))))

    def exchange(x):
        return plain(lax.all_to_all(plain(x), "ctx", 0, 0))

    def after(x, *others):
        return lax.optimization_barrier((x,) + others)

    stream = x_tokens.astype(f32)
    records = []
    for layer in range(L):
        qkv_w, out_w, up_w, down_w = weights[layer]
        xhat, _ = norm_parts(stream)
        n1 = (xhat * vector(0, layer) + vector(1, layer)).astype(bf16)
        q_b, v_b = vector(2, layer), vector(3, layer)
        bias = pack(jnp.concatenate([q_b, jnp.zeros_like(q_b), v_b])[None])[0]
        wide = []
        for s in range(S):
            half = C * 384
            cols = slice(half * s, half * (s + 1))
            w = qkv_w[:, cols].reshape(width, C, 384)
            b = bias[cols].reshape(C, 1, 384)
            wide.append((jnp.einsum("rd,dgc->grc", n1, w, preferred_element_type=f32) + b).astype(bf16))
        if S == 2:
            wide[1] = swap(wide[1])
        tail = (jnp.dot(n1, qkv_w[:, G * 384:], preferred_element_type=f32) + bias[G * 384:]).astype(bf16)
        kv16 = jnp.broadcast_to(tail[None, :, :128], (C, rows, 128))
        q16 = tail[:, 128:]
        heads, o, lse, o_back = [], [], [], []
        for s in range(S):
            t = wide[s]
            if s == S - 1:
                t = jnp.concatenate([t, kv16], axis=2)
            if s:
                t, heads[0] = after(t, heads[0])
            heads.append(exchange(t).reshape(1, N, -1))
        for s in range(S):
            o_s, lse_s = flash_fwd(heads[s], phase_inv[s], phase_nb[s], B)
            o.append(o_s)
            lse.append(lse_s)
            t = o_s.reshape(C, rows, 128)
            if s:
                t, o_back[0] = after(t, o_back[0])
            o_back.append(exchange(swap(t) if s else t))
        o16, lse16 = one_fwd(q16, heads[-1][0], own, B)
        o_all = jnp.concatenate(o_back, axis=0)
        mixed = jnp.concatenate([jnp.transpose(o_all, (1, 0, 2)).reshape(rows, HW), o16], axis=1)
        m = stream + jnp.dot(mixed, out_w, preferred_element_type=f32) + vector(4, layer)
        xhat2, _ = norm_parts(m)
        n2 = (xhat2 * vector(5, layer) + vector(6, layer)).astype(bf16)
        u = jnp.dot(n2, up_w, preferred_element_type=f32) + vector(8, layer)
        a, slope = gelu_parts(u)
        a = a.astype(bf16)
        slope = slope.astype(bf16)
        records.append((stream, n1, heads, q16, o, lse, o16, lse16, mixed, m, n2, a, slope))
        stream = m + jnp.dot(a, down_w, preferred_element_type=f32) + vector(7, layer)
    activations = (stream * live).astype(bf16)[None]

    def reduce_fsdp(g):
        return lax.psum_scatter(g.astype(bf16), FS, scatter_dimension=0, tiled=True)

    def reduce_ctx(g):
        return lax.psum(g, "ctx").astype(f32)

    grad = cotangent[0].astype(f32) * live
    matrices = [None] * L
    fours = [None] * L
    small = [None] * L

    def finish(layer):
        d_four, d_up, d_down = fours[layer]
        matrices[layer] = tuple(t.astype(f32) for t in lax.psum((d_four, d_up, d_down), "ctx"))

    for layer in reversed(range(L)):
        stream_in, n1, heads, q16, o, lse, o16, lse16, mixed, m, n2, a, slope = records[layer]
        qkv_w, out_w, up_w, down_w = weights[layer]
        gb = grad.astype(bf16)
        d_down_b = col_sum(gb)
        d_down = jnp.einsum("rf,rd->fd", a, gb, preferred_element_type=f32).astype(bf16)
        gb, d_down = after(gb, plain(d_down))
        d_down = reduce_fsdp(d_down)
        du = (jnp.einsum("rd,fd->rf", gb, down_w, preferred_element_type=f32) * slope.astype(f32)).astype(bf16)
        d_up_b = col_sum(du)
        d_up = jnp.einsum("rd,rf->df", n2, du, preferred_element_type=f32).astype(bf16)
        du, d_up = after(du, plain(d_up))
        d_up = reduce_fsdp(d_up)
        dn2 = jnp.einsum("rf,df->rd", du, up_w, preferred_element_type=f32)
        back, d_gain2, d_bias2 = norm_back(dn2, m, vector(5, layer))
        gm = grad + back
        gmb = gm.astype(bf16)
        d_out_b = col_sum(gmb)
        d_out = jnp.einsum("rd,re->de", mixed, gmb, preferred_element_type=f32).astype(bf16)
        d_o = []
        for s in range(S):
            w = out_w[C * 128 * s:C * 128 * (s + 1)].reshape(C, 128, width)
            d_o.append(jnp.einsum("re,gce->grc", gmb, w, preferred_element_type=f32).astype(bf16))
        d_o16 = jnp.einsum("re,ce->rc", gmb, out_w[HW:], preferred_element_type=f32).astype(bf16)
        dq16, dkv16 = one_bwd(q16, heads[-1][0], o16, d_o16, lse16, own, B)
        d_oh, d_wide = [], []
        for s in range(S):
            t = d_o[s]
            if s:
                t = swap(t)
            if s == S - 1:
                t = jnp.concatenate([t, dkv16.reshape(C, rows, 128)], axis=2)
            if s:
                t, d_oh[0] = after(t, d_oh[0])
            d_oh.append(exchange(t).reshape(1, N, -1))
        dkv16 = jnp.sum(d_oh[-1].reshape(C, rows, 256)[:, :, 128:].astype(f32), axis=0)
        for s in range(S):
            t = flash_bwd(heads[s], o[s], d_oh[s], lse[s], phase_inv[s], phase_nb[s], B)
            t = t.reshape(C, rows, 384)
            if s:
                t, d_wide[0], d_down = after(t, d_wide[0], d_down)
            if s == S - 1 and layer < L - 1:
                done = after(t, *fours[layer + 1])
                t, fours[layer + 1] = done[0], done[1:]
                finish(layer + 1)
            d_wide.append(exchange(swap(t) if s else t))
        d_wide = jnp.concatenate(d_wide, axis=0)
        d_tail = jnp.concatenate([dkv16.astype(bf16), dq16], axis=1)
        d_row = jnp.concatenate([jnp.transpose(d_wide, (1, 0, 2)).reshape(rows, G * 384), d_tail], axis=1)
        d_row, d_up = after(d_row, d_up)
        d_qkv = jnp.einsum("rd,rc->dc", n1, d_row, preferred_element_type=f32).astype(bf16)
        d_four = jnp.concatenate([d_qkv, d_out], axis=1)
        if layer:
            d_row, d_four = after(d_row, plain(d_four))
        d_four = reduce_fsdp(d_four)
        sums = unpack(col_sum(d_row)[None])[0]
        dn1 = jnp.einsum("rc,dc->rd", d_row, qkv_w, preferred_element_type=f32)
        back, d_gain1, d_bias1 = norm_back(dn1, stream_in, vector(0, layer))
        grad = gm + back
        fours[layer] = (d_four, d_up, d_down)
        if layer == 0:
            done = after(d_four, d_up, d_down, *matrices[1])
            fours[0], matrices[1] = done[:3], done[3:]
            finish(0)
        small[layer] = jnp.concatenate([
            t.reshape(-1, n) for t, n in (
                (d_gain1, shard), (d_bias1, shard), (sums[:width], shard), (sums[2 * width:], shard), (d_out_b, shard),
                (d_gain2, shard), (d_bias2, shard), (d_down_b, shard), (d_up_b, 4 * shard))], axis=1)

    vec_grads = jnp.stack(small, axis=1)
    vec_grads = lax.psum_scatter(vec_grads, FS, scatter_dimension=0, tiled=True)
    vec_grads = lax.psum(vec_grads, "ctx")[0]
    vg = [vec_grads[:, i * shard:(i + 1) * shard] for i in range(8)] + [vec_grads[:, 8 * shard:]]

    g_qkv = jnp.stack([unpack(matrices[layer][0][:, :3 * width]) for layer in range(L)])
    g_out = jnp.stack([matrices[layer][0][:, 3 * width:] for layer in range(L)])
    g_up = jnp.stack([matrices[layer][1] for layer in range(L)])
    g_down = jnp.stack([matrices[layer][2] for layer in range(L)])
    return (activations, grad[None], vg[0], vg[1], g_qkv, vg[2], vg[3], g_out, vg[4], vg[5], vg[6], g_up, vg[8], g_down, vg[7])


def solution(mesh):
    F, C = mesh.devices.shape
    inner = Mesh(mesh.devices.reshape(F // 2, 2, C), ("zz", "core", "ctx"))
    S = 2 if 16 // (2 * C) >= 2 else 1
    G = S * C
    rows = P(FS, "ctx", None)
    vec, mat = P(None, FS), P(None, FS, None)
    return jax.shard_map(
        functools.partial(local, G=G, S=S),
        mesh=inner,
        in_specs=(rows, rows, P(FS), P(FS, None), vec, vec, mat, vec, vec, mat, vec, vec, vec, mat, vec, mat, vec),
        out_specs=(rows, rows, vec, vec, mat, vec, vec, mat, vec, vec, vec, mat, vec, mat, vec),
        check_vma=False,
    )
```

```python
import functools
import jax, jax.numpy as jnp
from jax import lax
from jax.experimental import pallas as pl
from jax.experimental.pallas import tpu as pltpu
from jax.experimental.layout import Layout, with_layout_constraint
from jax.sharding import Mesh, PartitionSpec as P
f32=jnp.float32; bf16=jnp.bfloat16
NEG=-1e30
def dot_nt(a,b): return lax.dot_general(a,b,(((1,),(1,)),((),())),preferred_element_type=f32)
def dot_nn(a,b): return lax.dot_general(a,b,(((1,),(0,)),((),())),preferred_element_type=f32)

LOG2E=1.4426950408889634
def split(q,h,low):
    qs=q.astype(f32)*(0.125*LOG2E)
    hi=qs.astype(bf16).astype(f32); lo=qs-hi
    rl=pltpu.roll(lo,64,1)
    c=jnp.where(low,hi,rl) if h==0 else jnp.where(low,rl,hi)
    return c.astype(bf16)
def dup(k,h,low):
    kf=k.astype(f32); rl=pltpu.roll(kf,64,1)
    c=jnp.where(low,kf,rl) if h==0 else jnp.where(low,rl,kf)
    return c.astype(bf16)
def fwd_kernel(inv_ref, nb_ref, x_ref, o_ref, lse_ref, vt, kd, sb, acc, *, B, NB):
    s=pl.program_id(0)
    nb=nb_ref[s]
    lane=lax.broadcasted_iota(jnp.int32,(1,128),1)
    low=lane<64
    def tv(j,_):
        r=pl.multiple_of(inv_ref[s,j]*B,B)
        w=pl.multiple_of(j*B,B)
        t=x_ref[0,pl.ds(r,B),256:384].T
        one=(lax.broadcasted_iota(jnp.int32,(16,B),0)==0).astype(bf16)
        for h in range(2):
            vt[80*h:80*h+64,pl.ds(w,B)]=t[64*h:64*h+64,:]
            vt[80*h+64:80*h+80,pl.ds(w,B)]=one
            kd[h,pl.ds(w,B),:]=dup(x_ref[0,pl.ds(r,B),128:256],h,low)
        return 0
    lax.fori_loop(0,nb,tv,0)
    rr=lax.broadcasted_iota(jnp.int32,(B,B),0)
    cc=lax.broadcasted_iota(jnp.int32,(B,B),1)
    def qblock(i,_):
        r=pl.multiple_of(inv_ref[s,i]*B,B)
        q=x_ref[0,pl.ds(r,B),0:128]
        qh=[split(q,h,low) for h in range(2)]
        acc[...]=jnp.zeros_like(acc)
        def scores(j,slot):
            for h in range(2):
                sb[slot,h]=dot_nt(kd[h,pl.ds(pl.multiple_of(j*B,B),B),:],qh[h])
        def step(j,carry,diag):
            out=[]
            for h in range(2):
                m=carry[h]
                st=sb[j%2,h]
                if diag: st=jnp.where(rr<=cc,st,NEG)
                mn=jnp.maximum(m,jnp.max(st,axis=0,keepdims=True))
                p=jnp.exp2(st-mn)
                al=jnp.exp2(m-mn)
                v=vt[80*h:80*h+80,pl.ds(pl.multiple_of(j*B,B),B)]
                acc[h]=acc[h]*al+dot_nn(v,p.astype(bf16))
                out.append(mn)
            return tuple(out)
        scores(0,0)
        def both(j,c):
            scores(j+1,(j+1)%2)
            return step(j,c,False)
        n=jnp.full((1,B),NEG,f32)
        c=lax.fori_loop(0,i,both,(n,n))
        c=step(i,c,True)
        os=[]
        for h in range(2):
            l=acc[h,64:65,:]
            os.append(acc[h,0:64,:]*(1.0/l))
            lse_ref[0,pl.ds(h,1),pl.ds(r,B)]=c[h]+jnp.log2(l)
        o_ref[0,pl.ds(r,B),:]=jnp.concatenate(os,0).T.astype(bf16)
        return 0
    lax.fori_loop(0,nb,qblock,0)
    def pad(i,_):
        r=pl.multiple_of(inv_ref[s,i]*B,B)
        o_ref[0,pl.ds(r,B),:]=jnp.zeros((B,128),bf16)
        lse_ref[0,:,pl.ds(r,B)]=jnp.zeros((8,B),f32)
        return 0
    lax.fori_loop(nb,NB,pad,0)

def flash_fwd(x,inv,nb,B):
    S,N,_=x.shape
    NB=N//B
    return pl.pallas_call(functools.partial(fwd_kernel,B=B,NB=NB),
      out_shape=(jax.ShapeDtypeStruct((S,N,128),bf16),jax.ShapeDtypeStruct((S,8,N),f32)),
      grid_spec=pltpu.PrefetchScalarGridSpec(num_scalar_prefetch=2,grid=(S,),
        in_specs=[pl.BlockSpec((1,N,384),lambda s,*_:(s,0,0))],
        out_specs=[pl.BlockSpec((1,N,128),lambda s,*_:(s,0,0)),pl.BlockSpec((1,8,N),lambda s,*_:(s,0,0))],
        scratch_shapes=[pltpu.VMEM((160,N),bf16),pltpu.VMEM((2,N,128),bf16),pltpu.VMEM((2,2,B,B),f32),pltpu.VMEM((2,80,B),f32)]),
      compiler_params=pltpu.CompilerParams(vmem_limit_bytes=48<<20),
      cost_estimate=pl.CostEstimate(flops=S*4*N*N*128,bytes_accessed=S*N*1024,transcendentals=S*N*N),
      )(inv,nb,x)

def bwd_kernel(inv_ref, nb_ref, x_ref, o_ref, do_ref, lse_ref, dx_ref, kt, qd, dq, dk, dv, dl, *, B, NB):
    s=pl.program_id(0)
    nb=nb_ref[s]
    lane=lax.broadcasted_iota(jnp.int32,(1,128),1)
    low=lane<64
    hm=(lax.broadcasted_iota(jnp.int32,(8,128),1)//64==lax.broadcasted_iota(jnp.int32,(8,128),0)).astype(bf16)
    def prep(j,_):
        r=pl.multiple_of(inv_ref[s,j]*B,B)
        w=pl.multiple_of(j*B,B)
        kt[:,pl.ds(w,B)]=x_ref[0,pl.ds(r,B),128:256].T
        for h in range(2): qd[h,pl.ds(w,B),:]=split(x_ref[0,pl.ds(r,B),0:128],h,low)
        prod=o_ref[0,pl.ds(r,B),:].astype(f32)*do_ref[0,pl.ds(r,B),:].astype(f32)
        hi=prod.astype(bf16); lo=(prod-hi.astype(f32)).astype(bf16)
        dl[:,pl.ds(w,B)]=dot_nt(hm,hi)+dot_nt(hm,lo)
        dq[:,pl.ds(w,B)]=jnp.zeros((128,B),f32)
        return 0
    lax.fori_loop(0,nb,prep,0)
    rr=lax.broadcasted_iota(jnp.int32,(B,B),0)
    cc=lax.broadcasted_iota(jnp.int32,(B,B),1)
    def kblock(j,_):
        r=pl.multiple_of(inv_ref[s,j]*B,B)
        k=x_ref[0,pl.ds(r,B),128:256]
        v=x_ref[0,pl.ds(r,B),256:384]
        kdh=[dup(k,h,low) for h in range(2)]
        dk[...]=jnp.zeros_like(dk); dv[...]=jnp.zeros_like(dv)
        def step(i,diag):
            ri=pl.multiple_of(inv_ref[s,i]*B,B)
            wi=pl.multiple_of(i*B,B)
            q=x_ref[0,pl.ds(ri,B),0:128]*jnp.asarray(0.125,bf16)
            do=do_ref[0,pl.ds(ri,B),:]
            zero=jnp.zeros_like(q)
            dvs=[];dks=[]
            for h in range(2):
                qh=jnp.where(low,q,zero) if h==0 else jnp.where(low,zero,q)
                doh=jnp.where(low,do,zero) if h==0 else jnp.where(low,zero,do)
                st=dot_nt(kdh[h],qd[h,pl.ds(wi,B),:])
                p=jnp.exp2(st-lse_ref[0,pl.ds(h,1),pl.ds(ri,B)])
                if diag: p=jnp.where(rr<=cc,p,0.0)
                dvs.append(dot_nn(p.astype(bf16),doh))
                dp=dot_nt(v,doh)
                ds=(p*(dp-dl[pl.ds(h,1),pl.ds(wi,B)])).astype(bf16)
                dks.append(dot_nn(ds,qh))
                kh=kt[64*h:64*h+64,pl.ds(pl.multiple_of(j*B,B),B)]
                dq[64*h:64*h+64,pl.ds(wi,B)]+=dot_nn(kh,ds)
            dv[...]+=dvs[0]+dvs[1]
            dk[...]+=dks[0]+dks[1]
        step(j,True)
        def body(i,_):
            step(i,False); return 0
        lax.fori_loop(j+1,nb,body,0)
        dx_ref[0,pl.ds(r,B),128:256]=dk[...].astype(bf16)
        dx_ref[0,pl.ds(r,B),256:384]=dv[...].astype(bf16)
        return 0
    lax.fori_loop(0,nb,kblock,0)
    def fin(i,_):
        r=pl.multiple_of(inv_ref[s,i]*B,B)
        dx_ref[0,pl.ds(r,B),0:128]=(dq[:,pl.ds(pl.multiple_of(i*B,B),B)].T*0.125).astype(bf16)
        return 0
    lax.fori_loop(0,nb,fin,0)
    def pad(i,_):
        r=pl.multiple_of(inv_ref[s,i]*B,B)
        dx_ref[0,pl.ds(r,B),:]=jnp.zeros((B,384),bf16)
        return 0
    lax.fori_loop(nb,NB,pad,0)

def flash_bwd(x,o,do,lse,inv,nb,B):
    S,N,_=x.shape
    NB=N//B
    return pl.pallas_call(functools.partial(bwd_kernel,B=B,NB=NB),
      out_shape=jax.ShapeDtypeStruct((S,N,384),bf16),
      grid_spec=pltpu.PrefetchScalarGridSpec(num_scalar_prefetch=2,grid=(S,),
        in_specs=[pl.BlockSpec((1,N,384),lambda s,*_:(s,0,0)),pl.BlockSpec((1,N,128),lambda s,*_:(s,0,0)),
                  pl.BlockSpec((1,N,128),lambda s,*_:(s,0,0)),pl.BlockSpec((1,8,N),lambda s,*_:(s,0,0))],
        out_specs=pl.BlockSpec((1,N,384),lambda s,*_:(s,0,0)),
        scratch_shapes=[pltpu.VMEM((128,N),bf16),pltpu.VMEM((2,N,128),bf16),pltpu.VMEM((128,N),f32),pltpu.VMEM((B,128),f32),pltpu.VMEM((B,128),f32),pltpu.VMEM((8,N),f32)]),
      compiler_params=pltpu.CompilerParams(vmem_limit_bytes=48<<20),
      cost_estimate=pl.CostEstimate(flops=S*10*N*N*128,bytes_accessed=S*N*2400,transcendentals=S*N*N),
      )(inv,nb,x,o,do,lse)


def one_fwd_kernel(own_ref, q_ref, x_ref, o_ref, lse_ref, vt, sb, acc, *, B, NB):
    nb = own_ref[NB + 2]
    def tv(j,_):
        r=pl.multiple_of(own_ref[j]*B,B)
        t=x_ref[pl.ds(r,B),:].T
        w=pl.multiple_of(j*B,B)
        vt[0:64,pl.ds(w,B)]=t[64:128,:]
        vt[64:80,pl.ds(w,B)]=(lax.broadcasted_iota(jnp.int32,(16,B),0)==0).astype(bf16)
        return 0
    lax.fori_loop(0,nb,tv,0)
    rr=lax.broadcasted_iota(jnp.int32,(B,B),0)
    cc=lax.broadcasted_iota(jnp.int32,(B,B),1)
    for t in range(2):
        i=own_ref[NB+t]
        @pl.when(i>=nb)
        def _():
            o_ref[t*B:(t+1)*B,:]=jnp.zeros((B,64),bf16)
            lse_ref[:,t*B:(t+1)*B]=jnp.zeros((8,B),f32)
        @pl.when(i<nb)
        def _():
            qs=q_ref[t*B:(t+1)*B,:].astype(f32)*(0.125*LOG2E)
            q=qs.astype(bf16)
            ql=(qs-q.astype(f32)).astype(bf16)
            acc[...]=jnp.zeros_like(acc)
            def step(j,m,diag):
                k=x_ref[pl.ds(pl.multiple_of(own_ref[j]*B,B),B),0:64]
                st=dot_nt(k,q)+dot_nt(k,ql)
                if diag: st=jnp.where(rr<=cc,st,NEG)
                mn=jnp.maximum(m,jnp.max(st,axis=0,keepdims=True))
                p=jnp.exp2(st-mn)
                al=jnp.exp2(m-mn)
                v=vt[:,pl.ds(pl.multiple_of(j*B,B),B)]
                acc[...]=acc[...]*al+dot_nn(v,p.astype(bf16))
                return mn
            m=lax.fori_loop(0,i,lambda j,m: step(j,m,False),jnp.full((1,B),NEG,f32))
            m=step(i,m,True)
            l=acc[64:65,:]
            o_ref[t*B:(t+1)*B,:]=(acc[0:64,:]*(1.0/l)).T.astype(bf16)
            lse_ref[:,t*B:(t+1)*B]=jnp.broadcast_to(m+jnp.log2(l),(8,B))


def one_fwd(q,x,own,B):
    N=x.shape[0]; R=q.shape[0]; NB=N//B
    full=lambda *_:(0,0)
    last=lambda *_:(0,3)
    return pl.pallas_call(functools.partial(one_fwd_kernel,B=B,NB=NB),
      out_shape=(jax.ShapeDtypeStruct((R,64),bf16),jax.ShapeDtypeStruct((8,R),f32)),
      grid_spec=pltpu.PrefetchScalarGridSpec(num_scalar_prefetch=1,grid=(1,),
        in_specs=[pl.BlockSpec((R,64),full),pl.BlockSpec((N,128),last)],
        out_specs=[pl.BlockSpec((R,64),full),pl.BlockSpec((8,R),full)],
        scratch_shapes=[pltpu.VMEM((80,N),bf16),pltpu.VMEM((B,B),f32),pltpu.VMEM((80,B),f32)]),
      compiler_params=pltpu.CompilerParams(vmem_limit_bytes=48<<20),
      cost_estimate=pl.CostEstimate(flops=4*R*N*128,bytes_accessed=N*256+R*512,transcendentals=R*N),
      )(own,q,x)


def one_bwd_kernel(own_ref, q_ref, x_ref, o_ref, do_ref, lse_ref, dq_ref, dx_ref, dkv, dq, *, B, NB):
    nb = own_ref[NB + 2]
    rr=lax.broadcasted_iota(jnp.int32,(B,B),0)
    cc=lax.broadcasted_iota(jnp.int32,(B,B),1)
    ones=jnp.ones((8,64),bf16)
    dkv[...]=jnp.zeros_like(dkv)
    for t in range(2):
        i=own_ref[NB+t]
        sl=slice(t*B,(t+1)*B)
        @pl.when(i>=nb)
        def _():
            dq_ref[sl,:]=jnp.zeros((B,64),bf16)
        @pl.when(i<nb)
        def _():
            qr=q_ref[sl,:]
            qs=qr.astype(f32)*(0.125*LOG2E)
            q=qs.astype(bf16)
            ql=(qs-q.astype(f32)).astype(bf16)
            qd=qr*jnp.asarray(0.125,bf16)
            do=do_ref[sl,:]
            prod=o_ref[sl,:].astype(f32)*do.astype(f32)
            hi=prod.astype(bf16); lo=(prod-hi.astype(f32)).astype(bf16)
            dl=(dot_nt(ones,hi)+dot_nt(ones,lo))[0:1,:]
            lse=lse_ref[0:1,sl]
            dq[...]=jnp.zeros_like(dq)
            def step(j,diag):
                r=pl.multiple_of(own_ref[j]*B,B)
                k=x_ref[pl.ds(r,B),0:64]
                v=x_ref[pl.ds(r,B),64:128]
                st=dot_nt(k,q)+dot_nt(k,ql)
                p=jnp.exp2(st-lse)
                if diag: p=jnp.where(rr<=cc,p,0.0)
                dp=dot_nt(v,do)
                ds=(p*(dp-dl)).astype(bf16)
                dkv[pl.ds(r,B),64:128]+=dot_nn(p.astype(bf16),do)
                dkv[pl.ds(r,B),0:64]+=dot_nn(ds,qd)
                dq[...]+=dot_nn(k.T,ds)
            def body(j,_):
                step(j,False); return 0
            lax.fori_loop(0,i,body,0)
            step(i,True)
            dq_ref[sl,:]=(dq[...].T*0.125).astype(bf16)
    dx_ref[...]=dkv[...].astype(bf16)


def one_bwd(q,x,o,do,lse,own,B):
    N=x.shape[0]; R=q.shape[0]; NB=N//B
    full=lambda *_:(0,0)
    last=lambda *_:(0,3)
    return pl.pallas_call(functools.partial(one_bwd_kernel,B=B,NB=NB),
      out_shape=(jax.ShapeDtypeStruct((R,64),bf16),jax.ShapeDtypeStruct((N,128),bf16)),
      grid_spec=pltpu.PrefetchScalarGridSpec(num_scalar_prefetch=1,grid=(1,),
        in_specs=[pl.BlockSpec((R,64),full),pl.BlockSpec((N,128),last),pl.BlockSpec((R,64),full),pl.BlockSpec((R,64),full),pl.BlockSpec((8,R),full)],
        out_specs=[pl.BlockSpec((R,64),full),pl.BlockSpec((N,128),full)],
        scratch_shapes=[pltpu.VMEM((N,128),f32),pltpu.VMEM((64,B),f32)]),
      compiler_params=pltpu.CompilerParams(vmem_limit_bytes=48<<20),
      cost_estimate=pl.CostEstimate(flops=10*R*N*128,bytes_accessed=N*512+R*1024,transcendentals=R*N),
      )(own,q,x,o,do,lse)


HEADS = 17
EPSILON = 1e-05
FS = ("zz", "core")


def norm_parts(v):
    mean = jnp.mean(v, axis=-1, keepdims=True)
    c = v - mean
    r = lax.rsqrt(jnp.mean(c * c, axis=-1, keepdims=True) + EPSILON)
    return c * r, r


def norm_back(dn, v, gain):
    xhat, r = norm_parts(v)
    y = dn * gain
    a = jnp.mean(y, axis=-1, keepdims=True)
    b = jnp.mean(y * xhat, axis=-1, keepdims=True)
    return r * (y - a - xhat * b), jnp.sum(dn * xhat, axis=0), jnp.sum(dn, axis=0)


def col_sum(x):
    return jnp.dot(jnp.ones((16, x.shape[0]), bf16), x, preferred_element_type=f32)[0]


def gelu_parts(u):
    z = jnp.abs(u) * 0.7071067811865476
    t = 1.0 / (1.0 + 0.3275911 * z)
    e = jnp.exp(-z * z)
    poly = t * (0.254829592 + t * (-0.284496736 + t * (1.421413741 + t * (-1.453152027 + t * 1.061405429))))
    half = 0.5 * poly * e
    cdf = jnp.where(u >= 0, 1.0 - half, half)
    return u * cdf, cdf + u * e * 0.3989422804014327


def local(
    tokens, cotangent, lengths, block_order,
    ln1_gain, ln1_bias, qkv_weight, q_bias, v_bias, out_weight, out_bias,
    ln2_gain, ln2_bias, up_weight, up_bias, down_weight, down_bias,
    *, G, S,
):
    slots, rows, width = tokens.shape
    C = lax.axis_size("ctx")
    me = lax.axis_index("ctx")
    N = rows * C
    B = rows // 2
    NB = 2 * C
    L = ln1_gain.shape[0]
    shard = ln1_gain.shape[1]
    HW = G * 128
    x_tokens = tokens[0]

    steps = jnp.arange(NB, dtype=jnp.int32)
    order = block_order[0]
    inverse = jnp.sum(jnp.where(order[None, :] == steps[:, None], steps[None, :], 0), axis=1).astype(jnp.int32)
    count = (lengths + (B - 1)) // B
    meta = jnp.concatenate([inverse, count])
    def swap(x):
        return lax.ppermute(x, "core", [(0, 1), (1, 0)])

    metas = [meta, swap(meta)][:S]
    phase_inv = [t[None, :NB] for t in metas]
    phase_nb = [t[NB:] for t in metas]
    own = jnp.concatenate([inverse, lax.dynamic_slice_in_dim(order, 2 * me, 2, 0), count])
    own_pos = (lax.dynamic_slice_in_dim(order, 2 * me, 2, 0)[:, None] * B + jnp.arange(B, dtype=jnp.int32)).reshape(rows, 1)
    live = (own_pos < lengths[0]).astype(f32)

    vectors = [ln1_gain, ln1_bias, q_bias, v_bias, out_bias, ln2_gain, ln2_bias, down_bias, up_bias]
    vec = jnp.concatenate(vectors, axis=1).astype(bf16)
    vec = lax.all_gather(vec, FS).astype(f32)

    def vector(index, layer):
        if index < 8:
            return vec[:, layer, index * shard:(index + 1) * shard].reshape(-1)
        return vec[:, layer, 8 * shard:].reshape(-1)

    def pack(w):
        parts = []
        for g in range(G):
            parts += [w[:, kind * width + g * 128:kind * width + g * 128 + 128] for kind in range(3)]
        last = width - 64
        parts += [w[:, kind * width + last:kind * width + width] for kind in (1, 2, 0)]
        return jnp.concatenate(parts, axis=1)

    def unpack(w):
        tail = G * 384
        parts = []
        for kind, last in enumerate((128, 0, 64)):
            parts += [w[:, g * 384 + kind * 128:g * 384 + kind * 128 + 128] for g in range(G)]
            parts.append(w[:, tail + last:tail + last + 64])
        return jnp.concatenate(parts, axis=1)

    def fetch(w):
        return lax.all_gather(w.astype(bf16), FS, axis=0, tiled=True)

    weights = []
    for layer in range(L):
        weights.append((
            fetch(pack(qkv_weight[layer].astype(bf16))),
            fetch(out_weight[layer]),
            fetch(up_weight[layer]),
            fetch(down_weight[layer]),
        ))

    def plain(x):
        return with_layout_constraint(x, Layout(major_to_minor=tuple(range(x.ndim))))

    def exchange(x):
        return plain(lax.all_to_all(plain(x), "ctx", 0, 0))

    def after(x, *others):
        return lax.optimization_barrier((x,) + others)

    stream = x_tokens.astype(f32)
    records = []
    for layer in range(L):
        qkv_w, out_w, up_w, down_w = weights[layer]
        xhat, _ = norm_parts(stream)
        n1 = (xhat * vector(0, layer) + vector(1, layer)).astype(bf16)
        q_b, v_b = vector(2, layer), vector(3, layer)
        bias = pack(jnp.concatenate([q_b, jnp.zeros_like(q_b), v_b])[None])[0]
        wide = []
        for s in range(S):
            half = C * 384
            cols = slice(half * s, half * (s + 1))
            w = qkv_w[:, cols].reshape(width, C, 384)
            b = bias[cols].reshape(C, 1, 384)
            wide.append((jnp.einsum("rd,dgc->grc", n1, w, preferred_element_type=f32) + b).astype(bf16))
        if S == 2:
            wide[1] = swap(wide[1])
        tail = (jnp.dot(n1, qkv_w[:, G * 384:], preferred_element_type=f32) + bias[G * 384:]).astype(bf16)
        kv16 = jnp.broadcast_to(tail[None, :, :128], (C, rows, 128))
        q16 = tail[:, 128:]
        heads, o, lse, o_back = [], [], [], []
        for s in range(S):
            t = wide[s]
            if s == S - 1:
                t = jnp.concatenate([t, kv16], axis=2)
            if s:
                t, heads[0] = after(t, heads[0])
            heads.append(exchange(t).reshape(1, N, -1))
        for s in range(S):
            o_s, lse_s = flash_fwd(heads[s], phase_inv[s], phase_nb[s], B)
            o.append(o_s)
            lse.append(lse_s)
            t = o_s.reshape(C, rows, 128)
            if s:
                t, o_back[0] = after(t, o_back[0])
            o_back.append(exchange(swap(t) if s else t))
        o16, lse16 = one_fwd(q16, heads[-1][0], own, B)
        o_all = jnp.concatenate(o_back, axis=0)
        mixed = jnp.concatenate([jnp.transpose(o_all, (1, 0, 2)).reshape(rows, HW), o16], axis=1)
        m = stream + jnp.dot(mixed, out_w, preferred_element_type=f32) + vector(4, layer)
        xhat2, _ = norm_parts(m)
        n2 = (xhat2 * vector(5, layer) + vector(6, layer)).astype(bf16)
        u = jnp.dot(n2, up_w, preferred_element_type=f32) + vector(8, layer)
        a, slope = gelu_parts(u)
        a = a.astype(bf16)
        slope = slope.astype(bf16)
        records.append((stream, n1, heads, q16, o, lse, o16, lse16, mixed, m, n2, a, slope))
        stream = m + jnp.dot(a, down_w, preferred_element_type=f32) + vector(7, layer)
    activations = (stream * live).astype(bf16)[None]

    def reduce_fsdp(g):
        return lax.psum_scatter(g.astype(bf16), FS, scatter_dimension=0, tiled=True)

    def reduce_ctx(g):
        return lax.psum(g, "ctx").astype(f32)

    grad = cotangent[0].astype(f32) * live
    matrices = [None] * L
    fours = [None] * L
    ffns = [None] * L
    small = [None] * L

    def ctx_end(mine):
        return exchange(jnp.broadcast_to(mine[None], (C,) + mine.shape))

    def ctx_sum(shards):
        mine, sizes = ctx_begin(shards)
        return ctx_end(mine), sizes

    def ctx_begin(shards):
        pieces = []
        for t in shards:
            if t.shape[1] == width:
                pieces.append(t.reshape(C, -1, width))
            else:
                pieces.append(jnp.transpose(t.reshape(t.shape[0], C, -1), (1, 0, 2)).reshape(C, -1, width))
        sizes = [t.shape[1] for t in pieces]
        parts = exchange(jnp.concatenate(pieces, axis=1))
        mine = jnp.sum(parts.astype(f32), axis=0).astype(bf16)
        return mine, sizes

    def spread(summed, shapes):
        whole, sizes = summed
        out, at = [], 0
        for n, (r, c) in zip(sizes, shapes):
            t = whole[:, at:at + n].astype(f32)
            at += n
            if c == width:
                out.append(t.reshape(r, c))
            else:
                out.append(jnp.transpose(t.reshape(C, r, c // C), (1, 0, 2)).reshape(r, c))
        return out

    wide_shape, tall_shape = (shard, 4 * width), (4 * shard, width)
    for layer in reversed(range(L)):
        stream_in, n1, heads, q16, o, lse, o16, lse16, mixed, m, n2, a, slope = records[layer]
        qkv_w, out_w, up_w, down_w = weights[layer]
        gb = grad.astype(bf16)
        d_down_b = col_sum(gb)
        d_down = jnp.einsum("rf,rd->fd", a, gb, preferred_element_type=f32).astype(bf16)
        gb, d_down = after(gb, plain(d_down))
        if layer < L - 1:
            above = list(after(gb, *ffns[layer + 1]))
            gb = above.pop(0)
            mine, early_sizes = ctx_begin(above)
        d_down = reduce_fsdp(d_down)
        du = (jnp.einsum("rd,fd->rf", gb, down_w, preferred_element_type=f32) * slope.astype(f32)).astype(bf16)
        d_up_b = col_sum(du)
        d_up = jnp.einsum("rd,rf->df", n2, du, preferred_element_type=f32).astype(bf16)
        du, d_up = after(du, plain(d_up))
        if layer < L - 1:
            du, mine = after(du, mine)
            early = ctx_end(mine)
        d_up = reduce_fsdp(d_up)
        dn2 = jnp.einsum("rf,df->rd", du, up_w, preferred_element_type=f32)
        back, d_gain2, d_bias2 = norm_back(dn2, m, vector(5, layer))
        gm = grad + back
        gmb = gm.astype(bf16)
        d_out_b = col_sum(gmb)
        d_out = jnp.einsum("rd,re->de", mixed, gmb, preferred_element_type=f32).astype(bf16)
        if layer < L - 1:
            gmb, early = after(gmb, early)
            early = (early, early_sizes)
        d_o = []
        for s in range(S):
            w = out_w[C * 128 * s:C * 128 * (s + 1)].reshape(C, 128, width)
            d_o.append(jnp.einsum("re,gce->grc", gmb, w, preferred_element_type=f32).astype(bf16))
        d_o16 = jnp.einsum("re,ce->rc", gmb, out_w[HW:], preferred_element_type=f32).astype(bf16)
        dq16, dkv16 = one_bwd(q16, heads[-1][0], o16, d_o16, lse16, own, B)
        d_oh, d_wide = [], []
        for s in range(S):
            t = d_o[s]
            if s:
                t = swap(t)
            if s == S - 1:
                t = jnp.concatenate([t, dkv16.reshape(C, rows, 128)], axis=2)
            if s:
                t, d_oh[0] = after(t, d_oh[0])
            if s == S - 1 and layer < L - 1:
                t, fours[layer + 1] = after(t, fours[layer + 1])
            d_oh.append(exchange(t).reshape(1, N, -1))
        dkv16 = jnp.sum(d_oh[-1].reshape(C, rows, 256)[:, :, 128:].astype(f32), axis=0)
        for s in range(S):
            t = flash_bwd(heads[s], o[s], d_oh[s], lse[s], phase_inv[s], phase_nb[s], B)
            t = t.reshape(C, rows, 384)
            if s:
                t, d_wide[0], d_down = after(t, d_wide[0], d_down)
            d_wide.append(exchange(swap(t) if s else t))
        d_wide = jnp.concatenate(d_wide, axis=0)
        d_tail = jnp.concatenate([dkv16.astype(bf16), dq16], axis=1)
        d_row = jnp.concatenate([jnp.transpose(d_wide, (1, 0, 2)).reshape(rows, G * 384), d_tail], axis=1)
        d_row, d_up = after(d_row, d_up)
        if layer < L - 1:
            d_row, t1, t2, t3 = after(d_row, fours[layer + 1], d_up, d_down)
            middle_sum = ctx_sum([t1, t2, t3])
        d_qkv = jnp.einsum("rd,rc->dc", n1, d_row, preferred_element_type=f32).astype(bf16)
        d_four = jnp.concatenate([d_qkv, d_out], axis=1)
        if layer:
            d_row, d_four = after(d_row, plain(d_four))
        d_four = reduce_fsdp(d_four)
        sums = unpack(col_sum(d_row)[None])[0]
        dn1 = jnp.einsum("rc,dc->rd", d_row, qkv_w, preferred_element_type=f32)
        back, d_gain1, d_bias1 = norm_back(dn1, stream_in, vector(0, layer))
        grad = gm + back
        fours[layer] = d_four
        ffns[layer] = (d_up, d_down)
        if layer == 0:
            last = ctx_sum([d_four])
            matrices[1] = spread(middle_sum, [wide_shape]) + spread(early, [wide_shape, tall_shape])
            matrices[0] = spread(last, [wide_shape]) + spread((middle_sum[0][:, middle_sum[1][0]:], middle_sum[1][1:]), [wide_shape, tall_shape])
        small[layer] = jnp.concatenate([
            t.reshape(-1, n) for t, n in (
                (d_gain1, shard), (d_bias1, shard), (sums[:width], shard), (sums[2 * width:], shard), (d_out_b, shard),
                (d_gain2, shard), (d_bias2, shard), (d_down_b, shard), (d_up_b, 4 * shard))], axis=1)

    vec_grads = jnp.stack(small, axis=1)
    vec_grads = jnp.sum(lax.all_to_all(vec_grads, FS, 0, 0), axis=0)
    vec_grads = lax.psum(vec_grads, "ctx")
    vg = [vec_grads[:, i * shard:(i + 1) * shard] for i in range(8)] + [vec_grads[:, 8 * shard:]]

    g_qkv = jnp.stack([unpack(matrices[layer][0][:, :3 * width]) for layer in range(L)])
    g_out = jnp.stack([matrices[layer][0][:, 3 * width:] for layer in range(L)])
    g_up = jnp.stack([matrices[layer][1] for layer in range(L)])
    g_down = jnp.stack([matrices[layer][2] for layer in range(L)])
    return (activations, grad[None], vg[0], vg[1], g_qkv, vg[2], vg[3], g_out, vg[4], vg[5], vg[6], g_up, vg[8], g_down, vg[7])


def solution(mesh):
    F, C = mesh.devices.shape
    inner = Mesh(mesh.devices.reshape(F // 2, 2, C), ("zz", "core", "ctx"))
    S = 2 if 16 // (2 * C) >= 2 else 1
    G = S * C
    rows = P(FS, "ctx", None)
    vec, mat = P(None, FS), P(None, FS, None)
    return jax.shard_map(
        functools.partial(local, G=G, S=S),
        mesh=inner,
        in_specs=(rows, rows, P(FS), P(FS, None), vec, vec, mat, vec, vec, mat, vec, vec, vec, mat, vec, mat, vec),
        out_specs=(rows, rows, vec, vec, mat, vec, vec, mat, vec, vec, vec, mat, vec, mat, vec),
        check_vma=False,
    )
```

```python
import functools
import jax, jax.numpy as jnp
from jax import lax
from jax.experimental import pallas as pl
from jax.experimental.pallas import tpu as pltpu
from jax.experimental.layout import Layout, with_layout_constraint
from jax.sharding import Mesh, PartitionSpec as P
f32=jnp.float32; bf16=jnp.bfloat16
NEG=-1e30
def dot_nt(a,b): return lax.dot_general(a,b,(((1,),(1,)),((),())),preferred_element_type=f32)
def dot_nn(a,b): return lax.dot_general(a,b,(((1,),(0,)),((),())),preferred_element_type=f32)

LOG2E=1.4426950408889634
def split(q,h,low):
    qs=q.astype(f32)*(0.125*LOG2E)
    hi=qs.astype(bf16).astype(f32); lo=qs-hi
    rl=pltpu.roll(lo,64,1)
    c=jnp.where(low,hi,rl) if h==0 else jnp.where(low,rl,hi)
    return c.astype(bf16)
def dup(k,h,low):
    kf=k.astype(f32); rl=pltpu.roll(kf,64,1)
    c=jnp.where(low,kf,rl) if h==0 else jnp.where(low,rl,kf)
    return c.astype(bf16)
def fwd_kernel(inv_ref, nb_ref, x_ref, o_ref, lse_ref, vt, kd, sb, acc, *, B, NB):
    s=pl.program_id(0)
    nb=nb_ref[s]
    lane=lax.broadcasted_iota(jnp.int32,(1,128),1)
    low=lane<64
    def tv(j,_):
        r=pl.multiple_of(inv_ref[s,j]*B,B)
        w=pl.multiple_of(j*B,B)
        t=x_ref[0,pl.ds(r,B),256:384].T
        one=(lax.broadcasted_iota(jnp.int32,(16,B),0)==0).astype(bf16)
        for h in range(2):
            vt[80*h:80*h+64,pl.ds(w,B)]=t[64*h:64*h+64,:]
            vt[80*h+64:80*h+80,pl.ds(w,B)]=one
            kd[h,pl.ds(w,B),:]=dup(x_ref[0,pl.ds(r,B),128:256],h,low)
        return 0
    lax.fori_loop(0,nb,tv,0)
    rr=lax.broadcasted_iota(jnp.int32,(B,B),0)
    cc=lax.broadcasted_iota(jnp.int32,(B,B),1)
    def qblock(i,_):
        r=pl.multiple_of(inv_ref[s,i]*B,B)
        q=x_ref[0,pl.ds(r,B),0:128]
        qh=[split(q,h,low) for h in range(2)]
        acc[...]=jnp.zeros_like(acc)
        def scores(j,slot):
            for h in range(2):
                sb[slot,h]=dot_nt(kd[h,pl.ds(pl.multiple_of(j*B,B),B),:],qh[h])
        def step(j,carry,diag):
            out=[]
            for h in range(2):
                m=carry[h]
                st=sb[j%2,h]
                if diag: st=jnp.where(rr<=cc,st,NEG)
                mn=jnp.maximum(m,jnp.max(st,axis=0,keepdims=True))
                p=jnp.exp2(st-mn)
                al=jnp.exp2(m-mn)
                v=vt[80*h:80*h+80,pl.ds(pl.multiple_of(j*B,B),B)]
                acc[h]=acc[h]*al+dot_nn(v,p.astype(bf16))
                out.append(mn)
            return tuple(out)
        scores(0,0)
        def both(j,c):
            scores(j+1,(j+1)%2)
            return step(j,c,False)
        n=jnp.full((1,B),NEG,f32)
        c=lax.fori_loop(0,i,both,(n,n))
        c=step(i,c,True)
        os=[]
        for h in range(2):
            l=acc[h,64:65,:]
            os.append(acc[h,0:64,:]*(1.0/l))
            lse_ref[0,pl.ds(h,1),pl.ds(r,B)]=c[h]+jnp.log2(l)
        o_ref[0,pl.ds(r,B),:]=jnp.concatenate(os,0).T.astype(bf16)
        return 0
    lax.fori_loop(0,nb,qblock,0)
    def pad(i,_):
        r=pl.multiple_of(inv_ref[s,i]*B,B)
        o_ref[0,pl.ds(r,B),:]=jnp.zeros((B,128),bf16)
        lse_ref[0,:,pl.ds(r,B)]=jnp.zeros((8,B),f32)
        return 0
    lax.fori_loop(nb,NB,pad,0)

def flash_fwd(x,inv,nb,B):
    S,N,_=x.shape
    NB=N//B
    return pl.pallas_call(functools.partial(fwd_kernel,B=B,NB=NB),
      out_shape=(jax.ShapeDtypeStruct((S,N,128),bf16),jax.ShapeDtypeStruct((S,8,N),f32)),
      grid_spec=pltpu.PrefetchScalarGridSpec(num_scalar_prefetch=2,grid=(S,),
        in_specs=[pl.BlockSpec((1,N,384),lambda s,*_:(s,0,0))],
        out_specs=[pl.BlockSpec((1,N,128),lambda s,*_:(s,0,0)),pl.BlockSpec((1,8,N),lambda s,*_:(s,0,0))],
        scratch_shapes=[pltpu.VMEM((160,N),bf16),pltpu.VMEM((2,N,128),bf16),pltpu.VMEM((2,2,B,B),f32),pltpu.VMEM((2,80,B),f32)]),
      compiler_params=pltpu.CompilerParams(vmem_limit_bytes=48<<20),
      cost_estimate=pl.CostEstimate(flops=S*4*N*N*128,bytes_accessed=S*N*1024,transcendentals=S*N*N),
      )(inv,nb,x)

def bwd_kernel(inv_ref, nb_ref, x_ref, o_ref, do_ref, lse_ref, dx_ref, kt, qd, dq, dk, dv, dl, *, B, NB):
    s=pl.program_id(0)
    nb=nb_ref[s]
    lane=lax.broadcasted_iota(jnp.int32,(1,128),1)
    low=lane<64
    hm=(lax.broadcasted_iota(jnp.int32,(8,128),1)//64==lax.broadcasted_iota(jnp.int32,(8,128),0)).astype(bf16)
    def prep(j,_):
        r=pl.multiple_of(inv_ref[s,j]*B,B)
        w=pl.multiple_of(j*B,B)
        kt[:,pl.ds(w,B)]=x_ref[0,pl.ds(r,B),128:256].T
        for h in range(2): qd[h,pl.ds(w,B),:]=split(x_ref[0,pl.ds(r,B),0:128],h,low)
        prod=o_ref[0,pl.ds(r,B),:].astype(f32)*do_ref[0,pl.ds(r,B),:].astype(f32)
        hi=prod.astype(bf16); lo=(prod-hi.astype(f32)).astype(bf16)
        dl[:,pl.ds(w,B)]=dot_nt(hm,hi)+dot_nt(hm,lo)
        dq[:,pl.ds(w,B)]=jnp.zeros((128,B),f32)
        return 0
    lax.fori_loop(0,nb,prep,0)
    rr=lax.broadcasted_iota(jnp.int32,(B,B),0)
    cc=lax.broadcasted_iota(jnp.int32,(B,B),1)
    def kblock(j,_):
        r=pl.multiple_of(inv_ref[s,j]*B,B)
        k=x_ref[0,pl.ds(r,B),128:256]
        v=x_ref[0,pl.ds(r,B),256:384]
        kdh=[dup(k,h,low) for h in range(2)]
        dk[...]=jnp.zeros_like(dk); dv[...]=jnp.zeros_like(dv)
        def step(i,diag):
            ri=pl.multiple_of(inv_ref[s,i]*B,B)
            wi=pl.multiple_of(i*B,B)
            q=x_ref[0,pl.ds(ri,B),0:128]*jnp.asarray(0.125,bf16)
            do=do_ref[0,pl.ds(ri,B),:]
            zero=jnp.zeros_like(q)
            dvs=[];dks=[]
            for h in range(2):
                qh=jnp.where(low,q,zero) if h==0 else jnp.where(low,zero,q)
                doh=jnp.where(low,do,zero) if h==0 else jnp.where(low,zero,do)
                st=dot_nt(kdh[h],qd[h,pl.ds(wi,B),:])
                p=jnp.exp2(st-lse_ref[0,pl.ds(h,1),pl.ds(ri,B)])
                if diag: p=jnp.where(rr<=cc,p,0.0)
                dvs.append(dot_nn(p.astype(bf16),doh))
                dp=dot_nt(v,doh)
                ds=(p*(dp-dl[pl.ds(h,1),pl.ds(wi,B)])).astype(bf16)
                dks.append(dot_nn(ds,qh))
                kh=kt[64*h:64*h+64,pl.ds(pl.multiple_of(j*B,B),B)]
                dq[64*h:64*h+64,pl.ds(wi,B)]+=dot_nn(kh,ds)
            dv[...]+=dvs[0]+dvs[1]
            dk[...]+=dks[0]+dks[1]
        step(j,True)
        def body(i,_):
            step(i,False); return 0
        lax.fori_loop(j+1,nb,body,0)
        dx_ref[0,pl.ds(r,B),128:256]=dk[...].astype(bf16)
        dx_ref[0,pl.ds(r,B),256:384]=dv[...].astype(bf16)
        return 0
    lax.fori_loop(0,nb,kblock,0)
    def fin(i,_):
        r=pl.multiple_of(inv_ref[s,i]*B,B)
        dx_ref[0,pl.ds(r,B),0:128]=(dq[:,pl.ds(pl.multiple_of(i*B,B),B)].T*0.125).astype(bf16)
        return 0
    lax.fori_loop(0,nb,fin,0)
    def pad(i,_):
        r=pl.multiple_of(inv_ref[s,i]*B,B)
        dx_ref[0,pl.ds(r,B),:]=jnp.zeros((B,384),bf16)
        return 0
    lax.fori_loop(nb,NB,pad,0)

def flash_bwd(x,o,do,lse,inv,nb,B):
    S,N,_=x.shape
    NB=N//B
    return pl.pallas_call(functools.partial(bwd_kernel,B=B,NB=NB),
      out_shape=jax.ShapeDtypeStruct((S,N,384),bf16),
      grid_spec=pltpu.PrefetchScalarGridSpec(num_scalar_prefetch=2,grid=(S,),
        in_specs=[pl.BlockSpec((1,N,384),lambda s,*_:(s,0,0)),pl.BlockSpec((1,N,128),lambda s,*_:(s,0,0)),
                  pl.BlockSpec((1,N,128),lambda s,*_:(s,0,0)),pl.BlockSpec((1,8,N),lambda s,*_:(s,0,0))],
        out_specs=pl.BlockSpec((1,N,384),lambda s,*_:(s,0,0)),
        scratch_shapes=[pltpu.VMEM((128,N),bf16),pltpu.VMEM((2,N,128),bf16),pltpu.VMEM((128,N),f32),pltpu.VMEM((B,128),f32),pltpu.VMEM((B,128),f32),pltpu.VMEM((8,N),f32)]),
      compiler_params=pltpu.CompilerParams(vmem_limit_bytes=48<<20),
      cost_estimate=pl.CostEstimate(flops=S*10*N*N*128,bytes_accessed=S*N*2400,transcendentals=S*N*N),
      )(inv,nb,x,o,do,lse)


def one_fwd_kernel(own_ref, q_ref, x_ref, o_ref, lse_ref, vt, sb, acc, *, B, NB):
    nb = own_ref[NB + 2]
    def tv(j,_):
        r=pl.multiple_of(own_ref[j]*B,B)
        t=x_ref[pl.ds(r,B),:].T
        w=pl.multiple_of(j*B,B)
        vt[0:64,pl.ds(w,B)]=t[64:128,:]
        vt[64:80,pl.ds(w,B)]=(lax.broadcasted_iota(jnp.int32,(16,B),0)==0).astype(bf16)
        return 0
    lax.fori_loop(0,nb,tv,0)
    rr=lax.broadcasted_iota(jnp.int32,(B,B),0)
    cc=lax.broadcasted_iota(jnp.int32,(B,B),1)
    for t in range(2):
        i=own_ref[NB+t]
        @pl.when(i>=nb)
        def _():
            o_ref[t*B:(t+1)*B,:]=jnp.zeros((B,64),bf16)
            lse_ref[:,t*B:(t+1)*B]=jnp.zeros((8,B),f32)
        @pl.when(i<nb)
        def _():
            qs=q_ref[t*B:(t+1)*B,:].astype(f32)*(0.125*LOG2E)
            q=qs.astype(bf16)
            ql=(qs-q.astype(f32)).astype(bf16)
            acc[...]=jnp.zeros_like(acc)
            def step(j,m,diag):
                k=x_ref[pl.ds(pl.multiple_of(own_ref[j]*B,B),B),0:64]
                st=dot_nt(k,q)+dot_nt(k,ql)
                if diag: st=jnp.where(rr<=cc,st,NEG)
                mn=jnp.maximum(m,jnp.max(st,axis=0,keepdims=True))
                p=jnp.exp2(st-mn)
                al=jnp.exp2(m-mn)
                v=vt[:,pl.ds(pl.multiple_of(j*B,B),B)]
                acc[...]=acc[...]*al+dot_nn(v,p.astype(bf16))
                return mn
            m=lax.fori_loop(0,i,lambda j,m: step(j,m,False),jnp.full((1,B),NEG,f32))
            m=step(i,m,True)
            l=acc[64:65,:]
            o_ref[t*B:(t+1)*B,:]=(acc[0:64,:]*(1.0/l)).T.astype(bf16)
            lse_ref[:,t*B:(t+1)*B]=jnp.broadcast_to(m+jnp.log2(l),(8,B))


def one_fwd(q,x,own,B):
    N=x.shape[0]; R=q.shape[0]; NB=N//B
    full=lambda *_:(0,0)
    last=lambda *_:(0,3)
    return pl.pallas_call(functools.partial(one_fwd_kernel,B=B,NB=NB),
      out_shape=(jax.ShapeDtypeStruct((R,64),bf16),jax.ShapeDtypeStruct((8,R),f32)),
      grid_spec=pltpu.PrefetchScalarGridSpec(num_scalar_prefetch=1,grid=(1,),
        in_specs=[pl.BlockSpec((R,64),full),pl.BlockSpec((N,128),last)],
        out_specs=[pl.BlockSpec((R,64),full),pl.BlockSpec((8,R),full)],
        scratch_shapes=[pltpu.VMEM((80,N),bf16),pltpu.VMEM((B,B),f32),pltpu.VMEM((80,B),f32)]),
      compiler_params=pltpu.CompilerParams(vmem_limit_bytes=48<<20),
      cost_estimate=pl.CostEstimate(flops=4*R*N*128,bytes_accessed=N*256+R*512,transcendentals=R*N),
      )(own,q,x)


def one_bwd_kernel(own_ref, q_ref, x_ref, o_ref, do_ref, lse_ref, dq_ref, dx_ref, dkv, dq, *, B, NB):
    nb = own_ref[NB + 2]
    rr=lax.broadcasted_iota(jnp.int32,(B,B),0)
    cc=lax.broadcasted_iota(jnp.int32,(B,B),1)
    ones=jnp.ones((8,64),bf16)
    dkv[...]=jnp.zeros_like(dkv)
    for t in range(2):
        i=own_ref[NB+t]
        sl=slice(t*B,(t+1)*B)
        @pl.when(i>=nb)
        def _():
            dq_ref[sl,:]=jnp.zeros((B,64),bf16)
        @pl.when(i<nb)
        def _():
            qr=q_ref[sl,:]
            qs=qr.astype(f32)*(0.125*LOG2E)
            q=qs.astype(bf16)
            ql=(qs-q.astype(f32)).astype(bf16)
            qd=qr*jnp.asarray(0.125,bf16)
            do=do_ref[sl,:]
            prod=o_ref[sl,:].astype(f32)*do.astype(f32)
            hi=prod.astype(bf16); lo=(prod-hi.astype(f32)).astype(bf16)
            dl=(dot_nt(ones,hi)+dot_nt(ones,lo))[0:1,:]
            lse=lse_ref[0:1,sl]
            dq[...]=jnp.zeros_like(dq)
            def step(j,diag):
                r=pl.multiple_of(own_ref[j]*B,B)
                k=x_ref[pl.ds(r,B),0:64]
                v=x_ref[pl.ds(r,B),64:128]
                st=dot_nt(k,q)+dot_nt(k,ql)
                p=jnp.exp2(st-lse)
                if diag: p=jnp.where(rr<=cc,p,0.0)
                dp=dot_nt(v,do)
                ds=(p*(dp-dl)).astype(bf16)
                dkv[pl.ds(r,B),64:128]+=dot_nn(p.astype(bf16),do)
                dkv[pl.ds(r,B),0:64]+=dot_nn(ds,qd)
                dq[...]+=dot_nn(k.T,ds)
            def body(j,_):
                step(j,False); return 0
            lax.fori_loop(0,i,body,0)
            step(i,True)
            dq_ref[sl,:]=(dq[...].T*0.125).astype(bf16)
    dx_ref[...]=dkv[...].astype(bf16)


def one_bwd(q,x,o,do,lse,own,B):
    N=x.shape[0]; R=q.shape[0]; NB=N//B
    full=lambda *_:(0,0)
    last=lambda *_:(0,3)
    return pl.pallas_call(functools.partial(one_bwd_kernel,B=B,NB=NB),
      out_shape=(jax.ShapeDtypeStruct((R,64),bf16),jax.ShapeDtypeStruct((N,128),bf16)),
      grid_spec=pltpu.PrefetchScalarGridSpec(num_scalar_prefetch=1,grid=(1,),
        in_specs=[pl.BlockSpec((R,64),full),pl.BlockSpec((N,128),last),pl.BlockSpec((R,64),full),pl.BlockSpec((R,64),full),pl.BlockSpec((8,R),full)],
        out_specs=[pl.BlockSpec((R,64),full),pl.BlockSpec((N,128),full)],
        scratch_shapes=[pltpu.VMEM((N,128),f32),pltpu.VMEM((64,B),f32)]),
      compiler_params=pltpu.CompilerParams(vmem_limit_bytes=48<<20),
      cost_estimate=pl.CostEstimate(flops=10*R*N*128,bytes_accessed=N*512+R*1024,transcendentals=R*N),
      )(own,q,x,o,do,lse)


def join_kernel(*refs, count):
    t = pl.program_id(0)
    stacks, tail, out = refs[:-2], refs[-2], refs[-1]
    for i, ref in enumerate(stacks):
        @pl.when((t >= i * count) & (t < (i + 1) * count))
        def _(ref=ref):
            out[...] = ref[0]

    @pl.when(t >= len(stacks) * count)
    def _():
        out[:, :tail.shape[1]] = tail[...]


def join(stacks, tail):
    C, R, W = stacks[0].shape
    n = len(stacks)
    T = tail.shape[1]

    def at(i):
        return lambda t: (jnp.clip(t - i * C, 0, C - 1), 0, 0)
    return pl.pallas_call(functools.partial(join_kernel, count=C),
        out_shape=jax.ShapeDtypeStruct((R, n * C * W + T), bf16),
        grid=(n * C + 1,),
        in_specs=[pl.BlockSpec((1, R, W), at(i)) for i in range(n)] + [pl.BlockSpec((R, T), lambda t: (0, 0))],
        out_specs=pl.BlockSpec((R, W), lambda t: (0, t)),
        compiler_params=pltpu.CompilerParams(vmem_limit_bytes=56 << 20),
        cost_estimate=pl.CostEstimate(flops=0, bytes_accessed=4 * R * (n * C * W + T), transcendentals=0),
    )(*stacks, tail)


def deal_kernel(x_ref, o_ref):
    o_ref[0] = x_ref[...]


def deal(x, first, C, W):
    R = x.shape[0]
    return pl.pallas_call(deal_kernel,
        out_shape=jax.ShapeDtypeStruct((C, R, W), bf16),
        grid=(C,),
        in_specs=[pl.BlockSpec((R, W), lambda t: (0, first + t))],
        out_specs=pl.BlockSpec((1, R, W), lambda t: (t, 0, 0)),
        compiler_params=pltpu.CompilerParams(vmem_limit_bytes=56 << 20),
        cost_estimate=pl.CostEstimate(flops=0, bytes_accessed=4 * R * C * W, transcendentals=0),
    )(x)


def join_kernel(*refs, count):
    t = pl.program_id(0)
    stacks, tail, out = refs[:-2], refs[-2], refs[-1]
    for i, ref in enumerate(stacks):
        @pl.when((t >= i * count) & (t < (i + 1) * count))
        def _(ref=ref):
            out[...] = ref[0]

    @pl.when(t >= len(stacks) * count)
    def _():
        out[:, :tail.shape[1]] = tail[...]


def join(stacks, tail):
    C, R, W = stacks[0].shape
    n = len(stacks)
    T = tail.shape[1]

    def at(i):
        return lambda t: (jnp.clip(t - i * C, 0, C - 1), 0, 0)
    return pl.pallas_call(functools.partial(join_kernel, count=C),
        out_shape=jax.ShapeDtypeStruct((R, n * C * W + T), bf16),
        grid=(n * C + 1,),
        in_specs=[pl.BlockSpec((1, R, W), at(i)) for i in range(n)] + [pl.BlockSpec((R, T), lambda t: (0, 0))],
        out_specs=pl.BlockSpec((R, W), lambda t: (0, t)),
        compiler_params=pltpu.CompilerParams(vmem_limit_bytes=56 << 20),
        cost_estimate=pl.CostEstimate(flops=0, bytes_accessed=4 * R * (n * C * W + T), transcendentals=0),
    )(*stacks, tail)


def deal_kernel(x_ref, o_ref):
    o_ref[0] = x_ref[...]


def deal(x, first, C, W):
    R = x.shape[0]
    return pl.pallas_call(deal_kernel,
        out_shape=jax.ShapeDtypeStruct((C, R, W), bf16),
        grid=(C,),
        in_specs=[pl.BlockSpec((R, W), lambda t: (0, first + t))],
        out_specs=pl.BlockSpec((1, R, W), lambda t: (t, 0, 0)),
        compiler_params=pltpu.CompilerParams(vmem_limit_bytes=56 << 20),
        cost_estimate=pl.CostEstimate(flops=0, bytes_accessed=4 * R * C * W, transcendentals=0),
    )(x)


HEADS = 17
EPSILON = 1e-05
FS = ("zz", "core")


def norm_parts(v):
    mean = jnp.mean(v, axis=-1, keepdims=True)
    c = v - mean
    r = lax.rsqrt(jnp.mean(c * c, axis=-1, keepdims=True) + EPSILON)
    return c * r, r


def norm_back(dn, v, gain):
    xhat, r = norm_parts(v)
    y = dn * gain
    a = jnp.mean(y, axis=-1, keepdims=True)
    b = jnp.mean(y * xhat, axis=-1, keepdims=True)
    return r * (y - a - xhat * b), jnp.sum(dn * xhat, axis=0), jnp.sum(dn, axis=0)


def col_sum(x):
    return jnp.dot(jnp.ones((16, x.shape[0]), bf16), x, preferred_element_type=f32)[0]


def gelu_parts(u):
    z = jnp.abs(u) * 0.7071067811865476
    t = 1.0 / (1.0 + 0.3275911 * z)
    e = jnp.exp(-z * z)
    poly = t * (0.254829592 + t * (-0.284496736 + t * (1.421413741 + t * (-1.453152027 + t * 1.061405429))))
    half = 0.5 * poly * e
    cdf = jnp.where(u >= 0, 1.0 - half, half)
    return u * cdf, cdf + u * e * 0.3989422804014327


def local(
    tokens, cotangent, lengths, block_order,
    ln1_gain, ln1_bias, qkv_weight, q_bias, v_bias, out_weight, out_bias,
    ln2_gain, ln2_bias, up_weight, up_bias, down_weight, down_bias,
    *, G, S,
):
    slots, rows, width = tokens.shape
    C = lax.axis_size("ctx")
    me = lax.axis_index("ctx")
    N = rows * C
    B = rows // 2
    NB = 2 * C
    L = ln1_gain.shape[0]
    shard = ln1_gain.shape[1]
    HW = G * 128
    x_tokens = tokens[0]

    steps = jnp.arange(NB, dtype=jnp.int32)
    order = block_order[0]
    inverse = jnp.sum(jnp.where(order[None, :] == steps[:, None], steps[None, :], 0), axis=1).astype(jnp.int32)
    count = (lengths + (B - 1)) // B
    meta = jnp.concatenate([inverse, count])
    def swap(x):
        return lax.ppermute(x, "core", [(0, 1), (1, 0)])

    metas = [meta, swap(meta)][:S]
    phase_inv = [t[None, :NB] for t in metas]
    phase_nb = [t[NB:] for t in metas]
    own = jnp.concatenate([inverse, lax.dynamic_slice_in_dim(order, 2 * me, 2, 0), count])
    own_pos = (lax.dynamic_slice_in_dim(order, 2 * me, 2, 0)[:, None] * B + jnp.arange(B, dtype=jnp.int32)).reshape(rows, 1)
    live = (own_pos < lengths[0]).astype(f32)

    vectors = [ln1_gain, ln1_bias, q_bias, v_bias, out_bias, ln2_gain, ln2_bias, down_bias, up_bias]
    vec = jnp.concatenate(vectors, axis=1).astype(bf16)
    vec = lax.all_gather(vec, FS).astype(f32)

    def vector(index, layer):
        if index < 8:
            return vec[:, layer, index * shard:(index + 1) * shard].reshape(-1)
        return vec[:, layer, 8 * shard:].reshape(-1)

    def pack(w):
        parts = []
        for g in range(G):
            parts += [w[:, kind * width + g * 128:kind * width + g * 128 + 128] for kind in range(3)]
        last = width - 64
        parts += [w[:, kind * width + last:kind * width + width] for kind in (1, 2, 0)]
        return jnp.concatenate(parts, axis=1)

    def unpack(w):
        tail = G * 384
        parts = []
        for kind, last in enumerate((128, 0, 64)):
            parts += [w[:, g * 384 + kind * 128:g * 384 + kind * 128 + 128] for g in range(G)]
            parts.append(w[:, tail + last:tail + last + 64])
        return jnp.concatenate(parts, axis=1)

    def fetch(w):
        return lax.all_gather(w.astype(bf16), FS, axis=0, tiled=True)

    weights = []
    for layer in range(L):
        weights.append((
            fetch(pack(qkv_weight[layer].astype(bf16))),
            fetch(out_weight[layer]),
            fetch(up_weight[layer]),
            fetch(down_weight[layer]),
        ))

    def plain(x):
        return with_layout_constraint(x, Layout(major_to_minor=tuple(range(x.ndim))))

    def exchange(x):
        return plain(lax.all_to_all(plain(x), "ctx", 0, 0))

    def after(x, *others):
        return lax.optimization_barrier((x,) + others)

    stream = x_tokens.astype(f32)
    records = []
    for layer in range(L):
        qkv_w, out_w, up_w, down_w = weights[layer]
        xhat, _ = norm_parts(stream)
        n1 = (xhat * vector(0, layer) + vector(1, layer)).astype(bf16)
        q_b, v_b = vector(2, layer), vector(3, layer)
        bias = pack(jnp.concatenate([q_b, jnp.zeros_like(q_b), v_b])[None])[0]
        projected = (jnp.dot(n1, qkv_w, preferred_element_type=f32) + bias).astype(bf16)
        wide = [deal(projected, s * C, C, 384) for s in range(S)]
        tail = projected[:, G * 384:]
        if S == 2:
            wide[1] = swap(wide[1])
        kv16 = jnp.broadcast_to(tail[None, :, :128], (C, rows, 128))
        q16 = tail[:, 128:]
        heads, o, lse, o_back = [], [], [], []
        for s in range(S):
            t = wide[s]
            if s == S - 1:
                t = jnp.concatenate([t, kv16], axis=2)
            if s:
                t, heads[0] = after(t, heads[0])
            heads.append(exchange(t).reshape(1, N, -1))
        for s in range(S):
            o_s, lse_s = flash_fwd(heads[s], phase_inv[s], phase_nb[s], B)
            o.append(o_s)
            lse.append(lse_s)
            t = o_s.reshape(C, rows, 128)
            if s:
                t, o_back[0] = after(t, o_back[0])
            o_back.append(exchange(swap(t) if s else t))
        o16, lse16 = one_fwd(q16, heads[-1][0], own, B)
        mixed = join(o_back, o16)
        m = stream + jnp.dot(mixed, out_w, preferred_element_type=f32) + vector(4, layer)
        xhat2, _ = norm_parts(m)
        n2 = (xhat2 * vector(5, layer) + vector(6, layer)).astype(bf16)
        u = jnp.dot(n2, up_w, preferred_element_type=f32) + vector(8, layer)
        a, slope = gelu_parts(u)
        a = a.astype(bf16)
        slope = slope.astype(bf16)
        records.append((stream, n1, heads, q16, o, lse, o16, lse16, mixed, m, n2, a, slope))
        stream = m + jnp.dot(a, down_w, preferred_element_type=f32) + vector(7, layer)
    activations = (stream * live).astype(bf16)[None]

    def reduce_fsdp(g):
        return lax.psum_scatter(g.astype(bf16), FS, scatter_dimension=0, tiled=True)

    def reduce_ctx(g):
        return lax.psum(g, "ctx").astype(f32)

    grad = cotangent[0].astype(f32) * live
    matrices = [None] * L
    fours = [None] * L
    ffns = [None] * L
    small = [None] * L

    def ctx_end(mine):
        return exchange(jnp.broadcast_to(mine[None], (C,) + mine.shape))

    def ctx_sum(shards):
        mine, sizes = ctx_begin(shards)
        return ctx_end(mine), sizes

    def ctx_begin(shards):
        pieces = []
        for t in shards:
            if t.shape[1] == width:
                pieces.append(t.reshape(C, -1, width))
            else:
                pieces.append(jnp.transpose(t.reshape(t.shape[0], C, -1), (1, 0, 2)).reshape(C, -1, width))
        sizes = [t.shape[1] for t in pieces]
        parts = exchange(jnp.concatenate(pieces, axis=1))
        mine = jnp.sum(parts.astype(f32), axis=0).astype(bf16)
        return mine, sizes

    def spread(summed, shapes):
        whole, sizes = summed
        out, at = [], 0
        for n, (r, c) in zip(sizes, shapes):
            t = whole[:, at:at + n].astype(f32)
            at += n
            if c == width:
                out.append(t.reshape(r, c))
            else:
                out.append(jnp.transpose(t.reshape(C, r, c // C), (1, 0, 2)).reshape(r, c))
        return out

    wide_shape, tall_shape = (shard, 4 * width), (4 * shard, width)
    for layer in reversed(range(L)):
        stream_in, n1, heads, q16, o, lse, o16, lse16, mixed, m, n2, a, slope = records[layer]
        qkv_w, out_w, up_w, down_w = weights[layer]
        gb = grad.astype(bf16)
        d_down_b = col_sum(gb)
        d_down = jnp.einsum("rf,rd->fd", a, gb, preferred_element_type=f32).astype(bf16)
        gb, d_down = after(gb, plain(d_down))
        d_down = reduce_fsdp(d_down)
        du = (jnp.einsum("rd,fd->rf", gb, down_w, preferred_element_type=f32) * slope.astype(f32)).astype(bf16)
        d_up_b = col_sum(du)
        d_up = jnp.einsum("rd,rf->df", n2, du, preferred_element_type=f32).astype(bf16)
        du, d_up = after(du, plain(d_up))
        d_up = reduce_fsdp(d_up)
        dn2 = jnp.einsum("rf,df->rd", du, up_w, preferred_element_type=f32)
        back, d_gain2, d_bias2 = norm_back(dn2, m, vector(5, layer))
        gm = grad + back
        gmb = gm.astype(bf16)
        d_out_b = col_sum(gmb)
        d_out = jnp.einsum("rd,re->de", mixed, gmb, preferred_element_type=f32).astype(bf16)
        if layer < L - 1:
            done = after(gmb, *ffn_sum)
            gmb, ffn_sum = done[0], done[1:]
        d_o = []
        for s in range(S):
            w = out_w[C * 128 * s:C * 128 * (s + 1)].reshape(C, 128, width)
            d_o.append(jnp.einsum("re,gce->grc", gmb, w, preferred_element_type=f32).astype(bf16))
        d_o16 = jnp.einsum("re,ce->rc", gmb, out_w[HW:], preferred_element_type=f32).astype(bf16)
        dq16, dkv16 = one_bwd(q16, heads[-1][0], o16, d_o16, lse16, own, B)
        d_oh, d_wide = [], []
        for s in range(S):
            t = d_o[s]
            if s:
                t = swap(t)
            if s == S - 1:
                t = jnp.concatenate([t, dkv16.reshape(C, rows, 128)], axis=2)
            if s:
                t, d_oh[0] = after(t, d_oh[0])
            if s == S - 1 and layer < L - 1:
                t, fours[layer + 1] = after(t, fours[layer + 1])
            d_oh.append(exchange(t).reshape(1, N, -1))
        dkv16 = jnp.sum(d_oh[-1].reshape(C, rows, 256)[:, :, 128:].astype(f32), axis=0)
        for s in range(S):
            t = flash_bwd(heads[s], o[s], d_oh[s], lse[s], phase_inv[s], phase_nb[s], B)
            t = t.reshape(C, rows, 384)
            if s:
                t, d_wide[0], d_down = after(t, d_wide[0], d_down)
            if s == S - 1 and layer < L - 1:
                four_sum = lax.psum((fours[layer + 1], d_down), "ctx")
            d_wide.append(exchange(swap(t) if s else t))
        d_tail = jnp.concatenate([dkv16.astype(bf16), dq16], axis=1)
        d_row = join(d_wide, d_tail)
        d_row, d_up = after(d_row, d_up)
        if layer:
            ffn_sum = lax.psum((d_up, d_down), "ctx")
        else:
            up_sum = ctx_sum([d_up])
        d_qkv = jnp.einsum("rd,rc->dc", n1, d_row, preferred_element_type=f32).astype(bf16)
        d_four = jnp.concatenate([d_qkv, d_out], axis=1)
        if layer:
            d_row, d_four = after(d_row, plain(d_four))
        d_four = reduce_fsdp(d_four)
        sums = unpack(col_sum(d_row)[None])[0]
        dn1 = jnp.einsum("rc,dc->rd", d_row, qkv_w, preferred_element_type=f32)
        back, d_gain1, d_bias1 = norm_back(dn1, stream_in, vector(0, layer))
        grad = gm + back
        fours[layer] = d_four
        ffns[layer] = (d_up, d_down)
        if layer == 0:
            last = ctx_sum([d_four])
            matrices[1] = [four_sum[0].astype(f32), ffn_sum[0].astype(f32), ffn_sum[1].astype(f32)]
            matrices[0] = spread(last, [wide_shape]) + spread(up_sum, [wide_shape]) + [four_sum[1].astype(f32)]
        small[layer] = jnp.concatenate([
            t.reshape(-1, n) for t, n in (
                (d_gain1, shard), (d_bias1, shard), (sums[:width], shard), (sums[2 * width:], shard), (d_out_b, shard),
                (d_gain2, shard), (d_bias2, shard), (d_down_b, shard), (d_up_b, 4 * shard))], axis=1)

    vec_grads = jnp.stack(small, axis=1)
    vec_grads = jnp.sum(lax.all_to_all(vec_grads, FS, 0, 0), axis=0)
    vec_grads = lax.psum(vec_grads, "ctx")
    vg = [vec_grads[:, i * shard:(i + 1) * shard] for i in range(8)] + [vec_grads[:, 8 * shard:]]

    g_qkv = jnp.stack([unpack(matrices[layer][0][:, :3 * width]) for layer in range(L)])
    g_out = jnp.stack([matrices[layer][0][:, 3 * width:] for layer in range(L)])
    g_up = jnp.stack([matrices[layer][1] for layer in range(L)])
    g_down = jnp.stack([matrices[layer][2] for layer in range(L)])
    return (activations, grad[None], vg[0], vg[1], g_qkv, vg[2], vg[3], g_out, vg[4], vg[5], vg[6], g_up, vg[8], g_down, vg[7])


def solution(mesh):
    F, C = mesh.devices.shape
    inner = Mesh(mesh.devices.reshape(F // 2, 2, C), ("zz", "core", "ctx"))
    S = 2 if 16 // (2 * C) >= 2 else 1
    G = S * C
    rows = P(FS, "ctx", None)
    vec, mat = P(None, FS), P(None, FS, None)
    return jax.shard_map(
        functools.partial(local, G=G, S=S),
        mesh=inner,
        in_specs=(rows, rows, P(FS), P(FS, None), vec, vec, mat, vec, vec, mat, vec, vec, vec, mat, vec, mat, vec),
        out_specs=(rows, rows, vec, vec, mat, vec, vec, mat, vec, vec, vec, mat, vec, mat, vec),
        check_vma=False,
    )
```

```python
import functools
import jax, jax.numpy as jnp
from jax import lax
from jax.experimental import pallas as pl
from jax.experimental.pallas import tpu as pltpu
from jax.experimental.layout import Layout, with_layout_constraint
from jax.sharding import Mesh, PartitionSpec as P
f32=jnp.float32; bf16=jnp.bfloat16
NEG=-1e30
def dot_nt(a,b): return lax.dot_general(a,b,(((1,),(1,)),((),())),preferred_element_type=f32)
def dot_nn(a,b): return lax.dot_general(a,b,(((1,),(0,)),((),())),preferred_element_type=f32)

LOG2E=1.4426950408889634
def split(q,h,low):
    qs=q.astype(f32)*(0.125*LOG2E)
    hi=qs.astype(bf16).astype(f32); lo=qs-hi
    rl=pltpu.roll(lo,64,1)
    c=jnp.where(low,hi,rl) if h==0 else jnp.where(low,rl,hi)
    return c.astype(bf16)
def dup(k,h,low):
    kf=k.astype(f32); rl=pltpu.roll(kf,64,1)
    c=jnp.where(low,kf,rl) if h==0 else jnp.where(low,rl,kf)
    return c.astype(bf16)
def fwd_kernel(inv_ref, nb_ref, x_ref, o_ref, lse_ref, vt, kd, sb, acc, *, B, NB):
    s=pl.program_id(0)
    nb=nb_ref[s]
    lane=lax.broadcasted_iota(jnp.int32,(1,128),1)
    low=lane<64
    def tv(j,_):
        r=pl.multiple_of(inv_ref[s,j]*B,B)
        w=pl.multiple_of(j*B,B)
        t=x_ref[0,pl.ds(r,B),256:384].T
        one=(lax.broadcasted_iota(jnp.int32,(16,B),0)==0).astype(bf16)
        for h in range(2):
            vt[80*h:80*h+64,pl.ds(w,B)]=t[64*h:64*h+64,:]
            vt[80*h+64:80*h+80,pl.ds(w,B)]=one
            kd[h,pl.ds(w,B),:]=dup(x_ref[0,pl.ds(r,B),128:256],h,low)
        return 0
    lax.fori_loop(0,nb,tv,0)
    rr=lax.broadcasted_iota(jnp.int32,(B,B),0)
    cc=lax.broadcasted_iota(jnp.int32,(B,B),1)
    def qblock(i,_):
        r=pl.multiple_of(inv_ref[s,i]*B,B)
        q=x_ref[0,pl.ds(r,B),0:128]
        qh=[split(q,h,low) for h in range(2)]
        acc[...]=jnp.zeros_like(acc)
        def scores(j,slot):
            for h in range(2):
                sb[slot,h]=dot_nt(kd[h,pl.ds(pl.multiple_of(j*B,B),B),:],qh[h])
        def step(j,carry,diag):
            out=[]
            for h in range(2):
                m=carry[h]
                st=sb[j%2,h]
                if diag: st=jnp.where(rr<=cc,st,NEG)
                mn=jnp.maximum(m,jnp.max(st,axis=0,keepdims=True))
                p=jnp.exp2(st-mn)
                al=jnp.exp2(m-mn)
                v=vt[80*h:80*h+80,pl.ds(pl.multiple_of(j*B,B),B)]
                acc[h]=acc[h]*al+dot_nn(v,p.astype(bf16))
                out.append(mn)
            return tuple(out)
        scores(0,0)
        def both(j,c):
            scores(j+1,(j+1)%2)
            return step(j,c,False)
        n=jnp.full((1,B),NEG,f32)
        c=lax.fori_loop(0,i,both,(n,n))
        c=step(i,c,True)
        os=[]
        for h in range(2):
            l=acc[h,64:65,:]
            os.append(acc[h,0:64,:]*(1.0/l))
            lse_ref[0,pl.ds(h,1),pl.ds(r,B)]=c[h]+jnp.log2(l)
        o_ref[0,pl.ds(r,B),:]=jnp.concatenate(os,0).T.astype(bf16)
        return 0
    lax.fori_loop(0,nb,qblock,0)
    def pad(i,_):
        r=pl.multiple_of(inv_ref[s,i]*B,B)
        o_ref[0,pl.ds(r,B),:]=jnp.zeros((B,128),bf16)
        lse_ref[0,:,pl.ds(r,B)]=jnp.zeros((8,B),f32)
        return 0
    lax.fori_loop(nb,NB,pad,0)

def flash_fwd(x,inv,nb,B):
    S,N,_=x.shape
    NB=N//B
    return pl.pallas_call(functools.partial(fwd_kernel,B=B,NB=NB),
      out_shape=(jax.ShapeDtypeStruct((S,N,128),bf16),jax.ShapeDtypeStruct((S,8,N),f32)),
      grid_spec=pltpu.PrefetchScalarGridSpec(num_scalar_prefetch=2,grid=(S,),
        in_specs=[pl.BlockSpec((1,N,384),lambda s,*_:(s,0,0))],
        out_specs=[pl.BlockSpec((1,N,128),lambda s,*_:(s,0,0)),pl.BlockSpec((1,8,N),lambda s,*_:(s,0,0))],
        scratch_shapes=[pltpu.VMEM((160,N),bf16),pltpu.VMEM((2,N,128),bf16),pltpu.VMEM((2,2,B,B),f32),pltpu.VMEM((2,80,B),f32)]),
      compiler_params=pltpu.CompilerParams(vmem_limit_bytes=48<<20),
      cost_estimate=pl.CostEstimate(flops=S*4*N*N*128,bytes_accessed=S*N*1024,transcendentals=S*N*N),
      )(inv,nb,x)

def bwd_kernel(inv_ref, nb_ref, x_ref, o_ref, do_ref, lse_ref, dx_ref, kt, qd, dq, dk, dv, dl, *, B, NB):
    s=pl.program_id(0)
    nb=nb_ref[s]
    lane=lax.broadcasted_iota(jnp.int32,(1,128),1)
    low=lane<64
    hm=(lax.broadcasted_iota(jnp.int32,(8,128),1)//64==lax.broadcasted_iota(jnp.int32,(8,128),0)).astype(bf16)
    def prep(j,_):
        r=pl.multiple_of(inv_ref[s,j]*B,B)
        w=pl.multiple_of(j*B,B)
        kt[:,pl.ds(w,B)]=x_ref[0,pl.ds(r,B),128:256].T
        for h in range(2): qd[h,pl.ds(w,B),:]=split(x_ref[0,pl.ds(r,B),0:128],h,low)
        prod=o_ref[0,pl.ds(r,B),:].astype(f32)*do_ref[0,pl.ds(r,B),:].astype(f32)
        hi=prod.astype(bf16); lo=(prod-hi.astype(f32)).astype(bf16)
        dl[:,pl.ds(w,B)]=dot_nt(hm,hi)+dot_nt(hm,lo)
        dq[:,pl.ds(w,B)]=jnp.zeros((128,B),f32)
        return 0
    lax.fori_loop(0,nb,prep,0)
    rr=lax.broadcasted_iota(jnp.int32,(B,B),0)
    cc=lax.broadcasted_iota(jnp.int32,(B,B),1)
    def kblock(j,_):
        r=pl.multiple_of(inv_ref[s,j]*B,B)
        k=x_ref[0,pl.ds(r,B),128:256]
        v=x_ref[0,pl.ds(r,B),256:384]
        kdh=[dup(k,h,low) for h in range(2)]
        dk[...]=jnp.zeros_like(dk); dv[...]=jnp.zeros_like(dv)
        def step(i,diag):
            ri=pl.multiple_of(inv_ref[s,i]*B,B)
            wi=pl.multiple_of(i*B,B)
            q=x_ref[0,pl.ds(ri,B),0:128]*jnp.asarray(0.125,bf16)
            do=do_ref[0,pl.ds(ri,B),:]
            zero=jnp.zeros_like(q)
            dvs=[];dks=[]
            for h in range(2):
                qh=jnp.where(low,q,zero) if h==0 else jnp.where(low,zero,q)
                doh=jnp.where(low,do,zero) if h==0 else jnp.where(low,zero,do)
                st=dot_nt(kdh[h],qd[h,pl.ds(wi,B),:])
                p=jnp.exp2(st-lse_ref[0,pl.ds(h,1),pl.ds(ri,B)])
                if diag: p=jnp.where(rr<=cc,p,0.0)
                dvs.append(dot_nn(p.astype(bf16),doh))
                dp=dot_nt(v,doh)
                ds=(p*(dp-dl[pl.ds(h,1),pl.ds(wi,B)])).astype(bf16)
                dks.append(dot_nn(ds,qh))
                kh=kt[64*h:64*h+64,pl.ds(pl.multiple_of(j*B,B),B)]
                dq[64*h:64*h+64,pl.ds(wi,B)]+=dot_nn(kh,ds)
            dv[...]+=dvs[0]+dvs[1]
            dk[...]+=dks[0]+dks[1]
        step(j,True)
        def body(i,_):
            step(i,False); return 0
        lax.fori_loop(j+1,nb,body,0)
        dx_ref[0,pl.ds(r,B),128:256]=dk[...].astype(bf16)
        dx_ref[0,pl.ds(r,B),256:384]=dv[...].astype(bf16)
        return 0
    lax.fori_loop(0,nb,kblock,0)
    def fin(i,_):
        r=pl.multiple_of(inv_ref[s,i]*B,B)
        dx_ref[0,pl.ds(r,B),0:128]=(dq[:,pl.ds(pl.multiple_of(i*B,B),B)].T*0.125).astype(bf16)
        return 0
    lax.fori_loop(0,nb,fin,0)
    def pad(i,_):
        r=pl.multiple_of(inv_ref[s,i]*B,B)
        dx_ref[0,pl.ds(r,B),:]=jnp.zeros((B,384),bf16)
        return 0
    lax.fori_loop(nb,NB,pad,0)

def flash_bwd(x,o,do,lse,inv,nb,B):
    S,N,_=x.shape
    NB=N//B
    return pl.pallas_call(functools.partial(bwd_kernel,B=B,NB=NB),
      out_shape=jax.ShapeDtypeStruct((S,N,384),bf16),
      grid_spec=pltpu.PrefetchScalarGridSpec(num_scalar_prefetch=2,grid=(S,),
        in_specs=[pl.BlockSpec((1,N,384),lambda s,*_:(s,0,0)),pl.BlockSpec((1,N,128),lambda s,*_:(s,0,0)),
                  pl.BlockSpec((1,N,128),lambda s,*_:(s,0,0)),pl.BlockSpec((1,8,N),lambda s,*_:(s,0,0))],
        out_specs=pl.BlockSpec((1,N,384),lambda s,*_:(s,0,0)),
        scratch_shapes=[pltpu.VMEM((128,N),bf16),pltpu.VMEM((2,N,128),bf16),pltpu.VMEM((128,N),f32),pltpu.VMEM((B,128),f32),pltpu.VMEM((B,128),f32),pltpu.VMEM((8,N),f32)]),
      compiler_params=pltpu.CompilerParams(vmem_limit_bytes=48<<20),
      cost_estimate=pl.CostEstimate(flops=S*10*N*N*128,bytes_accessed=S*N*2400,transcendentals=S*N*N),
      )(inv,nb,x,o,do,lse)


def one_fwd_kernel(own_ref, q_ref, x_ref, o_ref, lse_ref, vt, sb, acc, *, B, NB):
    nb = own_ref[NB + 2]
    def tv(j,_):
        r=pl.multiple_of(own_ref[j]*B,B)
        t=x_ref[pl.ds(r,B),:].T
        w=pl.multiple_of(j*B,B)
        vt[0:64,pl.ds(w,B)]=t[64:128,:]
        vt[64:80,pl.ds(w,B)]=(lax.broadcasted_iota(jnp.int32,(16,B),0)==0).astype(bf16)
        return 0
    lax.fori_loop(0,nb,tv,0)
    rr=lax.broadcasted_iota(jnp.int32,(B,B),0)
    cc=lax.broadcasted_iota(jnp.int32,(B,B),1)
    for t in range(2):
        i=own_ref[NB+t]
        @pl.when(i>=nb)
        def _():
            o_ref[t*B:(t+1)*B,:]=jnp.zeros((B,64),bf16)
            lse_ref[:,t*B:(t+1)*B]=jnp.zeros((8,B),f32)
        @pl.when(i<nb)
        def _():
            qs=q_ref[t*B:(t+1)*B,:].astype(f32)*(0.125*LOG2E)
            q=qs.astype(bf16)
            ql=(qs-q.astype(f32)).astype(bf16)
            acc[...]=jnp.zeros_like(acc)
            def step(j,m,diag):
                k=x_ref[pl.ds(pl.multiple_of(own_ref[j]*B,B),B),0:64]
                st=dot_nt(k,q)+dot_nt(k,ql)
                if diag: st=jnp.where(rr<=cc,st,NEG)
                mn=jnp.maximum(m,jnp.max(st,axis=0,keepdims=True))
                p=jnp.exp2(st-mn)
                al=jnp.exp2(m-mn)
                v=vt[:,pl.ds(pl.multiple_of(j*B,B),B)]
                acc[...]=acc[...]*al+dot_nn(v,p.astype(bf16))
                return mn
            m=lax.fori_loop(0,i,lambda j,m: step(j,m,False),jnp.full((1,B),NEG,f32))
            m=step(i,m,True)
            l=acc[64:65,:]
            o_ref[t*B:(t+1)*B,:]=(acc[0:64,:]*(1.0/l)).T.astype(bf16)
            lse_ref[:,t*B:(t+1)*B]=jnp.broadcast_to(m+jnp.log2(l),(8,B))


def one_fwd(q,x,own,B):
    N=x.shape[0]; R=q.shape[0]; NB=N//B
    full=lambda *_:(0,0)
    last=lambda *_:(0,3)
    return pl.pallas_call(functools.partial(one_fwd_kernel,B=B,NB=NB),
      out_shape=(jax.ShapeDtypeStruct((R,64),bf16),jax.ShapeDtypeStruct((8,R),f32)),
      grid_spec=pltpu.PrefetchScalarGridSpec(num_scalar_prefetch=1,grid=(1,),
        in_specs=[pl.BlockSpec((R,64),full),pl.BlockSpec((N,128),last)],
        out_specs=[pl.BlockSpec((R,64),full),pl.BlockSpec((8,R),full)],
        scratch_shapes=[pltpu.VMEM((80,N),bf16),pltpu.VMEM((B,B),f32),pltpu.VMEM((80,B),f32)]),
      compiler_params=pltpu.CompilerParams(vmem_limit_bytes=48<<20),
      cost_estimate=pl.CostEstimate(flops=4*R*N*128,bytes_accessed=N*256+R*512,transcendentals=R*N),
      )(own,q,x)


def one_bwd_kernel(own_ref, q_ref, x_ref, o_ref, do_ref, lse_ref, dq_ref, dx_ref, dkv, dq, *, B, NB):
    nb = own_ref[NB + 2]
    rr=lax.broadcasted_iota(jnp.int32,(B,B),0)
    cc=lax.broadcasted_iota(jnp.int32,(B,B),1)
    ones=jnp.ones((8,64),bf16)
    dkv[...]=jnp.zeros_like(dkv)
    for t in range(2):
        i=own_ref[NB+t]
        sl=slice(t*B,(t+1)*B)
        @pl.when(i>=nb)
        def _():
            dq_ref[sl,:]=jnp.zeros((B,64),bf16)
        @pl.when(i<nb)
        def _():
            qr=q_ref[sl,:]
            qs=qr.astype(f32)*(0.125*LOG2E)
            q=qs.astype(bf16)
            ql=(qs-q.astype(f32)).astype(bf16)
            qd=qr*jnp.asarray(0.125,bf16)
            do=do_ref[sl,:]
            prod=o_ref[sl,:].astype(f32)*do.astype(f32)
            hi=prod.astype(bf16); lo=(prod-hi.astype(f32)).astype(bf16)
            dl=(dot_nt(ones,hi)+dot_nt(ones,lo))[0:1,:]
            lse=lse_ref[0:1,sl]
            dq[...]=jnp.zeros_like(dq)
            def step(j,diag):
                r=pl.multiple_of(own_ref[j]*B,B)
                k=x_ref[pl.ds(r,B),0:64]
                v=x_ref[pl.ds(r,B),64:128]
                st=dot_nt(k,q)+dot_nt(k,ql)
                p=jnp.exp2(st-lse)
                if diag: p=jnp.where(rr<=cc,p,0.0)
                dp=dot_nt(v,do)
                ds=(p*(dp-dl)).astype(bf16)
                dkv[pl.ds(r,B),64:128]+=dot_nn(p.astype(bf16),do)
                dkv[pl.ds(r,B),0:64]+=dot_nn(ds,qd)
                dq[...]+=dot_nn(k.T,ds)
            def body(j,_):
                step(j,False); return 0
            lax.fori_loop(0,i,body,0)
            step(i,True)
            dq_ref[sl,:]=(dq[...].T*0.125).astype(bf16)
    dx_ref[...]=dkv[...].astype(bf16)


def one_bwd(q,x,o,do,lse,own,B):
    N=x.shape[0]; R=q.shape[0]; NB=N//B
    full=lambda *_:(0,0)
    last=lambda *_:(0,3)
    return pl.pallas_call(functools.partial(one_bwd_kernel,B=B,NB=NB),
      out_shape=(jax.ShapeDtypeStruct((R,64),bf16),jax.ShapeDtypeStruct((N,128),bf16)),
      grid_spec=pltpu.PrefetchScalarGridSpec(num_scalar_prefetch=1,grid=(1,),
        in_specs=[pl.BlockSpec((R,64),full),pl.BlockSpec((N,128),last),pl.BlockSpec((R,64),full),pl.BlockSpec((R,64),full),pl.BlockSpec((8,R),full)],
        out_specs=[pl.BlockSpec((R,64),full),pl.BlockSpec((N,128),full)],
        scratch_shapes=[pltpu.VMEM((N,128),f32),pltpu.VMEM((64,B),f32)]),
      compiler_params=pltpu.CompilerParams(vmem_limit_bytes=48<<20),
      cost_estimate=pl.CostEstimate(flops=10*R*N*128,bytes_accessed=N*512+R*1024,transcendentals=R*N),
      )(own,q,x,o,do,lse)


def join_kernel(*refs, count):
    t = pl.program_id(0)
    stacks, tail, out = refs[:-2], refs[-2], refs[-1]
    for i, ref in enumerate(stacks):
        @pl.when((t >= i * count) & (t < (i + 1) * count))
        def _(ref=ref):
            out[...] = ref[0]

    @pl.when(t >= len(stacks) * count)
    def _():
        out[:, :tail.shape[1]] = tail[...]


def join(stacks, tail):
    C, R, W = stacks[0].shape
    n = len(stacks)
    T = tail.shape[1]

    def at(i):
        return lambda t: (jnp.clip(t - i * C, 0, C - 1), 0, 0)
    return pl.pallas_call(functools.partial(join_kernel, count=C),
        out_shape=jax.ShapeDtypeStruct((R, n * C * W + T), bf16),
        grid=(n * C + 1,),
        in_specs=[pl.BlockSpec((1, R, W), at(i)) for i in range(n)] + [pl.BlockSpec((R, T), lambda t: (0, 0))],
        out_specs=pl.BlockSpec((R, W), lambda t: (0, t)),
        compiler_params=pltpu.CompilerParams(vmem_limit_bytes=56 << 20),
        cost_estimate=pl.CostEstimate(flops=0, bytes_accessed=4 * R * (n * C * W + T), transcendentals=0),
    )(*stacks, tail)


def deal_kernel(x_ref, o_ref):
    o_ref[0] = x_ref[...]


def deal(x, first, C, W):
    R = x.shape[0]
    return pl.pallas_call(deal_kernel,
        out_shape=jax.ShapeDtypeStruct((C, R, W), bf16),
        grid=(C,),
        in_specs=[pl.BlockSpec((R, W), lambda t: (0, first + t))],
        out_specs=pl.BlockSpec((1, R, W), lambda t: (t, 0, 0)),
        compiler_params=pltpu.CompilerParams(vmem_limit_bytes=56 << 20),
        cost_estimate=pl.CostEstimate(flops=0, bytes_accessed=4 * R * C * W, transcendentals=0),
    )(x)


def gather_kernel(x_ref, o_ref, own_sem, zs, zr, xs, xr, cs, cr, *, Z, C, quarter):
    z, a, c = lax.axis_index("zz"), lax.axis_index("core"), lax.axis_index("ctx")
    mesh_id = pl.DeviceIdType.MESH
    other = 1 - a
    peers = [(lax.rem(z + k, Z), a, c) for k in range(1, Z)] + [(z, a, lax.rem(c + j, C)) for j in range(1, C)] + [(z, other, c)]
    barrier = pltpu.get_barrier_semaphore()
    for peer in peers:
        pl.semaphore_signal(barrier, inc=1, device_id=peer, device_id_type=mesh_id)
    pl.semaphore_wait(barrier, len(peers))

    f = 2 * z + a

    def cols(q):
        return pl.ds(pl.multiple_of(q * quarter, quarter), quarter)

    def send(src, dst, s, r, peer):
        copy = pltpu.make_async_remote_copy(src_ref=src, dst_ref=dst, send_sem=s, recv_sem=r, device_id=peer, device_id_type=mesh_id)
        copy.start()
        return copy

    along = []
    for k in range(1, Z):
        along.append(send(x_ref.at[:, cols(c)], o_ref.at[f, :, cols(c)], zs.at[k - 1], zr.at[k - 1], peers[k - 1]))
    own = pltpu.make_async_copy(x_ref, o_ref.at[f], own_sem)
    own.start()
    whole = send(x_ref, o_ref.at[f], cs.at[0], cr.at[0], peers[-1])
    plane, cross = [], []
    for k in range(1, Z):
        along[k - 1].wait_recv()
        fs = 2 * lax.rem(z + Z - k, Z) + a
        piece = o_ref.at[fs, :, cols(c)]
        for j in range(1, C):
            n = (k - 1) * (C - 1) + j - 1
            plane.append(send(piece, piece, xs.at[n], xr.at[n], peers[Z - 1 + j - 1]))
        n = 1 + (k - 1) * C
        cross.append(send(piece, piece, cs.at[n], cr.at[n], peers[-1]))
    for k in range(1, Z):
        fs = 2 * lax.rem(z + Z - k, Z) + a
        for j in range(1, C):
            plane[(k - 1) * (C - 1) + j - 1].wait_recv()
            piece = o_ref.at[fs, :, cols(lax.rem(c + C - j, C))]
            n = 1 + (k - 1) * C + j
            cross.append(send(piece, piece, cs.at[n], cr.at[n], peers[-1]))
    for copy in along + plane:
        copy.wait_send()
    whole.wait_send()
    whole.wait_recv()
    for copy in cross:
        copy.wait_send()
        copy.wait_recv()
    own.wait()


def gather_all(x, Z, C):
    R, W = x.shape
    dma = pltpu.SemaphoreType.DMA
    n, m = (Z - 1) * (C - 1), 1 + (Z - 1) * C
    return pl.pallas_call(functools.partial(gather_kernel, Z=Z, C=C, quarter=W // C),
        out_shape=jax.ShapeDtypeStruct((2 * Z, R, W), bf16),
        in_specs=[pl.BlockSpec(memory_space=pl.ANY)],
        out_specs=pl.BlockSpec(memory_space=pl.ANY),
        scratch_shapes=[dma(()), dma((Z - 1,)), dma((Z - 1,)), dma((n,)), dma((n,)), dma((m,)), dma((m,))],
        compiler_params=pltpu.CompilerParams(collective_id=0, has_side_effects=True, vmem_limit_bytes=56 << 20),
        cost_estimate=pl.CostEstimate(flops=0, bytes_accessed=20 * R * W * Z, transcendentals=0),
    )(x)


def join_kernel(*refs, count):
    t = pl.program_id(0)
    stacks, tail, out = refs[:-2], refs[-2], refs[-1]
    for i, ref in enumerate(stacks):
        @pl.when((t >= i * count) & (t < (i + 1) * count))
        def _(ref=ref):
            out[...] = ref[0]

    @pl.when(t >= len(stacks) * count)
    def _():
        out[:, :tail.shape[1]] = tail[...]


def join(stacks, tail):
    C, R, W = stacks[0].shape
    n = len(stacks)
    T = tail.shape[1]

    def at(i):
        return lambda t: (jnp.clip(t - i * C, 0, C - 1), 0, 0)
    return pl.pallas_call(functools.partial(join_kernel, count=C),
        out_shape=jax.ShapeDtypeStruct((R, n * C * W + T), bf16),
        grid=(n * C + 1,),
        in_specs=[pl.BlockSpec((1, R, W), at(i)) for i in range(n)] + [pl.BlockSpec((R, T), lambda t: (0, 0))],
        out_specs=pl.BlockSpec((R, W), lambda t: (0, t)),
        compiler_params=pltpu.CompilerParams(vmem_limit_bytes=56 << 20),
        cost_estimate=pl.CostEstimate(flops=0, bytes_accessed=4 * R * (n * C * W + T), transcendentals=0),
    )(*stacks, tail)


def deal_kernel(x_ref, o_ref):
    o_ref[0] = x_ref[...]


def deal(x, first, C, W):
    R = x.shape[0]
    return pl.pallas_call(deal_kernel,
        out_shape=jax.ShapeDtypeStruct((C, R, W), bf16),
        grid=(C,),
        in_specs=[pl.BlockSpec((R, W), lambda t: (0, first + t))],
        out_specs=pl.BlockSpec((1, R, W), lambda t: (t, 0, 0)),
        compiler_params=pltpu.CompilerParams(vmem_limit_bytes=56 << 20),
        cost_estimate=pl.CostEstimate(flops=0, bytes_accessed=4 * R * C * W, transcendentals=0),
    )(x)


def gather_kernel(x_ref, o_ref, own_sem, zs, zr, xs, xr, cs, cr, *, Z, C, quarter):
    z, a, c = lax.axis_index("zz"), lax.axis_index("core"), lax.axis_index("ctx")
    mesh_id = pl.DeviceIdType.MESH
    other = 1 - a
    peers = [(lax.rem(z + k, Z), a, c) for k in range(1, Z)] + [(z, a, lax.rem(c + j, C)) for j in range(1, C)] + [(z, other, c)]
    barrier = pltpu.get_barrier_semaphore()
    for peer in peers:
        pl.semaphore_signal(barrier, inc=1, device_id=peer, device_id_type=mesh_id)
    pl.semaphore_wait(barrier, len(peers))

    f = 2 * z + a

    def cols(q):
        return pl.ds(pl.multiple_of(q * quarter, quarter), quarter)

    def send(src, dst, s, r, peer):
        copy = pltpu.make_async_remote_copy(src_ref=src, dst_ref=dst, send_sem=s, recv_sem=r, device_id=peer, device_id_type=mesh_id)
        copy.start()
        return copy

    along = []
    for k in range(1, Z):
        along.append(send(x_ref.at[:, cols(c)], o_ref.at[f, :, cols(c)], zs.at[k - 1], zr.at[k - 1], peers[k - 1]))
    own = pltpu.make_async_copy(x_ref, o_ref.at[f], own_sem)
    own.start()
    whole = send(x_ref, o_ref.at[f], cs.at[0], cr.at[0], peers[-1])
    plane, cross = [], []
    for k in range(1, Z):
        along[k - 1].wait_recv()
        fs = 2 * lax.rem(z + Z - k, Z) + a
        piece = o_ref.at[fs, :, cols(c)]
        for j in range(1, C):
            n = (k - 1) * (C - 1) + j - 1
            plane.append(send(piece, piece, xs.at[n], xr.at[n], peers[Z - 1 + j - 1]))
        n = 1 + (k - 1) * C
        cross.append(send(piece, piece, cs.at[n], cr.at[n], peers[-1]))
    for k in range(1, Z):
        fs = 2 * lax.rem(z + Z - k, Z) + a
        for j in range(1, C):
            plane[(k - 1) * (C - 1) + j - 1].wait_recv()
            piece = o_ref.at[fs, :, cols(lax.rem(c + C - j, C))]
            n = 1 + (k - 1) * C + j
            cross.append(send(piece, piece, cs.at[n], cr.at[n], peers[-1]))
    for copy in along + plane:
        copy.wait_send()
    whole.wait_send()
    whole.wait_recv()
    for copy in cross:
        copy.wait_send()
        copy.wait_recv()
    own.wait()


def gather_all(x, Z, C):
    R, W = x.shape
    dma = pltpu.SemaphoreType.DMA
    n, m = (Z - 1) * (C - 1), 1 + (Z - 1) * C
    return pl.pallas_call(functools.partial(gather_kernel, Z=Z, C=C, quarter=W // C),
        out_shape=jax.ShapeDtypeStruct((2 * Z, R, W), bf16),
        in_specs=[pl.BlockSpec(memory_space=pl.ANY)],
        out_specs=pl.BlockSpec(memory_space=pl.ANY),
        scratch_shapes=[dma(()), dma((Z - 1,)), dma((Z - 1,)), dma((n,)), dma((n,)), dma((m,)), dma((m,))],
        compiler_params=pltpu.CompilerParams(collective_id=0, has_side_effects=True, vmem_limit_bytes=56 << 20),
        cost_estimate=pl.CostEstimate(flops=0, bytes_accessed=20 * R * W * Z, transcendentals=0),
    )(x)


HEADS = 17
EPSILON = 1e-05
FS = ("zz", "core")


def norm_parts(v):
    mean = jnp.mean(v, axis=-1, keepdims=True)
    c = v - mean
    r = lax.rsqrt(jnp.mean(c * c, axis=-1, keepdims=True) + EPSILON)
    return c * r, r


def norm_back(dn, v, gain):
    xhat, r = norm_parts(v)
    y = dn * gain
    a = jnp.mean(y, axis=-1, keepdims=True)
    b = jnp.mean(y * xhat, axis=-1, keepdims=True)
    return r * (y - a - xhat * b), jnp.sum(dn * xhat, axis=0), jnp.sum(dn, axis=0)


def col_sum(x):
    return jnp.dot(jnp.ones((16, x.shape[0]), bf16), x, preferred_element_type=f32)[0]


def gelu_parts(u):
    z = jnp.abs(u) * 0.7071067811865476
    t = 1.0 / (1.0 + 0.3275911 * z)
    e = jnp.exp(-z * z)
    poly = t * (0.254829592 + t * (-0.284496736 + t * (1.421413741 + t * (-1.453152027 + t * 1.061405429))))
    half = 0.5 * poly * e
    cdf = jnp.where(u >= 0, 1.0 - half, half)
    return u * cdf, cdf + u * e * 0.3989422804014327


def local(
    tokens, cotangent, lengths, block_order,
    ln1_gain, ln1_bias, qkv_weight, q_bias, v_bias, out_weight, out_bias,
    ln2_gain, ln2_bias, up_weight, up_bias, down_weight, down_bias,
    *, G, S,
):
    slots, rows, width = tokens.shape
    C = lax.axis_size("ctx")
    me = lax.axis_index("ctx")
    N = rows * C
    B = rows // 2
    NB = 2 * C
    L = ln1_gain.shape[0]
    shard = ln1_gain.shape[1]
    HW = G * 128
    x_tokens = tokens[0]

    steps = jnp.arange(NB, dtype=jnp.int32)
    order = block_order[0]
    inverse = jnp.sum(jnp.where(order[None, :] == steps[:, None], steps[None, :], 0), axis=1).astype(jnp.int32)
    count = (lengths + (B - 1)) // B
    meta = jnp.concatenate([inverse, count])
    def swap(x):
        return lax.ppermute(x, "core", [(0, 1), (1, 0)])

    metas = [meta, swap(meta)][:S]
    phase_inv = [t[None, :NB] for t in metas]
    phase_nb = [t[NB:] for t in metas]
    own = jnp.concatenate([inverse, lax.dynamic_slice_in_dim(order, 2 * me, 2, 0), count])
    own_pos = (lax.dynamic_slice_in_dim(order, 2 * me, 2, 0)[:, None] * B + jnp.arange(B, dtype=jnp.int32)).reshape(rows, 1)
    live = (own_pos < lengths[0]).astype(f32)

    def pack(w):
        parts = []
        for g in range(G):
            parts += [w[:, kind * width + g * 128:kind * width + g * 128 + 128] for kind in range(3)]
        last = width - 64
        parts += [w[:, kind * width + last:kind * width + width] for kind in (1, 2, 0)]
        return jnp.concatenate(parts, axis=1)

    def unpack(w):
        tail = G * 384
        parts = []
        for kind, last in enumerate((128, 0, 64)):
            parts += [w[:, g * 384 + kind * 128:g * 384 + kind * 128 + 128] for g in range(G)]
            parts.append(w[:, tail + last:tail + last + 64])
        return jnp.concatenate(parts, axis=1)

    def fetch(w):
        return lax.all_gather(w.astype(bf16), FS, axis=0, tiled=True)

    vectors = [ln1_gain, ln1_bias, q_bias, v_bias, out_bias, ln2_gain, ln2_bias, down_bias]
    vec = [t.astype(bf16).T for t in vectors] + [up_bias.astype(bf16).reshape(4 * L, shard).T]
    first = pack(qkv_weight[0].astype(bf16))
    block = jnp.concatenate([first] + vec, axis=1)
    used = block.shape[1]
    if C == 4 and lax.axis_size("zz") == 4:
        block = jnp.pad(block, ((0, 0), (0, -used % (128 * C))))
        block = gather_all(block, 4, C)
    else:
        block = lax.all_gather(block, FS)
    first_w = block[:, :, :3 * width].reshape(width, 3 * width)
    vec = jnp.transpose(block[:, :, 3 * width:used].reshape(width, used - 3 * width)).astype(f32)

    def vector(index, layer):
        if index < 8:
            return vec[L * index + layer]
        t = vec[8 * L + 4 * layer:8 * L + 4 * layer + 4]
        return jnp.transpose(t.reshape(4, -1, shard), (1, 0, 2)).reshape(-1)

    weights = []
    for layer in range(L):
        weights.append((
            fetch(pack(qkv_weight[layer].astype(bf16))) if layer else first_w,
            fetch(out_weight[layer]),
            fetch(up_weight[layer]),
            fetch(down_weight[layer]),
        ))

    def plain(x):
        return with_layout_constraint(x, Layout(major_to_minor=tuple(range(x.ndim))))

    def exchange(x):
        return plain(lax.all_to_all(plain(x), "ctx", 0, 0))

    def after(x, *others):
        return lax.optimization_barrier((x,) + others)

    stream = x_tokens.astype(f32)
    records = []
    for layer in range(L):
        qkv_w, out_w, up_w, down_w = weights[layer]
        xhat, _ = norm_parts(stream)
        n1 = (xhat * vector(0, layer) + vector(1, layer)).astype(bf16)
        q_b, v_b = vector(2, layer), vector(3, layer)
        bias = pack(jnp.concatenate([q_b, jnp.zeros_like(q_b), v_b])[None])[0]
        projected = (jnp.dot(n1, qkv_w, preferred_element_type=f32) + bias).astype(bf16)
        wide = [deal(projected, s * C, C, 384) for s in range(S)]
        tail = projected[:, G * 384:]
        if S == 2:
            wide[1] = swap(wide[1])
        kv16 = jnp.broadcast_to(tail[None, :, :128], (C, rows, 128))
        q16 = tail[:, 128:]
        heads, o, lse, o_back = [], [], [], []
        for s in range(S):
            t = wide[s]
            if s == S - 1:
                t = jnp.concatenate([t, kv16], axis=2)
            if s:
                t, heads[0] = after(t, heads[0])
            heads.append(exchange(t).reshape(1, N, -1))
        for s in range(S):
            o_s, lse_s = flash_fwd(heads[s], phase_inv[s], phase_nb[s], B)
            o.append(o_s)
            lse.append(lse_s)
            t = o_s.reshape(C, rows, 128)
            if s:
                t, o_back[0] = after(t, o_back[0])
            o_back.append(exchange(swap(t) if s else t))
        o16, lse16 = one_fwd(q16, heads[-1][0], own, B)
        mixed = join(o_back, o16)
        m = stream + jnp.dot(mixed, out_w, preferred_element_type=f32) + vector(4, layer)
        xhat2, _ = norm_parts(m)
        n2 = (xhat2 * vector(5, layer) + vector(6, layer)).astype(bf16)
        u = jnp.dot(n2, up_w, preferred_element_type=f32) + vector(8, layer)
        a, slope = gelu_parts(u)
        a = a.astype(bf16)
        slope = slope.astype(bf16)
        records.append((stream, n1, heads, q16, o, lse, o16, lse16, mixed, m, n2, a, slope))
        stream = m + jnp.dot(a, down_w, preferred_element_type=f32) + vector(7, layer)
    activations = (stream * live).astype(bf16)[None]

    def reduce_fsdp(g):
        return lax.psum_scatter(g.astype(bf16), FS, scatter_dimension=0, tiled=True)

    def reduce_ctx(g):
        return lax.psum(g, "ctx").astype(f32)

    grad = cotangent[0].astype(f32) * live
    matrices = [None] * L
    fours = [None] * L
    ffns = [None] * L
    small = [None] * L

    def ctx_end(mine):
        return exchange(jnp.broadcast_to(mine[None], (C,) + mine.shape))

    def ctx_sum(shards):
        mine, sizes = ctx_begin(shards)
        return ctx_end(mine), sizes

    def ctx_begin(shards):
        pieces = []
        for t in shards:
            if t.shape[1] == width:
                pieces.append(t.reshape(C, -1, width))
            else:
                pieces.append(jnp.transpose(t.reshape(t.shape[0], C, -1), (1, 0, 2)).reshape(C, -1, width))
        sizes = [t.shape[1] for t in pieces]
        parts = exchange(jnp.concatenate(pieces, axis=1))
        mine = jnp.sum(parts.astype(f32), axis=0).astype(bf16)
        return mine, sizes

    def spread(summed, shapes):
        whole, sizes = summed
        out, at = [], 0
        for n, (r, c) in zip(sizes, shapes):
            t = whole[:, at:at + n].astype(f32)
            at += n
            if c == width:
                out.append(t.reshape(r, c))
            else:
                out.append(jnp.transpose(t.reshape(C, r, c // C), (1, 0, 2)).reshape(r, c))
        return out

    wide_shape, tall_shape = (shard, 4 * width), (4 * shard, width)
    for layer in reversed(range(L)):
        stream_in, n1, heads, q16, o, lse, o16, lse16, mixed, m, n2, a, slope = records[layer]
        qkv_w, out_w, up_w, down_w = weights[layer]
        gb = grad.astype(bf16)
        d_down_b = col_sum(gb)
        d_down = jnp.einsum("rf,rd->fd", a, gb, preferred_element_type=f32).astype(bf16)
        gb, d_down = after(gb, plain(d_down))
        d_down = reduce_fsdp(d_down)
        du = (jnp.einsum("rd,fd->rf", gb, down_w, preferred_element_type=f32) * slope.astype(f32)).astype(bf16)
        d_up_b = col_sum(du)
        d_up = jnp.einsum("rd,rf->df", n2, du, preferred_element_type=f32).astype(bf16)
        du, d_up = after(du, plain(d_up))
        d_up = reduce_fsdp(d_up)
        dn2 = jnp.einsum("rf,df->rd", du, up_w, preferred_element_type=f32)
        back, d_gain2, d_bias2 = norm_back(dn2, m, vector(5, layer))
        gm = grad + back
        gmb = gm.astype(bf16)
        d_out_b = col_sum(gmb)
        d_out = jnp.einsum("rd,re->de", mixed, gmb, preferred_element_type=f32).astype(bf16)
        if layer < L - 1:
            done = after(gmb, *ffn_sum)
            gmb, ffn_sum = done[0], done[1:]
        d_o = []
        for s in range(S):
            w = out_w[C * 128 * s:C * 128 * (s + 1)].reshape(C, 128, width)
            d_o.append(jnp.einsum("re,gce->grc", gmb, w, preferred_element_type=f32).astype(bf16))
        d_o16 = jnp.einsum("re,ce->rc", gmb, out_w[HW:], preferred_element_type=f32).astype(bf16)
        dq16, dkv16 = one_bwd(q16, heads[-1][0], o16, d_o16, lse16, own, B)
        d_oh, d_wide = [], []
        for s in range(S):
            t = d_o[s]
            if s:
                t = swap(t)
            if s == S - 1:
                t = jnp.concatenate([t, dkv16.reshape(C, rows, 128)], axis=2)
            if s:
                t, d_oh[0] = after(t, d_oh[0])
            if s == S - 1 and layer < L - 1:
                t, fours[layer + 1] = after(t, fours[layer + 1])
            d_oh.append(exchange(t).reshape(1, N, -1))
        dkv16 = jnp.sum(d_oh[-1].reshape(C, rows, 256)[:, :, 128:].astype(f32), axis=0)
        for s in range(S):
            t = flash_bwd(heads[s], o[s], d_oh[s], lse[s], phase_inv[s], phase_nb[s], B)
            t = t.reshape(C, rows, 384)
            if s:
                t, d_wide[0] = after(t, d_wide[0])
            if s == S - 1:
                t, d_down = after(t, d_down)
            if s == S - 1 and layer:
                t, d_up = after(t, d_up)
                ffn_sum = lax.psum((d_up, d_down), "ctx")
            d_wide.append(exchange(swap(t) if s else t))
        d_tail = jnp.concatenate([dkv16.astype(bf16), dq16], axis=1)
        d_row = join(d_wide, d_tail)
        d_back = d_row
        if layer == 0:
            d_row, d_up = after(d_row, d_up)
            mine, middle_sizes = ctx_begin([fours[1], d_up, d_down])
            d_back, mine = after(d_row, mine)
            middle = ctx_end(mine)
        d_qkv = jnp.einsum("rd,rc->dc", n1, d_row, preferred_element_type=f32).astype(bf16)
        d_four = jnp.concatenate([d_qkv, d_out], axis=1)
        if layer:
            d_row, d_four = after(d_row, plain(d_four))
        d_four = reduce_fsdp(d_four)
        sums = unpack(col_sum(d_row)[None])[0]
        dn1 = jnp.einsum("rc,dc->rd", d_back, qkv_w, preferred_element_type=f32)
        back, d_gain1, d_bias1 = norm_back(dn1, stream_in, vector(0, layer))
        grad = gm + back
        fours[layer] = d_four
        ffns[layer] = (d_up, d_down)
        if layer == 0:
            last = ctx_sum([d_four])
            rest = spread((middle, middle_sizes), [wide_shape, wide_shape, tall_shape])
            matrices[1] = [rest[0], ffn_sum[0].astype(f32), ffn_sum[1].astype(f32)]
            matrices[0] = spread(last, [wide_shape]) + rest[1:]
        small[layer] = jnp.concatenate([
            t.reshape(-1, n) for t, n in (
                (d_gain1, shard), (d_bias1, shard), (sums[:width], shard), (sums[2 * width:], shard), (d_out_b, shard),
                (d_gain2, shard), (d_bias2, shard), (d_down_b, shard), (d_up_b, 4 * shard))], axis=1)

    vec_grads = jnp.stack(small, axis=1)
    vec_grads = jnp.sum(lax.all_to_all(vec_grads, FS, 0, 0), axis=0)
    vec_grads = lax.psum(vec_grads, "ctx")
    vg = [vec_grads[:, i * shard:(i + 1) * shard] for i in range(8)] + [vec_grads[:, 8 * shard:]]

    g_qkv = jnp.stack([unpack(matrices[layer][0][:, :3 * width]) for layer in range(L)])
    g_out = jnp.stack([matrices[layer][0][:, 3 * width:] for layer in range(L)])
    g_up = jnp.stack([matrices[layer][1] for layer in range(L)])
    g_down = jnp.stack([matrices[layer][2] for layer in range(L)])
    return (activations, grad[None], vg[0], vg[1], g_qkv, vg[2], vg[3], g_out, vg[4], vg[5], vg[6], g_up, vg[8], g_down, vg[7])


def solution(mesh):
    F, C = mesh.devices.shape
    inner = Mesh(mesh.devices.reshape(F // 2, 2, C), ("zz", "core", "ctx"))
    S = 2 if 16 // (2 * C) >= 2 else 1
    G = S * C
    rows = P(FS, "ctx", None)
    vec, mat = P(None, FS), P(None, FS, None)
    return jax.shard_map(
        functools.partial(local, G=G, S=S),
        mesh=inner,
        in_specs=(rows, rows, P(FS), P(FS, None), vec, vec, mat, vec, vec, mat, vec, vec, vec, mat, vec, mat, vec),
        out_specs=(rows, rows, vec, vec, mat, vec, vec, mat, vec, vec, vec, mat, vec, mat, vec),
        check_vma=False,
    )
```

```python
import functools
import jax, jax.numpy as jnp
from jax import lax
from jax.experimental import pallas as pl
from jax.experimental.pallas import tpu as pltpu
from jax.experimental.layout import Layout, with_layout_constraint
from jax.sharding import Mesh, PartitionSpec as P
f32=jnp.float32; bf16=jnp.bfloat16
NEG=-1e30
def dot_nt(a,b): return lax.dot_general(a,b,(((1,),(1,)),((),())),preferred_element_type=f32)
def dot_nn(a,b): return lax.dot_general(a,b,(((1,),(0,)),((),())),preferred_element_type=f32)

LOG2E=1.4426950408889634
def split(q,h,low):
    qs=q.astype(f32)*(0.125*LOG2E)
    hi=qs.astype(bf16).astype(f32); lo=qs-hi
    rl=pltpu.roll(lo,64,1)
    c=jnp.where(low,hi,rl) if h==0 else jnp.where(low,rl,hi)
    return c.astype(bf16)
def dup(k,h,low):
    kf=k.astype(f32); rl=pltpu.roll(kf,64,1)
    c=jnp.where(low,kf,rl) if h==0 else jnp.where(low,rl,kf)
    return c.astype(bf16)
def fwd_kernel(inv_ref, nb_ref, x_ref, o_ref, lse_ref, vt, kd, sb, acc, *, B, NB):
    s=pl.program_id(0)
    nb=nb_ref[s]
    lane=lax.broadcasted_iota(jnp.int32,(1,128),1)
    low=lane<64
    def tv(j,_):
        r=pl.multiple_of(inv_ref[s,j]*B,B)
        w=pl.multiple_of(j*B,B)
        t=x_ref[0,pl.ds(r,B),256:384].T
        one=(lax.broadcasted_iota(jnp.int32,(16,B),0)==0).astype(bf16)
        for h in range(2):
            vt[80*h:80*h+64,pl.ds(w,B)]=t[64*h:64*h+64,:]
            vt[80*h+64:80*h+80,pl.ds(w,B)]=one
            kd[h,pl.ds(w,B),:]=dup(x_ref[0,pl.ds(r,B),128:256],h,low)
        return 0
    lax.fori_loop(0,nb,tv,0)
    rr=lax.broadcasted_iota(jnp.int32,(B,B),0)
    cc=lax.broadcasted_iota(jnp.int32,(B,B),1)
    def qblock(i,_):
        r=pl.multiple_of(inv_ref[s,i]*B,B)
        q=x_ref[0,pl.ds(r,B),0:128]
        qh=[split(q,h,low) for h in range(2)]
        acc[...]=jnp.zeros_like(acc)
        def scores(j,slot):
            for h in range(2):
                sb[slot,h]=dot_nt(kd[h,pl.ds(pl.multiple_of(j*B,B),B),:],qh[h])
        def step(j,carry,diag):
            out=[]
            for h in range(2):
                m=carry[h]
                st=sb[j%2,h]
                if diag: st=jnp.where(rr<=cc,st,NEG)
                mn=jnp.maximum(m,jnp.max(st,axis=0,keepdims=True))
                p=jnp.exp2(st-mn)
                al=jnp.exp2(m-mn)
                v=vt[80*h:80*h+80,pl.ds(pl.multiple_of(j*B,B),B)]
                acc[h]=acc[h]*al+dot_nn(v,p.astype(bf16))
                out.append(mn)
            return tuple(out)
        scores(0,0)
        def both(j,c):
            scores(j+1,(j+1)%2)
            return step(j,c,False)
        n=jnp.full((1,B),NEG,f32)
        c=lax.fori_loop(0,i,both,(n,n))
        c=step(i,c,True)
        os=[]
        for h in range(2):
            l=acc[h,64:65,:]
            os.append(acc[h,0:64,:]*(1.0/l))
            lse_ref[0,pl.ds(h,1),pl.ds(r,B)]=c[h]+jnp.log2(l)
        o_ref[0,pl.ds(r,B),:]=jnp.concatenate(os,0).T.astype(bf16)
        return 0
    lax.fori_loop(0,nb,qblock,0)
    def pad(i,_):
        r=pl.multiple_of(inv_ref[s,i]*B,B)
        o_ref[0,pl.ds(r,B),:]=jnp.zeros((B,128),bf16)
        lse_ref[0,:,pl.ds(r,B)]=jnp.zeros((8,B),f32)
        return 0
    lax.fori_loop(nb,NB,pad,0)

def flash_fwd(x,inv,nb,B):
    S,N,_=x.shape
    NB=N//B
    return pl.pallas_call(functools.partial(fwd_kernel,B=B,NB=NB),
      out_shape=(jax.ShapeDtypeStruct((S,N,128),bf16),jax.ShapeDtypeStruct((S,8,N),f32)),
      grid_spec=pltpu.PrefetchScalarGridSpec(num_scalar_prefetch=2,grid=(S,),
        in_specs=[pl.BlockSpec((1,N,384),lambda s,*_:(s,0,0))],
        out_specs=[pl.BlockSpec((1,N,128),lambda s,*_:(s,0,0)),pl.BlockSpec((1,8,N),lambda s,*_:(s,0,0))],
        scratch_shapes=[pltpu.VMEM((160,N),bf16),pltpu.VMEM((2,N,128),bf16),pltpu.VMEM((2,2,B,B),f32),pltpu.VMEM((2,80,B),f32)]),
      compiler_params=pltpu.CompilerParams(vmem_limit_bytes=48<<20),
      cost_estimate=pl.CostEstimate(flops=S*4*N*N*128,bytes_accessed=S*N*1024,transcendentals=S*N*N),
      )(inv,nb,x)

def bwd_kernel(inv_ref, nb_ref, x_ref, o_ref, do_ref, lse_ref, dx_ref, kt, qd, dq, dk, dv, dl, *, B, NB):
    s=pl.program_id(0)
    nb=nb_ref[s]
    lane=lax.broadcasted_iota(jnp.int32,(1,128),1)
    low=lane<64
    hm=(lax.broadcasted_iota(jnp.int32,(8,128),1)//64==lax.broadcasted_iota(jnp.int32,(8,128),0)).astype(bf16)
    def prep(j,_):
        r=pl.multiple_of(inv_ref[s,j]*B,B)
        w=pl.multiple_of(j*B,B)
        kt[:,pl.ds(w,B)]=x_ref[0,pl.ds(r,B),128:256].T
        for h in range(2): qd[h,pl.ds(w,B),:]=split(x_ref[0,pl.ds(r,B),0:128],h,low)
        prod=o_ref[0,pl.ds(r,B),:].astype(f32)*do_ref[0,pl.ds(r,B),:].astype(f32)
        hi=prod.astype(bf16); lo=(prod-hi.astype(f32)).astype(bf16)
        dl[:,pl.ds(w,B)]=dot_nt(hm,hi)+dot_nt(hm,lo)
        dq[:,pl.ds(w,B)]=jnp.zeros((128,B),f32)
        return 0
    lax.fori_loop(0,nb,prep,0)
    rr=lax.broadcasted_iota(jnp.int32,(B,B),0)
    cc=lax.broadcasted_iota(jnp.int32,(B,B),1)
    def kblock(j,_):
        r=pl.multiple_of(inv_ref[s,j]*B,B)
        k=x_ref[0,pl.ds(r,B),128:256]
        v=x_ref[0,pl.ds(r,B),256:384]
        kdh=[dup(k,h,low) for h in range(2)]
        dk[...]=jnp.zeros_like(dk); dv[...]=jnp.zeros_like(dv)
        def step(i,diag):
            ri=pl.multiple_of(inv_ref[s,i]*B,B)
            wi=pl.multiple_of(i*B,B)
            q=x_ref[0,pl.ds(ri,B),0:128]*jnp.asarray(0.125,bf16)
            do=do_ref[0,pl.ds(ri,B),:]
            zero=jnp.zeros_like(q)
            dvs=[];dks=[]
            for h in range(2):
                qh=jnp.where(low,q,zero) if h==0 else jnp.where(low,zero,q)
                doh=jnp.where(low,do,zero) if h==0 else jnp.where(low,zero,do)
                st=dot_nt(kdh[h],qd[h,pl.ds(wi,B),:])
                p=jnp.exp2(st-lse_ref[0,pl.ds(h,1),pl.ds(ri,B)])
                if diag: p=jnp.where(rr<=cc,p,0.0)
                dvs.append(dot_nn(p.astype(bf16),doh))
                dp=dot_nt(v,doh)
                ds=(p*(dp-dl[pl.ds(h,1),pl.ds(wi,B)])).astype(bf16)
                dks.append(dot_nn(ds,qh))
                kh=kt[64*h:64*h+64,pl.ds(pl.multiple_of(j*B,B),B)]
                dq[64*h:64*h+64,pl.ds(wi,B)]+=dot_nn(kh,ds)
            dv[...]+=dvs[0]+dvs[1]
            dk[...]+=dks[0]+dks[1]
        step(j,True)
        def body(i,_):
            step(i,False); return 0
        lax.fori_loop(j+1,nb,body,0)
        dx_ref[0,pl.ds(r,B),128:256]=dk[...].astype(bf16)
        dx_ref[0,pl.ds(r,B),256:384]=dv[...].astype(bf16)
        return 0
    lax.fori_loop(0,nb,kblock,0)
    def fin(i,_):
        r=pl.multiple_of(inv_ref[s,i]*B,B)
        dx_ref[0,pl.ds(r,B),0:128]=(dq[:,pl.ds(pl.multiple_of(i*B,B),B)].T*0.125).astype(bf16)
        return 0
    lax.fori_loop(0,nb,fin,0)
    def pad(i,_):
        r=pl.multiple_of(inv_ref[s,i]*B,B)
        dx_ref[0,pl.ds(r,B),:]=jnp.zeros((B,384),bf16)
        return 0
    lax.fori_loop(nb,NB,pad,0)

def flash_bwd(x,o,do,lse,inv,nb,B):
    S,N,_=x.shape
    NB=N//B
    return pl.pallas_call(functools.partial(bwd_kernel,B=B,NB=NB),
      out_shape=jax.ShapeDtypeStruct((S,N,384),bf16),
      grid_spec=pltpu.PrefetchScalarGridSpec(num_scalar_prefetch=2,grid=(S,),
        in_specs=[pl.BlockSpec((1,N,384),lambda s,*_:(s,0,0)),pl.BlockSpec((1,N,128),lambda s,*_:(s,0,0)),
                  pl.BlockSpec((1,N,128),lambda s,*_:(s,0,0)),pl.BlockSpec((1,8,N),lambda s,*_:(s,0,0))],
        out_specs=pl.BlockSpec((1,N,384),lambda s,*_:(s,0,0)),
        scratch_shapes=[pltpu.VMEM((128,N),bf16),pltpu.VMEM((2,N,128),bf16),pltpu.VMEM((128,N),f32),pltpu.VMEM((B,128),f32),pltpu.VMEM((B,128),f32),pltpu.VMEM((8,N),f32)]),
      compiler_params=pltpu.CompilerParams(vmem_limit_bytes=48<<20),
      cost_estimate=pl.CostEstimate(flops=S*10*N*N*128,bytes_accessed=S*N*2400,transcendentals=S*N*N),
      )(inv,nb,x,o,do,lse)


def one_fwd_kernel(own_ref, q_ref, x_ref, o_ref, lse_ref, vt, kd, acc, *, B, NB):
    nb = own_ref[NB + 2]
    low = lax.broadcasted_iota(jnp.int32,(1,128),1)<64
    def tv(j,_):
        r=pl.multiple_of(own_ref[j]*B,B)
        t=x_ref[pl.ds(r,B),:].T
        w=pl.multiple_of(j*B,B)
        kd[pl.ds(w,B),:]=dup(x_ref[pl.ds(r,B),:],0,low)
        vt[0:64,pl.ds(w,B)]=t[64:128,:]
        vt[64:80,pl.ds(w,B)]=(lax.broadcasted_iota(jnp.int32,(16,B),0)==0).astype(bf16)
        return 0
    lax.fori_loop(0,nb,tv,0)
    rr=lax.broadcasted_iota(jnp.int32,(B,B),0)
    cc=lax.broadcasted_iota(jnp.int32,(B,B),1)
    for t in range(2):
        i=own_ref[NB+t]
        @pl.when(i>=nb)
        def _():
            o_ref[t*B:(t+1)*B,:]=jnp.zeros((B,64),bf16)
            lse_ref[:,t*B:(t+1)*B]=jnp.zeros((8,B),f32)
        @pl.when(i<nb)
        def _():
            qs=q_ref[t*B:(t+1)*B,:].astype(f32)*(0.125*LOG2E)
            hi=qs.astype(bf16)
            q=jnp.concatenate([hi.astype(f32),qs-hi.astype(f32)],axis=1).astype(bf16)
            acc[...]=jnp.zeros_like(acc)
            def step(j,m,diag):
                st=dot_nt(kd[pl.ds(pl.multiple_of(j*B,B),B),:],q)
                if diag: st=jnp.where(rr<=cc,st,NEG)
                mn=jnp.maximum(m,jnp.max(st,axis=0,keepdims=True))
                p=jnp.exp2(st-mn)
                al=jnp.exp2(m-mn)
                v=vt[:,pl.ds(pl.multiple_of(j*B,B),B)]
                acc[...]=acc[...]*al+dot_nn(v,p.astype(bf16))
                return mn
            m=lax.fori_loop(0,i,lambda j,m: step(j,m,False),jnp.full((1,B),NEG,f32))
            m=step(i,m,True)
            l=acc[64:65,:]
            o_ref[t*B:(t+1)*B,:]=(acc[0:64,:]*(1.0/l)).T.astype(bf16)
            lse_ref[:,t*B:(t+1)*B]=jnp.broadcast_to(m+jnp.log2(l),(8,B))


def one_fwd(q,x,own,B):
    N=x.shape[0]; R=q.shape[0]; NB=N//B
    full=lambda *_:(0,0)
    last=lambda *_:(0,3)
    return pl.pallas_call(functools.partial(one_fwd_kernel,B=B,NB=NB),
      out_shape=(jax.ShapeDtypeStruct((R,64),bf16),jax.ShapeDtypeStruct((8,R),f32)),
      grid_spec=pltpu.PrefetchScalarGridSpec(num_scalar_prefetch=1,grid=(1,),
        in_specs=[pl.BlockSpec((R,64),full),pl.BlockSpec((N,128),last)],
        out_specs=[pl.BlockSpec((R,64),full),pl.BlockSpec((8,R),full)],
        scratch_shapes=[pltpu.VMEM((80,N),bf16),pltpu.VMEM((N,128),bf16),pltpu.VMEM((80,B),f32)]),
      compiler_params=pltpu.CompilerParams(vmem_limit_bytes=48<<20),
      cost_estimate=pl.CostEstimate(flops=4*R*N*128,bytes_accessed=N*256+R*512,transcendentals=R*N),
      )(own,q,x)


def one_bwd_kernel(own_ref, q_ref, x_ref, o_ref, do_ref, lse_ref, dq_ref, dx_ref, dkv, dq, *, B, NB):
    nb = own_ref[NB + 2]
    low = lax.broadcasted_iota(jnp.int32,(1,128),1)<64
    rr=lax.broadcasted_iota(jnp.int32,(B,B),0)
    cc=lax.broadcasted_iota(jnp.int32,(B,B),1)
    ones=jnp.ones((8,64),bf16)
    dkv[...]=jnp.zeros_like(dkv)
    for t in range(2):
        i=own_ref[NB+t]
        sl=slice(t*B,(t+1)*B)
        @pl.when(i>=nb)
        def _():
            dq_ref[sl,:]=jnp.zeros((B,64),bf16)
        @pl.when(i<nb)
        def _():
            qr=q_ref[sl,:]
            qs=qr.astype(f32)*(0.125*LOG2E)
            hi=qs.astype(bf16)
            q=jnp.concatenate([hi.astype(f32),qs-hi.astype(f32)],axis=1).astype(bf16)
            qd=qr*jnp.asarray(0.125,bf16)
            do=do_ref[sl,:]
            prod=o_ref[sl,:].astype(f32)*do.astype(f32)
            hi=prod.astype(bf16); lo=(prod-hi.astype(f32)).astype(bf16)
            dl=(dot_nt(ones,hi)+dot_nt(ones,lo))[0:1,:]
            lse=lse_ref[0:1,sl]
            dq[...]=jnp.zeros_like(dq)
            def step(j,diag):
                r=pl.multiple_of(own_ref[j]*B,B)
                k=x_ref[pl.ds(r,B),0:64]
                v=x_ref[pl.ds(r,B),64:128]
                st=dot_nt(dup(x_ref[pl.ds(r,B),:],0,low),q)
                p=jnp.exp2(st-lse)
                if diag: p=jnp.where(rr<=cc,p,0.0)
                dp=dot_nt(v,do)
                ds=(p*(dp-dl)).astype(bf16)
                dkv[pl.ds(r,B),64:128]+=dot_nn(p.astype(bf16),do)
                dkv[pl.ds(r,B),0:64]+=dot_nn(ds,qd)
                dq[...]+=dot_nn(k.T,ds)
            def body(j,_):
                step(j,False); return 0
            lax.fori_loop(0,i,body,0)
            step(i,True)
            dq_ref[sl,:]=(dq[...].T*0.125).astype(bf16)
    dx_ref[...]=dkv[...].astype(bf16)


def one_bwd(q,x,o,do,lse,own,B):
    N=x.shape[0]; R=q.shape[0]; NB=N//B
    full=lambda *_:(0,0)
    last=lambda *_:(0,3)
    return pl.pallas_call(functools.partial(one_bwd_kernel,B=B,NB=NB),
      out_shape=(jax.ShapeDtypeStruct((R,64),bf16),jax.ShapeDtypeStruct((N,128),bf16)),
      grid_spec=pltpu.PrefetchScalarGridSpec(num_scalar_prefetch=1,grid=(1,),
        in_specs=[pl.BlockSpec((R,64),full),pl.BlockSpec((N,128),last),pl.BlockSpec((R,64),full),pl.BlockSpec((R,64),full),pl.BlockSpec((8,R),full)],
        out_specs=[pl.BlockSpec((R,64),full),pl.BlockSpec((N,128),full)],
        scratch_shapes=[pltpu.VMEM((N,128),f32),pltpu.VMEM((64,B),f32)]),
      compiler_params=pltpu.CompilerParams(vmem_limit_bytes=48<<20),
      cost_estimate=pl.CostEstimate(flops=10*R*N*128,bytes_accessed=N*512+R*1024,transcendentals=R*N),
      )(own,q,x,o,do,lse)


def join_kernel(*refs, count):
    t = pl.program_id(0)
    stacks, tail, out = refs[:-2], refs[-2], refs[-1]
    for i, ref in enumerate(stacks):
        @pl.when((t >= i * count) & (t < (i + 1) * count))
        def _(ref=ref):
            out[...] = ref[0]

    @pl.when(t >= len(stacks) * count)
    def _():
        out[:, :tail.shape[1]] = tail[...]


def join(stacks, tail):
    C, R, W = stacks[0].shape
    n = len(stacks)
    T = tail.shape[1]

    def at(i):
        return lambda t: (jnp.clip(t - i * C, 0, C - 1), 0, 0)
    return pl.pallas_call(functools.partial(join_kernel, count=C),
        out_shape=jax.ShapeDtypeStruct((R, n * C * W + T), bf16),
        grid=(n * C + 1,),
        in_specs=[pl.BlockSpec((1, R, W), at(i)) for i in range(n)] + [pl.BlockSpec((R, T), lambda t: (0, 0))],
        out_specs=pl.BlockSpec((R, W), lambda t: (0, t)),
        compiler_params=pltpu.CompilerParams(vmem_limit_bytes=56 << 20),
        cost_estimate=pl.CostEstimate(flops=0, bytes_accessed=4 * R * (n * C * W + T), transcendentals=0),
    )(*stacks, tail)


def deal_kernel(x_ref, o_ref):
    o_ref[0] = x_ref[...]


def deal(x, first, C, W):
    R = x.shape[0]
    return pl.pallas_call(deal_kernel,
        out_shape=jax.ShapeDtypeStruct((C, R, W), bf16),
        grid=(C,),
        in_specs=[pl.BlockSpec((R, W), lambda t: (0, first + t))],
        out_specs=pl.BlockSpec((1, R, W), lambda t: (t, 0, 0)),
        compiler_params=pltpu.CompilerParams(vmem_limit_bytes=56 << 20),
        cost_estimate=pl.CostEstimate(flops=0, bytes_accessed=4 * R * C * W, transcendentals=0),
    )(x)


def gather_kernel(x_ref, o_ref, own_sem, zs, zr, xs, xr, cs, cr, *, Z, C, quarter):
    z, a, c = lax.axis_index("zz"), lax.axis_index("core"), lax.axis_index("ctx")
    mesh_id = pl.DeviceIdType.MESH
    other = 1 - a
    peers = [(lax.rem(z + k, Z), a, c) for k in range(1, Z)] + [(z, a, lax.rem(c + j, C)) for j in range(1, C)] + [(z, other, c)]
    barrier = pltpu.get_barrier_semaphore()
    for peer in peers:
        pl.semaphore_signal(barrier, inc=1, device_id=peer, device_id_type=mesh_id)
    pl.semaphore_wait(barrier, len(peers))

    f = 2 * z + a

    def cols(q):
        return pl.ds(pl.multiple_of(q * quarter, quarter), quarter)

    def send(src, dst, s, r, peer):
        copy = pltpu.make_async_remote_copy(src_ref=src, dst_ref=dst, send_sem=s, recv_sem=r, device_id=peer, device_id_type=mesh_id)
        copy.start()
        return copy

    along = []
    for k in range(1, Z):
        along.append(send(x_ref.at[:, cols(c)], o_ref.at[f, :, cols(c)], zs.at[k - 1], zr.at[k - 1], peers[k - 1]))
    own = pltpu.make_async_copy(x_ref, o_ref.at[f], own_sem)
    own.start()
    whole = send(x_ref, o_ref.at[f], cs.at[0], cr.at[0], peers[-1])
    plane, cross = [], []
    for k in range(1, Z):
        along[k - 1].wait_recv()
        fs = 2 * lax.rem(z + Z - k, Z) + a
        piece = o_ref.at[fs, :, cols(c)]
        for j in range(1, C):
            n = (k - 1) * (C - 1) + j - 1
            plane.append(send(piece, piece, xs.at[n], xr.at[n], peers[Z - 1 + j - 1]))
        n = 1 + (k - 1) * C
        cross.append(send(piece, piece, cs.at[n], cr.at[n], peers[-1]))
    for k in range(1, Z):
        fs = 2 * lax.rem(z + Z - k, Z) + a
        for j in range(1, C):
            plane[(k - 1) * (C - 1) + j - 1].wait_recv()
            piece = o_ref.at[fs, :, cols(lax.rem(c + C - j, C))]
            n = 1 + (k - 1) * C + j
            cross.append(send(piece, piece, cs.at[n], cr.at[n], peers[-1]))
    for copy in along + plane:
        copy.wait_send()
    whole.wait_send()
    whole.wait_recv()
    for copy in cross:
        copy.wait_send()
        copy.wait_recv()
    own.wait()


def gather_all(x, Z, C):
    R, W = x.shape
    dma = pltpu.SemaphoreType.DMA
    n, m = (Z - 1) * (C - 1), 1 + (Z - 1) * C
    return pl.pallas_call(functools.partial(gather_kernel, Z=Z, C=C, quarter=W // C),
        out_shape=jax.ShapeDtypeStruct((2 * Z, R, W), bf16),
        in_specs=[pl.BlockSpec(memory_space=pl.ANY)],
        out_specs=pl.BlockSpec(memory_space=pl.ANY),
        scratch_shapes=[dma(()), dma((Z - 1,)), dma((Z - 1,)), dma((n,)), dma((n,)), dma((m,)), dma((m,))],
        compiler_params=pltpu.CompilerParams(collective_id=0, has_side_effects=True, vmem_limit_bytes=56 << 20),
        cost_estimate=pl.CostEstimate(flops=0, bytes_accessed=20 * R * W * Z, transcendentals=0),
    )(x)


def join_kernel(*refs, count):
    t = pl.program_id(0)
    stacks, tail, out = refs[:-2], refs[-2], refs[-1]
    for i, ref in enumerate(stacks):
        @pl.when((t >= i * count) & (t < (i + 1) * count))
        def _(ref=ref):
            out[...] = ref[0]

    @pl.when(t >= len(stacks) * count)
    def _():
        out[:, :tail.shape[1]] = tail[...]


def join(stacks, tail):
    C, R, W = stacks[0].shape
    n = len(stacks)
    T = tail.shape[1]

    def at(i):
        return lambda t: (jnp.clip(t - i * C, 0, C - 1), 0, 0)
    return pl.pallas_call(functools.partial(join_kernel, count=C),
        out_shape=jax.ShapeDtypeStruct((R, n * C * W + T), bf16),
        grid=(n * C + 1,),
        in_specs=[pl.BlockSpec((1, R, W), at(i)) for i in range(n)] + [pl.BlockSpec((R, T), lambda t: (0, 0))],
        out_specs=pl.BlockSpec((R, W), lambda t: (0, t)),
        compiler_params=pltpu.CompilerParams(vmem_limit_bytes=56 << 20),
        cost_estimate=pl.CostEstimate(flops=0, bytes_accessed=4 * R * (n * C * W + T), transcendentals=0),
    )(*stacks, tail)


def deal_kernel(x_ref, o_ref):
    o_ref[0] = x_ref[...]


def deal(x, first, C, W):
    R = x.shape[0]
    return pl.pallas_call(deal_kernel,
        out_shape=jax.ShapeDtypeStruct((C, R, W), bf16),
        grid=(C,),
        in_specs=[pl.BlockSpec((R, W), lambda t: (0, first + t))],
        out_specs=pl.BlockSpec((1, R, W), lambda t: (t, 0, 0)),
        compiler_params=pltpu.CompilerParams(vmem_limit_bytes=56 << 20),
        cost_estimate=pl.CostEstimate(flops=0, bytes_accessed=4 * R * C * W, transcendentals=0),
    )(x)


def gather_kernel(x_ref, o_ref, own_sem, zs, zr, xs, xr, cs, cr, *, Z, C, quarter):
    z, a, c = lax.axis_index("zz"), lax.axis_index("core"), lax.axis_index("ctx")
    mesh_id = pl.DeviceIdType.MESH
    other = 1 - a
    peers = [(lax.rem(z + k, Z), a, c) for k in range(1, Z)] + [(z, a, lax.rem(c + j, C)) for j in range(1, C)] + [(z, other, c)]
    barrier = pltpu.get_barrier_semaphore()
    for peer in peers:
        pl.semaphore_signal(barrier, inc=1, device_id=peer, device_id_type=mesh_id)
    pl.semaphore_wait(barrier, len(peers))

    f = 2 * z + a

    def cols(q):
        return pl.ds(pl.multiple_of(q * quarter, quarter), quarter)

    def send(src, dst, s, r, peer):
        copy = pltpu.make_async_remote_copy(src_ref=src, dst_ref=dst, send_sem=s, recv_sem=r, device_id=peer, device_id_type=mesh_id)
        copy.start()
        return copy

    along = []
    for k in range(1, Z):
        along.append(send(x_ref.at[:, cols(c)], o_ref.at[f, :, cols(c)], zs.at[k - 1], zr.at[k - 1], peers[k - 1]))
    own = pltpu.make_async_copy(x_ref, o_ref.at[f], own_sem)
    own.start()
    whole = send(x_ref, o_ref.at[f], cs.at[0], cr.at[0], peers[-1])
    plane, cross = [], []
    for k in range(1, Z):
        along[k - 1].wait_recv()
        fs = 2 * lax.rem(z + Z - k, Z) + a
        piece = o_ref.at[fs, :, cols(c)]
        for j in range(1, C):
            n = (k - 1) * (C - 1) + j - 1
            plane.append(send(piece, piece, xs.at[n], xr.at[n], peers[Z - 1 + j - 1]))
        n = 1 + (k - 1) * C
        cross.append(send(piece, piece, cs.at[n], cr.at[n], peers[-1]))
    for k in range(1, Z):
        fs = 2 * lax.rem(z + Z - k, Z) + a
        for j in range(1, C):
            plane[(k - 1) * (C - 1) + j - 1].wait_recv()
            piece = o_ref.at[fs, :, cols(lax.rem(c + C - j, C))]
            n = 1 + (k - 1) * C + j
            cross.append(send(piece, piece, cs.at[n], cr.at[n], peers[-1]))
    for copy in along + plane:
        copy.wait_send()
    whole.wait_send()
    whole.wait_recv()
    for copy in cross:
        copy.wait_send()
        copy.wait_recv()
    own.wait()


def gather_all(x, Z, C):
    R, W = x.shape
    dma = pltpu.SemaphoreType.DMA
    n, m = (Z - 1) * (C - 1), 1 + (Z - 1) * C
    return pl.pallas_call(functools.partial(gather_kernel, Z=Z, C=C, quarter=W // C),
        out_shape=jax.ShapeDtypeStruct((2 * Z, R, W), bf16),
        in_specs=[pl.BlockSpec(memory_space=pl.ANY)],
        out_specs=pl.BlockSpec(memory_space=pl.ANY),
        scratch_shapes=[dma(()), dma((Z - 1,)), dma((Z - 1,)), dma((n,)), dma((n,)), dma((m,)), dma((m,))],
        compiler_params=pltpu.CompilerParams(collective_id=0, has_side_effects=True, vmem_limit_bytes=56 << 20),
        cost_estimate=pl.CostEstimate(flops=0, bytes_accessed=20 * R * W * Z, transcendentals=0),
    )(x)


HEADS = 17
EPSILON = 1e-05
FS = ("zz", "core")


def norm_parts(v):
    mean = jnp.mean(v, axis=-1, keepdims=True)
    c = v - mean
    r = lax.rsqrt(jnp.mean(c * c, axis=-1, keepdims=True) + EPSILON)
    return c * r, r


def norm_back(dn, v, gain):
    xhat, r = norm_parts(v)
    y = dn * gain
    a = jnp.mean(y, axis=-1, keepdims=True)
    b = jnp.mean(y * xhat, axis=-1, keepdims=True)
    return r * (y - a - xhat * b), jnp.sum(dn * xhat, axis=0), jnp.sum(dn, axis=0)


def col_sum(x):
    return jnp.dot(jnp.ones((16, x.shape[0]), bf16), x, preferred_element_type=f32)[0]


def gelu_parts(u):
    z = jnp.abs(u) * 0.7071067811865476
    t = 1.0 / (1.0 + 0.3275911 * z)
    e = jnp.exp(-z * z)
    poly = t * (0.254829592 + t * (-0.284496736 + t * (1.421413741 + t * (-1.453152027 + t * 1.061405429))))
    half = 0.5 * poly * e
    cdf = jnp.where(u >= 0, 1.0 - half, half)
    return u * cdf, cdf + u * e * 0.3989422804014327


def local(
    tokens, cotangent, lengths, block_order,
    ln1_gain, ln1_bias, qkv_weight, q_bias, v_bias, out_weight, out_bias,
    ln2_gain, ln2_bias, up_weight, up_bias, down_weight, down_bias,
    *, G, S,
):
    slots, rows, width = tokens.shape
    C = lax.axis_size("ctx")
    me = lax.axis_index("ctx")
    N = rows * C
    B = rows // 2
    NB = 2 * C
    L = ln1_gain.shape[0]
    shard = ln1_gain.shape[1]
    HW = G * 128
    x_tokens = tokens[0]

    steps = jnp.arange(NB, dtype=jnp.int32)
    order = block_order[0]
    inverse = jnp.sum(jnp.where(order[None, :] == steps[:, None], steps[None, :], 0), axis=1).astype(jnp.int32)
    count = (lengths + (B - 1)) // B
    meta = jnp.concatenate([inverse, count])
    def swap(x):
        return lax.ppermute(x, "core", [(0, 1), (1, 0)])

    metas = [meta, swap(meta)][:S]
    phase_inv = [t[None, :NB] for t in metas]
    phase_nb = [t[NB:] for t in metas]
    own = jnp.concatenate([inverse, lax.dynamic_slice_in_dim(order, 2 * me, 2, 0), count])
    own_pos = (lax.dynamic_slice_in_dim(order, 2 * me, 2, 0)[:, None] * B + jnp.arange(B, dtype=jnp.int32)).reshape(rows, 1)
    live = (own_pos < lengths[0]).astype(f32)

    def pack(w):
        parts = []
        for g in range(G):
            parts += [w[:, kind * width + g * 128:kind * width + g * 128 + 128] for kind in range(3)]
        last = width - 64
        parts += [w[:, kind * width + last:kind * width + width] for kind in (1, 2, 0)]
        return jnp.concatenate(parts, axis=1)

    def unpack(w):
        tail = G * 384
        parts = []
        for kind, last in enumerate((128, 0, 64)):
            parts += [w[:, g * 384 + kind * 128:g * 384 + kind * 128 + 128] for g in range(G)]
            parts.append(w[:, tail + last:tail + last + 64])
        return jnp.concatenate(parts, axis=1)

    def fetch(w):
        return lax.all_gather(w.astype(bf16), FS, axis=0, tiled=True)

    vectors = [ln1_gain, ln1_bias, q_bias, v_bias, out_bias, ln2_gain, ln2_bias, down_bias]
    vec = [t.astype(bf16).T for t in vectors] + [up_bias.astype(bf16).reshape(4 * L, shard).T]
    first = pack(qkv_weight[0].astype(bf16))
    block = jnp.concatenate([first] + vec, axis=1)
    used = block.shape[1]
    if C == 4 and lax.axis_size("zz") == 4:
        block = jnp.pad(block, ((0, 0), (0, -used % (128 * C))))
        block = gather_all(block, 4, C)
    else:
        block = lax.all_gather(block, FS)
    first_w = block[:, :, :3 * width].reshape(width, 3 * width)
    vec = jnp.transpose(block[:, :, 3 * width:used].reshape(width, used - 3 * width)).astype(f32)

    def vector(index, layer):
        if index < 8:
            return vec[L * index + layer]
        t = vec[8 * L + 4 * layer:8 * L + 4 * layer + 4]
        return jnp.transpose(t.reshape(4, -1, shard), (1, 0, 2)).reshape(-1)

    weights = []
    for layer in range(L):
        weights.append((
            fetch(pack(qkv_weight[layer].astype(bf16))) if layer else first_w,
            fetch(out_weight[layer]),
            fetch(up_weight[layer]),
            fetch(down_weight[layer]),
        ))

    def plain(x):
        return with_layout_constraint(x, Layout(major_to_minor=tuple(range(x.ndim))))

    def exchange(x):
        return plain(lax.all_to_all(plain(x), "ctx", 0, 0))

    def after(x, *others):
        return lax.optimization_barrier((x,) + others)

    stream = x_tokens.astype(f32)
    records = []
    for layer in range(L):
        qkv_w, out_w, up_w, down_w = weights[layer]
        xhat, _ = norm_parts(stream)
        n1 = (xhat * vector(0, layer) + vector(1, layer)).astype(bf16)
        q_b, v_b = vector(2, layer), vector(3, layer)
        bias = pack(jnp.concatenate([q_b, jnp.zeros_like(q_b), v_b])[None])[0]
        projected = (jnp.dot(n1, qkv_w, preferred_element_type=f32) + bias).astype(bf16)
        wide = [deal(projected, s * C, C, 384) for s in range(S)]
        tail = projected[:, G * 384:]
        if S == 2:
            wide[1] = swap(wide[1])
        kv16 = jnp.broadcast_to(tail[None, :, :128], (C, rows, 128))
        q16 = tail[:, 128:]
        heads, o, lse, o_back = [], [], [], []
        for s in range(S):
            t = wide[s]
            if s == S - 1:
                t = jnp.concatenate([t, kv16], axis=2)
            if s:
                t, heads[0] = after(t, heads[0])
            heads.append(exchange(t).reshape(1, N, -1))
        for s in range(S):
            o_s, lse_s = flash_fwd(heads[s], phase_inv[s], phase_nb[s], B)
            o.append(o_s)
            lse.append(lse_s)
            t = o_s.reshape(C, rows, 128)
            if s:
                t, o_back[0] = after(t, o_back[0])
            o_back.append(exchange(swap(t) if s else t))
        o16, lse16 = one_fwd(q16, heads[-1][0], own, B)
        mixed = join(o_back, o16)
        m = stream + jnp.dot(mixed, out_w, preferred_element_type=f32) + vector(4, layer)
        xhat2, _ = norm_parts(m)
        n2 = (xhat2 * vector(5, layer) + vector(6, layer)).astype(bf16)
        u = jnp.dot(n2, up_w, preferred_element_type=f32) + vector(8, layer)
        a, slope = gelu_parts(u)
        a = a.astype(bf16)
        a, slope = after(a, slope.astype(bf16))
        records.append((stream, n1, heads, q16, o, lse, o16, lse16, mixed, m, n2, a, slope))
        stream = m + jnp.dot(a, down_w, preferred_element_type=f32) + vector(7, layer)
    activations = (stream * live).astype(bf16)[None]

    def reduce_fsdp(g):
        return lax.psum_scatter(g.astype(bf16), FS, scatter_dimension=0, tiled=True)

    def reduce_ctx(g):
        return lax.psum(g, "ctx").astype(f32)

    grad = cotangent[0].astype(f32) * live
    matrices = [None] * L
    fours = [None] * L
    ffns = [None] * L
    small = [None] * L

    def ctx_end(mine):
        return exchange(jnp.broadcast_to(mine[None], (C,) + mine.shape))

    def ctx_sum(shards):
        mine, sizes = ctx_begin(shards)
        return ctx_end(mine), sizes

    def ctx_begin(shards):
        pieces = []
        for t in shards:
            if t.shape[1] == width:
                pieces.append(t.reshape(C, -1, width))
            else:
                pieces.append(jnp.transpose(t.reshape(t.shape[0], C, -1), (1, 0, 2)).reshape(C, -1, width))
        sizes = [t.shape[1] for t in pieces]
        parts = exchange(jnp.concatenate(pieces, axis=1))
        mine = jnp.sum(parts.astype(f32), axis=0).astype(bf16)
        return mine, sizes

    def spread(summed, shapes):
        whole, sizes = summed
        out, at = [], 0
        for n, (r, c) in zip(sizes, shapes):
            t = whole[:, at:at + n].astype(f32)
            at += n
            if c == width:
                out.append(t.reshape(r, c))
            else:
                out.append(jnp.transpose(t.reshape(C, r, c // C), (1, 0, 2)).reshape(r, c))
        return out

    wide_shape, tall_shape = (shard, 4 * width), (4 * shard, width)
    for layer in reversed(range(L)):
        stream_in, n1, heads, q16, o, lse, o16, lse16, mixed, m, n2, a, slope = records[layer]
        qkv_w, out_w, up_w, down_w = weights[layer]
        gb = grad.astype(bf16)
        d_down_b = col_sum(gb)
        d_down = jnp.einsum("rf,rd->fd", a, gb, preferred_element_type=f32).astype(bf16)
        gb, d_down = after(gb, plain(d_down))
        d_down = reduce_fsdp(d_down)
        du = (jnp.einsum("rd,fd->rf", gb, down_w, preferred_element_type=f32) * slope.astype(f32)).astype(bf16)
        d_up_b = col_sum(du)
        d_up = jnp.einsum("rd,rf->df", n2, du, preferred_element_type=f32).astype(bf16)
        du, d_up = after(du, plain(d_up))
        d_up = reduce_fsdp(d_up)
        dn2 = jnp.einsum("rf,df->rd", du, up_w, preferred_element_type=f32)
        back, d_gain2, d_bias2 = norm_back(dn2, m, vector(5, layer))
        gm = grad + back
        gmb = gm.astype(bf16)
        d_out_b = col_sum(gmb)
        d_out = jnp.einsum("rd,re->de", mixed, gmb, preferred_element_type=f32).astype(bf16)
        if layer == 0:
            gmb, d_out = after(gmb, plain(d_out))
        if layer < L - 1:
            done = after(gmb, *ffn_sum)
            gmb, ffn_sum = done[0], done[1:]
        d_o = []
        for s in range(S):
            w = out_w[C * 128 * s:C * 128 * (s + 1)].reshape(C, 128, width)
            d_o.append(jnp.einsum("re,gce->grc", gmb, w, preferred_element_type=f32).astype(bf16))
        d_o16 = jnp.einsum("re,ce->rc", gmb, out_w[HW:], preferred_element_type=f32).astype(bf16)
        dq16, dkv16 = one_bwd(q16, heads[-1][0], o16, d_o16, lse16, own, B)
        d_oh, d_wide = [], []
        for s in range(S):
            t = d_o[s]
            if s:
                t = swap(t)
            if s == S - 1:
                t = jnp.concatenate([t, dkv16.reshape(C, rows, 128)], axis=2)
            if s:
                t, d_oh[0] = after(t, d_oh[0])
            if s == S - 1 and layer < L - 1:
                t, fours[layer + 1] = after(t, fours[layer + 1])
            d_oh.append(exchange(t).reshape(1, N, -1))
        dkv16 = jnp.sum(d_oh[-1].reshape(C, rows, 256)[:, :, 128:].astype(f32), axis=0)
        for s in range(S):
            t = flash_bwd(heads[s], o[s], d_oh[s], lse[s], phase_inv[s], phase_nb[s], B)
            t = t.reshape(C, rows, 384)
            if s:
                t, d_wide[0] = after(t, d_wide[0])
            if s == S - 1:
                t, d_down = after(t, d_down)
            if s == S - 1 and layer:
                t, d_up = after(t, d_up)
                ffn_sum = lax.psum((d_up, d_down), "ctx")
            d_wide.append(exchange(swap(t) if s else t))
        d_tail = jnp.concatenate([dkv16.astype(bf16), dq16], axis=1)
        d_row = join(d_wide, d_tail)
        d_back = d_row
        if layer == 0:
            d_row, d_up = after(d_row, d_up)
            mine, middle_sizes = ctx_begin([fours[1], d_up, d_down])
            d_back, mine = after(d_row, mine)
            middle = ctx_end(mine)
        d_qkv = jnp.einsum("rd,rc->dc", n1, d_row, preferred_element_type=f32).astype(bf16)
        if layer:
            d_row, d_four = after(d_row, plain(jnp.concatenate([d_qkv, d_out], axis=1)))
            d_four = reduce_fsdp(d_four)
        else:
            d_qkv, d_out = after(d_qkv, reduce_fsdp(d_out))
            d_four = jnp.concatenate([reduce_fsdp(d_qkv), d_out], axis=1)
        sums = unpack(col_sum(d_row)[None])[0]
        dn1 = jnp.einsum("rc,dc->rd", d_back, qkv_w, preferred_element_type=f32)
        back, d_gain1, d_bias1 = norm_back(dn1, stream_in, vector(0, layer))
        grad = gm + back
        fours[layer] = d_four
        ffns[layer] = (d_up, d_down)
        if layer == 0:
            last = ctx_sum([d_four])
        small[layer] = jnp.concatenate([
            t.reshape(-1, n) for t, n in (
                (d_gain1, shard), (d_bias1, shard), (sums[:width], shard), (sums[2 * width:], shard), (d_out_b, shard),
                (d_gain2, shard), (d_bias2, shard), (d_down_b, shard), (d_up_b, 4 * shard))], axis=1)

    vec_grads = jnp.stack(small, axis=1)
    vec_grads, middle, activations = after(vec_grads, middle, activations)
    vec_grads = jnp.sum(lax.all_to_all(vec_grads, FS, 0, 0), axis=0)
    vec_grads = jnp.sum(lax.all_to_all(jnp.broadcast_to(vec_grads[None], (C,) + vec_grads.shape), "ctx", 0, 0), axis=0)
    rest = spread((middle, middle_sizes), [wide_shape, wide_shape, tall_shape])
    matrices[1] = [rest[0], ffn_sum[0].astype(f32), ffn_sum[1].astype(f32)]
    matrices[0] = spread(last, [wide_shape]) + rest[1:]
    vg = [vec_grads[:, i * shard:(i + 1) * shard] for i in range(8)] + [vec_grads[:, 8 * shard:]]

    g_qkv = jnp.stack([unpack(matrices[layer][0][:, :3 * width]) for layer in range(L)])
    g_out = jnp.stack([matrices[layer][0][:, 3 * width:] for layer in range(L)])
    g_up = jnp.stack([matrices[layer][1] for layer in range(L)])
    g_down = jnp.stack([matrices[layer][2] for layer in range(L)])
    return (activations, grad[None], vg[0], vg[1], g_qkv, vg[2], vg[3], g_out, vg[4], vg[5], vg[6], g_up, vg[8], g_down, vg[7])


def solution(mesh):
    F, C = mesh.devices.shape
    inner = Mesh(mesh.devices.reshape(F // 2, 2, C), ("zz", "core", "ctx"))
    S = 2 if 16 // (2 * C) >= 2 else 1
    G = S * C
    rows = P(FS, "ctx", None)
    vec, mat = P(None, FS), P(None, FS, None)
    return jax.shard_map(
        functools.partial(local, G=G, S=S),
        mesh=inner,
        in_specs=(rows, rows, P(FS), P(FS, None), vec, vec, mat, vec, vec, mat, vec, vec, vec, mat, vec, mat, vec),
        out_specs=(rows, rows, vec, vec, mat, vec, vec, mat, vec, vec, vec, mat, vec, mat, vec),
        check_vma=False,
    )
```

```python
import functools
import jax, jax.numpy as jnp
from jax import lax
from jax.experimental import pallas as pl
from jax.experimental.pallas import tpu as pltpu
from jax.experimental.layout import Layout, with_layout_constraint
from jax.sharding import Mesh, PartitionSpec as P
f32=jnp.float32; bf16=jnp.bfloat16
NEG=-1e30
def dot_nt(a,b): return lax.dot_general(a,b,(((1,),(1,)),((),())),preferred_element_type=f32)
def dot_nn(a,b): return lax.dot_general(a,b,(((1,),(0,)),((),())),preferred_element_type=f32)

LOG2E=1.4426950408889634
def split(q,h,low):
    qs=q.astype(f32)*(0.125*LOG2E)
    hi=qs.astype(bf16).astype(f32); lo=qs-hi
    rl=pltpu.roll(lo,64,1)
    c=jnp.where(low,hi,rl) if h==0 else jnp.where(low,rl,hi)
    return c.astype(bf16)
def dup(k,h,low):
    kf=k.astype(f32); rl=pltpu.roll(kf,64,1)
    c=jnp.where(low,kf,rl) if h==0 else jnp.where(low,rl,kf)
    return c.astype(bf16)
def fwd_kernel(inv_ref, nb_ref, x_ref, o_ref, lse_ref, vt, kd, sb, acc, *, B, NB):
    s=pl.program_id(0)
    nb=nb_ref[s]
    lane=lax.broadcasted_iota(jnp.int32,(1,128),1)
    low=lane<64
    def tv(j,_):
        r=pl.multiple_of(inv_ref[s,j]*B,B)
        w=pl.multiple_of(j*B,B)
        t=x_ref[0,pl.ds(r,B),256:384].T
        one=(lax.broadcasted_iota(jnp.int32,(16,B),0)==0).astype(bf16)
        for h in range(2):
            vt[80*h:80*h+64,pl.ds(w,B)]=t[64*h:64*h+64,:]
            vt[80*h+64:80*h+80,pl.ds(w,B)]=one
            kd[h,pl.ds(w,B),:]=dup(x_ref[0,pl.ds(r,B),128:256],h,low)
        return 0
    lax.fori_loop(0,nb,tv,0)
    rr=lax.broadcasted_iota(jnp.int32,(B,B),0)
    cc=lax.broadcasted_iota(jnp.int32,(B,B),1)
    def qblock(i,_):
        r=pl.multiple_of(inv_ref[s,i]*B,B)
        q=x_ref[0,pl.ds(r,B),0:128]
        qh=[split(q,h,low) for h in range(2)]
        acc[...]=jnp.zeros_like(acc)
        def scores(j,slot):
            for h in range(2):
                sb[slot,h]=dot_nt(kd[h,pl.ds(pl.multiple_of(j*B,B),B),:],qh[h])
        def step(j,carry,diag):
            out=[]
            for h in range(2):
                m=carry[h]
                st=sb[j%2,h]
                if diag: st=jnp.where(rr<=cc,st,NEG)
                mn=jnp.maximum(m,jnp.max(st,axis=0,keepdims=True))
                p=jnp.exp2(st-mn)
                al=jnp.exp2(m-mn)
                v=vt[80*h:80*h+80,pl.ds(pl.multiple_of(j*B,B),B)]
                acc[h]=acc[h]*al+dot_nn(v,p.astype(bf16))
                out.append(mn)
            return tuple(out)
        scores(0,0)
        def both(j,c):
            scores(j+1,(j+1)%2)
            return step(j,c,False)
        n=jnp.full((1,B),NEG,f32)
        c=lax.fori_loop(0,i,both,(n,n))
        c=step(i,c,True)
        os=[]
        for h in range(2):
            l=acc[h,64:65,:]
            os.append(acc[h,0:64,:]*(1.0/l))
            lse_ref[0,pl.ds(h,1),pl.ds(r,B)]=c[h]+jnp.log2(l)
        o_ref[0,pl.ds(r,B),:]=jnp.concatenate(os,0).T.astype(bf16)
        return 0
    lax.fori_loop(0,nb,qblock,0)
    def pad(i,_):
        r=pl.multiple_of(inv_ref[s,i]*B,B)
        o_ref[0,pl.ds(r,B),:]=jnp.zeros((B,128),bf16)
        lse_ref[0,:,pl.ds(r,B)]=jnp.zeros((8,B),f32)
        return 0
    lax.fori_loop(nb,NB,pad,0)

def flash_fwd(x,inv,nb,B):
    S,N,_=x.shape
    NB=N//B
    return pl.pallas_call(functools.partial(fwd_kernel,B=B,NB=NB),
      out_shape=(jax.ShapeDtypeStruct((S,N,128),bf16),jax.ShapeDtypeStruct((S,8,N),f32)),
      grid_spec=pltpu.PrefetchScalarGridSpec(num_scalar_prefetch=2,grid=(S,),
        in_specs=[pl.BlockSpec((1,N,384),lambda s,*_:(s,0,0))],
        out_specs=[pl.BlockSpec((1,N,128),lambda s,*_:(s,0,0)),pl.BlockSpec((1,8,N),lambda s,*_:(s,0,0))],
        scratch_shapes=[pltpu.VMEM((160,N),bf16),pltpu.VMEM((2,N,128),bf16),pltpu.VMEM((2,2,B,B),f32),pltpu.VMEM((2,80,B),f32)]),
      compiler_params=pltpu.CompilerParams(vmem_limit_bytes=48<<20),
      cost_estimate=pl.CostEstimate(flops=S*4*N*N*128,bytes_accessed=S*N*1024,transcendentals=S*N*N),
      )(inv,nb,x)

def bwd_kernel(inv_ref, nb_ref, x_ref, o_ref, do_ref, lse_ref, dx_ref, kt, qd, dq, dk, dv, dl, *, B, NB):
    s=pl.program_id(0)
    nb=nb_ref[s]
    lane=lax.broadcasted_iota(jnp.int32,(1,128),1)
    low=lane<64
    hm=(lax.broadcasted_iota(jnp.int32,(8,128),1)//64==lax.broadcasted_iota(jnp.int32,(8,128),0)).astype(bf16)
    def prep(j,_):
        r=pl.multiple_of(inv_ref[s,j]*B,B)
        w=pl.multiple_of(j*B,B)
        kt[:,pl.ds(w,B)]=x_ref[0,pl.ds(r,B),128:256].T
        for h in range(2): qd[h,pl.ds(w,B),:]=split(x_ref[0,pl.ds(r,B),0:128],h,low)
        prod=o_ref[0,pl.ds(r,B),:].astype(f32)*do_ref[0,pl.ds(r,B),:].astype(f32)
        hi=prod.astype(bf16); lo=(prod-hi.astype(f32)).astype(bf16)
        dl[:,pl.ds(w,B)]=dot_nt(hm,hi)+dot_nt(hm,lo)
        dq[:,pl.ds(w,B)]=jnp.zeros((128,B),f32)
        return 0
    lax.fori_loop(0,nb,prep,0)
    rr=lax.broadcasted_iota(jnp.int32,(B,B),0)
    cc=lax.broadcasted_iota(jnp.int32,(B,B),1)
    def kblock(j,_):
        r=pl.multiple_of(inv_ref[s,j]*B,B)
        k=x_ref[0,pl.ds(r,B),128:256]
        v=x_ref[0,pl.ds(r,B),256:384]
        kdh=[dup(k,h,low) for h in range(2)]
        dk[...]=jnp.zeros_like(dk); dv[...]=jnp.zeros_like(dv)
        def step(i,diag):
            ri=pl.multiple_of(inv_ref[s,i]*B,B)
            wi=pl.multiple_of(i*B,B)
            q=x_ref[0,pl.ds(ri,B),0:128]*jnp.asarray(0.125,bf16)
            do=do_ref[0,pl.ds(ri,B),:]
            zero=jnp.zeros_like(q)
            dvs=[];dks=[]
            for h in range(2):
                qh=jnp.where(low,q,zero) if h==0 else jnp.where(low,zero,q)
                doh=jnp.where(low,do,zero) if h==0 else jnp.where(low,zero,do)
                st=dot_nt(kdh[h],qd[h,pl.ds(wi,B),:])
                p=jnp.exp2(st-lse_ref[0,pl.ds(h,1),pl.ds(ri,B)])
                if diag: p=jnp.where(rr<=cc,p,0.0)
                dvs.append(dot_nn(p.astype(bf16),doh))
                dp=dot_nt(v,doh)
                ds=(p*(dp-dl[pl.ds(h,1),pl.ds(wi,B)])).astype(bf16)
                dks.append(dot_nn(ds,qh))
                kh=kt[64*h:64*h+64,pl.ds(pl.multiple_of(j*B,B),B)]
                dq[64*h:64*h+64,pl.ds(wi,B)]+=dot_nn(kh,ds)
            dv[...]+=dvs[0]+dvs[1]
            dk[...]+=dks[0]+dks[1]
        step(j,True)
        def body(i,_):
            step(i,False); return 0
        lax.fori_loop(j+1,nb,body,0)
        dx_ref[0,pl.ds(r,B),128:256]=dk[...].astype(bf16)
        dx_ref[0,pl.ds(r,B),256:384]=dv[...].astype(bf16)
        return 0
    lax.fori_loop(0,nb,kblock,0)
    def fin(i,_):
        r=pl.multiple_of(inv_ref[s,i]*B,B)
        dx_ref[0,pl.ds(r,B),0:128]=(dq[:,pl.ds(pl.multiple_of(i*B,B),B)].T*0.125).astype(bf16)
        return 0
    lax.fori_loop(0,nb,fin,0)
    def pad(i,_):
        r=pl.multiple_of(inv_ref[s,i]*B,B)
        dx_ref[0,pl.ds(r,B),:]=jnp.zeros((B,384),bf16)
        return 0
    lax.fori_loop(nb,NB,pad,0)

def flash_bwd(x,o,do,lse,inv,nb,B):
    S,N,_=x.shape
    NB=N//B
    return pl.pallas_call(functools.partial(bwd_kernel,B=B,NB=NB),
      out_shape=jax.ShapeDtypeStruct((S,N,384),bf16),
      grid_spec=pltpu.PrefetchScalarGridSpec(num_scalar_prefetch=2,grid=(S,),
        in_specs=[pl.BlockSpec((1,N,384),lambda s,*_:(s,0,0)),pl.BlockSpec((1,N,128),lambda s,*_:(s,0,0)),
                  pl.BlockSpec((1,N,128),lambda s,*_:(s,0,0)),pl.BlockSpec((1,8,N),lambda s,*_:(s,0,0))],
        out_specs=pl.BlockSpec((1,N,384),lambda s,*_:(s,0,0)),
        scratch_shapes=[pltpu.VMEM((128,N),bf16),pltpu.VMEM((2,N,128),bf16),pltpu.VMEM((128,N),f32),pltpu.VMEM((B,128),f32),pltpu.VMEM((B,128),f32),pltpu.VMEM((8,N),f32)]),
      compiler_params=pltpu.CompilerParams(vmem_limit_bytes=48<<20),
      cost_estimate=pl.CostEstimate(flops=S*10*N*N*128,bytes_accessed=S*N*2400,transcendentals=S*N*N),
      )(inv,nb,x,o,do,lse)


def one_fwd_kernel(own_ref, q_ref, x_ref, o_ref, lse_ref, vt, kd, acc, *, B, NB):
    nb = own_ref[NB + 2]
    low = lax.broadcasted_iota(jnp.int32,(1,128),1)<64
    def tv(j,_):
        r=pl.multiple_of(own_ref[j]*B,B)
        t=x_ref[pl.ds(r,B),:].T
        w=pl.multiple_of(j*B,B)
        kd[pl.ds(w,B),:]=dup(x_ref[pl.ds(r,B),:],0,low)
        vt[0:64,pl.ds(w,B)]=t[64:128,:]
        vt[64:80,pl.ds(w,B)]=(lax.broadcasted_iota(jnp.int32,(16,B),0)==0).astype(bf16)
        return 0
    lax.fori_loop(0,nb,tv,0)
    rr=lax.broadcasted_iota(jnp.int32,(B,B),0)
    cc=lax.broadcasted_iota(jnp.int32,(B,B),1)
    for t in range(2):
        i=own_ref[NB+t]
        @pl.when(i>=nb)
        def _():
            o_ref[t*B:(t+1)*B,:]=jnp.zeros((B,64),bf16)
            lse_ref[:,t*B:(t+1)*B]=jnp.zeros((8,B),f32)
        @pl.when(i<nb)
        def _():
            qs=q_ref[t*B:(t+1)*B,:].astype(f32)*(0.125*LOG2E)
            hi=qs.astype(bf16)
            q=jnp.concatenate([hi.astype(f32),qs-hi.astype(f32)],axis=1).astype(bf16)
            acc[...]=jnp.zeros_like(acc)
            def step(j,m,diag):
                st=dot_nt(kd[pl.ds(pl.multiple_of(j*B,B),B),:],q)
                if diag: st=jnp.where(rr<=cc,st,NEG)
                mn=jnp.maximum(m,jnp.max(st,axis=0,keepdims=True))
                p=jnp.exp2(st-mn)
                al=jnp.exp2(m-mn)
                v=vt[:,pl.ds(pl.multiple_of(j*B,B),B)]
                acc[...]=acc[...]*al+dot_nn(v,p.astype(bf16))
                return mn
            m=lax.fori_loop(0,i,lambda j,m: step(j,m,False),jnp.full((1,B),NEG,f32))
            m=step(i,m,True)
            l=acc[64:65,:]
            o_ref[t*B:(t+1)*B,:]=(acc[0:64,:]*(1.0/l)).T.astype(bf16)
            lse_ref[:,t*B:(t+1)*B]=jnp.broadcast_to(m+jnp.log2(l),(8,B))


def one_fwd(q,x,own,B):
    N=x.shape[0]; R=q.shape[0]; NB=N//B
    full=lambda *_:(0,0)
    last=lambda *_:(0,3)
    return pl.pallas_call(functools.partial(one_fwd_kernel,B=B,NB=NB),
      out_shape=(jax.ShapeDtypeStruct((R,64),bf16),jax.ShapeDtypeStruct((8,R),f32)),
      grid_spec=pltpu.PrefetchScalarGridSpec(num_scalar_prefetch=1,grid=(1,),
        in_specs=[pl.BlockSpec((R,64),full),pl.BlockSpec((N,128),last)],
        out_specs=[pl.BlockSpec((R,64),full),pl.BlockSpec((8,R),full)],
        scratch_shapes=[pltpu.VMEM((80,N),bf16),pltpu.VMEM((N,128),bf16),pltpu.VMEM((80,B),f32)]),
      compiler_params=pltpu.CompilerParams(vmem_limit_bytes=48<<20),
      cost_estimate=pl.CostEstimate(flops=4*R*N*128,bytes_accessed=N*256+R*512,transcendentals=R*N),
      )(own,q,x)


def one_bwd_kernel(own_ref, q_ref, x_ref, o_ref, do_ref, lse_ref, dq_ref, dx_ref, dkv, dq, *, B, NB):
    nb = own_ref[NB + 2]
    low = lax.broadcasted_iota(jnp.int32,(1,128),1)<64
    rr=lax.broadcasted_iota(jnp.int32,(B,B),0)
    cc=lax.broadcasted_iota(jnp.int32,(B,B),1)
    ones=jnp.ones((8,64),bf16)
    dkv[...]=jnp.zeros_like(dkv)
    for t in range(2):
        i=own_ref[NB+t]
        sl=slice(t*B,(t+1)*B)
        @pl.when(i>=nb)
        def _():
            dq_ref[sl,:]=jnp.zeros((B,64),bf16)
        @pl.when(i<nb)
        def _():
            qr=q_ref[sl,:]
            qs=qr.astype(f32)*(0.125*LOG2E)
            hi=qs.astype(bf16)
            q=jnp.concatenate([hi.astype(f32),qs-hi.astype(f32)],axis=1).astype(bf16)
            qd=qr*jnp.asarray(0.125,bf16)
            do=do_ref[sl,:]
            prod=o_ref[sl,:].astype(f32)*do.astype(f32)
            hi=prod.astype(bf16); lo=(prod-hi.astype(f32)).astype(bf16)
            dl=(dot_nt(ones,hi)+dot_nt(ones,lo))[0:1,:]
            lse=lse_ref[0:1,sl]
            dq[...]=jnp.zeros_like(dq)
            def step(j,diag):
                r=pl.multiple_of(own_ref[j]*B,B)
                k=x_ref[pl.ds(r,B),0:64]
                v=x_ref[pl.ds(r,B),64:128]
                st=dot_nt(dup(x_ref[pl.ds(r,B),:],0,low),q)
                p=jnp.exp2(st-lse)
                if diag: p=jnp.where(rr<=cc,p,0.0)
                dp=dot_nt(v,do)
                ds=(p*(dp-dl)).astype(bf16)
                dkv[pl.ds(r,B),64:128]+=dot_nn(p.astype(bf16),do)
                dkv[pl.ds(r,B),0:64]+=dot_nn(ds,qd)
                dq[...]+=dot_nn(k.T,ds)
            def body(j,_):
                step(j,False); return 0
            lax.fori_loop(0,i,body,0)
            step(i,True)
            dq_ref[sl,:]=(dq[...].T*0.125).astype(bf16)
    dx_ref[...]=dkv[...].astype(bf16)


def one_bwd(q,x,o,do,lse,own,B):
    N=x.shape[0]; R=q.shape[0]; NB=N//B
    full=lambda *_:(0,0)
    last=lambda *_:(0,3)
    return pl.pallas_call(functools.partial(one_bwd_kernel,B=B,NB=NB),
      out_shape=(jax.ShapeDtypeStruct((R,64),bf16),jax.ShapeDtypeStruct((N,128),bf16)),
      grid_spec=pltpu.PrefetchScalarGridSpec(num_scalar_prefetch=1,grid=(1,),
        in_specs=[pl.BlockSpec((R,64),full),pl.BlockSpec((N,128),last),pl.BlockSpec((R,64),full),pl.BlockSpec((R,64),full),pl.BlockSpec((8,R),full)],
        out_specs=[pl.BlockSpec((R,64),full),pl.BlockSpec((N,128),full)],
        scratch_shapes=[pltpu.VMEM((N,128),f32),pltpu.VMEM((64,B),f32)]),
      compiler_params=pltpu.CompilerParams(vmem_limit_bytes=48<<20),
      cost_estimate=pl.CostEstimate(flops=10*R*N*128,bytes_accessed=N*512+R*1024,transcendentals=R*N),
      )(own,q,x,o,do,lse)


def join_kernel(*refs, count):
    t = pl.program_id(0)
    stacks, tail, out = refs[:-2], refs[-2], refs[-1]
    for i, ref in enumerate(stacks):
        @pl.when((t >= i * count) & (t < (i + 1) * count))
        def _(ref=ref):
            out[...] = ref[0]

    @pl.when(t >= len(stacks) * count)
    def _():
        out[:, :tail.shape[1]] = tail[...]


def join(stacks, tail):
    C, R, W = stacks[0].shape
    n = len(stacks)
    T = tail.shape[1]

    def at(i):
        return lambda t: (jnp.clip(t - i * C, 0, C - 1), 0, 0)
    return pl.pallas_call(functools.partial(join_kernel, count=C),
        out_shape=jax.ShapeDtypeStruct((R, n * C * W + T), bf16),
        grid=(n * C + 1,),
        in_specs=[pl.BlockSpec((1, R, W), at(i)) for i in range(n)] + [pl.BlockSpec((R, T), lambda t: (0, 0))],
        out_specs=pl.BlockSpec((R, W), lambda t: (0, t)),
        compiler_params=pltpu.CompilerParams(vmem_limit_bytes=56 << 20),
        cost_estimate=pl.CostEstimate(flops=0, bytes_accessed=4 * R * (n * C * W + T), transcendentals=0),
    )(*stacks, tail)


def deal_kernel(x_ref, o_ref):
    o_ref[0] = x_ref[...]


def deal(x, first, C, W):
    R = x.shape[0]
    return pl.pallas_call(deal_kernel,
        out_shape=jax.ShapeDtypeStruct((C, R, W), bf16),
        grid=(C,),
        in_specs=[pl.BlockSpec((R, W), lambda t: (0, first + t))],
        out_specs=pl.BlockSpec((1, R, W), lambda t: (t, 0, 0)),
        compiler_params=pltpu.CompilerParams(vmem_limit_bytes=56 << 20),
        cost_estimate=pl.CostEstimate(flops=0, bytes_accessed=4 * R * C * W, transcendentals=0),
    )(x)


def gather_kernel(x_ref, o_ref, own_sem, zs, zr, xs, xr, cs, cr, *, Z, C, quarter):
    z, a, c = lax.axis_index("zz"), lax.axis_index("core"), lax.axis_index("ctx")
    mesh_id = pl.DeviceIdType.MESH
    other = 1 - a
    peers = [(lax.rem(z + k, Z), a, c) for k in range(1, Z)] + [(z, a, lax.rem(c + j, C)) for j in range(1, C)] + [(z, other, c)]
    barrier = pltpu.get_barrier_semaphore()
    for peer in peers:
        pl.semaphore_signal(barrier, inc=1, device_id=peer, device_id_type=mesh_id)
    pl.semaphore_wait(barrier, len(peers))

    f = 2 * z + a

    def cols(q):
        return pl.ds(pl.multiple_of(q * quarter, quarter), quarter)

    def send(src, dst, s, r, peer):
        copy = pltpu.make_async_remote_copy(src_ref=src, dst_ref=dst, send_sem=s, recv_sem=r, device_id=peer, device_id_type=mesh_id)
        copy.start()
        return copy

    along = []
    for k in range(1, Z):
        along.append(send(x_ref.at[:, cols(c)], o_ref.at[f, :, cols(c)], zs.at[k - 1], zr.at[k - 1], peers[k - 1]))
    own = pltpu.make_async_copy(x_ref, o_ref.at[f], own_sem)
    own.start()
    whole = send(x_ref, o_ref.at[f], cs.at[0], cr.at[0], peers[-1])
    plane, cross = [], []
    for k in range(1, Z):
        along[k - 1].wait_recv()
        fs = 2 * lax.rem(z + Z - k, Z) + a
        piece = o_ref.at[fs, :, cols(c)]
        for j in range(1, C):
            n = (k - 1) * (C - 1) + j - 1
            plane.append(send(piece, piece, xs.at[n], xr.at[n], peers[Z - 1 + j - 1]))
        n = 1 + (k - 1) * C
        cross.append(send(piece, piece, cs.at[n], cr.at[n], peers[-1]))
    for k in range(1, Z):
        fs = 2 * lax.rem(z + Z - k, Z) + a
        for j in range(1, C):
            plane[(k - 1) * (C - 1) + j - 1].wait_recv()
            piece = o_ref.at[fs, :, cols(lax.rem(c + C - j, C))]
            n = 1 + (k - 1) * C + j
            cross.append(send(piece, piece, cs.at[n], cr.at[n], peers[-1]))
    for copy in along + plane:
        copy.wait_send()
    whole.wait_send()
    whole.wait_recv()
    for copy in cross:
        copy.wait_send()
        copy.wait_recv()
    own.wait()


def gather_all(x, Z, C):
    R, W = x.shape
    dma = pltpu.SemaphoreType.DMA
    n, m = (Z - 1) * (C - 1), 1 + (Z - 1) * C
    return pl.pallas_call(functools.partial(gather_kernel, Z=Z, C=C, quarter=W // C),
        out_shape=jax.ShapeDtypeStruct((2 * Z, R, W), bf16),
        in_specs=[pl.BlockSpec(memory_space=pl.ANY)],
        out_specs=pl.BlockSpec(memory_space=pl.ANY),
        scratch_shapes=[dma(()), dma((Z - 1,)), dma((Z - 1,)), dma((n,)), dma((n,)), dma((m,)), dma((m,))],
        compiler_params=pltpu.CompilerParams(collective_id=0, has_side_effects=True, vmem_limit_bytes=56 << 20),
        cost_estimate=pl.CostEstimate(flops=0, bytes_accessed=20 * R * W * Z, transcendentals=0),
    )(x)


def join_kernel(*refs, count):
    t = pl.program_id(0)
    stacks, tail, out = refs[:-2], refs[-2], refs[-1]
    for i, ref in enumerate(stacks):
        @pl.when((t >= i * count) & (t < (i + 1) * count))
        def _(ref=ref):
            out[...] = ref[0]

    @pl.when(t >= len(stacks) * count)
    def _():
        out[:, :tail.shape[1]] = tail[...]


def join(stacks, tail):
    C, R, W = stacks[0].shape
    n = len(stacks)
    T = tail.shape[1]

    def at(i):
        return lambda t: (jnp.clip(t - i * C, 0, C - 1), 0, 0)
    return pl.pallas_call(functools.partial(join_kernel, count=C),
        out_shape=jax.ShapeDtypeStruct((R, n * C * W + T), bf16),
        grid=(n * C + 1,),
        in_specs=[pl.BlockSpec((1, R, W), at(i)) for i in range(n)] + [pl.BlockSpec((R, T), lambda t: (0, 0))],
        out_specs=pl.BlockSpec((R, W), lambda t: (0, t)),
        compiler_params=pltpu.CompilerParams(vmem_limit_bytes=56 << 20),
        cost_estimate=pl.CostEstimate(flops=0, bytes_accessed=4 * R * (n * C * W + T), transcendentals=0),
    )(*stacks, tail)


def deal_kernel(x_ref, o_ref):
    o_ref[0] = x_ref[...]


def deal(x, first, C, W):
    R = x.shape[0]
    return pl.pallas_call(deal_kernel,
        out_shape=jax.ShapeDtypeStruct((C, R, W), bf16),
        grid=(C,),
        in_specs=[pl.BlockSpec((R, W), lambda t: (0, first + t))],
        out_specs=pl.BlockSpec((1, R, W), lambda t: (t, 0, 0)),
        compiler_params=pltpu.CompilerParams(vmem_limit_bytes=56 << 20),
        cost_estimate=pl.CostEstimate(flops=0, bytes_accessed=4 * R * C * W, transcendentals=0),
    )(x)


def gather_kernel(x_ref, o_ref, own_sem, zs, zr, xs, xr, cs, cr, *, Z, C, quarter):
    z, a, c = lax.axis_index("zz"), lax.axis_index("core"), lax.axis_index("ctx")
    mesh_id = pl.DeviceIdType.MESH
    other = 1 - a
    peers = [(lax.rem(z + k, Z), a, c) for k in range(1, Z)] + [(z, a, lax.rem(c + j, C)) for j in range(1, C)] + [(z, other, c)]
    barrier = pltpu.get_barrier_semaphore()
    for peer in peers:
        pl.semaphore_signal(barrier, inc=1, device_id=peer, device_id_type=mesh_id)
    pl.semaphore_wait(barrier, len(peers))

    f = 2 * z + a

    def cols(q):
        return pl.ds(pl.multiple_of(q * quarter, quarter), quarter)

    def send(src, dst, s, r, peer):
        copy = pltpu.make_async_remote_copy(src_ref=src, dst_ref=dst, send_sem=s, recv_sem=r, device_id=peer, device_id_type=mesh_id)
        copy.start()
        return copy

    along = []
    for k in range(1, Z):
        along.append(send(x_ref.at[:, cols(c)], o_ref.at[f, :, cols(c)], zs.at[k - 1], zr.at[k - 1], peers[k - 1]))
    own = pltpu.make_async_copy(x_ref, o_ref.at[f], own_sem)
    own.start()
    whole = send(x_ref, o_ref.at[f], cs.at[0], cr.at[0], peers[-1])
    plane, cross = [], []
    for k in range(1, Z):
        along[k - 1].wait_recv()
        fs = 2 * lax.rem(z + Z - k, Z) + a
        piece = o_ref.at[fs, :, cols(c)]
        for j in range(1, C):
            n = (k - 1) * (C - 1) + j - 1
            plane.append(send(piece, piece, xs.at[n], xr.at[n], peers[Z - 1 + j - 1]))
        n = 1 + (k - 1) * C
        cross.append(send(piece, piece, cs.at[n], cr.at[n], peers[-1]))
    for k in range(1, Z):
        fs = 2 * lax.rem(z + Z - k, Z) + a
        for j in range(1, C):
            plane[(k - 1) * (C - 1) + j - 1].wait_recv()
            piece = o_ref.at[fs, :, cols(lax.rem(c + C - j, C))]
            n = 1 + (k - 1) * C + j
            cross.append(send(piece, piece, cs.at[n], cr.at[n], peers[-1]))
    for copy in along + plane:
        copy.wait_send()
    whole.wait_send()
    whole.wait_recv()
    for copy in cross:
        copy.wait_send()
        copy.wait_recv()
    own.wait()


def gather_all(x, Z, C):
    R, W = x.shape
    dma = pltpu.SemaphoreType.DMA
    n, m = (Z - 1) * (C - 1), 1 + (Z - 1) * C
    return pl.pallas_call(functools.partial(gather_kernel, Z=Z, C=C, quarter=W // C),
        out_shape=jax.ShapeDtypeStruct((2 * Z, R, W), bf16),
        in_specs=[pl.BlockSpec(memory_space=pl.ANY)],
        out_specs=pl.BlockSpec(memory_space=pl.ANY),
        scratch_shapes=[dma(()), dma((Z - 1,)), dma((Z - 1,)), dma((n,)), dma((n,)), dma((m,)), dma((m,))],
        compiler_params=pltpu.CompilerParams(collective_id=0, has_side_effects=True, vmem_limit_bytes=56 << 20),
        cost_estimate=pl.CostEstimate(flops=0, bytes_accessed=20 * R * W * Z, transcendentals=0),
    )(x)


HEADS = 17
EPSILON = 1e-05
FS = ("zz", "core")


def norm_parts(v):
    mean = jnp.mean(v, axis=-1, keepdims=True)
    c = v - mean
    r = lax.rsqrt(jnp.mean(c * c, axis=-1, keepdims=True) + EPSILON)
    return c * r, r


def norm_back(dn, v, gain):
    xhat, r = norm_parts(v)
    y = dn * gain
    a = jnp.mean(y, axis=-1, keepdims=True)
    b = jnp.mean(y * xhat, axis=-1, keepdims=True)
    return r * (y - a - xhat * b), jnp.sum(dn * xhat, axis=0), jnp.sum(dn, axis=0)


def col_sum(x):
    return jnp.dot(jnp.ones((16, x.shape[0]), bf16), x, preferred_element_type=f32)[0]


def gelu_parts(u):
    z = jnp.abs(u) * 0.7071067811865476
    t = 1.0 / (1.0 + 0.3275911 * z)
    e = jnp.exp(-z * z)
    poly = t * (0.254829592 + t * (-0.284496736 + t * (1.421413741 + t * (-1.453152027 + t * 1.061405429))))
    half = 0.5 * poly * e
    cdf = jnp.where(u >= 0, 1.0 - half, half)
    return u * cdf, cdf + u * e * 0.3989422804014327


def local(
    tokens, cotangent, lengths, block_order,
    ln1_gain, ln1_bias, qkv_weight, q_bias, v_bias, out_weight, out_bias,
    ln2_gain, ln2_bias, up_weight, up_bias, down_weight, down_bias,
    *, G, S,
):
    slots, rows, width = tokens.shape
    C = lax.axis_size("ctx")
    me = lax.axis_index("ctx")
    N = rows * C
    B = rows // 2
    NB = 2 * C
    L = ln1_gain.shape[0]
    shard = ln1_gain.shape[1]
    HW = G * 128
    x_tokens = tokens[0]

    steps = jnp.arange(NB, dtype=jnp.int32)
    order = block_order[0]
    inverse = jnp.sum(jnp.where(order[None, :] == steps[:, None], steps[None, :], 0), axis=1).astype(jnp.int32)
    count = (lengths + (B - 1)) // B
    meta = jnp.concatenate([inverse, count])
    def swap(x):
        return lax.ppermute(x, "core", [(0, 1), (1, 0)])

    metas = [meta, swap(meta)][:S]
    phase_inv = [t[None, :NB] for t in metas]
    phase_nb = [t[NB:] for t in metas]
    own = jnp.concatenate([inverse, lax.dynamic_slice_in_dim(order, 2 * me, 2, 0), count])
    own_pos = (lax.dynamic_slice_in_dim(order, 2 * me, 2, 0)[:, None] * B + jnp.arange(B, dtype=jnp.int32)).reshape(rows, 1)
    live = (own_pos < lengths[0]).astype(f32)

    def pack(w):
        parts = []
        for g in range(G):
            parts += [w[:, kind * width + g * 128:kind * width + g * 128 + 128] for kind in range(3)]
        last = width - 64
        parts += [w[:, kind * width + last:kind * width + width] for kind in (1, 2, 0)]
        return jnp.concatenate(parts, axis=1)

    def unpack(w):
        tail = G * 384
        parts = []
        for kind, last in enumerate((128, 0, 64)):
            parts += [w[:, g * 384 + kind * 128:g * 384 + kind * 128 + 128] for g in range(G)]
            parts.append(w[:, tail + last:tail + last + 64])
        return jnp.concatenate(parts, axis=1)

    def fetch(w):
        return lax.all_gather(w.astype(bf16), FS, axis=0, tiled=True)

    vectors = [ln1_gain, ln1_bias, q_bias, v_bias, out_bias, ln2_gain, ln2_bias, down_bias]
    vec = [t.astype(bf16).T for t in vectors] + [up_bias.astype(bf16).reshape(4 * L, shard).T]
    first = pack(qkv_weight[0].astype(bf16))
    block = jnp.concatenate([first] + vec, axis=1)
    used = block.shape[1]
    if C == 4 and lax.axis_size("zz") == 4:
        block = jnp.pad(block, ((0, 0), (0, -used % (128 * C))))
        block = gather_all(block, 4, C)
    else:
        block = lax.all_gather(block, FS)
    first_w = block[:, :, :3 * width].reshape(width, 3 * width)
    vec = jnp.transpose(block[:, :, 3 * width:used].reshape(width, used - 3 * width)).astype(f32)

    def vector(index, layer):
        if index < 8:
            return vec[L * index + layer]
        t = vec[8 * L + 4 * layer:8 * L + 4 * layer + 4]
        return jnp.transpose(t.reshape(4, -1, shard), (1, 0, 2)).reshape(-1)

    weights = []
    for layer in range(L):
        weights.append((
            fetch(pack(qkv_weight[layer].astype(bf16))) if layer else first_w,
            fetch(out_weight[layer]),
            fetch(up_weight[layer]),
            fetch(down_weight[layer]),
        ))

    def plain(x):
        return with_layout_constraint(x, Layout(major_to_minor=tuple(range(x.ndim))))

    def exchange(x):
        return plain(lax.all_to_all(plain(x), "ctx", 0, 0))

    def after(x, *others):
        return lax.optimization_barrier((x,) + others)

    stream = x_tokens.astype(f32)
    records = []
    for layer in range(L):
        qkv_w, out_w, up_w, down_w = weights[layer]
        xhat, _ = norm_parts(stream)
        n1 = (xhat * vector(0, layer) + vector(1, layer)).astype(bf16)
        q_b, v_b = vector(2, layer), vector(3, layer)
        bias = pack(jnp.concatenate([q_b, jnp.zeros_like(q_b), v_b])[None])[0]
        projected = (jnp.dot(n1, qkv_w, preferred_element_type=f32) + bias).astype(bf16)
        wide = [deal(projected, s * C, C, 384) for s in range(S)]
        tail = projected[:, G * 384:]
        if S == 2:
            wide[1] = swap(wide[1])
        kv16 = jnp.broadcast_to(tail[None, :, :128], (C, rows, 128))
        q16 = tail[:, 128:]
        heads, o, lse, o_back = [], [], [], []
        for s in range(S):
            t = wide[s]
            if s == S - 1:
                t = jnp.concatenate([t, kv16], axis=2)
            if s:
                t, heads[0] = after(t, heads[0])
            heads.append(exchange(t).reshape(1, N, -1))
        for s in range(S):
            o_s, lse_s = flash_fwd(heads[s], phase_inv[s], phase_nb[s], B)
            o.append(o_s)
            lse.append(lse_s)
            t = o_s.reshape(C, rows, 128)
            if s:
                t, o_back[0] = after(t, o_back[0])
            o_back.append(exchange(swap(t) if s else t))
        o16, lse16 = one_fwd(q16, heads[-1][0], own, B)
        mixed = join(o_back, o16)
        m = stream + jnp.dot(mixed, out_w, preferred_element_type=f32) + vector(4, layer)
        xhat2, _ = norm_parts(m)
        n2 = (xhat2 * vector(5, layer) + vector(6, layer)).astype(bf16)
        u = jnp.dot(n2, up_w, preferred_element_type=f32) + vector(8, layer)
        a, slope = gelu_parts(u)
        a = a.astype(bf16)
        a, slope = after(a, slope.astype(bf16))
        records.append((stream, n1, heads, q16, o, lse, o16, lse16, mixed, m, n2, a, slope))
        stream = m + jnp.dot(a, down_w, preferred_element_type=f32) + vector(7, layer)
    activations = (stream * live).astype(bf16)[None]

    def reduce_fsdp(g):
        return lax.psum_scatter(g.astype(bf16), FS, scatter_dimension=0, tiled=True)

    def reduce_ctx(g):
        return lax.psum(g, "ctx").astype(f32)

    grad = cotangent[0].astype(f32) * live
    matrices = [None] * L
    fours = [None] * L
    ffns = [None] * L
    small = [None] * L

    def ctx_end(mine):
        return exchange(jnp.broadcast_to(mine[None], (C,) + mine.shape))

    def ctx_sum(shards):
        mine, sizes = ctx_begin(shards)
        return ctx_end(mine), sizes

    def ctx_begin(shards):
        pieces = []
        for t in shards:
            if t.shape[1] == width:
                pieces.append(t.reshape(C, -1, width))
            else:
                pieces.append(jnp.transpose(t.reshape(t.shape[0], C, -1), (1, 0, 2)).reshape(C, -1, width))
        sizes = [t.shape[1] for t in pieces]
        parts = exchange(jnp.concatenate(pieces, axis=1))
        mine = jnp.sum(parts.astype(f32), axis=0).astype(bf16)
        return mine, sizes

    def spread(summed, shapes):
        whole, sizes = summed
        out, at = [], 0
        for n, (r, c) in zip(sizes, shapes):
            t = whole[:, at:at + n].astype(f32)
            at += n
            if c == width:
                out.append(t.reshape(r, c))
            else:
                out.append(jnp.transpose(t.reshape(C, r, c // C), (1, 0, 2)).reshape(r, c))
        return out

    wide_shape, tall_shape = (shard, 4 * width), (4 * shard, width)
    for layer in reversed(range(L)):
        stream_in, n1, heads, q16, o, lse, o16, lse16, mixed, m, n2, a, slope = records[layer]
        qkv_w, out_w, up_w, down_w = weights[layer]
        gb = grad.astype(bf16)
        d_down_b = col_sum(gb)
        d_down = jnp.einsum("rf,rd->fd", a, gb, preferred_element_type=f32).astype(bf16)
        gb, d_down = after(gb, plain(d_down))
        if layer < L - 1:
            above = list(after(gb, *ffns[layer + 1]))
            gb = above.pop(0)
            mine_ffn, ffn_sizes = ctx_begin(above)
        d_down = reduce_fsdp(d_down)
        du = (jnp.einsum("rd,fd->rf", gb, down_w, preferred_element_type=f32) * slope.astype(f32)).astype(bf16)
        d_up_b = col_sum(du)
        if layer < L - 1:
            du, mine_ffn = after(du, mine_ffn)
            ffn_whole = ctx_end(mine_ffn)
        d_up = jnp.einsum("rd,rf->df", n2, du, preferred_element_type=f32).astype(bf16)
        du, d_up = after(du, plain(d_up))
        d_up = reduce_fsdp(d_up)
        dn2 = jnp.einsum("rf,df->rd", du, up_w, preferred_element_type=f32)
        back, d_gain2, d_bias2 = norm_back(dn2, m, vector(5, layer))
        gm = grad + back
        gmb = gm.astype(bf16)
        d_out_b = col_sum(gmb)
        d_out = jnp.einsum("rd,re->de", mixed, gmb, preferred_element_type=f32).astype(bf16)
        if layer == 0:
            gmb, d_out = after(gmb, plain(d_out))
        if layer < L - 1:
            gmb, ffn_whole = after(gmb, ffn_whole)
        d_o = []
        for s in range(S):
            w = out_w[C * 128 * s:C * 128 * (s + 1)].reshape(C, 128, width)
            d_o.append(jnp.einsum("re,gce->grc", gmb, w, preferred_element_type=f32).astype(bf16))
        d_o16 = jnp.einsum("re,ce->rc", gmb, out_w[HW:], preferred_element_type=f32).astype(bf16)
        dq16, dkv16 = one_bwd(q16, heads[-1][0], o16, d_o16, lse16, own, B)
        d_oh, d_wide = [], []
        for s in range(S):
            t = d_o[s]
            if s:
                t = swap(t)
            if s == S - 1:
                t = jnp.concatenate([t, dkv16.reshape(C, rows, 128)], axis=2)
            if s:
                t, d_oh[0] = after(t, d_oh[0])
            if s == S - 1 and layer < L - 1:
                t, fours[layer + 1] = after(t, fours[layer + 1])
            d_oh.append(exchange(t).reshape(1, N, -1))
        dkv16 = jnp.sum(d_oh[-1].reshape(C, rows, 256)[:, :, 128:].astype(f32), axis=0)
        for s in range(S):
            t = flash_bwd(heads[s], o[s], d_oh[s], lse[s], phase_inv[s], phase_nb[s], B)
            t = t.reshape(C, rows, 384)
            if s:
                t, d_wide[0] = after(t, d_wide[0])
            if s == S - 1:
                t, d_down = after(t, d_down)
            if s == S - 1 and layer:
                t, d_up = after(t, d_up)
            d_wide.append(exchange(swap(t) if s else t))
        d_tail = jnp.concatenate([dkv16.astype(bf16), dq16], axis=1)
        d_row = join(d_wide, d_tail)
        d_back = d_row
        if layer == 0:
            d_row, d_up = after(d_row, d_up)
            mine, middle_sizes = ctx_begin([fours[1], d_up, d_down])
            d_back, mine = after(d_row, mine)
        d_qkv = jnp.einsum("rd,rc->dc", n1, d_row, preferred_element_type=f32).astype(bf16)
        if layer:
            d_row, d_four = after(d_row, plain(jnp.concatenate([d_qkv, d_out], axis=1)))
            d_four = reduce_fsdp(d_four)
        else:
            d_qkv, d_out = after(d_qkv, reduce_fsdp(d_out))
            d_four = jnp.concatenate([reduce_fsdp(d_qkv), d_out], axis=1)
        sums = unpack(col_sum(d_row)[None])[0]
        dn1 = jnp.einsum("rc,dc->rd", d_back, qkv_w, preferred_element_type=f32)
        back, d_gain1, d_bias1 = norm_back(dn1, stream_in, vector(0, layer))
        grad = gm + back
        fours[layer] = d_four
        ffns[layer] = (d_up, d_down)
        small[layer] = jnp.concatenate([
            t.reshape(-1, n) for t, n in (
                (d_gain1, shard), (d_bias1, shard), (sums[:width], shard), (sums[2 * width:], shard), (d_out_b, shard),
                (d_gain2, shard), (d_bias2, shard), (d_down_b, shard), (d_up_b, 4 * shard))], axis=1)

    vec_grads = jnp.stack(small, axis=1)
    vec_grads, activations = after(vec_grads, activations)
    vec_grads = jnp.sum(lax.all_to_all(vec_grads, FS, 0, 0), axis=0)
    vec_grads = jnp.sum(lax.all_to_all(jnp.broadcast_to(vec_grads[None], (C,) + vec_grads.shape), "ctx", 0, 0), axis=0)
    end, vec_grads = after(fours[0], vec_grads)
    mine_last, last_sizes = ctx_begin([end])
    whole = ctx_end(jnp.concatenate([mine, mine_last], axis=0))
    rest = spread((whole, middle_sizes + last_sizes), [wide_shape, wide_shape, tall_shape, wide_shape])
    matrices[1] = [rest[0]] + spread((ffn_whole, ffn_sizes), [wide_shape, tall_shape])
    matrices[0] = [rest[3], rest[1], rest[2]]
    vg = [vec_grads[:, i * shard:(i + 1) * shard] for i in range(8)] + [vec_grads[:, 8 * shard:]]

    g_qkv = jnp.stack([unpack(matrices[layer][0][:, :3 * width]) for layer in range(L)])
    g_out = jnp.stack([matrices[layer][0][:, 3 * width:] for layer in range(L)])
    g_up = jnp.stack([matrices[layer][1] for layer in range(L)])
    g_down = jnp.stack([matrices[layer][2] for layer in range(L)])
    return (activations, grad[None], vg[0], vg[1], g_qkv, vg[2], vg[3], g_out, vg[4], vg[5], vg[6], g_up, vg[8], g_down, vg[7])


def solution(mesh):
    F, C = mesh.devices.shape
    inner = Mesh(mesh.devices.reshape(F // 2, 2, C), ("zz", "core", "ctx"))
    S = 2 if 16 // (2 * C) >= 2 else 1
    G = S * C
    rows = P(FS, "ctx", None)
    vec, mat = P(None, FS), P(None, FS, None)
    return jax.shard_map(
        functools.partial(local, G=G, S=S),
        mesh=inner,
        in_specs=(rows, rows, P(FS), P(FS, None), vec, vec, mat, vec, vec, mat, vec, vec, vec, mat, vec, mat, vec),
        out_specs=(rows, rows, vec, vec, mat, vec, vec, mat, vec, vec, vec, mat, vec, mat, vec),
        check_vma=False,
    )
```

```python
import functools
import jax, jax.numpy as jnp
from jax import lax
from jax.experimental import pallas as pl
from jax.experimental.pallas import tpu as pltpu
from jax.experimental.layout import Layout, with_layout_constraint
from jax.sharding import Mesh, PartitionSpec as P
f32=jnp.float32; bf16=jnp.bfloat16
NEG=-1e30
def dot_nt(a,b): return lax.dot_general(a,b,(((1,),(1,)),((),())),preferred_element_type=f32)
def dot_nn(a,b): return lax.dot_general(a,b,(((1,),(0,)),((),())),preferred_element_type=f32)

LOG2E=1.4426950408889634
def split(q,h,low):
    qs=q.astype(f32)*(0.125*LOG2E)
    hi=qs.astype(bf16).astype(f32); lo=qs-hi
    rl=pltpu.roll(lo,64,1)
    c=jnp.where(low,hi,rl) if h==0 else jnp.where(low,rl,hi)
    return c.astype(bf16)
def dup(k,h,low):
    kf=k.astype(f32); rl=pltpu.roll(kf,64,1)
    c=jnp.where(low,kf,rl) if h==0 else jnp.where(low,rl,kf)
    return c.astype(bf16)
def fwd_kernel(inv_ref, nb_ref, x_ref, o_ref, lse_ref, vt, kd, sb, acc, *, B, NB):
    s=pl.program_id(0)
    nb=nb_ref[s]
    lane=lax.broadcasted_iota(jnp.int32,(1,128),1)
    low=lane<64
    def tv(j,_):
        r=pl.multiple_of(inv_ref[s,j]*B,B)
        w=pl.multiple_of(j*B,B)
        t=x_ref[0,pl.ds(r,B),256:384].T
        one=(lax.broadcasted_iota(jnp.int32,(16,B),0)==0).astype(bf16)
        for h in range(2):
            vt[80*h:80*h+64,pl.ds(w,B)]=t[64*h:64*h+64,:]
            vt[80*h+64:80*h+80,pl.ds(w,B)]=one
            kd[h,pl.ds(w,B),:]=dup(x_ref[0,pl.ds(r,B),128:256],h,low)
        return 0
    lax.fori_loop(0,nb,tv,0)
    rr=lax.broadcasted_iota(jnp.int32,(B,B),0)
    cc=lax.broadcasted_iota(jnp.int32,(B,B),1)
    def qblock(i,_):
        r=pl.multiple_of(inv_ref[s,i]*B,B)
        q=x_ref[0,pl.ds(r,B),0:128]
        qh=[split(q,h,low) for h in range(2)]
        acc[...]=jnp.zeros_like(acc)
        def scores(j,slot):
            for h in range(2):
                sb[slot,h]=dot_nt(kd[h,pl.ds(pl.multiple_of(j*B,B),B),:],qh[h])
        def step(j,carry,diag):
            out=[]
            for h in range(2):
                m=carry[h]
                st=sb[j%2,h]
                if diag: st=jnp.where(rr<=cc,st,NEG)
                mn=jnp.maximum(m,jnp.max(st,axis=0,keepdims=True))
                p=jnp.exp2(st-mn)
                al=jnp.exp2(m-mn)
                v=vt[80*h:80*h+80,pl.ds(pl.multiple_of(j*B,B),B)]
                acc[h]=acc[h]*al+dot_nn(v,p.astype(bf16))
                out.append(mn)
            return tuple(out)
        scores(0,0)
        def both(j,c):
            scores(j+1,(j+1)%2)
            return step(j,c,False)
        n=jnp.full((1,B),NEG,f32)
        c=lax.fori_loop(0,i,both,(n,n))
        c=step(i,c,True)
        os=[]
        for h in range(2):
            l=acc[h,64:65,:]
            os.append(acc[h,0:64,:]*(1.0/l))
            lse_ref[0,pl.ds(h,1),pl.ds(r,B)]=c[h]+jnp.log2(l)
        o_ref[0,pl.ds(r,B),:]=jnp.concatenate(os,0).T.astype(bf16)
        return 0
    lax.fori_loop(0,nb,qblock,0)
    def pad(i,_):
        r=pl.multiple_of(inv_ref[s,i]*B,B)
        o_ref[0,pl.ds(r,B),:]=jnp.zeros((B,128),bf16)
        lse_ref[0,:,pl.ds(r,B)]=jnp.zeros((8,B),f32)
        return 0
    lax.fori_loop(nb,NB,pad,0)

def flash_fwd(x,inv,nb,B):
    S,N,_=x.shape
    NB=N//B
    return pl.pallas_call(functools.partial(fwd_kernel,B=B,NB=NB),
      out_shape=(jax.ShapeDtypeStruct((S,N,128),bf16),jax.ShapeDtypeStruct((S,8,N),f32)),
      grid_spec=pltpu.PrefetchScalarGridSpec(num_scalar_prefetch=2,grid=(S,),
        in_specs=[pl.BlockSpec((1,N,384),lambda s,*_:(s,0,0))],
        out_specs=[pl.BlockSpec((1,N,128),lambda s,*_:(s,0,0)),pl.BlockSpec((1,8,N),lambda s,*_:(s,0,0))],
        scratch_shapes=[pltpu.VMEM((160,N),bf16),pltpu.VMEM((2,N,128),bf16),pltpu.VMEM((2,2,B,B),f32),pltpu.VMEM((2,80,B),f32)]),
      compiler_params=pltpu.CompilerParams(vmem_limit_bytes=48<<20),
      cost_estimate=pl.CostEstimate(flops=S*4*N*N*128,bytes_accessed=S*N*1024,transcendentals=S*N*N),
      )(inv,nb,x)

def bwd_kernel(inv_ref, nb_ref, x_ref, o_ref, do_ref, lse_ref, dx_ref, kt, qd, dq, dk, dv, dl, *, B, NB):
    s=pl.program_id(0)
    nb=nb_ref[s]
    lane=lax.broadcasted_iota(jnp.int32,(1,128),1)
    low=lane<64
    hm=(lax.broadcasted_iota(jnp.int32,(8,128),1)//64==lax.broadcasted_iota(jnp.int32,(8,128),0)).astype(bf16)
    def prep(j,_):
        r=pl.multiple_of(inv_ref[s,j]*B,B)
        w=pl.multiple_of(j*B,B)
        kt[:,pl.ds(w,B)]=x_ref[0,pl.ds(r,B),128:256].T
        for h in range(2): qd[h,pl.ds(w,B),:]=split(x_ref[0,pl.ds(r,B),0:128],h,low)
        prod=o_ref[0,pl.ds(r,B),:].astype(f32)*do_ref[0,pl.ds(r,B),:].astype(f32)
        hi=prod.astype(bf16); lo=(prod-hi.astype(f32)).astype(bf16)
        dl[:,pl.ds(w,B)]=dot_nt(hm,hi)+dot_nt(hm,lo)
        dq[:,pl.ds(w,B)]=jnp.zeros((128,B),f32)
        return 0
    lax.fori_loop(0,nb,prep,0)
    rr=lax.broadcasted_iota(jnp.int32,(B,B),0)
    cc=lax.broadcasted_iota(jnp.int32,(B,B),1)
    def kblock(j,_):
        r=pl.multiple_of(inv_ref[s,j]*B,B)
        k=x_ref[0,pl.ds(r,B),128:256]
        v=x_ref[0,pl.ds(r,B),256:384]
        kdh=[dup(k,h,low) for h in range(2)]
        dk[...]=jnp.zeros_like(dk); dv[...]=jnp.zeros_like(dv)
        def step(i,diag):
            ri=pl.multiple_of(inv_ref[s,i]*B,B)
            wi=pl.multiple_of(i*B,B)
            q=x_ref[0,pl.ds(ri,B),0:128]*jnp.asarray(0.125,bf16)
            do=do_ref[0,pl.ds(ri,B),:]
            zero=jnp.zeros_like(q)
            dvs=[];dks=[]
            for h in range(2):
                qh=jnp.where(low,q,zero) if h==0 else jnp.where(low,zero,q)
                doh=jnp.where(low,do,zero) if h==0 else jnp.where(low,zero,do)
                st=dot_nt(kdh[h],qd[h,pl.ds(wi,B),:])
                p=jnp.exp2(st-lse_ref[0,pl.ds(h,1),pl.ds(ri,B)])
                if diag: p=jnp.where(rr<=cc,p,0.0)
                dvs.append(dot_nn(p.astype(bf16),doh))
                dp=dot_nt(v,doh)
                ds=(p*(dp-dl[pl.ds(h,1),pl.ds(wi,B)])).astype(bf16)
                dks.append(dot_nn(ds,qh))
                kh=kt[64*h:64*h+64,pl.ds(pl.multiple_of(j*B,B),B)]
                dq[64*h:64*h+64,pl.ds(wi,B)]+=dot_nn(kh,ds)
            dv[...]+=dvs[0]+dvs[1]
            dk[...]+=dks[0]+dks[1]
        step(j,True)
        def body(i,_):
            step(i,False); return 0
        lax.fori_loop(j+1,nb,body,0)
        dx_ref[0,pl.ds(r,B),128:256]=dk[...].astype(bf16)
        dx_ref[0,pl.ds(r,B),256:384]=dv[...].astype(bf16)
        return 0
    lax.fori_loop(0,nb,kblock,0)
    def fin(i,_):
        r=pl.multiple_of(inv_ref[s,i]*B,B)
        dx_ref[0,pl.ds(r,B),0:128]=(dq[:,pl.ds(pl.multiple_of(i*B,B),B)].T*0.125).astype(bf16)
        return 0
    lax.fori_loop(0,nb,fin,0)
    def pad(i,_):
        r=pl.multiple_of(inv_ref[s,i]*B,B)
        dx_ref[0,pl.ds(r,B),:]=jnp.zeros((B,384),bf16)
        return 0
    lax.fori_loop(nb,NB,pad,0)

def flash_bwd(x,o,do,lse,inv,nb,B):
    S,N,_=x.shape
    NB=N//B
    return pl.pallas_call(functools.partial(bwd_kernel,B=B,NB=NB),
      out_shape=jax.ShapeDtypeStruct((S,N,384),bf16),
      grid_spec=pltpu.PrefetchScalarGridSpec(num_scalar_prefetch=2,grid=(S,),
        in_specs=[pl.BlockSpec((1,N,384),lambda s,*_:(s,0,0)),pl.BlockSpec((1,N,128),lambda s,*_:(s,0,0)),
                  pl.BlockSpec((1,N,128),lambda s,*_:(s,0,0)),pl.BlockSpec((1,8,N),lambda s,*_:(s,0,0))],
        out_specs=pl.BlockSpec((1,N,384),lambda s,*_:(s,0,0)),
        scratch_shapes=[pltpu.VMEM((128,N),bf16),pltpu.VMEM((2,N,128),bf16),pltpu.VMEM((128,N),f32),pltpu.VMEM((B,128),f32),pltpu.VMEM((B,128),f32),pltpu.VMEM((8,N),f32)]),
      compiler_params=pltpu.CompilerParams(vmem_limit_bytes=48<<20),
      cost_estimate=pl.CostEstimate(flops=S*10*N*N*128,bytes_accessed=S*N*2400,transcendentals=S*N*N),
      )(inv,nb,x,o,do,lse)


def one_fwd_kernel(own_ref, q_ref, x_ref, o_ref, lse_ref, vt, kd, acc, *, B, NB):
    nb = own_ref[NB + 2]
    low = lax.broadcasted_iota(jnp.int32,(1,128),1)<64
    def tv(j,_):
        r=pl.multiple_of(own_ref[j]*B,B)
        t=x_ref[pl.ds(r,B),:].T
        w=pl.multiple_of(j*B,B)
        kd[pl.ds(w,B),:]=dup(x_ref[pl.ds(r,B),:],0,low)
        vt[0:64,pl.ds(w,B)]=t[64:128,:]
        vt[64:80,pl.ds(w,B)]=(lax.broadcasted_iota(jnp.int32,(16,B),0)==0).astype(bf16)
        return 0
    lax.fori_loop(0,nb,tv,0)
    rr=lax.broadcasted_iota(jnp.int32,(B,B),0)
    cc=lax.broadcasted_iota(jnp.int32,(B,B),1)
    for t in range(2):
        i=own_ref[NB+t]
        @pl.when(i>=nb)
        def _():
            o_ref[t*B:(t+1)*B,:]=jnp.zeros((B,64),bf16)
            lse_ref[:,t*B:(t+1)*B]=jnp.zeros((8,B),f32)
        @pl.when(i<nb)
        def _():
            qs=q_ref[t*B:(t+1)*B,:].astype(f32)*(0.125*LOG2E)
            hi=qs.astype(bf16)
            q=jnp.concatenate([hi.astype(f32),qs-hi.astype(f32)],axis=1).astype(bf16)
            acc[...]=jnp.zeros_like(acc)
            def step(j,m,diag):
                st=dot_nt(kd[pl.ds(pl.multiple_of(j*B,B),B),:],q)
                if diag: st=jnp.where(rr<=cc,st,NEG)
                mn=jnp.maximum(m,jnp.max(st,axis=0,keepdims=True))
                p=jnp.exp2(st-mn)
                al=jnp.exp2(m-mn)
                v=vt[:,pl.ds(pl.multiple_of(j*B,B),B)]
                acc[...]=acc[...]*al+dot_nn(v,p.astype(bf16))
                return mn
            m=lax.fori_loop(0,i,lambda j,m: step(j,m,False),jnp.full((1,B),NEG,f32))
            m=step(i,m,True)
            l=acc[64:65,:]
            o_ref[t*B:(t+1)*B,:]=(acc[0:64,:]*(1.0/l)).T.astype(bf16)
            lse_ref[:,t*B:(t+1)*B]=jnp.broadcast_to(m+jnp.log2(l),(8,B))


def one_fwd(q,x,own,B):
    N=x.shape[0]; R=q.shape[0]; NB=N//B
    full=lambda *_:(0,0)
    last=lambda *_:(0,3)
    return pl.pallas_call(functools.partial(one_fwd_kernel,B=B,NB=NB),
      out_shape=(jax.ShapeDtypeStruct((R,64),bf16),jax.ShapeDtypeStruct((8,R),f32)),
      grid_spec=pltpu.PrefetchScalarGridSpec(num_scalar_prefetch=1,grid=(1,),
        in_specs=[pl.BlockSpec((R,64),full),pl.BlockSpec((N,128),last)],
        out_specs=[pl.BlockSpec((R,64),full),pl.BlockSpec((8,R),full)],
        scratch_shapes=[pltpu.VMEM((80,N),bf16),pltpu.VMEM((N,128),bf16),pltpu.VMEM((80,B),f32)]),
      compiler_params=pltpu.CompilerParams(vmem_limit_bytes=48<<20),
      cost_estimate=pl.CostEstimate(flops=4*R*N*128,bytes_accessed=N*256+R*512,transcendentals=R*N),
      )(own,q,x)


def one_bwd_kernel(own_ref, q_ref, x_ref, o_ref, do_ref, lse_ref, dq_ref, dx_ref, dkv, dq, *, B, NB):
    nb = own_ref[NB + 2]
    low = lax.broadcasted_iota(jnp.int32,(1,128),1)<64
    rr=lax.broadcasted_iota(jnp.int32,(B,B),0)
    cc=lax.broadcasted_iota(jnp.int32,(B,B),1)
    ones=jnp.ones((8,64),bf16)
    dkv[...]=jnp.zeros_like(dkv)
    for t in range(2):
        i=own_ref[NB+t]
        sl=slice(t*B,(t+1)*B)
        @pl.when(i>=nb)
        def _():
            dq_ref[sl,:]=jnp.zeros((B,64),bf16)
        @pl.when(i<nb)
        def _():
            qr=q_ref[sl,:]
            qs=qr.astype(f32)*(0.125*LOG2E)
            hi=qs.astype(bf16)
            q=jnp.concatenate([hi.astype(f32),qs-hi.astype(f32)],axis=1).astype(bf16)
            qd=qr*jnp.asarray(0.125,bf16)
            do=do_ref[sl,:]
            prod=o_ref[sl,:].astype(f32)*do.astype(f32)
            hi=prod.astype(bf16); lo=(prod-hi.astype(f32)).astype(bf16)
            dl=(dot_nt(ones,hi)+dot_nt(ones,lo))[0:1,:]
            lse=lse_ref[0:1,sl]
            dq[...]=jnp.zeros_like(dq)
            def step(j,diag):
                r=pl.multiple_of(own_ref[j]*B,B)
                k=x_ref[pl.ds(r,B),0:64]
                v=x_ref[pl.ds(r,B),64:128]
                st=dot_nt(dup(x_ref[pl.ds(r,B),:],0,low),q)
                p=jnp.exp2(st-lse)
                if diag: p=jnp.where(rr<=cc,p,0.0)
                dp=dot_nt(v,do)
                ds=(p*(dp-dl)).astype(bf16)
                dkv[pl.ds(r,B),64:128]+=dot_nn(p.astype(bf16),do)
                dkv[pl.ds(r,B),0:64]+=dot_nn(ds,qd)
                dq[...]+=dot_nn(k.T,ds)
            def body(j,_):
                step(j,False); return 0
            lax.fori_loop(0,i,body,0)
            step(i,True)
            dq_ref[sl,:]=(dq[...].T*0.125).astype(bf16)
    dx_ref[...]=dkv[...].astype(bf16)


def one_bwd(q,x,o,do,lse,own,B):
    N=x.shape[0]; R=q.shape[0]; NB=N//B
    full=lambda *_:(0,0)
    last=lambda *_:(0,3)
    return pl.pallas_call(functools.partial(one_bwd_kernel,B=B,NB=NB),
      out_shape=(jax.ShapeDtypeStruct((R,64),bf16),jax.ShapeDtypeStruct((N,128),bf16)),
      grid_spec=pltpu.PrefetchScalarGridSpec(num_scalar_prefetch=1,grid=(1,),
        in_specs=[pl.BlockSpec((R,64),full),pl.BlockSpec((N,128),last),pl.BlockSpec((R,64),full),pl.BlockSpec((R,64),full),pl.BlockSpec((8,R),full)],
        out_specs=[pl.BlockSpec((R,64),full),pl.BlockSpec((N,128),full)],
        scratch_shapes=[pltpu.VMEM((N,128),f32),pltpu.VMEM((64,B),f32)]),
      compiler_params=pltpu.CompilerParams(vmem_limit_bytes=48<<20),
      cost_estimate=pl.CostEstimate(flops=10*R*N*128,bytes_accessed=N*512+R*1024,transcendentals=R*N),
      )(own,q,x,o,do,lse)


def join_kernel(*refs, count):
    t = pl.program_id(0)
    stacks, tail, out = refs[:-2], refs[-2], refs[-1]
    for i, ref in enumerate(stacks):
        @pl.when((t >= i * count) & (t < (i + 1) * count))
        def _(ref=ref):
            out[...] = ref[0]

    @pl.when(t >= len(stacks) * count)
    def _():
        out[:, :tail.shape[1]] = tail[...]


def join(stacks, tail):
    C, R, W = stacks[0].shape
    n = len(stacks)
    T = tail.shape[1]

    def at(i):
        return lambda t: (jnp.clip(t - i * C, 0, C - 1), 0, 0)
    return pl.pallas_call(functools.partial(join_kernel, count=C),
        out_shape=jax.ShapeDtypeStruct((R, n * C * W + T), bf16),
        grid=(n * C + 1,),
        in_specs=[pl.BlockSpec((1, R, W), at(i)) for i in range(n)] + [pl.BlockSpec((R, T), lambda t: (0, 0))],
        out_specs=pl.BlockSpec((R, W), lambda t: (0, t)),
        compiler_params=pltpu.CompilerParams(vmem_limit_bytes=56 << 20),
        cost_estimate=pl.CostEstimate(flops=0, bytes_accessed=4 * R * (n * C * W + T), transcendentals=0),
    )(*stacks, tail)


def deal_kernel(x_ref, o_ref):
    o_ref[0] = x_ref[...]


def deal(x, first, C, W):
    R = x.shape[0]
    return pl.pallas_call(deal_kernel,
        out_shape=jax.ShapeDtypeStruct((C, R, W), bf16),
        grid=(C,),
        in_specs=[pl.BlockSpec((R, W), lambda t: (0, first + t))],
        out_specs=pl.BlockSpec((1, R, W), lambda t: (t, 0, 0)),
        compiler_params=pltpu.CompilerParams(vmem_limit_bytes=56 << 20),
        cost_estimate=pl.CostEstimate(flops=0, bytes_accessed=4 * R * C * W, transcendentals=0),
    )(x)


def gather_kernel(x_ref, o_ref, own_sem, zs, zr, xs, xr, cs, cr, *, Z, C, quarter):
    z, a, c = lax.axis_index("zz"), lax.axis_index("core"), lax.axis_index("ctx")
    mesh_id = pl.DeviceIdType.MESH
    other = 1 - a
    peers = [(lax.rem(z + k, Z), a, c) for k in range(1, Z)] + [(z, a, lax.rem(c + j, C)) for j in range(1, C)] + [(z, other, c)]
    barrier = pltpu.get_barrier_semaphore()
    for peer in peers:
        pl.semaphore_signal(barrier, inc=1, device_id=peer, device_id_type=mesh_id)
    pl.semaphore_wait(barrier, len(peers))

    f = 2 * z + a

    def cols(q):
        return pl.ds(pl.multiple_of(q * quarter, quarter), quarter)

    def send(src, dst, s, r, peer):
        copy = pltpu.make_async_remote_copy(src_ref=src, dst_ref=dst, send_sem=s, recv_sem=r, device_id=peer, device_id_type=mesh_id)
        copy.start()
        return copy

    along = []
    for k in range(1, Z):
        along.append(send(x_ref.at[:, cols(c)], o_ref.at[f, :, cols(c)], zs.at[k - 1], zr.at[k - 1], peers[k - 1]))
    own = pltpu.make_async_copy(x_ref, o_ref.at[f], own_sem)
    own.start()
    whole = send(x_ref, o_ref.at[f], cs.at[0], cr.at[0], peers[-1])
    plane, cross = [], []
    for k in range(1, Z):
        along[k - 1].wait_recv()
        fs = 2 * lax.rem(z + Z - k, Z) + a
        piece = o_ref.at[fs, :, cols(c)]
        for j in range(1, C):
            n = (k - 1) * (C - 1) + j - 1
            plane.append(send(piece, piece, xs.at[n], xr.at[n], peers[Z - 1 + j - 1]))
        n = 1 + (k - 1) * C
        cross.append(send(piece, piece, cs.at[n], cr.at[n], peers[-1]))
    for k in range(1, Z):
        fs = 2 * lax.rem(z + Z - k, Z) + a
        for j in range(1, C):
            plane[(k - 1) * (C - 1) + j - 1].wait_recv()
            piece = o_ref.at[fs, :, cols(lax.rem(c + C - j, C))]
            n = 1 + (k - 1) * C + j
            cross.append(send(piece, piece, cs.at[n], cr.at[n], peers[-1]))
    for copy in along + plane:
        copy.wait_send()
    whole.wait_send()
    whole.wait_recv()
    for copy in cross:
        copy.wait_send()
        copy.wait_recv()
    own.wait()


def gather_all(x, Z, C):
    R, W = x.shape
    dma = pltpu.SemaphoreType.DMA
    n, m = (Z - 1) * (C - 1), 1 + (Z - 1) * C
    return pl.pallas_call(functools.partial(gather_kernel, Z=Z, C=C, quarter=W // C),
        out_shape=jax.ShapeDtypeStruct((2 * Z, R, W), bf16),
        in_specs=[pl.BlockSpec(memory_space=pl.ANY)],
        out_specs=pl.BlockSpec(memory_space=pl.ANY),
        scratch_shapes=[dma(()), dma((Z - 1,)), dma((Z - 1,)), dma((n,)), dma((n,)), dma((m,)), dma((m,))],
        compiler_params=pltpu.CompilerParams(collective_id=0, has_side_effects=True, vmem_limit_bytes=56 << 20),
        cost_estimate=pl.CostEstimate(flops=0, bytes_accessed=20 * R * W * Z, transcendentals=0),
    )(x)


def join_kernel(*refs, count):
    t = pl.program_id(0)
    stacks, tail, out = refs[:-2], refs[-2], refs[-1]
    for i, ref in enumerate(stacks):
        @pl.when((t >= i * count) & (t < (i + 1) * count))
        def _(ref=ref):
            out[...] = ref[0]

    @pl.when(t >= len(stacks) * count)
    def _():
        out[:, :tail.shape[1]] = tail[...]


def join(stacks, tail):
    C, R, W = stacks[0].shape
    n = len(stacks)
    T = tail.shape[1]

    def at(i):
        return lambda t: (jnp.clip(t - i * C, 0, C - 1), 0, 0)
    return pl.pallas_call(functools.partial(join_kernel, count=C),
        out_shape=jax.ShapeDtypeStruct((R, n * C * W + T), bf16),
        grid=(n * C + 1,),
        in_specs=[pl.BlockSpec((1, R, W), at(i)) for i in range(n)] + [pl.BlockSpec((R, T), lambda t: (0, 0))],
        out_specs=pl.BlockSpec((R, W), lambda t: (0, t)),
        compiler_params=pltpu.CompilerParams(vmem_limit_bytes=56 << 20),
        cost_estimate=pl.CostEstimate(flops=0, bytes_accessed=4 * R * (n * C * W + T), transcendentals=0),
    )(*stacks, tail)


def deal_kernel(x_ref, o_ref):
    o_ref[0] = x_ref[...]


def deal(x, first, C, W):
    R = x.shape[0]
    return pl.pallas_call(deal_kernel,
        out_shape=jax.ShapeDtypeStruct((C, R, W), bf16),
        grid=(C,),
        in_specs=[pl.BlockSpec((R, W), lambda t: (0, first + t))],
        out_specs=pl.BlockSpec((1, R, W), lambda t: (t, 0, 0)),
        compiler_params=pltpu.CompilerParams(vmem_limit_bytes=56 << 20),
        cost_estimate=pl.CostEstimate(flops=0, bytes_accessed=4 * R * C * W, transcendentals=0),
    )(x)


def gather_kernel(x_ref, o_ref, own_sem, zs, zr, xs, xr, cs, cr, *, Z, C, quarter):
    z, a, c = lax.axis_index("zz"), lax.axis_index("core"), lax.axis_index("ctx")
    mesh_id = pl.DeviceIdType.MESH
    other = 1 - a
    peers = [(lax.rem(z + k, Z), a, c) for k in range(1, Z)] + [(z, a, lax.rem(c + j, C)) for j in range(1, C)] + [(z, other, c)]
    barrier = pltpu.get_barrier_semaphore()
    for peer in peers:
        pl.semaphore_signal(barrier, inc=1, device_id=peer, device_id_type=mesh_id)
    pl.semaphore_wait(barrier, len(peers))

    f = 2 * z + a

    def cols(q):
        return pl.ds(pl.multiple_of(q * quarter, quarter), quarter)

    def send(src, dst, s, r, peer):
        copy = pltpu.make_async_remote_copy(src_ref=src, dst_ref=dst, send_sem=s, recv_sem=r, device_id=peer, device_id_type=mesh_id)
        copy.start()
        return copy

    along = []
    for k in range(1, Z):
        along.append(send(x_ref.at[:, cols(c)], o_ref.at[f, :, cols(c)], zs.at[k - 1], zr.at[k - 1], peers[k - 1]))
    own = pltpu.make_async_copy(x_ref, o_ref.at[f], own_sem)
    own.start()
    whole = send(x_ref, o_ref.at[f], cs.at[0], cr.at[0], peers[-1])
    plane, cross = [], []
    for k in range(1, Z):
        along[k - 1].wait_recv()
        fs = 2 * lax.rem(z + Z - k, Z) + a
        piece = o_ref.at[fs, :, cols(c)]
        for j in range(1, C):
            n = (k - 1) * (C - 1) + j - 1
            plane.append(send(piece, piece, xs.at[n], xr.at[n], peers[Z - 1 + j - 1]))
        n = 1 + (k - 1) * C
        cross.append(send(piece, piece, cs.at[n], cr.at[n], peers[-1]))
    for k in range(1, Z):
        fs = 2 * lax.rem(z + Z - k, Z) + a
        for j in range(1, C):
            plane[(k - 1) * (C - 1) + j - 1].wait_recv()
            piece = o_ref.at[fs, :, cols(lax.rem(c + C - j, C))]
            n = 1 + (k - 1) * C + j
            cross.append(send(piece, piece, cs.at[n], cr.at[n], peers[-1]))
    for copy in along + plane:
        copy.wait_send()
    whole.wait_send()
    whole.wait_recv()
    for copy in cross:
        copy.wait_send()
        copy.wait_recv()
    own.wait()


def gather_all(x, Z, C):
    R, W = x.shape
    dma = pltpu.SemaphoreType.DMA
    n, m = (Z - 1) * (C - 1), 1 + (Z - 1) * C
    return pl.pallas_call(functools.partial(gather_kernel, Z=Z, C=C, quarter=W // C),
        out_shape=jax.ShapeDtypeStruct((2 * Z, R, W), bf16),
        in_specs=[pl.BlockSpec(memory_space=pl.ANY)],
        out_specs=pl.BlockSpec(memory_space=pl.ANY),
        scratch_shapes=[dma(()), dma((Z - 1,)), dma((Z - 1,)), dma((n,)), dma((n,)), dma((m,)), dma((m,))],
        compiler_params=pltpu.CompilerParams(collective_id=0, has_side_effects=True, vmem_limit_bytes=56 << 20),
        cost_estimate=pl.CostEstimate(flops=0, bytes_accessed=20 * R * W * Z, transcendentals=0),
    )(x)


HEADS = 17
EPSILON = 1e-05
FS = ("zz", "core")


def norm_parts(v):
    mean = jnp.mean(v, axis=-1, keepdims=True)
    c = v - mean
    r = lax.rsqrt(jnp.mean(c * c, axis=-1, keepdims=True) + EPSILON)
    return c * r, r


def norm_back(dn, v, gain):
    xhat, r = norm_parts(v)
    y = dn * gain
    a = jnp.mean(y, axis=-1, keepdims=True)
    b = jnp.mean(y * xhat, axis=-1, keepdims=True)
    return r * (y - a - xhat * b), jnp.sum(dn * xhat, axis=0), jnp.sum(dn, axis=0)


def col_sum(x):
    return jnp.dot(jnp.ones((16, x.shape[0]), bf16), x, preferred_element_type=f32)[0]


def gelu_parts(u):
    z = jnp.abs(u) * 0.7071067811865476
    t = 1.0 / (1.0 + 0.3275911 * z)
    e = jnp.exp(-z * z)
    poly = t * (0.254829592 + t * (-0.284496736 + t * (1.421413741 + t * (-1.453152027 + t * 1.061405429))))
    half = 0.5 * poly * e
    cdf = jnp.where(u >= 0, 1.0 - half, half)
    return u * cdf, cdf + u * e * 0.3989422804014327


def local(
    tokens, cotangent, lengths, block_order,
    ln1_gain, ln1_bias, qkv_weight, q_bias, v_bias, out_weight, out_bias,
    ln2_gain, ln2_bias, up_weight, up_bias, down_weight, down_bias,
    *, G, S,
):
    slots, rows, width = tokens.shape
    C = lax.axis_size("ctx")
    me = lax.axis_index("ctx")
    N = rows * C
    B = rows // 2
    NB = 2 * C
    L = ln1_gain.shape[0]
    shard = ln1_gain.shape[1]
    HW = G * 128
    x_tokens = tokens[0]

    steps = jnp.arange(NB, dtype=jnp.int32)
    order = block_order[0]
    inverse = jnp.sum(jnp.where(order[None, :] == steps[:, None], steps[None, :], 0), axis=1).astype(jnp.int32)
    count = (lengths + (B - 1)) // B
    meta = jnp.concatenate([inverse, count])
    def swap(x):
        return lax.ppermute(x, "core", [(0, 1), (1, 0)])

    metas = [meta, swap(meta)][:S]
    phase_inv = [t[None, :NB] for t in metas]
    phase_nb = [t[NB:] for t in metas]
    own = jnp.concatenate([inverse, lax.dynamic_slice_in_dim(order, 2 * me, 2, 0), count])
    own_pos = (lax.dynamic_slice_in_dim(order, 2 * me, 2, 0)[:, None] * B + jnp.arange(B, dtype=jnp.int32)).reshape(rows, 1)
    live = (own_pos < lengths[0]).astype(f32)

    def pack(w):
        parts = []
        for g in range(G):
            parts += [w[:, kind * width + g * 128:kind * width + g * 128 + 128] for kind in range(3)]
        last = width - 64
        parts += [w[:, kind * width + last:kind * width + width] for kind in (1, 2, 0)]
        return jnp.concatenate(parts, axis=1)

    def unpack(w):
        tail = G * 384
        parts = []
        for kind, last in enumerate((128, 0, 64)):
            parts += [w[:, g * 384 + kind * 128:g * 384 + kind * 128 + 128] for g in range(G)]
            parts.append(w[:, tail + last:tail + last + 64])
        return jnp.concatenate(parts, axis=1)

    def fetch(w):
        return lax.all_gather(w.astype(bf16), FS, axis=0, tiled=True)

    vectors = [ln1_gain, ln1_bias, q_bias, v_bias, out_bias, ln2_gain, ln2_bias, down_bias]
    vec = [t.astype(bf16).T for t in vectors] + [up_bias.astype(bf16).reshape(4 * L, shard).T]
    first = pack(qkv_weight[0].astype(bf16))
    block = jnp.concatenate([first] + vec, axis=1)
    used = block.shape[1]
    if C == 4 and lax.axis_size("zz") == 4:
        block = jnp.pad(block, ((0, 0), (0, -used % (128 * C))))
        block = gather_all(block, 4, C)
    else:
        block = lax.all_gather(block, FS)
    first_w = block[:, :, :3 * width].reshape(width, 3 * width)
    vec = jnp.transpose(block[:, :, 3 * width:used].reshape(width, used - 3 * width)).astype(f32)

    def vector(index, layer):
        if index < 8:
            return vec[L * index + layer]
        t = vec[8 * L + 4 * layer:8 * L + 4 * layer + 4]
        return jnp.transpose(t.reshape(4, -1, shard), (1, 0, 2)).reshape(-1)

    weights = []
    for layer in range(L):
        weights.append((
            fetch(pack(qkv_weight[layer].astype(bf16))) if layer else first_w,
            fetch(out_weight[layer]),
            fetch(up_weight[layer]),
            fetch(down_weight[layer]),
        ))

    def plain(x):
        return with_layout_constraint(x, Layout(major_to_minor=tuple(range(x.ndim))))

    def exchange(x):
        return plain(lax.all_to_all(plain(x), "ctx", 0, 0))

    def after(x, *others):
        return lax.optimization_barrier((x,) + others)

    stream = x_tokens.astype(f32)
    records = []
    for layer in range(L):
        qkv_w, out_w, up_w, down_w = weights[layer]
        xhat, _ = norm_parts(stream)
        n1 = (xhat * vector(0, layer) + vector(1, layer)).astype(bf16)
        q_b, v_b = vector(2, layer), vector(3, layer)
        bias = pack(jnp.concatenate([q_b, jnp.zeros_like(q_b), v_b])[None])[0]
        projected = (jnp.dot(n1, qkv_w, preferred_element_type=f32) + bias).astype(bf16)
        wide = [deal(projected, s * C, C, 384) for s in range(S)]
        tail = projected[:, G * 384:]
        if S == 2:
            wide[1] = swap(wide[1])
        kv16 = jnp.broadcast_to(tail[None, :, :128], (C, rows, 128))
        q16 = tail[:, 128:]
        heads, o, lse, o_back = [], [], [], []
        for s in range(S):
            t = wide[s]
            if s == S - 1:
                t = jnp.concatenate([t, kv16], axis=2)
            if s:
                t, heads[0] = after(t, heads[0])
            heads.append(exchange(t).reshape(1, N, -1))
        for s in range(S):
            o_s, lse_s = flash_fwd(heads[s], phase_inv[s], phase_nb[s], B)
            o.append(o_s)
            lse.append(lse_s)
            t = o_s.reshape(C, rows, 128)
            if s:
                t, o_back[0] = after(t, o_back[0])
            o_back.append(exchange(swap(t) if s else t))
        o16, lse16 = one_fwd(q16, heads[-1][0], own, B)
        mixed = join(o_back, o16)
        m = stream + jnp.dot(mixed, out_w, preferred_element_type=f32) + vector(4, layer)
        xhat2, _ = norm_parts(m)
        n2 = (xhat2 * vector(5, layer) + vector(6, layer)).astype(bf16)
        u = jnp.dot(n2, up_w, preferred_element_type=f32) + vector(8, layer)
        a, slope = gelu_parts(u)
        a = a.astype(bf16)
        a, slope = after(a, slope.astype(bf16))
        records.append((stream, n1, heads, q16, o, lse, o16, lse16, mixed, m, n2, a, slope))
        if layer < L - 1:
            stream = m + jnp.dot(a, down_w, preferred_element_type=f32) + vector(7, layer)
    end_a, end_m, end_w, end_b = a, m, down_w, vector(7, L - 1)

    def reduce_fsdp(g):
        return lax.psum_scatter(g.astype(bf16), FS, scatter_dimension=0, tiled=True)

    def reduce_ctx(g):
        return lax.psum(g, "ctx").astype(f32)

    grad = cotangent[0].astype(f32) * live
    matrices = [None] * L
    fours = [None] * L
    ffns = [None] * L
    small = [None] * L

    def ctx_end(mine):
        return exchange(jnp.broadcast_to(mine[None], (C,) + mine.shape))

    def ctx_sum(shards):
        mine, sizes = ctx_begin(shards)
        return ctx_end(mine), sizes

    def ctx_begin(shards):
        pieces = []
        for t in shards:
            if t.shape[1] == width:
                pieces.append(t.reshape(C, -1, width))
            else:
                pieces.append(jnp.transpose(t.reshape(t.shape[0], C, -1), (1, 0, 2)).reshape(C, -1, width))
        sizes = [t.shape[1] for t in pieces]
        parts = exchange(jnp.concatenate(pieces, axis=1))
        mine = jnp.sum(parts.astype(f32), axis=0).astype(bf16)
        return mine, sizes

    def spread(summed, shapes):
        whole, sizes = summed
        out, at = [], 0
        for n, (r, c) in zip(sizes, shapes):
            t = whole[:, at:at + n].astype(f32)
            at += n
            if c == width:
                out.append(t.reshape(r, c))
            else:
                out.append(jnp.transpose(t.reshape(C, r, c // C), (1, 0, 2)).reshape(r, c))
        return out

    wide_shape, tall_shape = (shard, 4 * width), (4 * shard, width)
    for layer in reversed(range(L)):
        stream_in, n1, heads, q16, o, lse, o16, lse16, mixed, m, n2, a, slope = records[layer]
        qkv_w, out_w, up_w, down_w = weights[layer]
        gb = grad.astype(bf16)
        d_down_b = col_sum(gb)
        d_down = jnp.einsum("rf,rd->fd", a, gb, preferred_element_type=f32).astype(bf16)
        gb, d_down = after(gb, plain(d_down))
        if layer < L - 1:
            above = list(after(gb, *ffns[layer + 1]))
            gb = above.pop(0)
            mine_ffn, ffn_sizes = ctx_begin(above)
        d_down = reduce_fsdp(d_down)
        du = (jnp.einsum("rd,fd->rf", gb, down_w, preferred_element_type=f32) * slope.astype(f32)).astype(bf16)
        d_up_b = col_sum(du)
        if layer < L - 1:
            du, mine_ffn = after(du, mine_ffn)
            ffn_whole = ctx_end(mine_ffn)
        d_up = jnp.einsum("rd,rf->df", n2, du, preferred_element_type=f32).astype(bf16)
        du, d_up = after(du, plain(d_up))
        d_up = reduce_fsdp(d_up)
        dn2 = jnp.einsum("rf,df->rd", du, up_w, preferred_element_type=f32)
        back, d_gain2, d_bias2 = norm_back(dn2, m, vector(5, layer))
        gm = grad + back
        gmb = gm.astype(bf16)
        d_out_b = col_sum(gmb)
        d_out = jnp.einsum("rd,re->de", mixed, gmb, preferred_element_type=f32).astype(bf16)
        if layer == 0:
            gmb, d_out = after(gmb, plain(d_out))
        if layer < L - 1:
            gmb, ffn_whole = after(gmb, ffn_whole)
        d_o = []
        for s in range(S):
            w = out_w[C * 128 * s:C * 128 * (s + 1)].reshape(C, 128, width)
            d_o.append(jnp.einsum("re,gce->grc", gmb, w, preferred_element_type=f32).astype(bf16))
        d_o16 = jnp.einsum("re,ce->rc", gmb, out_w[HW:], preferred_element_type=f32).astype(bf16)
        dq16, dkv16 = one_bwd(q16, heads[-1][0], o16, d_o16, lse16, own, B)
        d_oh, d_wide = [], []
        for s in range(S):
            t = d_o[s]
            if s:
                t = swap(t)
            if s == S - 1:
                t = jnp.concatenate([t, dkv16.reshape(C, rows, 128)], axis=2)
            if s:
                t, d_oh[0] = after(t, d_oh[0])
            if s == S - 1 and layer < L - 1:
                t, fours[layer + 1] = after(t, fours[layer + 1])
            d_oh.append(exchange(t).reshape(1, N, -1))
        dkv16 = jnp.sum(d_oh[-1].reshape(C, rows, 256)[:, :, 128:].astype(f32), axis=0)
        for s in range(S):
            t = flash_bwd(heads[s], o[s], d_oh[s], lse[s], phase_inv[s], phase_nb[s], B)
            t = t.reshape(C, rows, 384)
            if s:
                t, d_wide[0] = after(t, d_wide[0])
            if s == S - 1:
                t, d_down = after(t, d_down)
            if s == S - 1 and layer:
                t, d_up = after(t, d_up)
            d_wide.append(exchange(swap(t) if s else t))
        d_tail = jnp.concatenate([dkv16.astype(bf16), dq16], axis=1)
        d_row = join(d_wide, d_tail)
        d_row, d_down_b, d_up_b, d_out_b = after(d_row, d_down_b, d_up_b, d_out_b)
        d_back = d_row
        if layer == 0:
            d_row, d_up = after(d_row, d_up)
            mine, middle_sizes = ctx_begin([fours[1], d_up, d_down])
            d_back, mine = after(d_row, mine)
        d_qkv = jnp.einsum("rd,rc->dc", n1, d_row, preferred_element_type=f32).astype(bf16)
        if layer:
            d_row, d_four = after(d_row, plain(jnp.concatenate([d_qkv, d_out], axis=1)))
            d_four = reduce_fsdp(d_four)
        else:
            d_qkv, d_out = after(d_qkv, reduce_fsdp(d_out))
            d_four = jnp.concatenate([reduce_fsdp(d_qkv), d_out], axis=1)
        sums = unpack(col_sum(d_row)[None])[0]
        dn1 = jnp.einsum("rc,dc->rd", d_back, qkv_w, preferred_element_type=f32)
        back, d_gain1, d_bias1 = norm_back(dn1, stream_in, vector(0, layer))
        grad = gm + back
        fours[layer] = d_four
        ffns[layer] = (d_up, d_down)
        small[layer] = jnp.concatenate([
            t.reshape(-1, n) for t, n in (
                (d_gain1, shard), (d_bias1, shard), (sums[:width], shard), (sums[2 * width:], shard), (d_out_b, shard),
                (d_gain2, shard), (d_bias2, shard), (d_down_b, shard), (d_up_b, 4 * shard))], axis=1)

    vec_grads = jnp.stack(small, axis=1)
    vec_grads = jnp.sum(lax.all_to_all(vec_grads, FS, 0, 0), axis=0)
    vec_grads = jnp.sum(lax.all_to_all(jnp.broadcast_to(vec_grads[None], (C,) + vec_grads.shape), "ctx", 0, 0), axis=0)
    end, vec_grads = after(fours[0], vec_grads)
    mine_last, last_sizes = ctx_begin([end])
    end_a, mine_last = after(end_a, mine_last)
    whole = ctx_end(jnp.concatenate([mine, mine_last], axis=0))
    stream = end_m + jnp.dot(end_a, end_w, preferred_element_type=f32) + end_b
    activations = (stream * live).astype(bf16)[None]
    activations, whole = after(activations, whole)
    rest = spread((whole, middle_sizes + last_sizes), [wide_shape, wide_shape, tall_shape, wide_shape])
    matrices[1] = [rest[0]] + spread((ffn_whole, ffn_sizes), [wide_shape, tall_shape])
    matrices[0] = [rest[3], rest[1], rest[2]]
    vg = [vec_grads[:, i * shard:(i + 1) * shard] for i in range(8)] + [vec_grads[:, 8 * shard:]]

    g_qkv = jnp.stack([unpack(matrices[layer][0][:, :3 * width]) for layer in range(L)])
    g_out = jnp.stack([matrices[layer][0][:, 3 * width:] for layer in range(L)])
    g_up = jnp.stack([matrices[layer][1] for layer in range(L)])
    g_down = jnp.stack([matrices[layer][2] for layer in range(L)])
    return (activations, grad[None], vg[0], vg[1], g_qkv, vg[2], vg[3], g_out, vg[4], vg[5], vg[6], g_up, vg[8], g_down, vg[7])


def solution(mesh):
    F, C = mesh.devices.shape
    inner = Mesh(mesh.devices.reshape(F // 2, 2, C), ("zz", "core", "ctx"))
    S = 2 if 16 // (2 * C) >= 2 else 1
    G = S * C
    rows = P(FS, "ctx", None)
    vec, mat = P(None, FS), P(None, FS, None)
    return jax.shard_map(
        functools.partial(local, G=G, S=S),
        mesh=inner,
        in_specs=(rows, rows, P(FS), P(FS, None), vec, vec, mat, vec, vec, mat, vec, vec, vec, mat, vec, mat, vec),
        out_specs=(rows, rows, vec, vec, mat, vec, vec, mat, vec, vec, vec, mat, vec, mat, vec),
        check_vma=False,
    )
```

```python
import functools
import jax, jax.numpy as jnp
from jax import lax
from jax.experimental import pallas as pl
from jax.experimental.pallas import tpu as pltpu
from jax.experimental.layout import Layout, with_layout_constraint
from jax.sharding import Mesh, PartitionSpec as P
f32=jnp.float32; bf16=jnp.bfloat16
NEG=-1e30
def dot_nt(a,b): return lax.dot_general(a,b,(((1,),(1,)),((),())),preferred_element_type=f32)
def dot_nn(a,b): return lax.dot_general(a,b,(((1,),(0,)),((),())),preferred_element_type=f32)

LOG2E=1.4426950408889634
def split(q,h,low):
    qs=q.astype(f32)*(0.125*LOG2E)
    hi=qs.astype(bf16).astype(f32); lo=qs-hi
    rl=pltpu.roll(lo,64,1)
    c=jnp.where(low,hi,rl) if h==0 else jnp.where(low,rl,hi)
    return c.astype(bf16)
def dup(k,h,low):
    kf=k.astype(f32); rl=pltpu.roll(kf,64,1)
    c=jnp.where(low,kf,rl) if h==0 else jnp.where(low,rl,kf)
    return c.astype(bf16)
def fwd_kernel(inv_ref, nb_ref, x_ref, o_ref, lse_ref, vt, kd, sb, acc, *, B, NB):
    s=pl.program_id(0)
    nb=nb_ref[s]
    lane=lax.broadcasted_iota(jnp.int32,(1,128),1)
    low=lane<64
    def tv(j,_):
        r=pl.multiple_of(inv_ref[s,j]*B,B)
        w=pl.multiple_of(j*B,B)
        t=x_ref[0,pl.ds(r,B),256:384].T
        one=(lax.broadcasted_iota(jnp.int32,(16,B),0)==0).astype(bf16)
        for h in range(2):
            vt[80*h:80*h+64,pl.ds(w,B)]=t[64*h:64*h+64,:]
            vt[80*h+64:80*h+80,pl.ds(w,B)]=one
            kd[h,pl.ds(w,B),:]=dup(x_ref[0,pl.ds(r,B),128:256],h,low)
        return 0
    lax.fori_loop(0,nb,tv,0)
    rr=lax.broadcasted_iota(jnp.int32,(B,B),0)
    cc=lax.broadcasted_iota(jnp.int32,(B,B),1)
    def qblock(i,_):
        r=pl.multiple_of(inv_ref[s,i]*B,B)
        q=x_ref[0,pl.ds(r,B),0:128]
        qh=[split(q,h,low) for h in range(2)]
        acc[...]=jnp.zeros_like(acc)
        def scores(j,slot):
            for h in range(2):
                sb[slot,h]=dot_nt(kd[h,pl.ds(pl.multiple_of(j*B,B),B),:],qh[h])
        def step(j,carry,diag):
            out=[]
            for h in range(2):
                m=carry[h]
                st=sb[j%2,h]
                if diag: st=jnp.where(rr<=cc,st,NEG)
                mn=jnp.maximum(m,jnp.max(st,axis=0,keepdims=True))
                p=jnp.exp2(st-mn)
                al=jnp.exp2(m-mn)
                v=vt[80*h:80*h+80,pl.ds(pl.multiple_of(j*B,B),B)]
                acc[h]=acc[h]*al+dot_nn(v,p.astype(bf16))
                out.append(mn)
            return tuple(out)
        scores(0,0)
        def both(j,c):
            scores(j+1,(j+1)%2)
            return step(j,c,False)
        n=jnp.full((1,B),NEG,f32)
        c=lax.fori_loop(0,i,both,(n,n))
        c=step(i,c,True)
        os=[]
        for h in range(2):
            l=acc[h,64:65,:]
            os.append(acc[h,0:64,:]*(1.0/l))
            lse_ref[0,pl.ds(h,1),pl.ds(r,B)]=c[h]+jnp.log2(l)
        o_ref[0,pl.ds(r,B),:]=jnp.concatenate(os,0).T.astype(bf16)
        return 0
    lax.fori_loop(0,nb,qblock,0)
    def pad(i,_):
        r=pl.multiple_of(inv_ref[s,i]*B,B)
        o_ref[0,pl.ds(r,B),:]=jnp.zeros((B,128),bf16)
        lse_ref[0,:,pl.ds(r,B)]=jnp.zeros((8,B),f32)
        return 0
    lax.fori_loop(nb,NB,pad,0)

def flash_fwd(x,inv,nb,B):
    S,N,_=x.shape
    NB=N//B
    return pl.pallas_call(functools.partial(fwd_kernel,B=B,NB=NB),
      out_shape=(jax.ShapeDtypeStruct((S,N,128),bf16),jax.ShapeDtypeStruct((S,8,N),f32)),
      grid_spec=pltpu.PrefetchScalarGridSpec(num_scalar_prefetch=2,grid=(S,),
        in_specs=[pl.BlockSpec((1,N,384),lambda s,*_:(s,0,0))],
        out_specs=[pl.BlockSpec((1,N,128),lambda s,*_:(s,0,0)),pl.BlockSpec((1,8,N),lambda s,*_:(s,0,0))],
        scratch_shapes=[pltpu.VMEM((160,N),bf16),pltpu.VMEM((2,N,128),bf16),pltpu.VMEM((2,2,B,B),f32),pltpu.VMEM((2,80,B),f32)]),
      compiler_params=pltpu.CompilerParams(vmem_limit_bytes=48<<20),
      cost_estimate=pl.CostEstimate(flops=S*4*N*N*128,bytes_accessed=S*N*1024,transcendentals=S*N*N),
      )(inv,nb,x)

def bwd_kernel(inv_ref, nb_ref, x_ref, o_ref, do_ref, lse_ref, dx_ref, kt, qd, dq, dk, dv, dl, *, B, NB):
    s=pl.program_id(0)
    nb=nb_ref[s]
    lane=lax.broadcasted_iota(jnp.int32,(1,128),1)
    low=lane<64
    hm=(lax.broadcasted_iota(jnp.int32,(8,128),1)//64==lax.broadcasted_iota(jnp.int32,(8,128),0)).astype(bf16)
    def prep(j,_):
        r=pl.multiple_of(inv_ref[s,j]*B,B)
        w=pl.multiple_of(j*B,B)
        kt[:,pl.ds(w,B)]=x_ref[0,pl.ds(r,B),128:256].T
        for h in range(2): qd[h,pl.ds(w,B),:]=split(x_ref[0,pl.ds(r,B),0:128],h,low)
        prod=o_ref[0,pl.ds(r,B),:].astype(f32)*do_ref[0,pl.ds(r,B),:].astype(f32)
        hi=prod.astype(bf16); lo=(prod-hi.astype(f32)).astype(bf16)
        dl[:,pl.ds(w,B)]=dot_nt(hm,hi)+dot_nt(hm,lo)
        dq[:,pl.ds(w,B)]=jnp.zeros((128,B),f32)
        return 0
    lax.fori_loop(0,nb,prep,0)
    rr=lax.broadcasted_iota(jnp.int32,(B,B),0)
    cc=lax.broadcasted_iota(jnp.int32,(B,B),1)
    def kblock(j,_):
        r=pl.multiple_of(inv_ref[s,j]*B,B)
        k=x_ref[0,pl.ds(r,B),128:256]
        v=x_ref[0,pl.ds(r,B),256:384]
        kdh=[dup(k,h,low) for h in range(2)]
        dk[...]=jnp.zeros_like(dk); dv[...]=jnp.zeros_like(dv)
        def step(i,diag):
            ri=pl.multiple_of(inv_ref[s,i]*B,B)
            wi=pl.multiple_of(i*B,B)
            q=x_ref[0,pl.ds(ri,B),0:128]*jnp.asarray(0.125,bf16)
            do=do_ref[0,pl.ds(ri,B),:]
            zero=jnp.zeros_like(q)
            dvs=[];dks=[]
            for h in range(2):
                qh=jnp.where(low,q,zero) if h==0 else jnp.where(low,zero,q)
                doh=jnp.where(low,do,zero) if h==0 else jnp.where(low,zero,do)
                st=dot_nt(kdh[h],qd[h,pl.ds(wi,B),:])
                p=jnp.exp2(st-lse_ref[0,pl.ds(h,1),pl.ds(ri,B)])
                if diag: p=jnp.where(rr<=cc,p,0.0)
                dvs.append(dot_nn(p.astype(bf16),doh))
                dp=dot_nt(v,doh)
                ds=(p*(dp-dl[pl.ds(h,1),pl.ds(wi,B)])).astype(bf16)
                dks.append(dot_nn(ds,qh))
                kh=kt[64*h:64*h+64,pl.ds(pl.multiple_of(j*B,B),B)]
                dq[64*h:64*h+64,pl.ds(wi,B)]+=dot_nn(kh,ds)
            dv[...]+=dvs[0]+dvs[1]
            dk[...]+=dks[0]+dks[1]
        step(j,True)
        def body(i,_):
            step(i,False); return 0
        lax.fori_loop(j+1,nb,body,0)
        dx_ref[0,pl.ds(r,B),128:256]=dk[...].astype(bf16)
        dx_ref[0,pl.ds(r,B),256:384]=dv[...].astype(bf16)
        return 0
    lax.fori_loop(0,nb,kblock,0)
    def fin(i,_):
        r=pl.multiple_of(inv_ref[s,i]*B,B)
        dx_ref[0,pl.ds(r,B),0:128]=(dq[:,pl.ds(pl.multiple_of(i*B,B),B)].T*0.125).astype(bf16)
        return 0
    lax.fori_loop(0,nb,fin,0)
    def pad(i,_):
        r=pl.multiple_of(inv_ref[s,i]*B,B)
        dx_ref[0,pl.ds(r,B),:]=jnp.zeros((B,384),bf16)
        return 0
    lax.fori_loop(nb,NB,pad,0)

def flash_bwd(x,o,do,lse,inv,nb,B):
    S,N,_=x.shape
    NB=N//B
    return pl.pallas_call(functools.partial(bwd_kernel,B=B,NB=NB),
      out_shape=jax.ShapeDtypeStruct((S,N,384),bf16),
      grid_spec=pltpu.PrefetchScalarGridSpec(num_scalar_prefetch=2,grid=(S,),
        in_specs=[pl.BlockSpec((1,N,384),lambda s,*_:(s,0,0)),pl.BlockSpec((1,N,128),lambda s,*_:(s,0,0)),
                  pl.BlockSpec((1,N,128),lambda s,*_:(s,0,0)),pl.BlockSpec((1,8,N),lambda s,*_:(s,0,0))],
        out_specs=pl.BlockSpec((1,N,384),lambda s,*_:(s,0,0)),
        scratch_shapes=[pltpu.VMEM((128,N),bf16),pltpu.VMEM((2,N,128),bf16),pltpu.VMEM((128,N),f32),pltpu.VMEM((B,128),f32),pltpu.VMEM((B,128),f32),pltpu.VMEM((8,N),f32)]),
      compiler_params=pltpu.CompilerParams(vmem_limit_bytes=48<<20),
      cost_estimate=pl.CostEstimate(flops=S*10*N*N*128,bytes_accessed=S*N*2400,transcendentals=S*N*N),
      )(inv,nb,x,o,do,lse)


def one_fwd_kernel(own_ref, q_ref, x_ref, o_ref, lse_ref, vt, kd, acc, *, B, NB):
    nb = own_ref[NB + 2]
    low = lax.broadcasted_iota(jnp.int32,(1,128),1)<64
    def tv(j,_):
        r=pl.multiple_of(own_ref[j]*B,B)
        t=x_ref[pl.ds(r,B),:].T
        w=pl.multiple_of(j*B,B)
        kd[pl.ds(w,B),:]=dup(x_ref[pl.ds(r,B),:],0,low)
        vt[0:64,pl.ds(w,B)]=t[64:128,:]
        vt[64:80,pl.ds(w,B)]=(lax.broadcasted_iota(jnp.int32,(16,B),0)==0).astype(bf16)
        return 0
    lax.fori_loop(0,nb,tv,0)
    rr=lax.broadcasted_iota(jnp.int32,(B,B),0)
    cc=lax.broadcasted_iota(jnp.int32,(B,B),1)
    for t in range(2):
        i=own_ref[NB+t]
        @pl.when(i>=nb)
        def _():
            o_ref[t*B:(t+1)*B,:]=jnp.zeros((B,64),bf16)
            lse_ref[:,t*B:(t+1)*B]=jnp.zeros((8,B),f32)
        @pl.when(i<nb)
        def _():
            qs=q_ref[t*B:(t+1)*B,:].astype(f32)*(0.125*LOG2E)
            hi=qs.astype(bf16)
            q=jnp.concatenate([hi.astype(f32),qs-hi.astype(f32)],axis=1).astype(bf16)
            acc[...]=jnp.zeros_like(acc)
            def step(j,m,diag):
                st=dot_nt(kd[pl.ds(pl.multiple_of(j*B,B),B),:],q)
                if diag: st=jnp.where(rr<=cc,st,NEG)
                mn=jnp.maximum(m,jnp.max(st,axis=0,keepdims=True))
                p=jnp.exp2(st-mn)
                al=jnp.exp2(m-mn)
                v=vt[:,pl.ds(pl.multiple_of(j*B,B),B)]
                acc[...]=acc[...]*al+dot_nn(v,p.astype(bf16))
                return mn
            m=lax.fori_loop(0,i,lambda j,m: step(j,m,False),jnp.full((1,B),NEG,f32))
            m=step(i,m,True)
            l=acc[64:65,:]
            o_ref[t*B:(t+1)*B,:]=(acc[0:64,:]*(1.0/l)).T.astype(bf16)
            lse_ref[:,t*B:(t+1)*B]=jnp.broadcast_to(m+jnp.log2(l),(8,B))


def one_fwd(q,x,own,B):
    N=x.shape[0]; R=q.shape[0]; NB=N//B
    full=lambda *_:(0,0)
    last=lambda *_:(0,3)
    return pl.pallas_call(functools.partial(one_fwd_kernel,B=B,NB=NB),
      out_shape=(jax.ShapeDtypeStruct((R,64),bf16),jax.ShapeDtypeStruct((8,R),f32)),
      grid_spec=pltpu.PrefetchScalarGridSpec(num_scalar_prefetch=1,grid=(1,),
        in_specs=[pl.BlockSpec((R,64),full),pl.BlockSpec((N,128),last)],
        out_specs=[pl.BlockSpec((R,64),full),pl.BlockSpec((8,R),full)],
        scratch_shapes=[pltpu.VMEM((80,N),bf16),pltpu.VMEM((N,128),bf16),pltpu.VMEM((80,B),f32)]),
      compiler_params=pltpu.CompilerParams(vmem_limit_bytes=48<<20),
      cost_estimate=pl.CostEstimate(flops=4*R*N*128,bytes_accessed=N*256+R*512,transcendentals=R*N),
      )(own,q,x)


def one_bwd_kernel(own_ref, q_ref, x_ref, o_ref, do_ref, lse_ref, dq_ref, dx_ref, dkv, dq, *, B, NB):
    nb = own_ref[NB + 2]
    low = lax.broadcasted_iota(jnp.int32,(1,128),1)<64
    rr=lax.broadcasted_iota(jnp.int32,(B,B),0)
    cc=lax.broadcasted_iota(jnp.int32,(B,B),1)
    ones=jnp.ones((8,64),bf16)
    dkv[...]=jnp.zeros_like(dkv)
    for t in range(2):
        i=own_ref[NB+t]
        sl=slice(t*B,(t+1)*B)
        @pl.when(i>=nb)
        def _():
            dq_ref[sl,:]=jnp.zeros((B,64),bf16)
        @pl.when(i<nb)
        def _():
            qr=q_ref[sl,:]
            qs=qr.astype(f32)*(0.125*LOG2E)
            hi=qs.astype(bf16)
            q=jnp.concatenate([hi.astype(f32),qs-hi.astype(f32)],axis=1).astype(bf16)
            qd=qr*jnp.asarray(0.125,bf16)
            do=do_ref[sl,:]
            prod=o_ref[sl,:].astype(f32)*do.astype(f32)
            hi=prod.astype(bf16); lo=(prod-hi.astype(f32)).astype(bf16)
            dl=(dot_nt(ones,hi)+dot_nt(ones,lo))[0:1,:]
            lse=lse_ref[0:1,sl]
            dq[...]=jnp.zeros_like(dq)
            def step(j,diag):
                r=pl.multiple_of(own_ref[j]*B,B)
                k=x_ref[pl.ds(r,B),0:64]
                v=x_ref[pl.ds(r,B),64:128]
                st=dot_nt(dup(x_ref[pl.ds(r,B),:],0,low),q)
                p=jnp.exp2(st-lse)
                if diag: p=jnp.where(rr<=cc,p,0.0)
                dp=dot_nt(v,do)
                ds=(p*(dp-dl)).astype(bf16)
                dkv[pl.ds(r,B),64:128]+=dot_nn(p.astype(bf16),do)
                dkv[pl.ds(r,B),0:64]+=dot_nn(ds,qd)
                dq[...]+=dot_nn(k.T,ds)
            def body(j,_):
                step(j,False); return 0
            lax.fori_loop(0,i,body,0)
            step(i,True)
            dq_ref[sl,:]=(dq[...].T*0.125).astype(bf16)
    dx_ref[...]=dkv[...].astype(bf16)


def one_bwd(q,x,o,do,lse,own,B):
    N=x.shape[0]; R=q.shape[0]; NB=N//B
    full=lambda *_:(0,0)
    last=lambda *_:(0,3)
    return pl.pallas_call(functools.partial(one_bwd_kernel,B=B,NB=NB),
      out_shape=(jax.ShapeDtypeStruct((R,64),bf16),jax.ShapeDtypeStruct((N,128),bf16)),
      grid_spec=pltpu.PrefetchScalarGridSpec(num_scalar_prefetch=1,grid=(1,),
        in_specs=[pl.BlockSpec((R,64),full),pl.BlockSpec((N,128),last),pl.BlockSpec((R,64),full),pl.BlockSpec((R,64),full),pl.BlockSpec((8,R),full)],
        out_specs=[pl.BlockSpec((R,64),full),pl.BlockSpec((N,128),full)],
        scratch_shapes=[pltpu.VMEM((N,128),f32),pltpu.VMEM((64,B),f32)]),
      compiler_params=pltpu.CompilerParams(vmem_limit_bytes=48<<20),
      cost_estimate=pl.CostEstimate(flops=10*R*N*128,bytes_accessed=N*512+R*1024,transcendentals=R*N),
      )(own,q,x,o,do,lse)


def join_kernel(*refs, count):
    t = pl.program_id(0)
    stacks, tail, out = refs[:-2], refs[-2], refs[-1]
    for i, ref in enumerate(stacks):
        @pl.when((t >= i * count) & (t < (i + 1) * count))
        def _(ref=ref):
            out[...] = ref[0]

    @pl.when(t >= len(stacks) * count)
    def _():
        out[:, :tail.shape[1]] = tail[...]


def join(stacks, tail):
    C, R, W = stacks[0].shape
    n = len(stacks)
    T = tail.shape[1]

    def at(i):
        return lambda t: (jnp.clip(t - i * C, 0, C - 1), 0, 0)
    return pl.pallas_call(functools.partial(join_kernel, count=C),
        out_shape=jax.ShapeDtypeStruct((R, n * C * W + T), bf16),
        grid=(n * C + 1,),
        in_specs=[pl.BlockSpec((1, R, W), at(i)) for i in range(n)] + [pl.BlockSpec((R, T), lambda t: (0, 0))],
        out_specs=pl.BlockSpec((R, W), lambda t: (0, t)),
        compiler_params=pltpu.CompilerParams(vmem_limit_bytes=56 << 20),
        cost_estimate=pl.CostEstimate(flops=0, bytes_accessed=4 * R * (n * C * W + T), transcendentals=0),
    )(*stacks, tail)


def deal_kernel(x_ref, o_ref):
    o_ref[0] = x_ref[...]


def deal(x, first, C, W):
    R = x.shape[0]
    return pl.pallas_call(deal_kernel,
        out_shape=jax.ShapeDtypeStruct((C, R, W), bf16),
        grid=(C,),
        in_specs=[pl.BlockSpec((R, W), lambda t: (0, first + t))],
        out_specs=pl.BlockSpec((1, R, W), lambda t: (t, 0, 0)),
        compiler_params=pltpu.CompilerParams(vmem_limit_bytes=56 << 20),
        cost_estimate=pl.CostEstimate(flops=0, bytes_accessed=4 * R * C * W, transcendentals=0),
    )(x)


def gather_kernel(x_ref, o_ref, own_sem, zs, zr, xs, xr, cs, cr, *, Z, C, quarter):
    z, a, c = lax.axis_index("zz"), lax.axis_index("core"), lax.axis_index("ctx")
    mesh_id = pl.DeviceIdType.MESH
    other = 1 - a
    peers = [(lax.rem(z + k, Z), a, c) for k in range(1, Z)] + [(z, a, lax.rem(c + j, C)) for j in range(1, C)] + [(z, other, c)]
    barrier = pltpu.get_barrier_semaphore()
    for peer in peers:
        pl.semaphore_signal(barrier, inc=1, device_id=peer, device_id_type=mesh_id)
    pl.semaphore_wait(barrier, len(peers))

    f = 2 * z + a

    def cols(q):
        return pl.ds(pl.multiple_of(q * quarter, quarter), quarter)

    def send(src, dst, s, r, peer):
        copy = pltpu.make_async_remote_copy(src_ref=src, dst_ref=dst, send_sem=s, recv_sem=r, device_id=peer, device_id_type=mesh_id)
        copy.start()
        return copy

    along = []
    for k in range(1, Z):
        along.append(send(x_ref.at[:, cols(c)], o_ref.at[f, :, cols(c)], zs.at[k - 1], zr.at[k - 1], peers[k - 1]))
    own = pltpu.make_async_copy(x_ref, o_ref.at[f], own_sem)
    own.start()
    whole = send(x_ref, o_ref.at[f], cs.at[0], cr.at[0], peers[-1])
    plane, cross = [], []
    for k in range(1, Z):
        along[k - 1].wait_recv()
        fs = 2 * lax.rem(z + Z - k, Z) + a
        piece = o_ref.at[fs, :, cols(c)]
        for j in range(1, C):
            n = (k - 1) * (C - 1) + j - 1
            plane.append(send(piece, piece, xs.at[n], xr.at[n], peers[Z - 1 + j - 1]))
        n = 1 + (k - 1) * C
        cross.append(send(piece, piece, cs.at[n], cr.at[n], peers[-1]))
    for k in range(1, Z):
        fs = 2 * lax.rem(z + Z - k, Z) + a
        for j in range(1, C):
            plane[(k - 1) * (C - 1) + j - 1].wait_recv()
            piece = o_ref.at[fs, :, cols(lax.rem(c + C - j, C))]
            n = 1 + (k - 1) * C + j
            cross.append(send(piece, piece, cs.at[n], cr.at[n], peers[-1]))
    for copy in along + plane:
        copy.wait_send()
    whole.wait_send()
    whole.wait_recv()
    for copy in cross:
        copy.wait_send()
        copy.wait_recv()
    own.wait()


def gather_all(x, Z, C):
    R, W = x.shape
    dma = pltpu.SemaphoreType.DMA
    n, m = (Z - 1) * (C - 1), 1 + (Z - 1) * C
    return pl.pallas_call(functools.partial(gather_kernel, Z=Z, C=C, quarter=W // C),
        out_shape=jax.ShapeDtypeStruct((2 * Z, R, W), bf16),
        in_specs=[pl.BlockSpec(memory_space=pl.ANY)],
        out_specs=pl.BlockSpec(memory_space=pl.ANY),
        scratch_shapes=[dma(()), dma((Z - 1,)), dma((Z - 1,)), dma((n,)), dma((n,)), dma((m,)), dma((m,))],
        compiler_params=pltpu.CompilerParams(collective_id=0, has_side_effects=True, vmem_limit_bytes=56 << 20),
        cost_estimate=pl.CostEstimate(flops=0, bytes_accessed=20 * R * W * Z, transcendentals=0),
    )(x)


def join_kernel(*refs, count):
    t = pl.program_id(0)
    stacks, tail, out = refs[:-2], refs[-2], refs[-1]
    for i, ref in enumerate(stacks):
        @pl.when((t >= i * count) & (t < (i + 1) * count))
        def _(ref=ref):
            out[...] = ref[0]

    @pl.when(t >= len(stacks) * count)
    def _():
        out[:, :tail.shape[1]] = tail[...]


def join(stacks, tail):
    C, R, W = stacks[0].shape
    n = len(stacks)
    T = tail.shape[1]

    def at(i):
        return lambda t: (jnp.clip(t - i * C, 0, C - 1), 0, 0)
    return pl.pallas_call(functools.partial(join_kernel, count=C),
        out_shape=jax.ShapeDtypeStruct((R, n * C * W + T), bf16),
        grid=(n * C + 1,),
        in_specs=[pl.BlockSpec((1, R, W), at(i)) for i in range(n)] + [pl.BlockSpec((R, T), lambda t: (0, 0))],
        out_specs=pl.BlockSpec((R, W), lambda t: (0, t)),
        compiler_params=pltpu.CompilerParams(vmem_limit_bytes=56 << 20),
        cost_estimate=pl.CostEstimate(flops=0, bytes_accessed=4 * R * (n * C * W + T), transcendentals=0),
    )(*stacks, tail)


def deal_kernel(x_ref, o_ref):
    o_ref[0] = x_ref[...]


def deal(x, first, C, W):
    R = x.shape[0]
    return pl.pallas_call(deal_kernel,
        out_shape=jax.ShapeDtypeStruct((C, R, W), bf16),
        grid=(C,),
        in_specs=[pl.BlockSpec((R, W), lambda t: (0, first + t))],
        out_specs=pl.BlockSpec((1, R, W), lambda t: (t, 0, 0)),
        compiler_params=pltpu.CompilerParams(vmem_limit_bytes=56 << 20),
        cost_estimate=pl.CostEstimate(flops=0, bytes_accessed=4 * R * C * W, transcendentals=0),
    )(x)


def gather_kernel(x_ref, o_ref, own_sem, zs, zr, xs, xr, cs, cr, *, Z, C, quarter):
    z, a, c = lax.axis_index("zz"), lax.axis_index("core"), lax.axis_index("ctx")
    mesh_id = pl.DeviceIdType.MESH
    other = 1 - a
    peers = [(lax.rem(z + k, Z), a, c) for k in range(1, Z)] + [(z, a, lax.rem(c + j, C)) for j in range(1, C)] + [(z, other, c)]
    barrier = pltpu.get_barrier_semaphore()
    for peer in peers:
        pl.semaphore_signal(barrier, inc=1, device_id=peer, device_id_type=mesh_id)
    pl.semaphore_wait(barrier, len(peers))

    f = 2 * z + a

    def cols(q):
        return pl.ds(pl.multiple_of(q * quarter, quarter), quarter)

    def send(src, dst, s, r, peer):
        copy = pltpu.make_async_remote_copy(src_ref=src, dst_ref=dst, send_sem=s, recv_sem=r, device_id=peer, device_id_type=mesh_id)
        copy.start()
        return copy

    along = []
    for k in range(1, Z):
        along.append(send(x_ref.at[:, cols(c)], o_ref.at[f, :, cols(c)], zs.at[k - 1], zr.at[k - 1], peers[k - 1]))
    own = pltpu.make_async_copy(x_ref, o_ref.at[f], own_sem)
    own.start()
    whole = send(x_ref, o_ref.at[f], cs.at[0], cr.at[0], peers[-1])
    plane, cross = [], []
    for k in range(1, Z):
        along[k - 1].wait_recv()
        fs = 2 * lax.rem(z + Z - k, Z) + a
        piece = o_ref.at[fs, :, cols(c)]
        for j in range(1, C):
            n = (k - 1) * (C - 1) + j - 1
            plane.append(send(piece, piece, xs.at[n], xr.at[n], peers[Z - 1 + j - 1]))
        n = 1 + (k - 1) * C
        cross.append(send(piece, piece, cs.at[n], cr.at[n], peers[-1]))
    for k in range(1, Z):
        fs = 2 * lax.rem(z + Z - k, Z) + a
        for j in range(1, C):
            plane[(k - 1) * (C - 1) + j - 1].wait_recv()
            piece = o_ref.at[fs, :, cols(lax.rem(c + C - j, C))]
            n = 1 + (k - 1) * C + j
            cross.append(send(piece, piece, cs.at[n], cr.at[n], peers[-1]))
    for copy in along + plane:
        copy.wait_send()
    whole.wait_send()
    whole.wait_recv()
    for copy in cross:
        copy.wait_send()
        copy.wait_recv()
    own.wait()


def gather_all(x, Z, C):
    R, W = x.shape
    dma = pltpu.SemaphoreType.DMA
    n, m = (Z - 1) * (C - 1), 1 + (Z - 1) * C
    return pl.pallas_call(functools.partial(gather_kernel, Z=Z, C=C, quarter=W // C),
        out_shape=jax.ShapeDtypeStruct((2 * Z, R, W), bf16),
        in_specs=[pl.BlockSpec(memory_space=pl.ANY)],
        out_specs=pl.BlockSpec(memory_space=pl.ANY),
        scratch_shapes=[dma(()), dma((Z - 1,)), dma((Z - 1,)), dma((n,)), dma((n,)), dma((m,)), dma((m,))],
        compiler_params=pltpu.CompilerParams(collective_id=0, has_side_effects=True, vmem_limit_bytes=56 << 20),
        cost_estimate=pl.CostEstimate(flops=0, bytes_accessed=20 * R * W * Z, transcendentals=0),
    )(x)


HEADS = 17
EPSILON = 1e-05
FS = ("zz", "core")


def norm_parts(v):
    mean = jnp.mean(v, axis=-1, keepdims=True)
    c = v - mean
    r = lax.rsqrt(jnp.mean(c * c, axis=-1, keepdims=True) + EPSILON)
    return c * r, r


def norm_back(dn, v, gain):
    xhat, r = norm_parts(v)
    y = dn * gain
    a = jnp.mean(y, axis=-1, keepdims=True)
    b = jnp.mean(y * xhat, axis=-1, keepdims=True)
    return r * (y - a - xhat * b), jnp.sum(dn * xhat, axis=0), jnp.sum(dn, axis=0)


def col_sum(x):
    return jnp.dot(jnp.ones((16, x.shape[0]), bf16), x, preferred_element_type=f32)[0]


def gelu_parts(u):
    z = jnp.abs(u) * 0.7071067811865476
    t = 1.0 / (1.0 + 0.3275911 * z)
    e = jnp.exp(-z * z)
    poly = t * (0.254829592 + t * (-0.284496736 + t * (1.421413741 + t * (-1.453152027 + t * 1.061405429))))
    half = 0.5 * poly * e
    cdf = jnp.where(u >= 0, 1.0 - half, half)
    return u * cdf, cdf + u * e * 0.3989422804014327


def local(
    tokens, cotangent, lengths, block_order,
    ln1_gain, ln1_bias, qkv_weight, q_bias, v_bias, out_weight, out_bias,
    ln2_gain, ln2_bias, up_weight, up_bias, down_weight, down_bias,
    *, G, S,
):
    slots, rows, width = tokens.shape
    C = lax.axis_size("ctx")
    me = lax.axis_index("ctx")
    N = rows * C
    B = rows // 2
    NB = 2 * C
    L = ln1_gain.shape[0]
    shard = ln1_gain.shape[1]
    HW = G * 128
    x_tokens = tokens[0]

    steps = jnp.arange(NB, dtype=jnp.int32)
    order = block_order[0]
    inverse = jnp.sum(jnp.where(order[None, :] == steps[:, None], steps[None, :], 0), axis=1).astype(jnp.int32)
    count = (lengths + (B - 1)) // B
    meta = jnp.concatenate([inverse, count])
    def swap(x):
        return lax.ppermute(x, "core", [(0, 1), (1, 0)])

    metas = [meta, swap(meta)][:S]
    phase_inv = [t[None, :NB] for t in metas]
    phase_nb = [t[NB:] for t in metas]
    own = jnp.concatenate([inverse, lax.dynamic_slice_in_dim(order, 2 * me, 2, 0), count])
    own_pos = (lax.dynamic_slice_in_dim(order, 2 * me, 2, 0)[:, None] * B + jnp.arange(B, dtype=jnp.int32)).reshape(rows, 1)
    live = (own_pos < lengths[0]).astype(f32)

    def pack(w):
        parts = []
        for g in range(G):
            parts += [w[:, kind * width + g * 128:kind * width + g * 128 + 128] for kind in range(3)]
        last = width - 64
        parts += [w[:, kind * width + last:kind * width + width] for kind in (1, 2, 0)]
        return jnp.concatenate(parts, axis=1)

    def unpack(w):
        tail = G * 384
        parts = []
        for kind, last in enumerate((128, 0, 64)):
            parts += [w[:, g * 384 + kind * 128:g * 384 + kind * 128 + 128] for g in range(G)]
            parts.append(w[:, tail + last:tail + last + 64])
        return jnp.concatenate(parts, axis=1)

    def fetch(w):
        return lax.all_gather(w.astype(bf16), FS, axis=0, tiled=True)

    vectors = [ln1_gain, ln1_bias, q_bias, v_bias, out_bias, ln2_gain, ln2_bias, down_bias]
    vec = [t.astype(bf16).T for t in vectors] + [up_bias.astype(bf16).reshape(4 * L, shard).T]
    first = pack(qkv_weight[0].astype(bf16))
    block = jnp.concatenate([first] + vec, axis=1)
    used = block.shape[1]
    if C == 4 and lax.axis_size("zz") == 4:
        block = jnp.pad(block, ((0, 0), (0, -used % (128 * C))))
        block = gather_all(block, 4, C)
    else:
        block = lax.all_gather(block, FS)
    first_w = block[:, :, :3 * width].reshape(width, 3 * width)
    vec = jnp.transpose(block[:, :, 3 * width:used].reshape(width, used - 3 * width)).astype(f32)

    def vector(index, layer):
        if index < 8:
            return vec[L * index + layer]
        t = vec[8 * L + 4 * layer:8 * L + 4 * layer + 4]
        return jnp.transpose(t.reshape(4, -1, shard), (1, 0, 2)).reshape(-1)

    weights = []
    for layer in range(L):
        weights.append((
            fetch(pack(qkv_weight[layer].astype(bf16))) if layer else first_w,
            fetch(out_weight[layer]),
            fetch(up_weight[layer]),
            fetch(down_weight[layer]),
        ))

    def plain(x):
        return with_layout_constraint(x, Layout(major_to_minor=tuple(range(x.ndim))))

    def exchange(x):
        return plain(lax.all_to_all(plain(x), "ctx", 0, 0))

    def after(x, *others):
        return lax.optimization_barrier((x,) + others)

    stream = x_tokens.astype(f32)
    records = []
    for layer in range(L):
        qkv_w, out_w, up_w, down_w = weights[layer]
        xhat, _ = norm_parts(stream)
        n1 = (xhat * vector(0, layer) + vector(1, layer)).astype(bf16)
        q_b, v_b = vector(2, layer), vector(3, layer)
        bias = pack(jnp.concatenate([q_b, jnp.zeros_like(q_b), v_b])[None])[0]
        projected = (jnp.dot(n1, qkv_w, preferred_element_type=f32) + bias).astype(bf16)
        wide = [deal(projected, s * C, C, 384) for s in range(S)]
        tail = projected[:, G * 384:]
        if S == 2:
            wide[1] = swap(wide[1])
        kv16 = jnp.broadcast_to(tail[None, :, :128], (C, rows, 128))
        q16 = tail[:, 128:]
        heads, o, lse, o_back = [], [], [], []
        for s in range(S):
            t = wide[s]
            if s == S - 1:
                t = jnp.concatenate([t, kv16], axis=2)
            if s:
                t, heads[0] = after(t, heads[0])
            heads.append(exchange(t).reshape(1, N, -1))
        for s in range(S):
            o_s, lse_s = flash_fwd(heads[s], phase_inv[s], phase_nb[s], B)
            o.append(o_s)
            lse.append(lse_s)
            t = o_s.reshape(C, rows, 128)
            if s:
                t, o_back[0] = after(t, o_back[0])
            o_back.append(exchange(swap(t) if s else t))
        o16, lse16 = one_fwd(q16, heads[-1][0], own, B)
        mixed = join(o_back, o16)
        m = stream + jnp.dot(mixed, out_w, preferred_element_type=f32) + vector(4, layer)
        xhat2, _ = norm_parts(m)
        n2 = (xhat2 * vector(5, layer) + vector(6, layer)).astype(bf16)
        u = jnp.dot(n2, up_w, preferred_element_type=f32) + vector(8, layer)
        a, slope = gelu_parts(u)
        a = a.astype(bf16)
        a, slope = after(a, slope.astype(bf16))
        records.append((stream, n1, heads, q16, o, lse, o16, lse16, mixed, m, n2, a, slope))
        if layer < L - 1:
            stream = m + jnp.dot(a, down_w, preferred_element_type=f32) + vector(7, layer)
    end_a, end_m, end_w, end_b = a, m, down_w, vector(7, L - 1)

    def reduce_fsdp(g):
        return lax.psum_scatter(g.astype(bf16), FS, scatter_dimension=0, tiled=True)

    def reduce_ctx(g):
        return lax.psum(g, "ctx").astype(f32)

    grad = cotangent[0].astype(f32) * live
    matrices = [None] * L
    fours = [None] * L
    ffns = [None] * L
    small = [None] * L

    def ctx_end(mine):
        return exchange(jnp.broadcast_to(mine[None], (C,) + mine.shape))

    def ctx_sum(shards):
        mine, sizes = ctx_begin(shards)
        return ctx_end(mine), sizes

    def ctx_begin(shards):
        pieces = []
        for t in shards:
            if t.shape[1] == width:
                pieces.append(t.reshape(C, -1, width))
            else:
                pieces.append(jnp.transpose(t.reshape(t.shape[0], C, -1), (1, 0, 2)).reshape(C, -1, width))
        sizes = [t.shape[1] for t in pieces]
        parts = exchange(jnp.concatenate(pieces, axis=1))
        mine = jnp.sum(parts.astype(f32), axis=0).astype(bf16)
        return mine, sizes

    def spread(summed, shapes):
        whole, sizes = summed
        out, at = [], 0
        for n, (r, c) in zip(sizes, shapes):
            t = whole[:, at:at + n].astype(f32)
            at += n
            if c == width:
                out.append(t.reshape(r, c))
            else:
                out.append(jnp.transpose(t.reshape(C, r, c // C), (1, 0, 2)).reshape(r, c))
        return out

    wide_shape, tall_shape = (shard, 4 * width), (4 * shard, width)
    for layer in reversed(range(L)):
        stream_in, n1, heads, q16, o, lse, o16, lse16, mixed, m, n2, a, slope = records[layer]
        qkv_w, out_w, up_w, down_w = weights[layer]
        gb = grad.astype(bf16)
        d_down_b = col_sum(gb)
        d_down = jnp.einsum("rf,rd->fd", a, gb, preferred_element_type=f32).astype(bf16)
        gb, d_down = after(gb, plain(d_down))
        if layer < L - 1:
            above = list(after(gb, *ffns[layer + 1]))
            gb = above.pop(0)
            mine_ffn, ffn_sizes = ctx_begin(above)
        d_down = reduce_fsdp(d_down)
        du = (jnp.einsum("rd,fd->rf", gb, down_w, preferred_element_type=f32) * slope.astype(f32)).astype(bf16)
        d_up_b = col_sum(du)
        if layer < L - 1:
            du, mine_ffn = after(du, mine_ffn)
            ffn_whole = ctx_end(mine_ffn)
        d_up = jnp.einsum("rd,rf->df", n2, du, preferred_element_type=f32).astype(bf16)
        du, d_up = after(du, plain(d_up))
        d_up = reduce_fsdp(d_up)
        dn2 = jnp.einsum("rf,df->rd", du, up_w, preferred_element_type=f32)
        back, d_gain2, d_bias2 = norm_back(dn2, m, vector(5, layer))
        gm = grad + back
        gmb = gm.astype(bf16)
        d_out_b = col_sum(gmb)
        d_out = jnp.einsum("rd,re->de", mixed, gmb, preferred_element_type=f32).astype(bf16)
        if layer == 0:
            gmb, d_out = after(gmb, plain(d_out))
        if layer < L - 1:
            gmb, ffn_whole = after(gmb, ffn_whole)
        d_o = []
        for s in range(S):
            w = out_w[C * 128 * s:C * 128 * (s + 1)].reshape(C, 128, width)
            d_o.append(jnp.einsum("re,gce->grc", gmb, w, preferred_element_type=f32).astype(bf16))
        d_o16 = jnp.einsum("re,ce->rc", gmb, out_w[HW:], preferred_element_type=f32).astype(bf16)
        dq16, dkv16 = one_bwd(q16, heads[-1][0], o16, d_o16, lse16, own, B)
        d_oh, d_wide = [], []
        for s in range(S):
            t = d_o[s]
            if s:
                t = swap(t)
            if s == S - 1:
                t = jnp.concatenate([t, dkv16.reshape(C, rows, 128)], axis=2)
            if s:
                t, d_oh[0] = after(t, d_oh[0])
            if s == S - 1 and layer < L - 1:
                t, fours[layer + 1] = after(t, fours[layer + 1])
            d_oh.append(exchange(t).reshape(1, N, -1))
        dkv16 = jnp.sum(d_oh[-1].reshape(C, rows, 256)[:, :, 128:].astype(f32), axis=0)
        for s in range(S):
            t = flash_bwd(heads[s], o[s], d_oh[s], lse[s], phase_inv[s], phase_nb[s], B)
            t = t.reshape(C, rows, 384)
            if s:
                t, d_wide[0] = after(t, d_wide[0])
            if s == S - 1:
                t, d_down = after(t, d_down)
            if s == S - 1 and layer:
                t, d_up = after(t, d_up)
            d_wide.append(exchange(swap(t) if s else t))
        d_tail = jnp.concatenate([dkv16.astype(bf16), dq16], axis=1)
        d_row = join(d_wide, d_tail)
        d_row, d_down_b, d_up_b, d_out_b = after(d_row, d_down_b, d_up_b, d_out_b)
        d_back = d_row
        if layer == 0:
            d_row, d_up = after(d_row, d_up)
            mine, middle_sizes = ctx_begin([fours[1], d_up, d_down])
            d_back, mine = after(d_row, mine)
            end_a, mine = after(end_a, mine)
            middle = ctx_end(mine)
        d_qkv = jnp.einsum("rd,rc->dc", n1, d_row, preferred_element_type=f32).astype(bf16)
        if layer:
            d_row, d_four = after(d_row, plain(jnp.concatenate([d_qkv, d_out], axis=1)))
            d_four = reduce_fsdp(d_four)
        else:
            d_qkv, d_out = after(d_qkv, reduce_fsdp(d_out))
            d_four = jnp.concatenate([reduce_fsdp(d_qkv), d_out], axis=1)
        sums = unpack(col_sum(d_row)[None])[0]
        dn1 = jnp.einsum("rc,dc->rd", d_back, qkv_w, preferred_element_type=f32)
        back, d_gain1, d_bias1 = norm_back(dn1, stream_in, vector(0, layer))
        grad = gm + back
        fours[layer] = d_four
        ffns[layer] = (d_up, d_down)
        small[layer] = jnp.concatenate([
            t.reshape(-1, n) for t, n in (
                (d_gain1, shard), (d_bias1, shard), (sums[:width], shard), (sums[2 * width:], shard), (d_out_b, shard),
                (d_gain2, shard), (d_bias2, shard), (d_down_b, shard), (d_up_b, 4 * shard))], axis=1)

    vec_grads = jnp.stack(small, axis=1)
    stream = end_m + jnp.dot(end_a, end_w, preferred_element_type=f32) + end_b
    activations = (stream * live).astype(bf16)[None]
    vec_grads, middle, activations = after(vec_grads, middle, activations)
    vec_grads = jnp.sum(lax.all_to_all(vec_grads, FS, 0, 0), axis=0)
    vec_grads = jnp.sum(lax.all_to_all(jnp.broadcast_to(vec_grads[None], (C,) + vec_grads.shape), "ctx", 0, 0), axis=0)
    end, vec_grads = after(fours[0], vec_grads)
    rest = spread((middle, middle_sizes), [wide_shape, wide_shape, tall_shape]) + spread(ctx_sum([end]), [wide_shape])
    matrices[1] = [rest[0]] + spread((ffn_whole, ffn_sizes), [wide_shape, tall_shape])
    matrices[0] = [rest[3], rest[1], rest[2]]
    vg = [vec_grads[:, i * shard:(i + 1) * shard] for i in range(8)] + [vec_grads[:, 8 * shard:]]

    g_qkv = jnp.stack([unpack(matrices[layer][0][:, :3 * width]) for layer in range(L)])
    g_out = jnp.stack([matrices[layer][0][:, 3 * width:] for layer in range(L)])
    g_up = jnp.stack([matrices[layer][1] for layer in range(L)])
    g_down = jnp.stack([matrices[layer][2] for layer in range(L)])
    return (activations, grad[None], vg[0], vg[1], g_qkv, vg[2], vg[3], g_out, vg[4], vg[5], vg[6], g_up, vg[8], g_down, vg[7])


def solution(mesh):
    F, C = mesh.devices.shape
    inner = Mesh(mesh.devices.reshape(F // 2, 2, C), ("zz", "core", "ctx"))
    S = 2 if 16 // (2 * C) >= 2 else 1
    G = S * C
    rows = P(FS, "ctx", None)
    vec, mat = P(None, FS), P(None, FS, None)
    return jax.shard_map(
        functools.partial(local, G=G, S=S),
        mesh=inner,
        in_specs=(rows, rows, P(FS), P(FS, None), vec, vec, mat, vec, vec, mat, vec, vec, vec, mat, vec, mat, vec),
        out_specs=(rows, rows, vec, vec, mat, vec, vec, mat, vec, vec, vec, mat, vec, mat, vec),
        check_vma=False,
    )
```

```python
import functools
import jax, jax.numpy as jnp
from jax import lax
from jax.experimental import pallas as pl
from jax.experimental.pallas import tpu as pltpu
from jax.experimental.layout import Layout, with_layout_constraint
from jax.sharding import Mesh, PartitionSpec as P
f32=jnp.float32; bf16=jnp.bfloat16
NEG=-1e30
def dot_nt(a,b): return lax.dot_general(a,b,(((1,),(1,)),((),())),preferred_element_type=f32)
def dot_nn(a,b): return lax.dot_general(a,b,(((1,),(0,)),((),())),preferred_element_type=f32)

LOG2E=1.4426950408889634
def split(q,h,low):
    qs=q.astype(f32)*(0.125*LOG2E)
    hi=qs.astype(bf16).astype(f32); lo=qs-hi
    rl=pltpu.roll(lo,64,1)
    c=jnp.where(low,hi,rl) if h==0 else jnp.where(low,rl,hi)
    return c.astype(bf16)
def dup(k,h,low):
    kf=k.astype(f32); rl=pltpu.roll(kf,64,1)
    c=jnp.where(low,kf,rl) if h==0 else jnp.where(low,rl,kf)
    return c.astype(bf16)
def fwd_kernel(inv_ref, nb_ref, x_ref, o_ref, lse_ref, vt, kd, sb, acc, *, B, NB):
    s=pl.program_id(0)
    nb=nb_ref[s]
    lane=lax.broadcasted_iota(jnp.int32,(1,128),1)
    low=lane<64
    def tv(j,_):
        r=pl.multiple_of(inv_ref[s,j]*B,B)
        w=pl.multiple_of(j*B,B)
        t=x_ref[0,pl.ds(r,B),256:384].T
        one=(lax.broadcasted_iota(jnp.int32,(16,B),0)==0).astype(bf16)
        for h in range(2):
            vt[80*h:80*h+64,pl.ds(w,B)]=t[64*h:64*h+64,:]
            vt[80*h+64:80*h+80,pl.ds(w,B)]=one
            kd[h,pl.ds(w,B),:]=dup(x_ref[0,pl.ds(r,B),128:256],h,low)
        return 0
    lax.fori_loop(0,nb,tv,0)
    rr=lax.broadcasted_iota(jnp.int32,(B,B),0)
    cc=lax.broadcasted_iota(jnp.int32,(B,B),1)
    def qblock(i,_):
        r=pl.multiple_of(inv_ref[s,i]*B,B)
        q=x_ref[0,pl.ds(r,B),0:128]
        qh=[split(q,h,low) for h in range(2)]
        acc[...]=jnp.zeros_like(acc)
        def scores(j,slot):
            for h in range(2):
                sb[slot,h]=dot_nt(kd[h,pl.ds(pl.multiple_of(j*B,B),B),:],qh[h])
        def step(j,carry,diag):
            out=[]
            for h in range(2):
                m=carry[h]
                st=sb[j%2,h]
                if diag: st=jnp.where(rr<=cc,st,NEG)
                mn=jnp.maximum(m,jnp.max(st,axis=0,keepdims=True))
                p=jnp.exp2(st-mn)
                al=jnp.exp2(m-mn)
                v=vt[80*h:80*h+80,pl.ds(pl.multiple_of(j*B,B),B)]
                acc[h]=acc[h]*al+dot_nn(v,p.astype(bf16))
                out.append(mn)
            return tuple(out)
        scores(0,0)
        def both(j,c):
            scores(j+1,(j+1)%2)
            return step(j,c,False)
        n=jnp.full((1,B),NEG,f32)
        c=lax.fori_loop(0,i,both,(n,n))
        c=step(i,c,True)
        os=[]
        for h in range(2):
            l=acc[h,64:65,:]
            os.append(acc[h,0:64,:]*(1.0/l))
            lse_ref[0,pl.ds(h,1),pl.ds(r,B)]=c[h]+jnp.log2(l)
        o_ref[0,pl.ds(r,B),:]=jnp.concatenate(os,0).T.astype(bf16)
        return 0
    lax.fori_loop(0,nb,qblock,0)
    def pad(i,_):
        r=pl.multiple_of(inv_ref[s,i]*B,B)
        o_ref[0,pl.ds(r,B),:]=jnp.zeros((B,128),bf16)
        lse_ref[0,:,pl.ds(r,B)]=jnp.zeros((8,B),f32)
        return 0
    lax.fori_loop(nb,NB,pad,0)

def flash_fwd(x,inv,nb,B):
    S,N,_=x.shape
    NB=N//B
    return pl.pallas_call(functools.partial(fwd_kernel,B=B,NB=NB),
      out_shape=(jax.ShapeDtypeStruct((S,N,128),bf16),jax.ShapeDtypeStruct((S,8,N),f32)),
      grid_spec=pltpu.PrefetchScalarGridSpec(num_scalar_prefetch=2,grid=(S,),
        in_specs=[pl.BlockSpec((1,N,384),lambda s,*_:(s,0,0))],
        out_specs=[pl.BlockSpec((1,N,128),lambda s,*_:(s,0,0)),pl.BlockSpec((1,8,N),lambda s,*_:(s,0,0))],
        scratch_shapes=[pltpu.VMEM((160,N),bf16),pltpu.VMEM((2,N,128),bf16),pltpu.VMEM((2,2,B,B),f32),pltpu.VMEM((2,80,B),f32)]),
      compiler_params=pltpu.CompilerParams(vmem_limit_bytes=48<<20),
      cost_estimate=pl.CostEstimate(flops=S*4*N*N*128,bytes_accessed=S*N*1024,transcendentals=S*N*N),
      )(inv,nb,x)

def bwd_kernel(inv_ref, nb_ref, x_ref, o_ref, do_ref, lse_ref, dx_ref, kt, qd, dq, dk, dv, dl, *, B, NB):
    s=pl.program_id(0)
    nb=nb_ref[s]
    lane=lax.broadcasted_iota(jnp.int32,(1,128),1)
    low=lane<64
    hm=(lax.broadcasted_iota(jnp.int32,(8,128),1)//64==lax.broadcasted_iota(jnp.int32,(8,128),0)).astype(bf16)
    def prep(j,_):
        r=pl.multiple_of(inv_ref[s,j]*B,B)
        w=pl.multiple_of(j*B,B)
        kt[:,pl.ds(w,B)]=x_ref[0,pl.ds(r,B),128:256].T
        for h in range(2): qd[h,pl.ds(w,B),:]=split(x_ref[0,pl.ds(r,B),0:128],h,low)
        prod=o_ref[0,pl.ds(r,B),:].astype(f32)*do_ref[0,pl.ds(r,B),:].astype(f32)
        hi=prod.astype(bf16); lo=(prod-hi.astype(f32)).astype(bf16)
        dl[:,pl.ds(w,B)]=dot_nt(hm,hi)+dot_nt(hm,lo)
        dq[:,pl.ds(w,B)]=jnp.zeros((128,B),f32)
        return 0
    lax.fori_loop(0,nb,prep,0)
    rr=lax.broadcasted_iota(jnp.int32,(B,B),0)
    cc=lax.broadcasted_iota(jnp.int32,(B,B),1)
    def kblock(j,_):
        r=pl.multiple_of(inv_ref[s,j]*B,B)
        k=x_ref[0,pl.ds(r,B),128:256]
        v=x_ref[0,pl.ds(r,B),256:384]
        kdh=[dup(k,h,low) for h in range(2)]
        dk[...]=jnp.zeros_like(dk); dv[...]=jnp.zeros_like(dv)
        def step(i,diag):
            ri=pl.multiple_of(inv_ref[s,i]*B,B)
            wi=pl.multiple_of(i*B,B)
            q=x_ref[0,pl.ds(ri,B),0:128]*jnp.asarray(0.125,bf16)
            do=do_ref[0,pl.ds(ri,B),:]
            zero=jnp.zeros_like(q)
            dvs=[];dks=[]
            for h in range(2):
                qh=jnp.where(low,q,zero) if h==0 else jnp.where(low,zero,q)
                doh=jnp.where(low,do,zero) if h==0 else jnp.where(low,zero,do)
                st=dot_nt(kdh[h],qd[h,pl.ds(wi,B),:])
                p=jnp.exp2(st-lse_ref[0,pl.ds(h,1),pl.ds(ri,B)])
                if diag: p=jnp.where(rr<=cc,p,0.0)
                dvs.append(dot_nn(p.astype(bf16),doh))
                dp=dot_nt(v,doh)
                ds=(p*(dp-dl[pl.ds(h,1),pl.ds(wi,B)])).astype(bf16)
                dks.append(dot_nn(ds,qh))
                kh=kt[64*h:64*h+64,pl.ds(pl.multiple_of(j*B,B),B)]
                dq[64*h:64*h+64,pl.ds(wi,B)]+=dot_nn(kh,ds)
            dv[...]+=dvs[0]+dvs[1]
            dk[...]+=dks[0]+dks[1]
        step(j,True)
        def body(i,_):
            step(i,False); return 0
        lax.fori_loop(j+1,nb,body,0)
        dx_ref[0,pl.ds(r,B),128:256]=dk[...].astype(bf16)
        dx_ref[0,pl.ds(r,B),256:384]=dv[...].astype(bf16)
        return 0
    lax.fori_loop(0,nb,kblock,0)
    def fin(i,_):
        r=pl.multiple_of(inv_ref[s,i]*B,B)
        dx_ref[0,pl.ds(r,B),0:128]=(dq[:,pl.ds(pl.multiple_of(i*B,B),B)].T*0.125).astype(bf16)
        return 0
    lax.fori_loop(0,nb,fin,0)
    def pad(i,_):
        r=pl.multiple_of(inv_ref[s,i]*B,B)
        dx_ref[0,pl.ds(r,B),:]=jnp.zeros((B,384),bf16)
        return 0
    lax.fori_loop(nb,NB,pad,0)

def flash_bwd(x,o,do,lse,inv,nb,B):
    S,N,_=x.shape
    NB=N//B
    return pl.pallas_call(functools.partial(bwd_kernel,B=B,NB=NB),
      out_shape=jax.ShapeDtypeStruct((S,N,384),bf16),
      grid_spec=pltpu.PrefetchScalarGridSpec(num_scalar_prefetch=2,grid=(S,),
        in_specs=[pl.BlockSpec((1,N,384),lambda s,*_:(s,0,0)),pl.BlockSpec((1,N,128),lambda s,*_:(s,0,0)),
                  pl.BlockSpec((1,N,128),lambda s,*_:(s,0,0)),pl.BlockSpec((1,8,N),lambda s,*_:(s,0,0))],
        out_specs=pl.BlockSpec((1,N,384),lambda s,*_:(s,0,0)),
        scratch_shapes=[pltpu.VMEM((128,N),bf16),pltpu.VMEM((2,N,128),bf16),pltpu.VMEM((128,N),f32),pltpu.VMEM((B,128),f32),pltpu.VMEM((B,128),f32),pltpu.VMEM((8,N),f32)]),
      compiler_params=pltpu.CompilerParams(vmem_limit_bytes=48<<20),
      cost_estimate=pl.CostEstimate(flops=S*10*N*N*128,bytes_accessed=S*N*2400,transcendentals=S*N*N),
      )(inv,nb,x,o,do,lse)


def one_fwd_kernel(own_ref, q_ref, x_ref, o_ref, lse_ref, vt, kd, acc, *, B, NB):
    nb = own_ref[NB + 2]
    low = lax.broadcasted_iota(jnp.int32,(1,128),1)<64
    def tv(j,_):
        r=pl.multiple_of(own_ref[j]*B,B)
        t=x_ref[pl.ds(r,B),:].T
        w=pl.multiple_of(j*B,B)
        kd[pl.ds(w,B),:]=dup(x_ref[pl.ds(r,B),:],0,low)
        vt[0:64,pl.ds(w,B)]=t[64:128,:]
        vt[64:80,pl.ds(w,B)]=(lax.broadcasted_iota(jnp.int32,(16,B),0)==0).astype(bf16)
        return 0
    lax.fori_loop(0,nb,tv,0)
    rr=lax.broadcasted_iota(jnp.int32,(B,B),0)
    cc=lax.broadcasted_iota(jnp.int32,(B,B),1)
    for t in range(2):
        i=own_ref[NB+t]
        @pl.when(i>=nb)
        def _():
            o_ref[t*B:(t+1)*B,:]=jnp.zeros((B,64),bf16)
            lse_ref[:,t*B:(t+1)*B]=jnp.zeros((8,B),f32)
        @pl.when(i<nb)
        def _():
            qs=q_ref[t*B:(t+1)*B,:].astype(f32)*(0.125*LOG2E)
            hi=qs.astype(bf16)
            q=jnp.concatenate([hi.astype(f32),qs-hi.astype(f32)],axis=1).astype(bf16)
            acc[...]=jnp.zeros_like(acc)
            def step(j,m,diag):
                st=dot_nt(kd[pl.ds(pl.multiple_of(j*B,B),B),:],q)
                if diag: st=jnp.where(rr<=cc,st,NEG)
                mn=jnp.maximum(m,jnp.max(st,axis=0,keepdims=True))
                p=jnp.exp2(st-mn)
                al=jnp.exp2(m-mn)
                v=vt[:,pl.ds(pl.multiple_of(j*B,B),B)]
                acc[...]=acc[...]*al+dot_nn(v,p.astype(bf16))
                return mn
            m=lax.fori_loop(0,i,lambda j,m: step(j,m,False),jnp.full((1,B),NEG,f32))
            m=step(i,m,True)
            l=acc[64:65,:]
            o_ref[t*B:(t+1)*B,:]=(acc[0:64,:]*(1.0/l)).T.astype(bf16)
            lse_ref[:,t*B:(t+1)*B]=jnp.broadcast_to(m+jnp.log2(l),(8,B))


def one_fwd(q,x,own,B):
    N=x.shape[0]; R=q.shape[0]; NB=N//B
    full=lambda *_:(0,0)
    last=lambda *_:(0,3)
    return pl.pallas_call(functools.partial(one_fwd_kernel,B=B,NB=NB),
      out_shape=(jax.ShapeDtypeStruct((R,64),bf16),jax.ShapeDtypeStruct((8,R),f32)),
      grid_spec=pltpu.PrefetchScalarGridSpec(num_scalar_prefetch=1,grid=(1,),
        in_specs=[pl.BlockSpec((R,64),full),pl.BlockSpec((N,128),last)],
        out_specs=[pl.BlockSpec((R,64),full),pl.BlockSpec((8,R),full)],
        scratch_shapes=[pltpu.VMEM((80,N),bf16),pltpu.VMEM((N,128),bf16),pltpu.VMEM((80,B),f32)]),
      compiler_params=pltpu.CompilerParams(vmem_limit_bytes=48<<20),
      cost_estimate=pl.CostEstimate(flops=4*R*N*128,bytes_accessed=N*256+R*512,transcendentals=R*N),
      )(own,q,x)


def one_bwd_kernel(own_ref, q_ref, x_ref, o_ref, do_ref, lse_ref, dq_ref, dx_ref, dkv, dq, *, B, NB):
    nb = own_ref[NB + 2]
    low = lax.broadcasted_iota(jnp.int32,(1,128),1)<64
    rr=lax.broadcasted_iota(jnp.int32,(B,B),0)
    cc=lax.broadcasted_iota(jnp.int32,(B,B),1)
    ones=jnp.ones((8,64),bf16)
    dkv[...]=jnp.zeros_like(dkv)
    for t in range(2):
        i=own_ref[NB+t]
        sl=slice(t*B,(t+1)*B)
        @pl.when(i>=nb)
        def _():
            dq_ref[sl,:]=jnp.zeros((B,64),bf16)
        @pl.when(i<nb)
        def _():
            qr=q_ref[sl,:]
            qs=qr.astype(f32)*(0.125*LOG2E)
            hi=qs.astype(bf16)
            q=jnp.concatenate([hi.astype(f32),qs-hi.astype(f32)],axis=1).astype(bf16)
            qd=qr*jnp.asarray(0.125,bf16)
            do=do_ref[sl,:]
            prod=o_ref[sl,:].astype(f32)*do.astype(f32)
            hi=prod.astype(bf16); lo=(prod-hi.astype(f32)).astype(bf16)
            dl=(dot_nt(ones,hi)+dot_nt(ones,lo))[0:1,:]
            lse=lse_ref[0:1,sl]
            dq[...]=jnp.zeros_like(dq)
            def step(j,diag):
                r=pl.multiple_of(own_ref[j]*B,B)
                k=x_ref[pl.ds(r,B),0:64]
                v=x_ref[pl.ds(r,B),64:128]
                st=dot_nt(dup(x_ref[pl.ds(r,B),:],0,low),q)
                p=jnp.exp2(st-lse)
                if diag: p=jnp.where(rr<=cc,p,0.0)
                dp=dot_nt(v,do)
                ds=(p*(dp-dl)).astype(bf16)
                dkv[pl.ds(r,B),64:128]+=dot_nn(p.astype(bf16),do)
                dkv[pl.ds(r,B),0:64]+=dot_nn(ds,qd)
                dq[...]+=dot_nn(k.T,ds)
            def body(j,_):
                step(j,False); return 0
            lax.fori_loop(0,i,body,0)
            step(i,True)
            dq_ref[sl,:]=(dq[...].T*0.125).astype(bf16)
    dx_ref[...]=dkv[...].astype(bf16)


def one_bwd(q,x,o,do,lse,own,B):
    N=x.shape[0]; R=q.shape[0]; NB=N//B
    full=lambda *_:(0,0)
    last=lambda *_:(0,3)
    return pl.pallas_call(functools.partial(one_bwd_kernel,B=B,NB=NB),
      out_shape=(jax.ShapeDtypeStruct((R,64),bf16),jax.ShapeDtypeStruct((N,128),bf16)),
      grid_spec=pltpu.PrefetchScalarGridSpec(num_scalar_prefetch=1,grid=(1,),
        in_specs=[pl.BlockSpec((R,64),full),pl.BlockSpec((N,128),last),pl.BlockSpec((R,64),full),pl.BlockSpec((R,64),full),pl.BlockSpec((8,R),full)],
        out_specs=[pl.BlockSpec((R,64),full),pl.BlockSpec((N,128),full)],
        scratch_shapes=[pltpu.VMEM((N,128),f32),pltpu.VMEM((64,B),f32)]),
      compiler_params=pltpu.CompilerParams(vmem_limit_bytes=48<<20),
      cost_estimate=pl.CostEstimate(flops=10*R*N*128,bytes_accessed=N*512+R*1024,transcendentals=R*N),
      )(own,q,x,o,do,lse)


def join_kernel(*refs, count):
    t = pl.program_id(0)
    stacks, tail, out = refs[:-2], refs[-2], refs[-1]
    for i, ref in enumerate(stacks):
        @pl.when((t >= i * count) & (t < (i + 1) * count))
        def _(ref=ref):
            out[...] = ref[0]

    @pl.when(t >= len(stacks) * count)
    def _():
        out[:, :tail.shape[1]] = tail[...]


def join(stacks, tail):
    C, R, W = stacks[0].shape
    n = len(stacks)
    T = tail.shape[1]

    def at(i):
        return lambda t: (jnp.clip(t - i * C, 0, C - 1), 0, 0)
    return pl.pallas_call(functools.partial(join_kernel, count=C),
        out_shape=jax.ShapeDtypeStruct((R, n * C * W + T), bf16),
        grid=(n * C + 1,),
        in_specs=[pl.BlockSpec((1, R, W), at(i)) for i in range(n)] + [pl.BlockSpec((R, T), lambda t: (0, 0))],
        out_specs=pl.BlockSpec((R, W), lambda t: (0, t)),
        compiler_params=pltpu.CompilerParams(vmem_limit_bytes=56 << 20),
        cost_estimate=pl.CostEstimate(flops=0, bytes_accessed=4 * R * (n * C * W + T), transcendentals=0),
    )(*stacks, tail)


def deal_kernel(x_ref, o_ref):
    o_ref[0] = x_ref[...]


def deal(x, first, C, W):
    R = x.shape[0]
    return pl.pallas_call(deal_kernel,
        out_shape=jax.ShapeDtypeStruct((C, R, W), bf16),
        grid=(C,),
        in_specs=[pl.BlockSpec((R, W), lambda t: (0, first + t))],
        out_specs=pl.BlockSpec((1, R, W), lambda t: (t, 0, 0)),
        compiler_params=pltpu.CompilerParams(vmem_limit_bytes=56 << 20),
        cost_estimate=pl.CostEstimate(flops=0, bytes_accessed=4 * R * C * W, transcendentals=0),
    )(x)


def gather_kernel(x_ref, o_ref, own_sem, zs, zr, xs, xr, cs, cr, *, Z, C, quarter):
    z, a, c = lax.axis_index("zz"), lax.axis_index("core"), lax.axis_index("ctx")
    mesh_id = pl.DeviceIdType.MESH
    other = 1 - a
    peers = [(lax.rem(z + k, Z), a, c) for k in range(1, Z)] + [(z, a, lax.rem(c + j, C)) for j in range(1, C)] + [(z, other, c)]
    barrier = pltpu.get_barrier_semaphore()
    for peer in peers:
        pl.semaphore_signal(barrier, inc=1, device_id=peer, device_id_type=mesh_id)
    pl.semaphore_wait(barrier, len(peers))

    f = 2 * z + a

    def cols(q):
        return pl.ds(pl.multiple_of(q * quarter, quarter), quarter)

    def send(src, dst, s, r, peer):
        copy = pltpu.make_async_remote_copy(src_ref=src, dst_ref=dst, send_sem=s, recv_sem=r, device_id=peer, device_id_type=mesh_id)
        copy.start()
        return copy

    along = []
    for k in range(1, Z):
        along.append(send(x_ref.at[:, cols(c)], o_ref.at[f, :, cols(c)], zs.at[k - 1], zr.at[k - 1], peers[k - 1]))
    own = pltpu.make_async_copy(x_ref, o_ref.at[f], own_sem)
    own.start()
    whole = send(x_ref, o_ref.at[f], cs.at[0], cr.at[0], peers[-1])
    plane, cross = [], []
    for k in range(1, Z):
        along[k - 1].wait_recv()
        fs = 2 * lax.rem(z + Z - k, Z) + a
        piece = o_ref.at[fs, :, cols(c)]
        for j in range(1, C):
            n = (k - 1) * (C - 1) + j - 1
            plane.append(send(piece, piece, xs.at[n], xr.at[n], peers[Z - 1 + j - 1]))
        n = 1 + (k - 1) * C
        cross.append(send(piece, piece, cs.at[n], cr.at[n], peers[-1]))
    for k in range(1, Z):
        fs = 2 * lax.rem(z + Z - k, Z) + a
        for j in range(1, C):
            plane[(k - 1) * (C - 1) + j - 1].wait_recv()
            piece = o_ref.at[fs, :, cols(lax.rem(c + C - j, C))]
            n = 1 + (k - 1) * C + j
            cross.append(send(piece, piece, cs.at[n], cr.at[n], peers[-1]))
    for copy in along + plane:
        copy.wait_send()
    whole.wait_send()
    whole.wait_recv()
    for copy in cross:
        copy.wait_send()
        copy.wait_recv()
    own.wait()


def gather_all(x, Z, C):
    R, W = x.shape
    dma = pltpu.SemaphoreType.DMA
    n, m = (Z - 1) * (C - 1), 1 + (Z - 1) * C
    return pl.pallas_call(functools.partial(gather_kernel, Z=Z, C=C, quarter=W // C),
        out_shape=jax.ShapeDtypeStruct((2 * Z, R, W), bf16),
        in_specs=[pl.BlockSpec(memory_space=pl.ANY)],
        out_specs=pl.BlockSpec(memory_space=pl.ANY),
        scratch_shapes=[dma(()), dma((Z - 1,)), dma((Z - 1,)), dma((n,)), dma((n,)), dma((m,)), dma((m,))],
        compiler_params=pltpu.CompilerParams(collective_id=0, has_side_effects=True, vmem_limit_bytes=56 << 20),
        cost_estimate=pl.CostEstimate(flops=0, bytes_accessed=20 * R * W * Z, transcendentals=0),
    )(x)


def join_kernel(*refs, count):
    t = pl.program_id(0)
    stacks, tail, out = refs[:-2], refs[-2], refs[-1]
    for i, ref in enumerate(stacks):
        @pl.when((t >= i * count) & (t < (i + 1) * count))
        def _(ref=ref):
            out[...] = ref[0]

    @pl.when(t >= len(stacks) * count)
    def _():
        out[:, :tail.shape[1]] = tail[...]


def join(stacks, tail):
    C, R, W = stacks[0].shape
    n = len(stacks)
    T = tail.shape[1]

    def at(i):
        return lambda t: (jnp.clip(t - i * C, 0, C - 1), 0, 0)
    return pl.pallas_call(functools.partial(join_kernel, count=C),
        out_shape=jax.ShapeDtypeStruct((R, n * C * W + T), bf16),
        grid=(n * C + 1,),
        in_specs=[pl.BlockSpec((1, R, W), at(i)) for i in range(n)] + [pl.BlockSpec((R, T), lambda t: (0, 0))],
        out_specs=pl.BlockSpec((R, W), lambda t: (0, t)),
        compiler_params=pltpu.CompilerParams(vmem_limit_bytes=56 << 20),
        cost_estimate=pl.CostEstimate(flops=0, bytes_accessed=4 * R * (n * C * W + T), transcendentals=0),
    )(*stacks, tail)


def deal_kernel(x_ref, o_ref):
    o_ref[0] = x_ref[...]


def deal(x, first, C, W):
    R = x.shape[0]
    return pl.pallas_call(deal_kernel,
        out_shape=jax.ShapeDtypeStruct((C, R, W), bf16),
        grid=(C,),
        in_specs=[pl.BlockSpec((R, W), lambda t: (0, first + t))],
        out_specs=pl.BlockSpec((1, R, W), lambda t: (t, 0, 0)),
        compiler_params=pltpu.CompilerParams(vmem_limit_bytes=56 << 20),
        cost_estimate=pl.CostEstimate(flops=0, bytes_accessed=4 * R * C * W, transcendentals=0),
    )(x)


def gather_kernel(x_ref, o_ref, own_sem, zs, zr, xs, xr, cs, cr, *, Z, C, quarter):
    z, a, c = lax.axis_index("zz"), lax.axis_index("core"), lax.axis_index("ctx")
    mesh_id = pl.DeviceIdType.MESH
    other = 1 - a
    peers = [(lax.rem(z + k, Z), a, c) for k in range(1, Z)] + [(z, a, lax.rem(c + j, C)) for j in range(1, C)] + [(z, other, c)]
    barrier = pltpu.get_barrier_semaphore()
    for peer in peers:
        pl.semaphore_signal(barrier, inc=1, device_id=peer, device_id_type=mesh_id)
    pl.semaphore_wait(barrier, len(peers))

    f = 2 * z + a

    def cols(q):
        return pl.ds(pl.multiple_of(q * quarter, quarter), quarter)

    def send(src, dst, s, r, peer):
        copy = pltpu.make_async_remote_copy(src_ref=src, dst_ref=dst, send_sem=s, recv_sem=r, device_id=peer, device_id_type=mesh_id)
        copy.start()
        return copy

    along = []
    for k in range(1, Z):
        along.append(send(x_ref.at[:, cols(c)], o_ref.at[f, :, cols(c)], zs.at[k - 1], zr.at[k - 1], peers[k - 1]))
    own = pltpu.make_async_copy(x_ref, o_ref.at[f], own_sem)
    own.start()
    whole = send(x_ref, o_ref.at[f], cs.at[0], cr.at[0], peers[-1])
    plane, cross = [], []
    for k in range(1, Z):
        along[k - 1].wait_recv()
        fs = 2 * lax.rem(z + Z - k, Z) + a
        piece = o_ref.at[fs, :, cols(c)]
        for j in range(1, C):
            n = (k - 1) * (C - 1) + j - 1
            plane.append(send(piece, piece, xs.at[n], xr.at[n], peers[Z - 1 + j - 1]))
        n = 1 + (k - 1) * C
        cross.append(send(piece, piece, cs.at[n], cr.at[n], peers[-1]))
    for k in range(1, Z):
        fs = 2 * lax.rem(z + Z - k, Z) + a
        for j in range(1, C):
            plane[(k - 1) * (C - 1) + j - 1].wait_recv()
            piece = o_ref.at[fs, :, cols(lax.rem(c + C - j, C))]
            n = 1 + (k - 1) * C + j
            cross.append(send(piece, piece, cs.at[n], cr.at[n], peers[-1]))
    for copy in along + plane:
        copy.wait_send()
    whole.wait_send()
    whole.wait_recv()
    for copy in cross:
        copy.wait_send()
        copy.wait_recv()
    own.wait()


def gather_all(x, Z, C):
    R, W = x.shape
    dma = pltpu.SemaphoreType.DMA
    n, m = (Z - 1) * (C - 1), 1 + (Z - 1) * C
    return pl.pallas_call(functools.partial(gather_kernel, Z=Z, C=C, quarter=W // C),
        out_shape=jax.ShapeDtypeStruct((2 * Z, R, W), bf16),
        in_specs=[pl.BlockSpec(memory_space=pl.ANY)],
        out_specs=pl.BlockSpec(memory_space=pl.ANY),
        scratch_shapes=[dma(()), dma((Z - 1,)), dma((Z - 1,)), dma((n,)), dma((n,)), dma((m,)), dma((m,))],
        compiler_params=pltpu.CompilerParams(collective_id=0, has_side_effects=True, vmem_limit_bytes=56 << 20),
        cost_estimate=pl.CostEstimate(flops=0, bytes_accessed=20 * R * W * Z, transcendentals=0),
    )(x)


HEADS = 17
EPSILON = 1e-05
FS = ("zz", "core")


def norm_parts(v):
    mean = jnp.mean(v, axis=-1, keepdims=True)
    c = v - mean
    r = lax.rsqrt(jnp.mean(c * c, axis=-1, keepdims=True) + EPSILON)
    return c * r, r


def norm_back(dn, v, gain):
    xhat, r = norm_parts(v)
    y = dn * gain
    a = jnp.mean(y, axis=-1, keepdims=True)
    b = jnp.mean(y * xhat, axis=-1, keepdims=True)
    return r * (y - a - xhat * b), jnp.sum(dn * xhat, axis=0), jnp.sum(dn, axis=0)


def col_sum(x):
    return jnp.dot(jnp.ones((16, x.shape[0]), bf16), x, preferred_element_type=f32)[0]


def gelu_parts(u):
    t = 1.0 / (1.0 + 0.2316418882 * jnp.abs(u))
    e = jnp.exp2(u * u * -0.7213475204444817)
    poly = 0.127414796 + t * (-0.142248368 + t * (0.7107068705 + t * (-0.7265760135 + t * 0.5307027145)))
    half = e * (t * poly)
    cdf = jnp.where(u >= 0, 1.0 - half, half)
    return u * cdf, cdf + (u * 0.3989422804014327) * e


def local(
    tokens, cotangent, lengths, block_order,
    ln1_gain, ln1_bias, qkv_weight, q_bias, v_bias, out_weight, out_bias,
    ln2_gain, ln2_bias, up_weight, up_bias, down_weight, down_bias,
    *, G, S,
):
    slots, rows, width = tokens.shape
    C = lax.axis_size("ctx")
    me = lax.axis_index("ctx")
    N = rows * C
    B = rows // 2
    NB = 2 * C
    L = ln1_gain.shape[0]
    shard = ln1_gain.shape[1]
    HW = G * 128
    x_tokens = tokens[0]

    steps = jnp.arange(NB, dtype=jnp.int32)
    order = block_order[0]
    inverse = jnp.sum(jnp.where(order[None, :] == steps[:, None], steps[None, :], 0), axis=1).astype(jnp.int32)
    count = (lengths + (B - 1)) // B
    meta = jnp.concatenate([inverse, count])
    def swap(x):
        return lax.ppermute(x, "core", [(0, 1), (1, 0)])

    metas = [meta, swap(meta)][:S]
    phase_inv = [t[None, :NB] for t in metas]
    phase_nb = [t[NB:] for t in metas]
    own = jnp.concatenate([inverse, lax.dynamic_slice_in_dim(order, 2 * me, 2, 0), count])
    own_pos = (lax.dynamic_slice_in_dim(order, 2 * me, 2, 0)[:, None] * B + jnp.arange(B, dtype=jnp.int32)).reshape(rows, 1)
    live = (own_pos < lengths[0]).astype(f32)

    def pack(w):
        parts = []
        for g in range(G):
            parts += [w[:, kind * width + g * 128:kind * width + g * 128 + 128] for kind in range(3)]
        last = width - 64
        parts += [w[:, kind * width + last:kind * width + width] for kind in (1, 2, 0)]
        return jnp.concatenate(parts, axis=1)

    def unpack(w):
        tail = G * 384
        parts = []
        for kind, last in enumerate((128, 0, 64)):
            parts += [w[:, g * 384 + kind * 128:g * 384 + kind * 128 + 128] for g in range(G)]
            parts.append(w[:, tail + last:tail + last + 64])
        return jnp.concatenate(parts, axis=1)

    def fetch(w):
        return lax.all_gather(w.astype(bf16), FS, axis=0, tiled=True)

    vectors = [ln1_gain, ln1_bias, q_bias, v_bias, out_bias, ln2_gain, ln2_bias, down_bias]
    vec = [t.astype(bf16).T for t in vectors] + [up_bias.astype(bf16).reshape(4 * L, shard).T]
    first = pack(qkv_weight[0].astype(bf16))
    block = jnp.concatenate([first] + vec, axis=1)
    used = block.shape[1]
    if C == 4 and lax.axis_size("zz") == 4:
        block = jnp.pad(block, ((0, 0), (0, -used % (128 * C))))
        block = gather_all(block, 4, C)
    else:
        block = lax.all_gather(block, FS)
    first_w = block[:, :, :3 * width].reshape(width, 3 * width)
    vec = jnp.transpose(block[:, :, 3 * width:used].reshape(width, used - 3 * width)).astype(f32)

    def vector(index, layer):
        if index < 8:
            return vec[L * index + layer]
        t = vec[8 * L + 4 * layer:8 * L + 4 * layer + 4]
        return jnp.transpose(t.reshape(4, -1, shard), (1, 0, 2)).reshape(-1)

    weights = []
    for layer in range(L):
        weights.append((
            fetch(pack(qkv_weight[layer].astype(bf16))) if layer else first_w,
            fetch(out_weight[layer]),
            fetch(up_weight[layer]),
            fetch(down_weight[layer]),
        ))

    def plain(x):
        return with_layout_constraint(x, Layout(major_to_minor=tuple(range(x.ndim))))

    def exchange(x):
        return plain(lax.all_to_all(plain(x), "ctx", 0, 0))

    def after(x, *others):
        return lax.optimization_barrier((x,) + others)

    stream = x_tokens.astype(f32)
    records = []
    for layer in range(L):
        qkv_w, out_w, up_w, down_w = weights[layer]
        xhat, _ = norm_parts(stream)
        n1 = (xhat * vector(0, layer) + vector(1, layer)).astype(bf16)
        q_b, v_b = vector(2, layer), vector(3, layer)
        bias = pack(jnp.concatenate([q_b, jnp.zeros_like(q_b), v_b])[None])[0]
        projected = (jnp.dot(n1, qkv_w, preferred_element_type=f32) + bias).astype(bf16)
        wide = [deal(projected, s * C, C, 384) for s in range(S)]
        tail = projected[:, G * 384:]
        if S == 2:
            wide[1] = swap(wide[1])
        kv16 = jnp.broadcast_to(tail[None, :, :128], (C, rows, 128))
        q16 = tail[:, 128:]
        heads, o, lse, o_back = [], [], [], []
        for s in range(S):
            t = wide[s]
            if s == S - 1:
                t = jnp.concatenate([t, kv16], axis=2)
            if s:
                t, heads[0] = after(t, heads[0])
            heads.append(exchange(t).reshape(1, N, -1))
        for s in range(S):
            o_s, lse_s = flash_fwd(heads[s], phase_inv[s], phase_nb[s], B)
            o.append(o_s)
            lse.append(lse_s)
            t = o_s.reshape(C, rows, 128)
            if s:
                t, o_back[0] = after(t, o_back[0])
            o_back.append(exchange(swap(t) if s else t))
        o16, lse16 = one_fwd(q16, heads[-1][0], own, B)
        mixed = join(o_back, o16)
        m = stream + jnp.dot(mixed, out_w, preferred_element_type=f32) + vector(4, layer)
        xhat2, _ = norm_parts(m)
        n2 = (xhat2 * vector(5, layer) + vector(6, layer)).astype(bf16)
        u = jnp.dot(n2, up_w, preferred_element_type=f32) + vector(8, layer)
        a, slope = gelu_parts(u)
        a = a.astype(bf16)
        a, slope = after(a, slope.astype(bf16))
        records.append((stream, n1, heads, q16, o, lse, o16, lse16, mixed, m, n2, a, slope))
        if layer < L - 1:
            stream = m + jnp.dot(a, down_w, preferred_element_type=f32) + vector(7, layer)
    end_a, end_m, end_w, end_b = a, m, down_w, vector(7, L - 1)

    def reduce_fsdp(g):
        return lax.psum_scatter(g.astype(bf16), FS, scatter_dimension=0, tiled=True)

    def reduce_ctx(g):
        return lax.psum(g, "ctx").astype(f32)

    grad = cotangent[0].astype(f32) * live
    matrices = [None] * L
    fours = [None] * L
    ffns = [None] * L
    small = [None] * L

    def ctx_end(mine):
        return exchange(jnp.broadcast_to(mine[None], (C,) + mine.shape))

    def ctx_sum(shards):
        mine, sizes = ctx_begin(shards)
        return ctx_end(mine), sizes

    def ctx_begin(shards):
        pieces = []
        for t in shards:
            if t.shape[1] == width:
                pieces.append(t.reshape(C, -1, width))
            else:
                pieces.append(jnp.transpose(t.reshape(t.shape[0], C, -1), (1, 0, 2)).reshape(C, -1, width))
        sizes = [t.shape[1] for t in pieces]
        parts = exchange(jnp.concatenate(pieces, axis=1))
        mine = jnp.sum(parts.astype(f32), axis=0).astype(bf16)
        return mine, sizes

    def spread(summed, shapes):
        whole, sizes = summed
        out, at = [], 0
        for n, (r, c) in zip(sizes, shapes):
            t = whole[:, at:at + n].astype(f32)
            at += n
            if c == width:
                out.append(t.reshape(r, c))
            else:
                out.append(jnp.transpose(t.reshape(C, r, c // C), (1, 0, 2)).reshape(r, c))
        return out

    wide_shape, tall_shape = (shard, 4 * width), (4 * shard, width)
    for layer in reversed(range(L)):
        stream_in, n1, heads, q16, o, lse, o16, lse16, mixed, m, n2, a, slope = records[layer]
        qkv_w, out_w, up_w, down_w = weights[layer]
        gb = grad.astype(bf16)
        d_down_b = col_sum(gb)
        d_down = jnp.einsum("rf,rd->fd", a, gb, preferred_element_type=f32).astype(bf16)
        gb, d_down = after(gb, plain(d_down))
        if layer < L - 1:
            above = list(after(gb, *ffns[layer + 1]))
            gb = above.pop(0)
            mine_ffn, ffn_sizes = ctx_begin(above)
        d_down = reduce_fsdp(d_down)
        du = (jnp.einsum("rd,fd->rf", gb, down_w, preferred_element_type=f32) * slope.astype(f32)).astype(bf16)
        d_up_b = col_sum(du)
        if layer < L - 1:
            du, mine_ffn = after(du, mine_ffn)
            ffn_whole = ctx_end(mine_ffn)
        d_up = jnp.einsum("rd,rf->df", n2, du, preferred_element_type=f32).astype(bf16)
        du, d_up = after(du, plain(d_up))
        d_up = reduce_fsdp(d_up)
        dn2 = jnp.einsum("rf,df->rd", du, up_w, preferred_element_type=f32)
        back, d_gain2, d_bias2 = norm_back(dn2, m, vector(5, layer))
        gm = grad + back
        gmb = gm.astype(bf16)
        d_out_b = col_sum(gmb)
        d_out = jnp.einsum("rd,re->de", mixed, gmb, preferred_element_type=f32).astype(bf16)
        if layer == 0:
            gmb, d_out = after(gmb, plain(d_out))
        if layer < L - 1:
            gmb, ffn_whole = after(gmb, ffn_whole)
        d_o = []
        for s in range(S):
            w = out_w[C * 128 * s:C * 128 * (s + 1)].reshape(C, 128, width)
            d_o.append(jnp.einsum("re,gce->grc", gmb, w, preferred_element_type=f32).astype(bf16))
        d_o16 = jnp.einsum("re,ce->rc", gmb, out_w[HW:], preferred_element_type=f32).astype(bf16)
        dq16, dkv16 = one_bwd(q16, heads[-1][0], o16, d_o16, lse16, own, B)
        d_oh, d_wide = [], []
        for s in range(S):
            t = d_o[s]
            if s:
                t = swap(t)
            if s == S - 1:
                t = jnp.concatenate([t, dkv16.reshape(C, rows, 128)], axis=2)
            if s:
                t, d_oh[0] = after(t, d_oh[0])
            if s == S - 1 and layer < L - 1:
                t, fours[layer + 1] = after(t, fours[layer + 1])
            d_oh.append(exchange(t).reshape(1, N, -1))
        dkv16 = jnp.sum(d_oh[-1].reshape(C, rows, 256)[:, :, 128:].astype(f32), axis=0)
        for s in range(S):
            t = flash_bwd(heads[s], o[s], d_oh[s], lse[s], phase_inv[s], phase_nb[s], B)
            t = t.reshape(C, rows, 384)
            if s:
                t, d_wide[0] = after(t, d_wide[0])
            if s == S - 1:
                t, d_down = after(t, d_down)
            if s == S - 1 and layer:
                t, d_up = after(t, d_up)
            d_wide.append(exchange(swap(t) if s else t))
        d_tail = jnp.concatenate([dkv16.astype(bf16), dq16], axis=1)
        d_row = join(d_wide, d_tail)
        d_row, d_down_b, d_up_b, d_out_b = after(d_row, d_down_b, d_up_b, d_out_b)
        d_back = d_row
        if layer == 0:
            d_row, d_up = after(d_row, d_up)
            mine, middle_sizes = ctx_begin([fours[1], d_up, d_down])
            d_back, mine = after(d_row, mine)
            end_a, mine = after(end_a, mine)
            middle = ctx_end(mine)
        d_qkv = jnp.einsum("rd,rc->dc", n1, d_row, preferred_element_type=f32).astype(bf16)
        if layer:
            d_row, d_four = after(d_row, plain(jnp.concatenate([d_qkv, d_out], axis=1)))
            d_four = reduce_fsdp(d_four)
        else:
            d_qkv, d_out = after(d_qkv, reduce_fsdp(d_out))
            d_four = jnp.concatenate([reduce_fsdp(d_qkv), d_out], axis=1)
        sums = unpack(col_sum(d_row)[None])[0]
        dn1 = jnp.einsum("rc,dc->rd", d_back, qkv_w, preferred_element_type=f32)
        back, d_gain1, d_bias1 = norm_back(dn1, stream_in, vector(0, layer))
        grad = gm + back
        fours[layer] = d_four
        ffns[layer] = (d_up, d_down)
        small[layer] = jnp.concatenate([
            t.reshape(-1, n) for t, n in (
                (d_gain1, shard), (d_bias1, shard), (sums[:width], shard), (sums[2 * width:], shard), (d_out_b, shard),
                (d_gain2, shard), (d_bias2, shard), (d_down_b, shard), (d_up_b, 4 * shard))], axis=1)

    vec_grads = jnp.stack(small, axis=1)
    stream = end_m + jnp.dot(end_a, end_w, preferred_element_type=f32) + end_b
    activations = (stream * live).astype(bf16)[None]
    vec_grads, middle, activations = after(vec_grads, middle, activations)
    vec_grads = jnp.sum(lax.all_to_all(vec_grads, FS, 0, 0), axis=0)
    vec_grads = jnp.sum(lax.all_to_all(jnp.broadcast_to(vec_grads[None], (C,) + vec_grads.shape), "ctx", 0, 0), axis=0)
    end, vec_grads = after(fours[0], vec_grads)
    rest = spread((middle, middle_sizes), [wide_shape, wide_shape, tall_shape]) + spread(ctx_sum([end]), [wide_shape])
    matrices[1] = [rest[0]] + spread((ffn_whole, ffn_sizes), [wide_shape, tall_shape])
    matrices[0] = [rest[3], rest[1], rest[2]]
    vg = [vec_grads[:, i * shard:(i + 1) * shard] for i in range(8)] + [vec_grads[:, 8 * shard:]]

    g_qkv = jnp.stack([unpack(matrices[layer][0][:, :3 * width]) for layer in range(L)])
    g_out = jnp.stack([matrices[layer][0][:, 3 * width:] for layer in range(L)])
    g_up = jnp.stack([matrices[layer][1] for layer in range(L)])
    g_down = jnp.stack([matrices[layer][2] for layer in range(L)])
    return (activations, grad[None], vg[0], vg[1], g_qkv, vg[2], vg[3], g_out, vg[4], vg[5], vg[6], g_up, vg[8], g_down, vg[7])


def solution(mesh):
    F, C = mesh.devices.shape
    inner = Mesh(mesh.devices.reshape(F // 2, 2, C), ("zz", "core", "ctx"))
    S = 2 if 16 // (2 * C) >= 2 else 1
    G = S * C
    rows = P(FS, "ctx", None)
    vec, mat = P(None, FS), P(None, FS, None)
    return jax.shard_map(
        functools.partial(local, G=G, S=S),
        mesh=inner,
        in_specs=(rows, rows, P(FS), P(FS, None), vec, vec, mat, vec, vec, mat, vec, vec, vec, mat, vec, mat, vec),
        out_specs=(rows, rows, vec, vec, mat, vec, vec, mat, vec, vec, vec, mat, vec, mat, vec),
        check_vma=False,
    )
```
